32 devices in a mesh: dp: 4 (over x, core), fsdp: 8 (over z, y).
Axes of the slice: x: 2, y: 2, z: 4, core: 2. Of those that a mesh axis runs over, the one named last changes fastest.
Arguments:
- hidden: bfloat16 [4096, 8192], P(('dp', 'fsdp')), may hold values from -6 to 6
- d_attn: bfloat16 [4096, 1024], P(('dp', 'fsdp')), may hold values from -24 to 24
- w_query: bfloat16 [8192, 1024], P('fsdp'), may hold values from -0.0625 to 0.0625
- w_key: bfloat16 [8192, 128], P('fsdp'), may hold values from -0.0625 to 0.0625
- w_value: bfloat16 [8192, 128], P('fsdp'), may hold values from -0.0625 to 0.0625
- cache_keys: bfloat16 [2048, 128], P('fsdp'), may hold values from -700 to 700
- cache_values: bfloat16 [2048, 128], P('fsdp'), may hold values from -6 to 6
- lengths: int32 [4, 4], P('dp'), may hold values from 1 to 768, 1024 in all within a row
Outputs:
- grad_keys: float32 [2048, 128], P('fsdp')
- grad_values: float32 [2048, 128], P('fsdp')
The draws below stay inside these ranges and needn't reach their ends.
Inputs may be any that keep to these rules, and one draw needn't show every extreme that they name: `lengths`: each row sums to 1024 and its longest conversation has exactly 768 tokens.
All inputs are finite; a program needn't handle non-finite values.
Results may differ from the reference program's by a relative error of at most 0.0075.
The reference program's roundings to bfloat16 on the way count: a program that leaves them out, or rounds other values in their place, can miss the bound.
Values may be sent and summed in bfloat16 or wider, within the bound.
No kernel may reach another device: no remote copies, remote signals or barrier semaphores. Data moves between devices by JAX's collectives and lax.ppermute only.
A program may use at most 128 MiB of HBM per device.

```python
import math
import jax
import jax.numpy as jnp
import numpy as np
from jax import lax

D = 8192
HD = 128
QH = 8
CACHE = 2048
CONV_G = 4
TOK_DEV = 128
GROUP_TOK = 1024
MOST = 768
TOKENS = 4096
N_DP = 4
N_FSDP = 8


def draw_cache_keys(key, part):
    first = jax.random.fold_in(key, 0)
    base = jax.random.truncated_normal(first, -6.0, 6.0, (CACHE, HD), jnp.float32)
    return base.astype(jnp.bfloat16)


def levels(rng, shape, cuts, least, top_value):
    loudness, own = 1.0, jax.random.fold_in(rng, 6)
    for dim, parts in cuts:
        steps = jnp.exp(jax.random.uniform(jax.random.fold_in(own, dim), (parts,), jnp.float32, least / len(cuts), top_value / len(cuts)))
        loudness = loudness * jnp.repeat(steps, shape[dim] // parts).reshape([-1 if axis == dim else 1 for axis in range(len(shape))])
    return loudness


def split_up(amount, total, reach, skew):
    loads = [(1 << 20) // math.isqrt(standing ** skew) + 1 for standing in range(2, amount + 1)]
    rest, given = total - reach - (amount - 1), [1] * (amount - 1)
    while rest > 0:
        candidates = [i for i in range(amount - 1) if given[i] < reach]
        whole, left = sum([loads[i] for i in candidates]), rest
        for i in candidates:
            more = min(reach - given[i], max(1, left * loads[i] // whole), rest)
            given[i] = given[i] + more
            rest = rest - more
    return np.array([reach] + given)


def uneven_parts(rng, count, total, reach, slope):
    if count == 2:
        one = jax.random.randint(rng, (), max(1, total - reach), min(reach, total - 1) + 1)
        return jnp.stack([one, total - one])
    sizes = jnp.asarray(split_up(count, total, reach, slope), jnp.int32)
    twos = (count - 1) // 2
    source_of, receiver = sizes[1:1 + 2 * twos:2], sizes[2:2 + 2 * twos:2]
    slack = jnp.minimum(source_of - 1, reach - receiver)
    passed = jax.random.randint(jax.random.fold_in(rng, 1), (twos,), 0, 1 << 20) % (slack + 1)
    sizes = sizes.at[1:1 + 2 * twos:2].set(source_of - passed).at[2:2 + 2 * twos:2].set(receiver + passed)
    return sizes[jax.random.permutation(jax.random.fold_in(rng, 2), count)]


def normal_values(key, shape, width, most, cuts=(), held_as=jnp.bfloat16):
    result = width * jax.random.normal(key, shape, jnp.float32)
    if cuts:
        result = result * levels(key, shape, cuts, -0.22, 0.18)
    return jnp.clip(result, -most, most).astype(held_as)


def setup_inputs(seed: int = 0) -> dict:
    splits = jax.random.split(jax.random.key(seed), 9)
    return {
        "hidden": normal_values(splits[0], (TOKENS, D), 1.0, 6.0, ((0, 32),)),
        "d_attn": normal_values(splits[1], (TOKENS, QH * HD), 4.0, 24.0, ((0, 32),)),
        "w_query": normal_values(splits[2], (D, QH * HD), D ** -0.5, 0.0625, ((0, 8),)),
        "w_key": normal_values(splits[3], (D, HD), D ** -0.5, 0.0625, ((0, 8),)),
        "w_value": normal_values(splits[4], (D, HD), D ** -0.5, 0.0625, ((0, 8),)),
        "cache_keys": draw_cache_keys(jax.random.fold_in(splits[8], 71), 0),
        "cache_values": normal_values(splits[6], (CACHE, HD), 1.0, 6.0, ((0, 8),)),
        "lengths": jax.vmap(lambda own: uneven_parts(own, CONV_G, GROUP_TOK, MOST, 2))(jax.random.split(splits[7], N_DP)).reshape((N_DP, CONV_G)).astype(jnp.int32),
    }


def reference(hidden, d_attn, w_query, w_key, w_value, cache_keys, cache_values, lengths):
    group_tok = TOK_DEV * N_FSDP
    scale = HD ** -0.5
    hid = hidden.reshape(N_DP, group_tok, D)
    grads = d_attn.reshape(N_DP, group_tok, QH * HD)

    def step(carry, item):
        xg, dg, lens = item
        query = jnp.dot(xg, w_query, preferred_element_type=jnp.float32).astype(jnp.bfloat16)
        keys = jnp.dot(xg, w_key, preferred_element_type=jnp.float32).astype(jnp.bfloat16)
        values = jnp.dot(xg, w_value, preferred_element_type=jnp.float32).astype(jnp.bfloat16)
        ends = jnp.cumsum(lens).astype(jnp.int32)
        position = jnp.arange(group_tok).astype(jnp.int32)
        conv = jnp.sum((position[:, None] >= ends[None, :]).astype(jnp.int32), axis=1)
        rows_q = query.reshape(group_tok * QH, HD)
        rows_d = dg.reshape(group_tok * QH, HD)
        q_pos = jnp.repeat(position, QH)
        q_conv = jnp.repeat(conv, QH)
        allowed = (q_conv[:, None] == conv[None, :]) & (position[None, :] <= q_pos[:, None])
        dims = (((1,), (1,)), ((), ()))
        s_cache = lax.dot_general(rows_q, cache_keys, dims, preferred_element_type=jnp.float32) * scale
        s_group = lax.dot_general(rows_q, keys, dims, preferred_element_type=jnp.float32) * scale
        top = jnp.maximum(jnp.max(s_cache, axis=1), jnp.max(jnp.where(allowed, s_group, -jnp.inf), axis=1))
        e_cache = jnp.exp(s_cache - top[:, None])
        e_group = jnp.where(allowed, jnp.exp(s_group - top[:, None]), jnp.float32(0.0))
        total = jnp.sum(e_cache, axis=1) + jnp.sum(e_group, axis=1)
        p_cache = e_cache / total[:, None]
        probs_cache = p_cache.astype(jnp.bfloat16)
        probs_group = (e_group / total[:, None]).astype(jnp.bfloat16)
        attended = jnp.dot(probs_cache, cache_values, preferred_element_type=jnp.float32) + jnp.dot(probs_group, values, preferred_element_type=jnp.float32)
        delta = jnp.sum(rows_d.astype(jnp.float32) * attended, axis=1)
        d_probs = lax.dot_general(rows_d, cache_values, dims, preferred_element_type=jnp.float32)
        d_score = (p_cache * (d_probs - delta[:, None])).astype(jnp.bfloat16)
        back = (((0,), (0,)), ((), ()))
        grad_v = lax.dot_general(probs_cache, rows_d, back, preferred_element_type=jnp.float32)
        grad_k = lax.dot_general(d_score, rows_q, back, preferred_element_type=jnp.float32) * scale
        return (carry[0] + grad_k, carry[1] + grad_v), None

    start = (jnp.zeros((CACHE, HD), jnp.float32), jnp.zeros((CACHE, HD), jnp.float32))
    (grad_keys, grad_values), _ = lax.scan(step, start, (hid, grads, lengths))
    return grad_keys, grad_values
```

```python
import jax
import jax.numpy as jnp
from jax import lax
from jax.sharding import PartitionSpec as P


def swap(value, axis, size, bit):
    return lax.ppermute(value, axis, [(i, i ^ bit) for i in range(size)])


def make_on_device(n_dp, n_fsdp):
    inner = n_fsdp // 2

    def on_device(hidden, d_attn, w_query, w_key, w_value, cache_keys, cache_values, lengths):
        tokens_here, width = hidden.shape
        rows_w = w_query.shape[0]
        q_width = w_query.shape[1]
        head_dim = w_key.shape[1]
        heads = q_width // head_dim
        scale = head_dim ** (-0.5)
        me = lax.axis_index("fsdp")
        dp = lax.axis_index("dp")

        share = rows_w // n_dp
        w_own = jnp.concatenate([w_query, w_key, w_value], axis=1)
        cols = w_own.shape[1]
        part = lax.dynamic_slice_in_dim(w_own, dp * share, share, 0)
        part = swap(part, "fsdp", n_fsdp, inner)
        piece = part[None]
        order = [0]
        bit = n_dp // 2
        while bit:
            other = swap(piece, "dp", n_dp, bit)
            piece = jnp.concatenate([piece, other])
            order = order + [o ^ bit for o in order]
            bit //= 2
        w_far = piece.reshape(rows_w, cols)

        def columns_for(k):
            near = lax.dynamic_slice_in_dim(hidden, (me ^ k) * rows_w, rows_w, 1)
            start = (me ^ k ^ inner) * rows_w
            far = [
                lax.dynamic_slice_in_dim(hidden, start + (dp ^ o) * share, share, 1) for o in order
            ]
            return jnp.concatenate([near] + far, axis=1)

        w_both = jnp.concatenate([w_own, w_far], axis=0)
        total = None
        for k in list(range(1, inner)) + [0]:
            block = columns_for(k)
            if k:
                block = swap(block, "fsdp", n_fsdp, k)
            product = jnp.dot(block, w_both, preferred_element_type=jnp.float32)
            if k:
                product = swap(product, "fsdp", n_fsdp, k)
            total = product if total is None else total + product
        projected = total.astype(jnp.bfloat16)
        query = projected[:, :q_width]
        kv_own = projected[:, q_width:]

        def gather(block):
            got = [block] + [swap(block, "fsdp", n_fsdp, k) for k in range(1, n_fsdp)]
            size = block.shape[0]
            out = jnp.zeros((n_fsdp * size,) + block.shape[1:], block.dtype)
            for k, value in enumerate(got):
                out = lax.dynamic_update_slice_in_dim(out, value, (me ^ k) * size, 0)
            return out

        cache = gather(jnp.concatenate([cache_keys, cache_values], axis=1))
        cache_k, cache_v = cache[:, :head_dim], cache[:, head_dim:]
        group = gather(kv_own)
        group_k, group_v = group[:, :head_dim], group[:, head_dim:]

        group_tok = group_k.shape[0]
        ends = jnp.cumsum(lengths[0])
        position = jnp.arange(group_tok, dtype=jnp.int32)
        conv = jnp.sum((position[:, None] >= ends[None, :]).astype(jnp.int32), axis=1)
        own = me * tokens_here + jnp.arange(tokens_here, dtype=jnp.int32)
        own_conv = jnp.sum((own[:, None] >= ends[None, :]).astype(jnp.int32), axis=1)
        q_pos = jnp.repeat(own, heads)
        q_conv = jnp.repeat(own_conv, heads)
        allowed = (q_conv[:, None] == conv[None, :]) & (position[None, :] <= q_pos[:, None])
        rows_q = query.reshape(tokens_here * heads, head_dim)
        rows_d = d_attn.reshape(tokens_here * heads, head_dim)
        dims = (((1,), (1,)), ((), ()))
        s_cache = lax.dot_general(rows_q, cache_k, dims, preferred_element_type=jnp.float32) * scale
        s_group = lax.dot_general(rows_q, group_k, dims, preferred_element_type=jnp.float32) * scale
        top = jnp.maximum(
            jnp.max(s_cache, axis=1), jnp.max(jnp.where(allowed, s_group, -jnp.inf), axis=1)
        )
        e_cache = jnp.exp(s_cache - top[:, None])
        e_group = jnp.where(allowed, jnp.exp(s_group - top[:, None]), jnp.float32(0.0))
        total = jnp.sum(e_cache, axis=1) + jnp.sum(e_group, axis=1)
        p_cache = e_cache / total[:, None]
        probs_cache = p_cache.astype(jnp.bfloat16)
        probs_group = (e_group / total[:, None]).astype(jnp.bfloat16)
        attended = jnp.dot(probs_cache, cache_v, preferred_element_type=jnp.float32) + jnp.dot(
            probs_group, group_v, preferred_element_type=jnp.float32
        )
        delta = jnp.sum(rows_d.astype(jnp.float32) * attended, axis=1)
        d_probs = lax.dot_general(rows_d, cache_v, dims, preferred_element_type=jnp.float32)
        d_score = (p_cache * (d_probs - delta[:, None])).astype(jnp.bfloat16)
        back = (((0,), (0,)), ((), ()))
        grad_v = lax.dot_general(probs_cache, rows_d, back, preferred_element_type=jnp.float32)
        grad_k = (
            lax.dot_general(d_score, rows_q, back, preferred_element_type=jnp.float32) * scale
        )

        odd = dp % 2
        keep = jnp.where(odd == 0, grad_k, grad_v)
        give = jnp.where(odd == 0, grad_v, grad_k)
        half = keep + swap(give, "dp", n_dp, 1)
        size = half.shape[0] // n_fsdp
        mine = lax.dynamic_slice_in_dim(half, me * size, size, 0)
        for k in range(1, n_fsdp):
            out = lax.dynamic_slice_in_dim(half, (me ^ k) * size, size, 0)
            mine = mine + swap(out, "fsdp", n_fsdp, k)
        bit = n_dp // 2
        while bit > 1:
            mine = mine + swap(mine, "dp", n_dp, bit)
            bit //= 2
        other = swap(mine, "dp", n_dp, 1)
        return jnp.where(odd == 0, mine, other), jnp.where(odd == 0, other, mine)

    return on_device


def solution(mesh):
    placed = (
        P(("dp", "fsdp"), None),
        P(("dp", "fsdp"), None),
        P("fsdp", None),
        P("fsdp", None),
        P("fsdp", None),
        P("fsdp", None),
        P("fsdp", None),
        P("dp", None),
    )
    return jax.shard_map(
        make_on_device(mesh.shape["dp"], mesh.shape["fsdp"]),
        mesh=mesh,
        in_specs=placed,
        out_specs=(P("fsdp", None), P("fsdp", None)),
        check_vma=False,
    )
```

```python
import functools
import math

import jax
import jax.numpy as jnp
from jax import lax
from jax.experimental import pallas as pl
from jax.experimental.pallas import tpu as pltpu
from jax.sharding import PartitionSpec as P

F32 = jnp.float32
BF16 = jnp.bfloat16
VMEM_LIMIT = 56 * 1024 * 1024


def swap(value, axis, size, bit):
    return lax.ppermute(value, axis, [(i, i ^ bit) for i in range(size)])


def bits_down(size):
    bits = []
    bit = size // 2
    while bit:
        bits.append(bit)
        bit //= 2
    return bits


def doubled(block, axis, size):
    block, order = block[None], [0]
    for bit in bits_down(size):
        block = jnp.concatenate([block, swap(block, axis, size, bit)])
        order = order + [o ^ bit for o in order]
    return block, order


def params():
    return pltpu.CompilerParams(vmem_limit_bytes=VMEM_LIMIT)


def run_copies(copies):
    for copy in copies:
        copy.start()
    for copy in copies:
        copy.wait()


def prepare(where, hidden, w_query, w_key, w_value, n_dp, n_fsdp, q_cut):
    inner = n_fsdp // 2
    tokens = hidden.shape[0]
    rows_w, q_width = w_query.shape
    head_dim = w_key.shape[1]
    share = rows_w // n_dp

    def body(where_ref, hidden_ref, wq_ref, wk_ref, wv_ref, *rest):
        sent, part_a, part_b, sems = rest[: inner - 1], rest[-3], rest[-2], rest[-1]
        me, dp = where_ref[0], where_ref[1]
        rows = pl.ds(pl.multiple_of(dp * share, 16), share)
        pairs = [
            (wk_ref.at[rows], part_a.at[:, pl.ds(0, head_dim)]),
            (wv_ref.at[rows], part_a.at[:, pl.ds(head_dim, head_dim)]),
            (wq_ref.at[rows, pl.ds(0, q_cut)], part_a.at[:, pl.ds(2 * head_dim, q_cut)]),
            (wq_ref.at[rows, pl.ds(q_cut, q_width - q_cut)], part_b),
        ]
        for k in range(1, inner):
            for side, bit in enumerate((0, inner)):
                start = pl.multiple_of((me ^ k ^ bit) * rows_w, 128)
                pairs.append(
                    (hidden_ref.at[:, pl.ds(start, rows_w)], sent[k - 1].at[:, pl.ds(side * rows_w, rows_w)])
                )
        run_copies([pltpu.make_async_copy(a, b, sems.at[i]) for i, (a, b) in enumerate(pairs)])

    moved = 2 * (tokens * 2 * rows_w * 2 * (inner - 1) + share * (q_width + 2 * head_dim) * 2)
    out = pl.pallas_call(
        body,
        in_specs=[pl.BlockSpec(memory_space=pltpu.SMEM)] + [pl.BlockSpec(memory_space=pl.ANY)] * 4,
        out_specs=[pl.BlockSpec(memory_space=pl.ANY)] * (inner + 1),
        out_shape=[jax.ShapeDtypeStruct((tokens, 2 * rows_w), BF16)] * (inner - 1)
        + [
            jax.ShapeDtypeStruct((share, 2 * head_dim + q_cut), BF16),
            jax.ShapeDtypeStruct((share, q_width - q_cut), BF16),
        ],
        scratch_shapes=[pltpu.SemaphoreType.DMA((4 + 2 * (inner - 1),))],
        compiler_params=params(),
        cost_estimate=pl.CostEstimate(flops=0, bytes_accessed=moved, transcendentals=0),
        name="prepare",
    )(where, hidden, w_query, w_key, w_value)
    return out[: inner - 1], out[-2], out[-1]


def multiply(where, hidden, received, near, far, order, n_fsdp):
    inner = n_fsdp // 2
    tokens = hidden.shape[0]
    n_dp, share, cols = far.shape
    rows_w = n_dp * share
    step = math.gcd(cols, 256)
    spans = []
    at = 0
    for _, start, wide in near:
        spans.append((start, at, wide))
        at += wide

    def body(where_ref, hidden_ref, *rest):
        blocks = rest[: inner - 1]
        near_refs = rest[inner - 1 : inner - 1 + len(near)]
        far_ref = rest[inner - 1 + len(near)]
        outs = rest[inner + len(near) : 2 * inner + len(near)]
        x_all, w_all, sems = rest[-3:]
        me, dp = where_ref[0], where_ref[1]
        pairs = []
        for side, bit in enumerate((0, inner)):
            start = pl.multiple_of((me ^ bit) * rows_w, 128)
            pairs.append(
                (
                    hidden_ref.at[:, pl.ds(start, rows_w)],
                    x_all.at[pl.ds(0, tokens), pl.ds(side * rows_w, rows_w)],
                )
            )
        for k in range(1, inner):
            pairs.append((blocks[k - 1], x_all.at[pl.ds(k * tokens, tokens)]))
        for ref, (start, to, wide) in zip(near_refs, spans):
            pairs.append((ref.at[:, pl.ds(start, wide)], w_all.at[pl.ds(0, rows_w), pl.ds(to, wide)]))
        for slot, o in enumerate(order):
            to = pl.multiple_of(rows_w + (dp ^ o) * share, 16)
            pairs.append((far_ref.at[slot], w_all.at[pl.ds(to, share)]))
        run_copies([pltpu.make_async_copy(a, b, sems.at[i]) for i, (a, b) in enumerate(pairs)])

        @pl.loop(0, cols // step)
        def _(n):
            at = pl.multiple_of(n * step, 128)
            product = jnp.dot(x_all[...], w_all[:, pl.ds(at, step)], preferred_element_type=F32)
            for k in range(inner):
                outs[k][:, pl.ds(at, step)] = product[k * tokens : (k + 1) * tokens]

    copies = 2 + (inner - 1) + len(near) + n_dp
    moved = inner * tokens * 2 * rows_w * 2 + 2 * rows_w * cols * 2 + inner * tokens * cols * 4
    return pl.pallas_call(
        body,
        in_specs=[pl.BlockSpec(memory_space=pltpu.SMEM)]
        + [pl.BlockSpec(memory_space=pl.ANY)] * (inner + len(near) + 1),
        out_specs=[pl.BlockSpec(memory_space=pltpu.VMEM)] * inner,
        out_shape=[jax.ShapeDtypeStruct((tokens, cols), F32)] * inner,
        scratch_shapes=[
            pltpu.VMEM((inner * tokens, 2 * rows_w), BF16),
            pltpu.VMEM((2 * rows_w, cols), BF16),
            pltpu.SemaphoreType.DMA((copies,)),
        ],
        compiler_params=params(),
        cost_estimate=pl.CostEstimate(
            flops=2 * inner * tokens * 2 * rows_w * cols, bytes_accessed=moved, transcendentals=0
        ),
        name="multiply",
    )(where, hidden, *received, *[ref for ref, _, _ in near], far)


def attend(where, lengths, parts, q_at, d_attn, first_head, n_heads, cache, group, f_order, sums):
    tokens = d_attn.shape[0]
    n_blocks, block, twice = cache.shape
    head_dim = twice // 2
    n_convs = lengths.shape[1]
    scale = head_dim ** (-0.5)
    to_log2 = scale * math.log2(math.e)
    pair = 2 if n_heads % 2 == 0 else 1
    lanes = pair * tokens
    n_cache = n_blocks * block
    n_group = n_blocks * tokens
    chunk = 512
    n_sum = len(sums)
    n_part = len(parts)

    def body(where_ref, len_ref, d_ref, cache_ref, group_ref, *rest):
        part_refs = rest[:n_part]
        sum_refs = rest[n_part : n_part + n_sum]
        keep_ref, give_ref, gk, gv, s_ref, p_ref, q_ref = rest[n_part + n_sum :]
        me, dp = where_ref[0], where_ref[1]

        q_all = part_refs[0][:, pl.ds(q_at, n_heads * head_dim)]
        for ref in part_refs[1:]:
            q_all = q_all + ref[:, pl.ds(q_at, n_heads * head_dim)]
        q_all = q_all.astype(BF16)
        for h in range(n_heads):
            q_ref[h, 0] = q_all[:, h * head_dim : (h + 1) * head_dim]
            at = (first_head + h) * head_dim
            q_ref[h, 1] = d_ref[:, at : at + head_dim]

        q_pos = me * tokens + lax.broadcasted_iota(jnp.int32, (1, lanes), 1) % tokens
        begin = jnp.zeros((1, lanes), jnp.int32)
        end = jnp.int32(0)
        for i in range(n_convs):
            end = end + len_ref[0, i]
            begin = jnp.where(end <= q_pos, end, begin)

        @pl.loop(0, n_heads // pair)
        def _(step):
            rows_q = jnp.concatenate([q_ref[step * pair + i, 0] for i in range(pair)], axis=0)
            rows_d = jnp.concatenate([q_ref[step * pair + i, 1] for i in range(pair)], axis=0)
            dims = (((1,), (1,)), ((), ()))
            top = jnp.full((1, lanes), -jnp.inf, F32)
            cache_spans = [
                (b, r, min(chunk, block)) for b in range(n_blocks) for r in range(0, block, min(chunk, block))
            ]
            for b, r, size in cache_spans:
                s = lax.dot_general(
                    cache_ref[b, r : r + size, :head_dim], rows_q, dims, preferred_element_type=F32
                )
                s_ref[pl.ds(b * block + r, size)] = s
                top = jnp.maximum(top, jnp.max(s, axis=0, keepdims=True))
            for b in range(n_blocks):
                s = lax.dot_general(group_ref[b, :, :head_dim], rows_q, dims, preferred_element_type=F32)
                pos = (me ^ f_order[b]) * tokens + lax.broadcasted_iota(jnp.int32, (tokens, lanes), 0)
                s = jnp.where((pos <= q_pos) & (pos >= begin), s, -jnp.inf)
                s_ref[pl.ds(n_cache + b * tokens, tokens)] = s
                top = jnp.maximum(top, jnp.max(s, axis=0, keepdims=True))
            total = jnp.zeros((1, lanes), F32)
            for r in range(0, n_cache + n_group, chunk):
                e = jnp.exp2((s_ref[pl.ds(r, chunk)] - top) * to_log2)
                s_ref[pl.ds(r, chunk)] = e
                total = total + jnp.sum(e, axis=0, keepdims=True)
            inv = 1.0 / total
            delta = jnp.zeros((1, lanes), F32)
            for b in range(n_blocks):
                p = s_ref[pl.ds(n_cache + b * tokens, tokens)] * inv
                dp_ = lax.dot_general(group_ref[b, :, head_dim:], rows_d, dims, preferred_element_type=F32)
                delta = delta + jnp.sum(p.astype(BF16).astype(F32) * dp_, axis=0, keepdims=True)
            first = n_sum == 0
            for b, r, size in cache_spans:
                at = pl.ds(b * block + r, size)
                p = s_ref[at] * inv
                pb = p.astype(BF16)
                dp_ = lax.dot_general(
                    cache_ref[b, r : r + size, head_dim:], rows_d, dims, preferred_element_type=F32
                )
                s_ref[at] = p
                p_ref[at] = dp_
                delta = delta + jnp.sum(pb.astype(F32) * dp_, axis=0, keepdims=True)
                g = jnp.dot(pb, rows_d, preferred_element_type=F32)
                before = gv[at] if first else gv[at]
                gv[at] = jnp.where(step == 0, 0.0, before) + g
            for b, r, size in cache_spans:
                at = pl.ds(b * block + r, size)
                ds = (s_ref[at] * (p_ref[at] - delta)).astype(BF16)
                g = jnp.dot(ds, rows_q, preferred_element_type=F32)
                gk[at] = jnp.where(step == 0, 0.0, gk[at]) + g

        even = dp % 2 == 0
        if n_sum:
            keep_in, give_in = sum_refs[0][...], sum_refs[1][...]
        else:
            keep_in = give_in = 0.0

        @pl.when(even)
        def _():
            keep_ref[...] = keep_in + gk[...] * scale
            give_ref[...] = give_in + gv[...]

        @pl.when(jnp.logical_not(even))
        def _():
            keep_ref[...] = keep_in + gv[...]
            give_ref[...] = give_in + gk[...] * scale

    rows = n_heads * tokens
    flops = 2 * rows * head_dim * (5 * n_cache + 2 * n_group)
    return pl.pallas_call(
        body,
        in_specs=[pl.BlockSpec(memory_space=pltpu.SMEM)] * 2
        + [pl.BlockSpec(memory_space=pltpu.VMEM)] * (3 + n_part + n_sum),
        out_specs=[pl.BlockSpec(memory_space=pltpu.VMEM)] * 2,
        out_shape=[jax.ShapeDtypeStruct((n_cache, head_dim), F32)] * 2,
        scratch_shapes=[
            pltpu.VMEM((n_cache, head_dim), F32),
            pltpu.VMEM((n_cache, head_dim), F32),
            pltpu.VMEM((n_cache + n_group, lanes), F32),
            pltpu.VMEM((n_cache, lanes), F32),
            pltpu.VMEM((n_heads, 2, tokens, head_dim), BF16),
        ],
        compiler_params=params(),
        cost_estimate=pl.CostEstimate(
            flops=flops,
            bytes_accessed=12 * n_cache * head_dim,
            transcendentals=rows * (n_cache + n_group),
        ),
        name="attend",
    )(where, lengths, d_attn, cache, group, *parts, *sums)


def make_on_device(n_dp, n_fsdp):
    inner = n_fsdp // 2

    def on_device(hidden, d_attn, w_query, w_key, w_value, cache_keys, cache_values, lengths):
        head_dim = w_key.shape[1]
        q_width = w_query.shape[1]
        heads = q_width // head_dim
        me = lax.axis_index("fsdp")
        dp = lax.axis_index("dp")
        where = jnp.stack([me, dp]).astype(jnp.int32)
        heads_a = heads // 4
        q_cut = heads_a * head_dim

        sent, part_a, part_b = prepare(
            where, hidden, w_query, w_key, w_value, n_dp, n_fsdp, q_cut
        )
        part_a = swap(part_a, "fsdp", n_fsdp, inner)
        received = [swap(block, "fsdp", n_fsdp, k + 1) for k, block in enumerate(sent)]
        part_b = swap(part_b, "fsdp", n_fsdp, inner)
        cache, f_order = doubled(
            jnp.concatenate([cache_keys, cache_values], axis=1), "fsdp", n_fsdp
        )
        part_a, *received = lax.optimization_barrier((part_a, *received))
        far_a, d_order = doubled(part_a, "dp", n_dp)
        far_b, _ = doubled(part_b, "dp", n_dp)

        near_a = [(w_key, 0, head_dim), (w_value, 0, head_dim), (w_query, 0, q_cut)]
        near_b = [(w_query, q_cut, q_width - q_cut)]
        own_a, *away_a = multiply(where, hidden, received, near_a, far_a, d_order, n_fsdp)
        own_b, *away_b = multiply(where, hidden, received, near_b, far_b, d_order, n_fsdp)
        parts_a = [own_a] + [swap(x, "fsdp", n_fsdp, k + 1) for k, x in enumerate(away_a)]
        parts_b = [own_b] + [swap(x, "fsdp", n_fsdp, k + 1) for k, x in enumerate(away_b)]
        kv_own = functools.reduce(lambda a, b: a + b, [x[:, : 2 * head_dim] for x in parts_a])
        group, _ = doubled(kv_own.astype(BF16), "fsdp", n_fsdp)

        sums = attend(
            where, lengths, parts_a, 2 * head_dim, d_attn, 0, heads_a, cache, group, f_order, ()
        )
        keep, give = attend(
            where, lengths, parts_b, 0, d_attn, heads_a, heads - heads_a, cache, group, f_order, sums
        )

        half = keep + swap(give, "dp", n_dp, 1)
        size = half.shape[0] // n_fsdp
        mine = half[:size]
        for slot in range(1, n_fsdp):
            out = half[slot * size : (slot + 1) * size].astype(BF16)
            mine = mine + swap(out, "fsdp", n_fsdp, f_order[slot]).astype(F32)
        for bit in bits_down(n_dp)[:-1]:
            mine = mine + swap(mine, "dp", n_dp, bit)
        other = swap(mine, "dp", n_dp, 1)
        even = dp % 2 == 0
        return jnp.where(even, mine, other), jnp.where(even, other, mine)

    return on_device


def solution(mesh):
    placed = (
        P(("dp", "fsdp"), None),
        P(("dp", "fsdp"), None),
        P("fsdp", None),
        P("fsdp", None),
        P("fsdp", None),
        P("fsdp", None),
        P("fsdp", None),
        P("dp", None),
    )
    return jax.shard_map(
        make_on_device(mesh.shape["dp"], mesh.shape["fsdp"]),
        mesh=mesh,
        in_specs=placed,
        out_specs=(P("fsdp", None), P("fsdp", None)),
        check_vma=False,
    )
```

```python
import functools
import math

import jax
import jax.numpy as jnp
from jax import lax
from jax.experimental import pallas as pl
from jax.experimental.pallas import tpu as pltpu
from jax.sharding import PartitionSpec as P

F32 = jnp.float32
BF16 = jnp.bfloat16
VMEM_LIMIT = 56 * 1024 * 1024


def swap(value, axis, size, bit):
    return lax.ppermute(value, axis, [(i, i ^ bit) for i in range(size)])


def bits_down(size):
    bits = []
    bit = size // 2
    while bit:
        bits.append(bit)
        bit //= 2
    return bits


def double(block, order, axis, size, bit):
    return jnp.concatenate([block, swap(block, axis, size, bit)]), order + [o ^ bit for o in order]


def finish(block, order, axis, size, bits):
    for bit in bits:
        block, order = double(block, order, axis, size, bit)
    return block, order


def together(*values):
    return lax.optimization_barrier(values)


def params():
    return pltpu.CompilerParams(vmem_limit_bytes=VMEM_LIMIT)


def run_copies(copies):
    for copy in copies:
        copy.start()
    for copy in copies:
        copy.wait()


def prepare(where, hidden, w_query, w_key, w_value, n_dp, n_fsdp, q_cut):
    inner = n_fsdp // 2
    tokens = hidden.shape[0]
    rows_w, q_width = w_query.shape
    head_dim = w_key.shape[1]
    share = rows_w // n_dp

    def body(where_ref, hidden_ref, wq_ref, wk_ref, wv_ref, *rest):
        sent, part_a, part_b, sems = rest[: inner - 1], rest[-3], rest[-2], rest[-1]
        me, dp = where_ref[0], where_ref[1]
        rows = pl.ds(pl.multiple_of(dp * share, 16), share)
        pairs = [
            (wk_ref.at[rows], part_a.at[:, pl.ds(0, head_dim)]),
            (wv_ref.at[rows], part_a.at[:, pl.ds(head_dim, head_dim)]),
            (wq_ref.at[rows, pl.ds(0, q_cut)], part_a.at[:, pl.ds(2 * head_dim, q_cut)]),
            (wq_ref.at[rows, pl.ds(q_cut, q_width - q_cut)], part_b),
        ]
        for k in range(1, inner):
            for side, bit in enumerate((0, inner)):
                start = pl.multiple_of((me ^ k ^ bit) * rows_w, 128)
                pairs.append(
                    (hidden_ref.at[:, pl.ds(start, rows_w)], sent[k - 1].at[:, pl.ds(side * rows_w, rows_w)])
                )
        run_copies([pltpu.make_async_copy(a, b, sems.at[i]) for i, (a, b) in enumerate(pairs)])

    moved = 2 * (tokens * 2 * rows_w * 2 * (inner - 1) + share * (q_width + 2 * head_dim) * 2)
    out = pl.pallas_call(
        body,
        in_specs=[pl.BlockSpec(memory_space=pltpu.SMEM)] + [pl.BlockSpec(memory_space=pl.ANY)] * 4,
        out_specs=[pl.BlockSpec(memory_space=pltpu.VMEM)] * (inner + 1),
        out_shape=[jax.ShapeDtypeStruct((tokens, 2 * rows_w), BF16)] * (inner - 1)
        + [
            jax.ShapeDtypeStruct((share, 2 * head_dim + q_cut), BF16),
            jax.ShapeDtypeStruct((share, q_width - q_cut), BF16),
        ],
        scratch_shapes=[pltpu.SemaphoreType.DMA((4 + 2 * (inner - 1),))],
        compiler_params=params(),
        cost_estimate=pl.CostEstimate(flops=0, bytes_accessed=moved, transcendentals=0),
        name="prepare",
    )(where, hidden, w_query, w_key, w_value)
    return out[: inner - 1], out[-2], out[-1]


def multiply(where, hidden, received, near, far, order, n_fsdp, groups):
    inner = n_fsdp // 2
    tokens = hidden.shape[0]
    n_dp, share, cols = far.shape
    rows_w = n_dp * share
    step = 256 if all(g % 256 == 0 for g in groups) else 128
    spans = []
    at = 0
    for _, start, wide in near:
        spans.append((start, at, wide))
        at += wide

    def body(where_ref, hidden_ref, *rest):
        blocks = rest[: inner - 1]
        near_refs = rest[inner - 1 : inner - 1 + len(near)]
        far_ref = rest[inner - 1 + len(near)]
        outs = rest[inner + len(near) : -3]
        x_all, w_all, sems = rest[-3:]
        me, dp = where_ref[0], where_ref[1]
        pairs = []
        for side, bit in enumerate((0, inner)):
            start = pl.multiple_of((me ^ bit) * rows_w, 128)
            pairs.append(
                (
                    hidden_ref.at[:, pl.ds(start, rows_w)],
                    x_all.at[pl.ds(0, tokens), pl.ds(side * rows_w, rows_w)],
                )
            )
        for k in range(1, inner):
            pairs.append((blocks[k - 1], x_all.at[pl.ds(k * tokens, tokens)]))
        for ref, (start, to, wide) in zip(near_refs, spans):
            pairs.append((ref.at[:, pl.ds(start, wide)], w_all.at[pl.ds(0, rows_w), pl.ds(to, wide)]))
        for slot, o in enumerate(order):
            to = pl.multiple_of(rows_w + (dp ^ o) * share, 16)
            pairs.append((far_ref.at[slot], w_all.at[pl.ds(to, share)]))
        run_copies([pltpu.make_async_copy(a, b, sems.at[i]) for i, (a, b) in enumerate(pairs)])

        base = 0
        for g, wide in enumerate(groups):

            @pl.loop(0, wide // step)
            def _(n, g=g, base=base):
                at = pl.multiple_of(n * step, 128)
                product = jnp.dot(x_all[...], w_all[:, pl.ds(base + at, step)], preferred_element_type=F32)
                for k in range(inner):
                    outs[g * inner + k][:, pl.ds(at, step)] = product[k * tokens : (k + 1) * tokens]

            base += wide

    copies = 2 + (inner - 1) + len(near) + n_dp
    moved = inner * tokens * 2 * rows_w * 2 + 2 * rows_w * cols * 2 + inner * tokens * cols * 4
    out = pl.pallas_call(
        body,
        in_specs=[pl.BlockSpec(memory_space=pltpu.SMEM)]
        + [pl.BlockSpec(memory_space=pl.ANY)] * (inner + len(near) + 1),
        out_specs=[pl.BlockSpec(memory_space=pltpu.VMEM)] * (inner * len(groups)),
        out_shape=[jax.ShapeDtypeStruct((tokens, g), F32) for g in groups for _ in range(inner)],
        scratch_shapes=[
            pltpu.VMEM((inner * tokens, 2 * rows_w), BF16),
            pltpu.VMEM((2 * rows_w, cols), BF16),
            pltpu.SemaphoreType.DMA((copies,)),
        ],
        compiler_params=params(),
        cost_estimate=pl.CostEstimate(
            flops=2 * inner * tokens * 2 * rows_w * cols, bytes_accessed=moved, transcendentals=0
        ),
        name="multiply",
    )(where, hidden, *received, *[ref for ref, _, _ in near], far)
    return [list(out[g * inner : (g + 1) * inner]) for g in range(len(groups))]


def attend(where, lengths, partials, d_attn, cache, group, f_order):
    tokens = d_attn.shape[0]
    n_blocks, block, twice = cache.shape
    head_dim = twice // 2
    n_convs = lengths.shape[1]
    scale = head_dim ** (-0.5)
    to_log2 = scale * math.log2(math.e)
    n_heads = d_attn.shape[1] // head_dim
    pair = 2 if n_heads % 2 == 0 else 1
    lanes = pair * tokens
    n_cache = n_blocks * block
    n_group = n_blocks * tokens
    chunk = 512
    n_part = sum(len(terms) for terms in partials)

    def body(where_ref, len_ref, d_ref, cache_ref, group_ref, *rest):
        part_refs = list(rest[:n_part])
        keep_ref, give_ref, gk, gv, s_ref, p_ref, q_ref = rest[n_part:]
        me, dp = where_ref[0], where_ref[1]

        h = 0
        for terms in partials:
            refs, part_refs = part_refs[: len(terms)], part_refs[len(terms) :]
            for at in range(0, terms[0].shape[1], head_dim):
                q = refs[0][:, at : at + head_dim]
                for ref in refs[1:]:
                    q = q + ref[:, at : at + head_dim]
                q_ref[h, 0] = q.astype(BF16)
                q_ref[h, 1] = d_ref[:, h * head_dim : (h + 1) * head_dim]
                h += 1

        q_pos = me * tokens + lax.broadcasted_iota(jnp.int32, (1, lanes), 1) % tokens
        begin = jnp.zeros((1, lanes), jnp.int32)
        end = jnp.int32(0)
        for i in range(n_convs):
            end = end + len_ref[0, i]
            begin = jnp.where(end <= q_pos, end, begin)

        @pl.loop(0, n_heads // pair)
        def _(step):
            rows_q = jnp.concatenate([q_ref[step * pair + i, 0] for i in range(pair)], axis=0)
            rows_d = jnp.concatenate([q_ref[step * pair + i, 1] for i in range(pair)], axis=0)
            dims = (((1,), (1,)), ((), ()))
            top = jnp.full((1, lanes), -jnp.inf, F32)
            cache_spans = [
                (b, r, min(chunk, block)) for b in range(n_blocks) for r in range(0, block, min(chunk, block))
            ]
            for b, r, size in cache_spans:
                s = lax.dot_general(
                    cache_ref[b, r : r + size, :head_dim], rows_q, dims, preferred_element_type=F32
                )
                s_ref[pl.ds(b * block + r, size)] = s
                top = jnp.maximum(top, jnp.max(s, axis=0, keepdims=True))
            for b in range(n_blocks):
                s = lax.dot_general(group_ref[b, :, :head_dim], rows_q, dims, preferred_element_type=F32)
                pos = (me ^ f_order[b]) * tokens + lax.broadcasted_iota(jnp.int32, (tokens, lanes), 0)
                s = jnp.where((pos <= q_pos) & (pos >= begin), s, -jnp.inf)
                s_ref[pl.ds(n_cache + b * tokens, tokens)] = s
                top = jnp.maximum(top, jnp.max(s, axis=0, keepdims=True))
            total = jnp.zeros((1, lanes), F32)
            for r in range(0, n_cache + n_group, chunk):
                e = jnp.exp2((s_ref[pl.ds(r, chunk)] - top) * to_log2)
                s_ref[pl.ds(r, chunk)] = e
                total = total + jnp.sum(e, axis=0, keepdims=True)
            inv = 1.0 / total
            delta = jnp.zeros((1, lanes), F32)
            for b in range(n_blocks):
                p = s_ref[pl.ds(n_cache + b * tokens, tokens)] * inv
                dp_ = lax.dot_general(group_ref[b, :, head_dim:], rows_d, dims, preferred_element_type=F32)
                delta = delta + jnp.sum(p.astype(BF16).astype(F32) * dp_, axis=0, keepdims=True)
            for b, r, size in cache_spans:
                at = pl.ds(b * block + r, size)
                p = s_ref[at] * inv
                pb = p.astype(BF16)
                dp_ = lax.dot_general(
                    cache_ref[b, r : r + size, head_dim:], rows_d, dims, preferred_element_type=F32
                )
                s_ref[at] = p
                p_ref[at] = dp_
                delta = delta + jnp.sum(pb.astype(F32) * dp_, axis=0, keepdims=True)
                g = jnp.dot(pb, rows_d, preferred_element_type=F32)
                gv[at] = jnp.where(step == 0, 0.0, gv[at]) + g
            for b, r, size in cache_spans:
                at = pl.ds(b * block + r, size)
                ds = (s_ref[at] * (p_ref[at] - delta)).astype(BF16)
                g = jnp.dot(ds, rows_q, preferred_element_type=F32)
                gk[at] = jnp.where(step == 0, 0.0, gk[at]) + g

        even = dp % 2 == 0
        @pl.when(even)
        def _():
            keep_ref[...] = gk[...] * scale
            give_ref[...] = gv[...]

        @pl.when(jnp.logical_not(even))
        def _():
            keep_ref[...] = gv[...]
            give_ref[...] = gk[...] * scale

    rows = n_heads * tokens
    flops = 2 * rows * head_dim * (5 * n_cache + 2 * n_group)
    return pl.pallas_call(
        body,
        in_specs=[pl.BlockSpec(memory_space=pltpu.SMEM)] * 2
        + [pl.BlockSpec(memory_space=pltpu.VMEM)] * (3 + n_part),
        out_specs=[pl.BlockSpec(memory_space=pltpu.VMEM)] * 2,
        out_shape=[jax.ShapeDtypeStruct((n_cache, head_dim), F32)] * 2,
        scratch_shapes=[
            pltpu.VMEM((n_cache, head_dim), F32),
            pltpu.VMEM((n_cache, head_dim), F32),
            pltpu.VMEM((n_cache + n_group, lanes), F32),
            pltpu.VMEM((n_cache, lanes), F32),
            pltpu.VMEM((n_heads, 2, tokens, head_dim), BF16),
        ],
        compiler_params=params(),
        cost_estimate=pl.CostEstimate(
            flops=flops,
            bytes_accessed=12 * n_cache * head_dim,
            transcendentals=rows * (n_cache + n_group),
        ),
        name="attend",
    )(where, lengths, d_attn, cache, group, *[term for terms in partials for term in terms])


def make_on_device(n_dp, n_fsdp):
    inner = n_fsdp // 2

    def on_device(hidden, d_attn, w_query, w_key, w_value, cache_keys, cache_values, lengths):
        head_dim = w_key.shape[1]
        q_width = w_query.shape[1]
        heads = q_width // head_dim
        me = lax.axis_index("fsdp")
        dp = lax.axis_index("dp")
        where = jnp.stack([me, dp]).astype(jnp.int32)
        heads_a = heads // 2
        q_cut = heads_a * head_dim

        def from_owners(products):
            return [products[0]] + [swap(x, "fsdp", n_fsdp, k + 1) for k, x in enumerate(products[1:])]

        f_bits, d_bits = bits_down(n_fsdp), bits_down(n_dp)
        cache = jnp.concatenate([cache_keys, cache_values], axis=1)[None]
        sent, part_a, part_b = prepare(
            where, hidden, w_query, w_key, w_value, n_dp, n_fsdp, q_cut
        )
        cache, f_order = double(cache, [0], "fsdp", n_fsdp, f_bits[0])
        part_a = swap(part_a, "fsdp", n_fsdp, inner)
        received = [swap(block, "fsdp", n_fsdp, k + 1) for k, block in enumerate(sent[:2])]
        part_a, cache, *received = together(part_a, cache, *received)
        received += [swap(block, "fsdp", n_fsdp, k + 3) for k, block in enumerate(sent[2:])]
        part_b = swap(part_b, "fsdp", n_fsdp, inner)
        cache, f_order = double(cache, f_order, "fsdp", n_fsdp, f_bits[1])
        far_a, d_order = double(part_a[None], [0], "dp", n_dp, d_bits[0])
        far_a, part_b, cache, *received = together(far_a, part_b, cache, *received)
        far_a, d_order = finish(far_a, d_order, "dp", n_dp, d_bits[1:])
        far_b, _ = finish(part_b[None], [0], "dp", n_dp, d_bits)
        cache, f_order = finish(cache, f_order, "fsdp", n_fsdp, f_bits[2:])
        far_b, cache = together(far_b, cache)

        near_a = [(w_key, 0, head_dim), (w_value, 0, head_dim), (w_query, 0, q_cut)]
        near_b = [(w_query, q_cut, q_width - q_cut)]
        out_kv, out_a = multiply(
            where, hidden, received, near_a, far_a, d_order, n_fsdp, (2 * head_dim, q_cut)
        )
        (out_b,) = multiply(
            where, hidden, received, near_b, far_b, d_order, n_fsdp, (q_width - q_cut,)
        )
        parts_kv = from_owners(out_kv)
        parts_a = from_owners(out_a)
        *parts_kv, out_b[0] = together(*parts_kv, out_b[0])
        parts_b = from_owners(out_b)
        group = functools.reduce(lambda a, b: a + b, parts_kv).astype(BF16)[None]
        group, g_order = double(group, [0], "fsdp", n_fsdp, f_bits[0])
        group, *parts_a = together(group, *parts_a)
        group, g_order = finish(group, g_order, "fsdp", n_fsdp, f_bits[1:-1])
        group, *parts_b = together(group, *parts_b)
        group, _ = finish(group, g_order, "fsdp", n_fsdp, f_bits[-1:])

        keep, give = attend(where, lengths, [parts_a, parts_b], d_attn, cache, group, f_order)

        half = keep + swap(give, "dp", n_dp, 1)
        size = half.shape[0] // n_fsdp
        mine = half[:size]
        for slot in range(1, n_fsdp):
            out = half[slot * size : (slot + 1) * size].astype(BF16)
            mine = mine + swap(out, "fsdp", n_fsdp, f_order[slot]).astype(F32)
        for bit in bits_down(n_dp)[:-2]:
            mine = mine + swap(mine, "dp", n_dp, bit)
        beside, other, across = (swap(mine, "dp", n_dp, bit) for bit in (2, 1, 3))
        mine = mine + beside
        other = other + across
        even = dp % 2 == 0
        return jnp.where(even, mine, other), jnp.where(even, other, mine)

    return on_device


def solution(mesh):
    placed = (
        P(("dp", "fsdp"), None),
        P(("dp", "fsdp"), None),
        P("fsdp", None),
        P("fsdp", None),
        P("fsdp", None),
        P("fsdp", None),
        P("fsdp", None),
        P("dp", None),
    )
    return jax.shard_map(
        make_on_device(mesh.shape["dp"], mesh.shape["fsdp"]),
        mesh=mesh,
        in_specs=placed,
        out_specs=(P("fsdp", None), P("fsdp", None)),
        check_vma=False,
    )
```

```python
import functools
import math

import jax
import jax.numpy as jnp
from jax import lax
from jax.experimental import pallas as pl
from jax.experimental.pallas import tpu as pltpu
from jax.sharding import PartitionSpec as P

F32 = jnp.float32
BF16 = jnp.bfloat16
VMEM_LIMIT = 56 * 1024 * 1024


def swap(value, axis, size, bit):
    return lax.ppermute(value, axis, [(i, i ^ bit) for i in range(size)])


def bits_down(size):
    bits = []
    bit = size // 2
    while bit:
        bits.append(bit)
        bit //= 2
    return bits


def double(block, order, axis, size, bit):
    return jnp.concatenate([block, swap(block, axis, size, bit)]), order + [o ^ bit for o in order]


def finish(block, order, axis, size, bits):
    for bit in bits[:-1]:
        block, order = double(block, order, axis, size, bit)
    return [block, swap(block, axis, size, bits[-1])], order + [o ^ bits[-1] for o in order]


def together(*values):
    return lax.optimization_barrier(values)


def params():
    return pltpu.CompilerParams(vmem_limit_bytes=VMEM_LIMIT)


def run_copies(copies):
    for copy in copies:
        copy.start()
    for copy in copies:
        copy.wait()


def prepare(where, hidden, w_query, w_key, w_value, n_dp, n_fsdp):
    inner = n_fsdp // 2
    tokens = hidden.shape[0]
    rows_w, q_width = w_query.shape
    head_dim = w_key.shape[1]
    share = rows_w // n_dp

    def body(where_ref, hidden_ref, wq_ref, wk_ref, wv_ref, *rest):
        sent, part_kv, part_q, sems = rest[: inner - 1], rest[-3], rest[-2], rest[-1]
        me, dp = where_ref[0], where_ref[1]
        rows = pl.ds(pl.multiple_of(dp * share, 16), share)
        pairs = [
            (wk_ref.at[rows], part_kv.at[:, pl.ds(0, head_dim)]),
            (wv_ref.at[rows], part_kv.at[:, pl.ds(head_dim, head_dim)]),
            (wq_ref.at[rows], part_q),
        ]
        for k in range(1, inner):
            for side, bit in enumerate((0, inner)):
                start = pl.multiple_of((me ^ k ^ bit) * rows_w, 128)
                pairs.append(
                    (hidden_ref.at[:, pl.ds(start, rows_w)], sent[k - 1].at[:, pl.ds(side * rows_w, rows_w)])
                )
        run_copies([pltpu.make_async_copy(a, b, sems.at[i]) for i, (a, b) in enumerate(pairs)])

    moved = 2 * (tokens * 2 * rows_w * 2 * (inner - 1) + share * (q_width + 2 * head_dim) * 2)
    out = pl.pallas_call(
        body,
        in_specs=[pl.BlockSpec(memory_space=pltpu.SMEM)] + [pl.BlockSpec(memory_space=pl.ANY)] * 4,
        out_specs=[pl.BlockSpec(memory_space=pltpu.VMEM)] * (inner + 1),
        out_shape=[jax.ShapeDtypeStruct((tokens, 2 * rows_w), BF16)] * (inner - 1)
        + [
            jax.ShapeDtypeStruct((share, 2 * head_dim), BF16),
            jax.ShapeDtypeStruct((share, q_width), BF16),
        ],
        scratch_shapes=[pltpu.SemaphoreType.DMA((3 + 2 * (inner - 1),))],
        compiler_params=params(),
        cost_estimate=pl.CostEstimate(flops=0, bytes_accessed=moved, transcendentals=0),
        name="prepare",
    )(where, hidden, w_query, w_key, w_value)
    return out[: inner - 1], out[-2], out[-1]


def multiply(where, hidden, received, near, far, order, n_fsdp):
    inner = n_fsdp // 2
    tokens = hidden.shape[0]
    slots, share, cols = far[0].shape
    n_dp = slots * len(far)
    rows_w = n_dp * share
    step = 256 if cols % 256 == 0 else 128
    n_in = inner - 1 + len(near) + len(far)

    def body(where_ref, hidden_ref, *rest):
        blocks, rest = rest[: inner - 1], rest[inner - 1 :]
        near_refs, rest = rest[: len(near)], rest[len(near) :]
        far_refs, rest = rest[: len(far)], rest[len(far) :]
        outs = rest[:-3]
        x_all, w_all, sems = rest[-3:]
        me, dp = where_ref[0], where_ref[1]
        pairs = []
        for side, bit in enumerate((0, inner)):
            start = pl.multiple_of((me ^ bit) * rows_w, 128)
            pairs.append(
                (
                    hidden_ref.at[:, pl.ds(start, rows_w)],
                    x_all.at[pl.ds(0, tokens), pl.ds(side * rows_w, rows_w)],
                )
            )
        for k in range(1, inner):
            pairs.append((blocks[k - 1], x_all.at[pl.ds(k * tokens, tokens)]))
        to = 0
        for ref in near_refs:
            wide = ref.shape[1]
            pairs.append((ref, w_all.at[pl.ds(0, rows_w), pl.ds(to, wide)]))
            to += wide
        for slot, o in enumerate(order):
            to = pl.multiple_of(rows_w + (dp ^ o) * share, 16)
            pairs.append((far_refs[slot // slots].at[slot % slots], w_all.at[pl.ds(to, share)]))
        run_copies([pltpu.make_async_copy(a, b, sems.at[i]) for i, (a, b) in enumerate(pairs)])

        @pl.loop(0, cols // step)
        def _(n):
            at = pl.multiple_of(n * step, 128)
            product = jnp.dot(x_all[...], w_all[:, pl.ds(at, step)], preferred_element_type=F32)
            for k in range(inner):
                outs[k][:, pl.ds(at, step)] = product[k * tokens : (k + 1) * tokens]

    copies = 2 + (inner - 1) + len(near) + n_dp
    moved = inner * tokens * 2 * rows_w * 2 + 2 * rows_w * cols * 2 + inner * tokens * cols * 4
    out = pl.pallas_call(
        body,
        in_specs=[pl.BlockSpec(memory_space=pltpu.SMEM)]
        + [pl.BlockSpec(memory_space=pl.ANY)] * (1 + n_in),
        out_specs=[pl.BlockSpec(memory_space=pltpu.VMEM)] * inner,
        out_shape=[jax.ShapeDtypeStruct((tokens, cols), F32)] * inner,
        scratch_shapes=[
            pltpu.VMEM((inner * tokens, 2 * rows_w), BF16),
            pltpu.VMEM((2 * rows_w, cols), BF16),
            pltpu.SemaphoreType.DMA((copies,)),
        ],
        compiler_params=params(),
        cost_estimate=pl.CostEstimate(
            flops=2 * inner * tokens * 2 * rows_w * cols, bytes_accessed=moved, transcendentals=0
        ),
        name="multiply",
    )(where, hidden, *received, *near, *far)
    return list(out)


def attend(where, lengths, partials, d_attn, cache, group, f_order):
    tokens = d_attn.shape[0]
    slots, block, twice = cache[0].shape
    n_blocks = slots * len(cache)
    head_dim = twice // 2
    n_convs = lengths.shape[1]
    scale = head_dim ** (-0.5)
    to_log2 = scale * math.log2(math.e)
    n_heads = d_attn.shape[1] // head_dim
    pair = 2 if n_heads % 2 == 0 else 1
    lanes = pair * tokens
    n_cache = n_blocks * block
    n_group = n_blocks * tokens
    chunk = 512
    n_part = sum(len(terms) for terms in partials)

    def body(where_ref, len_ref, d_ref, *rest):
        cache_refs, rest = rest[: len(cache)], rest[len(cache) :]
        group_refs, rest = rest[: len(group)], rest[len(group) :]
        part_refs = list(rest[:n_part])
        keep_ref, give_ref, gk, gv, s_ref, p_ref, q_ref = rest[n_part:]
        me, dp = where_ref[0], where_ref[1]

        h = 0
        for terms in partials:
            refs, part_refs = part_refs[: len(terms)], part_refs[len(terms) :]
            for at in range(0, terms[0].shape[1], head_dim):
                q = refs[0][:, at : at + head_dim]
                for ref in refs[1:]:
                    q = q + ref[:, at : at + head_dim]
                q_ref[h, 0] = q.astype(BF16)
                q_ref[h, 1] = d_ref[:, h * head_dim : (h + 1) * head_dim]
                h += 1

        q_pos = me * tokens + lax.broadcasted_iota(jnp.int32, (1, lanes), 1) % tokens
        begin = jnp.zeros((1, lanes), jnp.int32)
        end = jnp.int32(0)
        for i in range(n_convs):
            end = end + len_ref[0, i]
            begin = jnp.where(end <= q_pos, end, begin)

        @pl.loop(0, n_heads // pair)
        def _(step):
            rows_q = jnp.concatenate([q_ref[step * pair + i, 0] for i in range(pair)], axis=0)
            rows_d = jnp.concatenate([q_ref[step * pair + i, 1] for i in range(pair)], axis=0)
            dims = (((1,), (1,)), ((), ()))
            top = jnp.full((1, lanes), -jnp.inf, F32)
            cache_spans = [
                (b, r, min(chunk, block)) for b in range(n_blocks) for r in range(0, block, min(chunk, block))
            ]
            for b, r, size in cache_spans:
                s = lax.dot_general(
                    cache_refs[b // slots][b % slots, r : r + size, :head_dim], rows_q, dims, preferred_element_type=F32
                )
                s_ref[pl.ds(b * block + r, size)] = s
                top = jnp.maximum(top, jnp.max(s, axis=0, keepdims=True))
            for b in range(n_blocks):
                s = lax.dot_general(group_refs[b // slots][b % slots, :, :head_dim], rows_q, dims, preferred_element_type=F32)
                pos = (me ^ f_order[b]) * tokens + lax.broadcasted_iota(jnp.int32, (tokens, lanes), 0)
                s = jnp.where((pos <= q_pos) & (pos >= begin), s, -jnp.inf)
                s_ref[pl.ds(n_cache + b * tokens, tokens)] = s
                top = jnp.maximum(top, jnp.max(s, axis=0, keepdims=True))
            total = jnp.zeros((1, lanes), F32)
            for r in range(0, n_cache + n_group, chunk):
                e = jnp.exp2((s_ref[pl.ds(r, chunk)] - top) * to_log2)
                s_ref[pl.ds(r, chunk)] = e
                total = total + jnp.sum(e, axis=0, keepdims=True)
            inv = 1.0 / total
            delta = jnp.zeros((1, lanes), F32)
            for b in range(n_blocks):
                p = s_ref[pl.ds(n_cache + b * tokens, tokens)] * inv
                dp_ = lax.dot_general(group_refs[b // slots][b % slots, :, head_dim:], rows_d, dims, preferred_element_type=F32)
                delta = delta + jnp.sum(p.astype(BF16).astype(F32) * dp_, axis=0, keepdims=True)
            for b, r, size in cache_spans:
                at = pl.ds(b * block + r, size)
                p = s_ref[at] * inv
                pb = p.astype(BF16)
                dp_ = lax.dot_general(
                    cache_refs[b // slots][b % slots, r : r + size, head_dim:], rows_d, dims, preferred_element_type=F32
                )
                s_ref[at] = p
                p_ref[at] = dp_
                delta = delta + jnp.sum(pb.astype(F32) * dp_, axis=0, keepdims=True)
                g = jnp.dot(pb, rows_d, preferred_element_type=F32)
                gv[at] = jnp.where(step == 0, 0.0, gv[at]) + g
            for b, r, size in cache_spans:
                at = pl.ds(b * block + r, size)
                ds = (s_ref[at] * (p_ref[at] - delta)).astype(BF16)
                g = jnp.dot(ds, rows_q, preferred_element_type=F32)
                gk[at] = jnp.where(step == 0, 0.0, gk[at]) + g

        even = dp % 2 == 0
        @pl.when(even)
        def _():
            keep_ref[...] = gk[...] * scale
            give_ref[...] = gv[...]

        @pl.when(jnp.logical_not(even))
        def _():
            keep_ref[...] = gv[...]
            give_ref[...] = gk[...] * scale

    rows = n_heads * tokens
    flops = 2 * rows * head_dim * (5 * n_cache + 2 * n_group)
    return pl.pallas_call(
        body,
        in_specs=[pl.BlockSpec(memory_space=pltpu.SMEM)] * 2
        + [pl.BlockSpec(memory_space=pltpu.VMEM)] * (1 + len(cache) + len(group) + n_part),
        out_specs=[pl.BlockSpec(memory_space=pltpu.VMEM)] * 2,
        out_shape=[jax.ShapeDtypeStruct((n_cache, head_dim), F32)] * 2,
        scratch_shapes=[
            pltpu.VMEM((n_cache, head_dim), F32),
            pltpu.VMEM((n_cache, head_dim), F32),
            pltpu.VMEM((n_cache + n_group, lanes), F32),
            pltpu.VMEM((n_cache, lanes), F32),
            pltpu.VMEM((n_heads, 2, tokens, head_dim), BF16),
        ],
        compiler_params=params(),
        cost_estimate=pl.CostEstimate(
            flops=flops,
            bytes_accessed=12 * n_cache * head_dim,
            transcendentals=rows * (n_cache + n_group),
        ),
        name="attend",
    )(where, lengths, d_attn, *cache, *group, *[term for terms in partials for term in terms])


def make_on_device(n_dp, n_fsdp):
    inner = n_fsdp // 2

    def on_device(hidden, d_attn, w_query, w_key, w_value, cache_keys, cache_values, lengths):
        me = lax.axis_index("fsdp")
        dp = lax.axis_index("dp")
        where = jnp.stack([me, dp]).astype(jnp.int32)
        f_bits, d_bits = bits_down(n_fsdp), bits_down(n_dp)

        def from_owners(products):
            return [products[0]] + [swap(x, "fsdp", n_fsdp, k + 1) for k, x in enumerate(products[1:])]

        sent, part_kv, part_q = prepare(where, hidden, w_query, w_key, w_value, n_dp, n_fsdp)
        received = [swap(block, "fsdp", n_fsdp, k + 1) for k, block in enumerate(sent)]
        part_q = swap(part_q, "fsdp", n_fsdp, inner)
        part_kv = swap(part_kv, "fsdp", n_fsdp, inner)
        far_kv, d_order = finish(part_kv[None], [0], "dp", n_dp, d_bits)
        far_kv[-1], part_q, *received = together(far_kv[-1], part_q, *received)
        far_q, q_order = double(part_q[None], [0], "dp", n_dp, d_bits[0])
        cache = jnp.concatenate([cache_keys, cache_values], axis=1)[None]
        cache, f_order = finish(cache, [0], "fsdp", n_fsdp, f_bits)
        parts_kv = from_owners(
            multiply(where, hidden, received, [w_key, w_value], far_kv, d_order, n_fsdp)
        )
        far_q, *parts_kv = together(far_q, *parts_kv)
        far_q, _ = finish(far_q, q_order, "dp", n_dp, d_bits[1:])
        out_q = multiply(where, hidden, received, [w_query], far_q, d_order, n_fsdp)
        parts_q = from_owners(out_q)
        group = functools.reduce(lambda a, b: a + b, parts_kv).astype(BF16)[None]
        group, _ = finish(group, [0], "fsdp", n_fsdp, f_bits)

        keep, give = attend(where, lengths, [parts_q], d_attn, cache, group, f_order)

        half = keep + swap(give, "dp", n_dp, 1)
        size = half.shape[0] // n_fsdp
        mine = half[:size]
        for slot in range(1, n_fsdp):
            out = half[slot * size : (slot + 1) * size].astype(BF16)
            mine = mine + swap(out, "fsdp", n_fsdp, f_order[slot]).astype(F32)
        for bit in bits_down(n_dp)[:-2]:
            mine = mine + swap(mine, "dp", n_dp, bit)
        beside, other, across = (swap(mine, "dp", n_dp, bit) for bit in (2, 1, 3))
        mine = mine + beside
        other = other + across
        even = dp % 2 == 0
        return jnp.where(even, mine, other), jnp.where(even, other, mine)

    return on_device


def solution(mesh):
    placed = (
        P(("dp", "fsdp"), None),
        P(("dp", "fsdp"), None),
        P("fsdp", None),
        P("fsdp", None),
        P("fsdp", None),
        P("fsdp", None),
        P("fsdp", None),
        P("dp", None),
    )
    return jax.shard_map(
        make_on_device(mesh.shape["dp"], mesh.shape["fsdp"]),
        mesh=mesh,
        in_specs=placed,
        out_specs=(P("fsdp", None), P("fsdp", None)),
        check_vma=False,
    )
```

```python
import functools
import math

import jax
import jax.numpy as jnp
from jax import lax
from jax.experimental import pallas as pl
from jax.experimental.pallas import tpu as pltpu
from jax.sharding import PartitionSpec as P

F32 = jnp.float32
BF16 = jnp.bfloat16
VMEM_LIMIT = 56 * 1024 * 1024


def swap(value, axis, size, bit):
    return lax.ppermute(value, axis, [(i, i ^ bit) for i in range(size)])


def bits_down(size):
    bits = []
    bit = size // 2
    while bit:
        bits.append(bit)
        bit //= 2
    return bits


def double(block, order, axis, size, bit):
    return jnp.concatenate([block, swap(block, axis, size, bit)]), order + [o ^ bit for o in order]


def finish(block, order, axis, size, bits):
    for bit in bits[:-1]:
        block, order = double(block, order, axis, size, bit)
    return [block, swap(block, axis, size, bits[-1])], order + [o ^ bits[-1] for o in order]


def together(*values):
    return lax.optimization_barrier(values)


def params():
    return pltpu.CompilerParams(vmem_limit_bytes=VMEM_LIMIT)


def run_copies(copies):
    for copy in copies:
        copy.start()
    for copy in copies:
        copy.wait()


def prepare(where, hidden, w_query, w_key, w_value, n_dp, n_fsdp):
    inner = n_fsdp // 2
    tokens = hidden.shape[0]
    rows_w, q_width = w_query.shape
    head_dim = w_key.shape[1]
    share = rows_w // n_dp

    def body(where_ref, hidden_ref, wq_ref, wk_ref, wv_ref, *rest):
        sent, part_kv, part_q, sems = rest[: inner - 1], rest[-3], rest[-2], rest[-1]
        me, dp = where_ref[0], where_ref[1]
        rows = pl.ds(pl.multiple_of(dp * share, 16), share)
        pairs = [
            (wk_ref.at[rows], part_kv.at[:, pl.ds(0, head_dim)]),
            (wv_ref.at[rows], part_kv.at[:, pl.ds(head_dim, head_dim)]),
            (wq_ref.at[rows], part_q),
        ]
        for k in range(1, inner):
            for side, bit in enumerate((0, inner)):
                start = pl.multiple_of((me ^ k ^ bit) * rows_w, 128)
                pairs.append(
                    (hidden_ref.at[:, pl.ds(start, rows_w)], sent[k - 1].at[:, pl.ds(side * rows_w, rows_w)])
                )
        run_copies([pltpu.make_async_copy(a, b, sems.at[i]) for i, (a, b) in enumerate(pairs)])

    moved = 2 * (tokens * 2 * rows_w * 2 * (inner - 1) + share * (q_width + 2 * head_dim) * 2)
    out = pl.pallas_call(
        body,
        in_specs=[pl.BlockSpec(memory_space=pltpu.SMEM)] + [pl.BlockSpec(memory_space=pl.ANY)] * 4,
        out_specs=[pl.BlockSpec(memory_space=pltpu.VMEM)] * (inner + 1),
        out_shape=[jax.ShapeDtypeStruct((tokens, 2 * rows_w), BF16)] * (inner - 1)
        + [
            jax.ShapeDtypeStruct((share, 2 * head_dim), BF16),
            jax.ShapeDtypeStruct((share, q_width), BF16),
        ],
        scratch_shapes=[pltpu.SemaphoreType.DMA((3 + 2 * (inner - 1),))],
        compiler_params=params(),
        cost_estimate=pl.CostEstimate(flops=0, bytes_accessed=moved, transcendentals=0),
        name="prepare",
    )(where, hidden, w_query, w_key, w_value)
    return out[: inner - 1], out[-2], out[-1]


def multiply(where, hidden, received, near, far, order, n_fsdp):
    inner = n_fsdp // 2
    tokens = hidden.shape[0]
    slots, share, cols = far[0].shape
    n_dp = slots * len(far)
    rows_w = n_dp * share
    step = 256 if cols % 256 == 0 else 128
    n_in = inner - 1 + len(near) + len(far)

    def body(where_ref, hidden_ref, *rest):
        blocks, rest = rest[: inner - 1], rest[inner - 1 :]
        near_refs, rest = rest[: len(near)], rest[len(near) :]
        far_refs, rest = rest[: len(far)], rest[len(far) :]
        outs = rest[:-3]
        x_all, w_all, sems = rest[-3:]
        me, dp = where_ref[0], where_ref[1]
        pairs = []
        for side, bit in enumerate((0, inner)):
            start = pl.multiple_of((me ^ bit) * rows_w, 128)
            pairs.append(
                (
                    hidden_ref.at[:, pl.ds(start, rows_w)],
                    x_all.at[pl.ds(0, tokens), pl.ds(side * rows_w, rows_w)],
                )
            )
        for k in range(1, inner):
            pairs.append((blocks[k - 1], x_all.at[pl.ds(k * tokens, tokens)]))
        to = 0
        for ref in near_refs:
            wide = ref.shape[1]
            pairs.append((ref, w_all.at[pl.ds(0, rows_w), pl.ds(to, wide)]))
            to += wide
        for slot, o in enumerate(order):
            to = pl.multiple_of(rows_w + (dp ^ o) * share, 16)
            pairs.append((far_refs[slot // slots].at[slot % slots], w_all.at[pl.ds(to, share)]))
        run_copies([pltpu.make_async_copy(a, b, sems.at[i]) for i, (a, b) in enumerate(pairs)])

        @pl.loop(0, cols // step)
        def _(n):
            at = pl.multiple_of(n * step, 128)
            product = jnp.dot(x_all[...], w_all[:, pl.ds(at, step)], preferred_element_type=F32)
            for k in range(inner):
                outs[k][:, pl.ds(at, step)] = product[k * tokens : (k + 1) * tokens]

    copies = 2 + (inner - 1) + len(near) + n_dp
    moved = inner * tokens * 2 * rows_w * 2 + 2 * rows_w * cols * 2 + inner * tokens * cols * 4
    out = pl.pallas_call(
        body,
        in_specs=[pl.BlockSpec(memory_space=pltpu.SMEM)]
        + [pl.BlockSpec(memory_space=pl.ANY)] * (1 + n_in),
        out_specs=[pl.BlockSpec(memory_space=pltpu.VMEM)] * inner,
        out_shape=[jax.ShapeDtypeStruct((tokens, cols), F32)] * inner,
        scratch_shapes=[
            pltpu.VMEM((inner * tokens, 2 * rows_w), BF16),
            pltpu.VMEM((2 * rows_w, cols), BF16),
            pltpu.SemaphoreType.DMA((copies,)),
        ],
        compiler_params=params(),
        cost_estimate=pl.CostEstimate(
            flops=2 * inner * tokens * 2 * rows_w * cols, bytes_accessed=moved, transcendentals=0
        ),
        name="multiply",
    )(where, hidden, *received, *near, *far)
    return list(out)


def attend(where, lengths, partials, d_attn, cache, group, f_order):
    tokens = d_attn.shape[0]
    slots, block, twice = cache[0].shape
    n_blocks = slots * len(cache)
    head_dim = twice // 2
    n_convs = lengths.shape[1]
    scale = head_dim ** (-0.5)
    to_log2 = scale * math.log2(math.e)
    n_heads = d_attn.shape[1] // head_dim
    pair = 2 if n_heads % 2 == 0 else 1
    lanes = pair * tokens
    n_cache = n_blocks * block
    n_group = n_blocks * tokens
    chunk = 512
    n_part = sum(len(terms) for terms in partials)

    def body(where_ref, len_ref, d_ref, *rest):
        cache_refs, rest = rest[: len(cache)], rest[len(cache) :]
        group_refs, rest = rest[: len(group)], rest[len(group) :]
        part_refs = list(rest[:n_part])
        keep_ref, give_ref, gk, gv, s_ref, p_ref, q_ref = rest[n_part:]
        me, dp = where_ref[0], where_ref[1]

        h = 0
        for terms in partials:
            refs, part_refs = part_refs[: len(terms)], part_refs[len(terms) :]
            for at in range(0, terms[0].shape[1], head_dim):
                q = refs[0][:, at : at + head_dim]
                for ref in refs[1:]:
                    q = q + ref[:, at : at + head_dim]
                q_ref[h, 0] = q.astype(BF16)
                q_ref[h, 1] = d_ref[:, h * head_dim : (h + 1) * head_dim]
                h += 1

        q_pos = me * tokens + lax.broadcasted_iota(jnp.int32, (1, lanes), 1) % tokens
        begin = jnp.zeros((1, lanes), jnp.int32)
        end = jnp.int32(0)
        for i in range(n_convs):
            end = end + len_ref[0, i]
            begin = jnp.where(end <= q_pos, end, begin)

        @pl.loop(0, n_heads // pair)
        def _(step):
            rows_q = jnp.concatenate([q_ref[step * pair + i, 0] for i in range(pair)], axis=0)
            rows_d = jnp.concatenate([q_ref[step * pair + i, 1] for i in range(pair)], axis=0)
            dims = (((1,), (1,)), ((), ()))
            top = jnp.full((1, lanes), -jnp.inf, F32)
            cache_spans = [
                (b, r, min(chunk, block)) for b in range(n_blocks) for r in range(0, block, min(chunk, block))
            ]
            for b, r, size in cache_spans:
                s = lax.dot_general(
                    cache_refs[b // slots][b % slots, r : r + size, :head_dim], rows_q, dims, preferred_element_type=F32
                )
                s_ref[pl.ds(b * block + r, size)] = s
                top = jnp.maximum(top, jnp.max(s, axis=0, keepdims=True))
            for b in range(n_blocks):
                s = lax.dot_general(group_refs[b // slots][b % slots, :, :head_dim], rows_q, dims, preferred_element_type=F32)
                pos = (me ^ f_order[b]) * tokens + lax.broadcasted_iota(jnp.int32, (tokens, lanes), 0)
                s = jnp.where((pos <= q_pos) & (pos >= begin), s, -jnp.inf)
                s_ref[pl.ds(n_cache + b * tokens, tokens)] = s
                top = jnp.maximum(top, jnp.max(s, axis=0, keepdims=True))
            total = jnp.zeros((1, lanes), F32)
            for r in range(0, n_cache + n_group, chunk):
                e = jnp.exp2((s_ref[pl.ds(r, chunk)] - top) * to_log2)
                s_ref[pl.ds(r, chunk)] = e
                total = total + jnp.sum(e, axis=0, keepdims=True)
            inv = 1.0 / total
            delta = jnp.zeros((1, lanes), F32)
            for b in range(n_blocks):
                p = s_ref[pl.ds(n_cache + b * tokens, tokens)] * inv
                dp_ = lax.dot_general(group_refs[b // slots][b % slots, :, head_dim:], rows_d, dims, preferred_element_type=F32)
                delta = delta + jnp.sum(p.astype(BF16).astype(F32) * dp_, axis=0, keepdims=True)
            for b, r, size in cache_spans:
                at = pl.ds(b * block + r, size)
                p = s_ref[at] * inv
                pb = p.astype(BF16)
                dp_ = lax.dot_general(
                    cache_refs[b // slots][b % slots, r : r + size, head_dim:], rows_d, dims, preferred_element_type=F32
                )
                s_ref[at] = p
                p_ref[at] = dp_
                delta = delta + jnp.sum(pb.astype(F32) * dp_, axis=0, keepdims=True)
                g = jnp.dot(pb, rows_d, preferred_element_type=F32)
                gv[at] = jnp.where(step == 0, 0.0, gv[at]) + g
            for b, r, size in cache_spans:
                at = pl.ds(b * block + r, size)
                ds = (s_ref[at] * (p_ref[at] - delta)).astype(BF16)
                g = jnp.dot(ds, rows_q, preferred_element_type=F32)
                gk[at] = jnp.where(step == 0, 0.0, gk[at]) + g

        even = dp % 2 == 0
        @pl.when(even)
        def _():
            keep_ref[...] = gk[...] * scale
            give_ref[...] = gv[...]

        @pl.when(jnp.logical_not(even))
        def _():
            keep_ref[...] = gv[...]
            give_ref[...] = gk[...] * scale

    rows = n_heads * tokens
    flops = 2 * rows * head_dim * (5 * n_cache + 2 * n_group)
    return pl.pallas_call(
        body,
        in_specs=[pl.BlockSpec(memory_space=pltpu.SMEM)] * 2
        + [pl.BlockSpec(memory_space=pltpu.VMEM)] * (1 + len(cache) + len(group) + n_part),
        out_specs=[pl.BlockSpec(memory_space=pltpu.VMEM)] * 2,
        out_shape=[jax.ShapeDtypeStruct((n_cache, head_dim), F32)] * 2,
        scratch_shapes=[
            pltpu.VMEM((n_cache, head_dim), F32),
            pltpu.VMEM((n_cache, head_dim), F32),
            pltpu.VMEM((n_cache + n_group, lanes), F32),
            pltpu.VMEM((n_cache, lanes), F32),
            pltpu.VMEM((n_heads, 2, tokens, head_dim), BF16),
        ],
        compiler_params=params(),
        cost_estimate=pl.CostEstimate(
            flops=flops,
            bytes_accessed=12 * n_cache * head_dim,
            transcendentals=rows * (n_cache + n_group),
        ),
        name="attend",
    )(where, lengths, d_attn, *cache, *group, *[term for terms in partials for term in terms])


def make_on_device(n_dp, n_fsdp):
    inner = n_fsdp // 2

    def on_device(hidden, d_attn, w_query, w_key, w_value, cache_keys, cache_values, lengths):
        me = lax.axis_index("fsdp")
        dp = lax.axis_index("dp")
        where = jnp.stack([me, dp]).astype(jnp.int32)
        f_bits, d_bits = bits_down(n_fsdp), bits_down(n_dp)

        def from_owners(products):
            return [products[0]] + [swap(x, "fsdp", n_fsdp, k + 1) for k, x in enumerate(products[1:])]

        sent, part_kv, part_q = prepare(where, hidden, w_query, w_key, w_value, n_dp, n_fsdp)
        received = [swap(block, "fsdp", n_fsdp, k + 1) for k, block in enumerate(sent)]
        part_q = swap(part_q, "fsdp", n_fsdp, inner)
        part_kv = swap(part_kv, "fsdp", n_fsdp, inner)
        far_kv, q_order = double(part_kv[None], [0], "dp", n_dp, d_bits[0])
        far_kv, part_q, *received[:2] = together(far_kv, part_q, *received[:2])
        far_kv, d_order = finish(far_kv, q_order, "dp", n_dp, d_bits[1:])
        far_q, q_order = double(part_q[None], [0], "dp", n_dp, d_bits[0])
        cache, f_order = jnp.concatenate([cache_keys, cache_values], axis=1)[None], [0]
        for bit in f_bits[:0:-1]:
            cache, f_order = double(cache, f_order, "fsdp", n_fsdp, bit)
        parts_kv = from_owners(
            multiply(where, hidden, received, [w_key, w_value], far_kv, d_order, n_fsdp)
        )
        far_q, cache, *parts_kv = together(far_q, cache, *parts_kv)
        far_q, _ = finish(far_q, q_order, "dp", n_dp, d_bits[1:])
        cache, f_order = finish(cache, f_order, "fsdp", n_fsdp, f_bits[:1])
        own = functools.reduce(lambda a, b: a + b, parts_kv).astype(BF16)
        group = [own] + [swap(own, "fsdp", n_fsdp, k) for k in range(1, inner)]
        group, g_order = jnp.stack([group[k] for k in f_order[:inner]]), f_order[:inner]
        far_q[-1], group = together(far_q[-1], group)
        group, _ = finish(group, g_order, "fsdp", n_fsdp, f_bits[:1])
        out_q = multiply(where, hidden, received, [w_query], far_q, d_order, n_fsdp)
        parts_q = from_owners(out_q)

        keep, give = attend(where, lengths, [parts_q], d_attn, cache, group, f_order)

        half = keep + swap(give, "dp", n_dp, 1)
        size = half.shape[0] // n_fsdp
        mine = half[:size]
        for slot in range(1, n_fsdp):
            out = half[slot * size : (slot + 1) * size].astype(BF16)
            mine = mine + swap(out, "fsdp", n_fsdp, f_order[slot]).astype(F32)
        for bit in bits_down(n_dp)[:-2]:
            mine = mine + swap(mine, "dp", n_dp, bit)
        beside, other, across = (swap(mine, "dp", n_dp, bit) for bit in (2, 1, 3))
        mine = mine + beside
        other = other + across
        even = dp % 2 == 0
        return jnp.where(even, mine, other), jnp.where(even, other, mine)

    return on_device


def solution(mesh):
    placed = (
        P(("dp", "fsdp"), None),
        P(("dp", "fsdp"), None),
        P("fsdp", None),
        P("fsdp", None),
        P("fsdp", None),
        P("fsdp", None),
        P("fsdp", None),
        P("dp", None),
    )
    return jax.shard_map(
        make_on_device(mesh.shape["dp"], mesh.shape["fsdp"]),
        mesh=mesh,
        in_specs=placed,
        out_specs=(P("fsdp", None), P("fsdp", None)),
        check_vma=False,
    )
```

```python
import functools
import math

import jax
import jax.numpy as jnp
from jax import lax
from jax.experimental import pallas as pl
from jax.experimental.pallas import tpu as pltpu
from jax.sharding import PartitionSpec as P

F32 = jnp.float32
BF16 = jnp.bfloat16
VMEM_LIMIT = 56 * 1024 * 1024


def swap(value, axis, size, bit):
    return lax.ppermute(value, axis, [(i, i ^ bit) for i in range(size)])


def bits_down(size):
    bits = []
    bit = size // 2
    while bit:
        bits.append(bit)
        bit //= 2
    return bits


def double(block, order, axis, size, bit):
    return jnp.concatenate([block, swap(block, axis, size, bit)]), order + [o ^ bit for o in order]


def finish(block, order, axis, size, bits):
    for bit in bits[:-1]:
        block, order = double(block, order, axis, size, bit)
    return [block, swap(block, axis, size, bits[-1])], order + [o ^ bits[-1] for o in order]


def together(*values):
    return lax.optimization_barrier(values)


def params():
    return pltpu.CompilerParams(vmem_limit_bytes=VMEM_LIMIT)


def run_copies(copies):
    for copy in copies:
        copy.start()
    for copy in copies:
        copy.wait()


def prepare(where, hidden, w_query, w_key, w_value, n_dp, n_fsdp, q_cut):
    inner = n_fsdp // 2
    tokens = hidden.shape[0]
    rows_w, q_width = w_query.shape
    head_dim = w_key.shape[1]
    share = rows_w // n_dp

    def body(where_ref, hidden_ref, wq_ref, wk_ref, wv_ref, *rest):
        sent, part_a, part_b, sems = rest[: inner - 1], rest[-3], rest[-2], rest[-1]
        me, dp = where_ref[0], where_ref[1]
        rows = pl.ds(pl.multiple_of(dp * share, 16), share)
        pairs = [
            (wk_ref.at[rows], part_a.at[:, pl.ds(0, head_dim)]),
            (wv_ref.at[rows], part_a.at[:, pl.ds(head_dim, head_dim)]),
            (wq_ref.at[rows, pl.ds(0, q_cut)], part_a.at[:, pl.ds(2 * head_dim, q_cut)]),
            (wq_ref.at[rows, pl.ds(q_cut, q_width - q_cut)], part_b),
        ]
        for k in range(1, inner):
            for side, bit in enumerate((0, inner)):
                start = pl.multiple_of((me ^ k ^ bit) * rows_w, 128)
                pairs.append(
                    (hidden_ref.at[:, pl.ds(start, rows_w)], sent[k - 1].at[:, pl.ds(side * rows_w, rows_w)])
                )
        run_copies([pltpu.make_async_copy(a, b, sems.at[i]) for i, (a, b) in enumerate(pairs)])

    moved = 2 * (tokens * 2 * rows_w * 2 * (inner - 1) + share * (q_width + 2 * head_dim) * 2)
    out = pl.pallas_call(
        body,
        in_specs=[pl.BlockSpec(memory_space=pltpu.SMEM)] + [pl.BlockSpec(memory_space=pl.ANY)] * 4,
        out_specs=[pl.BlockSpec(memory_space=pltpu.VMEM)] * (inner + 1),
        out_shape=[jax.ShapeDtypeStruct((tokens, 2 * rows_w), BF16)] * (inner - 1)
        + [
            jax.ShapeDtypeStruct((share, 2 * head_dim + q_cut), BF16),
            jax.ShapeDtypeStruct((share, q_width - q_cut), BF16),
        ],
        scratch_shapes=[pltpu.SemaphoreType.DMA((4 + 2 * (inner - 1),))],
        compiler_params=params(),
        cost_estimate=pl.CostEstimate(flops=0, bytes_accessed=moved, transcendentals=0),
        name="prepare",
    )(where, hidden, w_query, w_key, w_value)
    return out[: inner - 1], out[-2], out[-1]


def multiply(where, hidden, received, near, far, order, n_fsdp, groups):
    inner = n_fsdp // 2
    tokens = hidden.shape[0]
    slots, share, cols = far[0].shape
    n_dp = slots * len(far)
    rows_w = n_dp * share
    step = 256 if all(g % 256 == 0 for g in groups) else 128
    n_in = inner - 1 + len(near) + len(far)

    def body(where_ref, hidden_ref, *rest):
        blocks, rest = rest[: inner - 1], rest[inner - 1 :]
        near_refs, rest = rest[: len(near)], rest[len(near) :]
        far_refs, rest = rest[: len(far)], rest[len(far) :]
        outs = rest[:-3]
        x_all, w_all, sems = rest[-3:]
        me, dp = where_ref[0], where_ref[1]
        pairs = []
        for side, bit in enumerate((0, inner)):
            start = pl.multiple_of((me ^ bit) * rows_w, 128)
            pairs.append(
                (
                    hidden_ref.at[:, pl.ds(start, rows_w)],
                    x_all.at[pl.ds(0, tokens), pl.ds(side * rows_w, rows_w)],
                )
            )
        for k in range(1, inner):
            pairs.append((blocks[k - 1], x_all.at[pl.ds(k * tokens, tokens)]))
        to = 0
        for ref, (_, start, wide) in zip(near_refs, near):
            pairs.append((ref.at[:, pl.ds(start, wide)], w_all.at[pl.ds(0, rows_w), pl.ds(to, wide)]))
            to += wide
        for slot, o in enumerate(order):
            to = pl.multiple_of(rows_w + (dp ^ o) * share, 16)
            pairs.append((far_refs[slot // slots].at[slot % slots], w_all.at[pl.ds(to, share)]))
        run_copies([pltpu.make_async_copy(a, b, sems.at[i]) for i, (a, b) in enumerate(pairs)])

        base = 0
        for g, wide in enumerate(groups):

            @pl.loop(0, wide // step)
            def _(n, g=g, base=base):
                at = pl.multiple_of(n * step, 128)
                product = jnp.dot(
                    x_all[...], w_all[:, pl.ds(base + at, step)], preferred_element_type=F32
                )
                for k in range(inner):
                    outs[g * inner + k][:, pl.ds(at, step)] = product[k * tokens : (k + 1) * tokens]

            base += wide

    copies = 2 + (inner - 1) + len(near) + n_dp
    moved = inner * tokens * 2 * rows_w * 2 + 2 * rows_w * cols * 2 + inner * tokens * cols * 4
    out = pl.pallas_call(
        body,
        in_specs=[pl.BlockSpec(memory_space=pltpu.SMEM)]
        + [pl.BlockSpec(memory_space=pl.ANY)] * (1 + n_in),
        out_specs=[pl.BlockSpec(memory_space=pltpu.VMEM)] * (inner * len(groups)),
        out_shape=[jax.ShapeDtypeStruct((tokens, g), F32) for g in groups for _ in range(inner)],
        scratch_shapes=[
            pltpu.VMEM((inner * tokens, 2 * rows_w), BF16),
            pltpu.VMEM((2 * rows_w, cols), BF16),
            pltpu.SemaphoreType.DMA((copies,)),
        ],
        compiler_params=params(),
        cost_estimate=pl.CostEstimate(
            flops=2 * inner * tokens * 2 * rows_w * cols, bytes_accessed=moved, transcendentals=0
        ),
        name="multiply",
    )(where, hidden, *received, *[array for array, _, _ in near], *far)
    return [list(out[g * inner : (g + 1) * inner]) for g in range(len(groups))]


def attend(where, lengths, partials, d_attn, cache, group, f_order):
    tokens = d_attn.shape[0]
    n_blocks, block, head_dim = cache[0].shape
    slots = n_blocks // len(group)
    n_convs = lengths.shape[1]
    scale = head_dim ** (-0.5)
    to_log2 = scale * math.log2(math.e)
    n_heads = d_attn.shape[1] // head_dim
    pair = 2 if n_heads % 2 == 0 else 1
    lanes = pair * tokens
    n_cache = n_blocks * block
    n_group = n_blocks * tokens
    chunk = 512
    n_part = sum(len(terms) for terms in partials)

    def body(where_ref, len_ref, d_ref, *rest):
        cache_refs, rest = rest[:2], rest[2:]
        group_refs, rest = rest[: len(group)], rest[len(group) :]
        part_refs = list(rest[:n_part])
        keep_ref, give_ref, gk, gv, s_ref, p_ref, q_ref, ck_ref, cv_ref = rest[n_part:]
        me, dp = where_ref[0], where_ref[1]
        even = dp % 2 == 0

        @pl.when(even)
        def _():
            ck_ref[...] = cache_refs[0][...]
            cv_ref[...] = cache_refs[1][...]

        @pl.when(jnp.logical_not(even))
        def _():
            ck_ref[...] = cache_refs[1][...]
            cv_ref[...] = cache_refs[0][...]

        h = 0
        for terms in partials:
            refs, part_refs = part_refs[: len(terms)], part_refs[len(terms) :]
            for at in range(0, terms[0].shape[1], head_dim):
                q = refs[0][:, at : at + head_dim]
                for ref in refs[1:]:
                    q = q + ref[:, at : at + head_dim]
                q_ref[h, 0] = q.astype(BF16)
                q_ref[h, 1] = d_ref[:, h * head_dim : (h + 1) * head_dim]
                h += 1

        q_pos = me * tokens + lax.broadcasted_iota(jnp.int32, (1, lanes), 1) % tokens
        begin = jnp.zeros((1, lanes), jnp.int32)
        end = jnp.int32(0)
        for i in range(n_convs):
            end = end + len_ref[0, i]
            begin = jnp.where(end <= q_pos, end, begin)

        @pl.loop(0, n_heads // pair)
        def _(step):
            rows_q = jnp.concatenate([q_ref[step * pair + i, 0] for i in range(pair)], axis=0)
            rows_d = jnp.concatenate([q_ref[step * pair + i, 1] for i in range(pair)], axis=0)
            dims = (((1,), (1,)), ((), ()))
            top = jnp.full((1, lanes), -jnp.inf, F32)
            cache_spans = [
                (b, r, min(chunk, block)) for b in range(n_blocks) for r in range(0, block, min(chunk, block))
            ]
            for b, r, size in cache_spans:
                s = lax.dot_general(
                    ck_ref[b, r : r + size], rows_q, dims, preferred_element_type=F32
                )
                s_ref[pl.ds(b * block + r, size)] = s
                top = jnp.maximum(top, jnp.max(s, axis=0, keepdims=True))
            for b in range(n_blocks):
                s = lax.dot_general(group_refs[b // slots][b % slots, :, :head_dim], rows_q, dims, preferred_element_type=F32)
                pos = (me ^ f_order[b]) * tokens + lax.broadcasted_iota(jnp.int32, (tokens, lanes), 0)
                s = jnp.where((pos <= q_pos) & (pos >= begin), s, -jnp.inf)
                s_ref[pl.ds(n_cache + b * tokens, tokens)] = s
                top = jnp.maximum(top, jnp.max(s, axis=0, keepdims=True))
            total = jnp.zeros((1, lanes), F32)
            for r in range(0, n_cache + n_group, chunk):
                e = jnp.exp2((s_ref[pl.ds(r, chunk)] - top) * to_log2)
                s_ref[pl.ds(r, chunk)] = e
                total = total + jnp.sum(e, axis=0, keepdims=True)
            inv = 1.0 / total
            delta = jnp.zeros((1, lanes), F32)
            for b in range(n_blocks):
                p = s_ref[pl.ds(n_cache + b * tokens, tokens)] * inv
                dp_ = lax.dot_general(group_refs[b // slots][b % slots, :, head_dim:], rows_d, dims, preferred_element_type=F32)
                delta = delta + jnp.sum(p.astype(BF16).astype(F32) * dp_, axis=0, keepdims=True)
            for b, r, size in cache_spans:
                at = pl.ds(b * block + r, size)
                p = s_ref[at] * inv
                pb = p.astype(BF16)
                dp_ = lax.dot_general(
                    cv_ref[b, r : r + size], rows_d, dims, preferred_element_type=F32
                )
                s_ref[at] = p
                p_ref[at] = dp_
                delta = delta + jnp.sum(pb.astype(F32) * dp_, axis=0, keepdims=True)
                g = jnp.dot(pb, rows_d, preferred_element_type=F32)
                gv[at] = jnp.where(step == 0, 0.0, gv[at]) + g
            for b, r, size in cache_spans:
                at = pl.ds(b * block + r, size)
                ds = (s_ref[at] * (p_ref[at] - delta)).astype(BF16)
                g = jnp.dot(ds, rows_q, preferred_element_type=F32)
                gk[at] = jnp.where(step == 0, 0.0, gk[at]) + g

        @pl.when(even)
        def _():
            keep_ref[...] = gk[...] * scale
            give_ref[...] = gv[...]

        @pl.when(jnp.logical_not(even))
        def _():
            keep_ref[...] = gv[...]
            give_ref[...] = gk[...] * scale

    rows = n_heads * tokens
    flops = 2 * rows * head_dim * (5 * n_cache + 2 * n_group)
    return pl.pallas_call(
        body,
        in_specs=[pl.BlockSpec(memory_space=pltpu.SMEM)] * 2
        + [pl.BlockSpec(memory_space=pltpu.VMEM)] * (3 + len(group) + n_part),
        out_specs=[pl.BlockSpec(memory_space=pltpu.VMEM)] * 2,
        out_shape=[jax.ShapeDtypeStruct((n_cache, head_dim), F32)] * 2,
        scratch_shapes=[
            pltpu.VMEM((n_cache, head_dim), F32),
            pltpu.VMEM((n_cache, head_dim), F32),
            pltpu.VMEM((n_cache + n_group, lanes), F32),
            pltpu.VMEM((n_cache, lanes), F32),
            pltpu.VMEM((n_heads, 2, tokens, head_dim), BF16),
            pltpu.VMEM((n_blocks, block, head_dim), BF16),
            pltpu.VMEM((n_blocks, block, head_dim), BF16),
        ],
        compiler_params=params(),
        cost_estimate=pl.CostEstimate(
            flops=flops,
            bytes_accessed=12 * n_cache * head_dim,
            transcendentals=rows * (n_cache + n_group),
        ),
        name="attend",
    )(where, lengths, d_attn, *cache, *group, *[term for terms in partials for term in terms])


def make_on_device(n_dp, n_fsdp):
    inner = n_fsdp // 2

    def on_device(hidden, d_attn, w_query, w_key, w_value, cache_keys, cache_values, lengths):
        me = lax.axis_index("fsdp")
        dp = lax.axis_index("dp")
        where = jnp.stack([me, dp]).astype(jnp.int32)
        head_dim = w_key.shape[1]
        q_width = w_query.shape[1]
        q_cut = q_width // head_dim // 4 * head_dim
        even = dp % 2 == 0
        f_bits, d_bits = bits_down(n_fsdp), bits_down(n_dp)

        def from_owners(products):
            return [products[0]] + [swap(x, "fsdp", n_fsdp, k + 1) for k, x in enumerate(products[1:])]

        cache = jnp.where(even, cache_keys, cache_values)[None]
        sent, part_a, part_b = prepare(where, hidden, w_query, w_key, w_value, n_dp, n_fsdp, q_cut)
        received = [swap(block, "fsdp", n_fsdp, k + 1) for k, block in enumerate(sent)]
        part_b = swap(part_b, "fsdp", n_fsdp, inner)
        part_a = swap(part_a, "fsdp", n_fsdp, inner)
        far_a, order = double(part_a[None], [0], "dp", n_dp, d_bits[0])
        cache, f_order = double(cache, [0], "fsdp", n_fsdp, f_bits[0])
        far_a, part_b, cache, *received = together(far_a, part_b, cache, *received)
        far_a, d_order = finish(far_a, order, "dp", n_dp, d_bits[1:])
        far_b, order = double(part_b[None], [0], "dp", n_dp, d_bits[0])
        cache, f_order = double(cache, f_order, "fsdp", n_fsdp, f_bits[1])
        near_a = [(w_key, 0, head_dim), (w_value, 0, head_dim), (w_query, 0, q_cut)]
        near_b = [(w_query, q_cut, q_width - q_cut)]
        out_kv, out_a = multiply(
            where, hidden, received, near_a, far_a, d_order, n_fsdp, (2 * head_dim, q_cut)
        )
        far_b, cache, out_kv[0] = together(far_b, cache, out_kv[0])
        far_b, _ = finish(far_b, order, "dp", n_dp, d_bits[1:])
        for bit in f_bits[2:]:
            cache, f_order = double(cache, f_order, "fsdp", n_fsdp, bit)
        parts_kv = from_owners(out_kv)
        parts_a = from_owners(out_a)
        own = functools.reduce(lambda a, b: a + b, parts_kv).astype(BF16)
        group, _ = double(own[None], [0], "fsdp", n_fsdp, inner)
        (out_b,) = multiply(
            where, hidden, received, near_b, far_b, d_order, n_fsdp, (q_width - q_cut,)
        )
        near_group = [group] + [swap(group, "fsdp", n_fsdp, k) for k in range(1, inner)]
        tied = together(*out_b, *parts_a, *near_group)
        out_b, parts_a, near_group = tied[:inner], tied[inner : 2 * inner], tied[2 * inner :]
        parts_b = from_owners(out_b)
        group = []
        for o in f_order[::2]:
            group.append(near_group[o % inner])
        cache = (cache, swap(cache, "dp", n_dp, 1))

        keep, give = attend(where, lengths, [parts_a, parts_b], d_attn, cache, group, f_order)

        half = keep + swap(give, "dp", n_dp, 1)
        size = half.shape[0] // n_fsdp
        mine = half[:size]
        for slot in range(1, n_fsdp):
            out = half[slot * size : (slot + 1) * size].astype(BF16)
            mine = mine + swap(out, "fsdp", n_fsdp, f_order[slot]).astype(F32)
        for bit in bits_down(n_dp)[:-2]:
            mine = mine + swap(mine, "dp", n_dp, bit)
        beside, other, across = (swap(mine, "dp", n_dp, bit) for bit in (2, 1, 3))
        mine = mine + beside
        other = other + across
        return jnp.where(even, mine, other), jnp.where(even, other, mine)

    return on_device


def solution(mesh):
    placed = (
        P(("dp", "fsdp"), None),
        P(("dp", "fsdp"), None),
        P("fsdp", None),
        P("fsdp", None),
        P("fsdp", None),
        P("fsdp", None),
        P("fsdp", None),
        P("dp", None),
    )
    return jax.shard_map(
        make_on_device(mesh.shape["dp"], mesh.shape["fsdp"]),
        mesh=mesh,
        in_specs=placed,
        out_specs=(P("fsdp", None), P("fsdp", None)),
        check_vma=False,
    )
```

```python
import functools
import math

import jax
import jax.numpy as jnp
from jax import lax
from jax.experimental import pallas as pl
from jax.experimental.pallas import tpu as pltpu
from jax.sharding import PartitionSpec as P

F32 = jnp.float32
BF16 = jnp.bfloat16
VMEM_LIMIT = 56 * 1024 * 1024


def swap(value, axis, size, bit):
    return lax.ppermute(value, axis, [(i, i ^ bit) for i in range(size)])


def bits_down(size):
    bits = []
    bit = size // 2
    while bit:
        bits.append(bit)
        bit //= 2
    return bits


def double(block, order, axis, size, bit):
    return jnp.concatenate([block, swap(block, axis, size, bit)]), order + [o ^ bit for o in order]


def finish(block, order, axis, size, bits):
    for bit in bits[:-1]:
        block, order = double(block, order, axis, size, bit)
    return [block, swap(block, axis, size, bits[-1])], order + [o ^ bits[-1] for o in order]


def together(*values):
    return lax.optimization_barrier(values)


def params():
    return pltpu.CompilerParams(vmem_limit_bytes=VMEM_LIMIT)


def run_copies(copies):
    for copy in copies:
        copy.start()
    for copy in copies:
        copy.wait()


def prepare(where, hidden, w_query, w_key, w_value, n_dp, n_fsdp):
    inner = n_fsdp // 2
    tokens = hidden.shape[0]
    rows_w, q_width = w_query.shape
    head_dim = w_key.shape[1]
    share = rows_w // n_dp

    def body(where_ref, hidden_ref, wq_ref, wk_ref, wv_ref, *rest):
        sent, part_kv, part_q, sems = rest[: inner - 1], rest[-3], rest[-2], rest[-1]
        me, dp = where_ref[0], where_ref[1]
        rows = pl.ds(pl.multiple_of(dp * share, 16), share)
        pairs = [
            (wk_ref.at[rows], part_kv.at[:, pl.ds(0, head_dim)]),
            (wv_ref.at[rows], part_kv.at[:, pl.ds(head_dim, head_dim)]),
            (wq_ref.at[rows], part_q),
        ]
        for k in range(1, inner):
            for side, bit in enumerate((0, inner)):
                start = pl.multiple_of((me ^ k ^ bit) * rows_w, 128)
                pairs.append(
                    (hidden_ref.at[:, pl.ds(start, rows_w)], sent[k - 1].at[:, pl.ds(side * rows_w, rows_w)])
                )
        run_copies([pltpu.make_async_copy(a, b, sems.at[i]) for i, (a, b) in enumerate(pairs)])

    moved = 2 * (tokens * 2 * rows_w * 2 * (inner - 1) + share * (q_width + 2 * head_dim) * 2)
    out = pl.pallas_call(
        body,
        in_specs=[pl.BlockSpec(memory_space=pltpu.SMEM)] + [pl.BlockSpec(memory_space=pl.ANY)] * 4,
        out_specs=[pl.BlockSpec(memory_space=pltpu.VMEM)] * (inner + 1),
        out_shape=[jax.ShapeDtypeStruct((tokens, 2 * rows_w), BF16)] * (inner - 1)
        + [
            jax.ShapeDtypeStruct((share, 2 * head_dim), BF16),
            jax.ShapeDtypeStruct((share, q_width), BF16),
        ],
        scratch_shapes=[pltpu.SemaphoreType.DMA((3 + 2 * (inner - 1),))],
        compiler_params=params(),
        cost_estimate=pl.CostEstimate(flops=0, bytes_accessed=moved, transcendentals=0),
        name="prepare",
    )(where, hidden, w_query, w_key, w_value)
    return out[: inner - 1], out[-2], out[-1]


def multiply(where, hidden, received, near, far, order, n_fsdp, groups):
    inner = n_fsdp // 2
    tokens = hidden.shape[0]
    slots, share, cols = far[0].shape
    n_dp = slots * len(far)
    rows_w = n_dp * share
    step = 256 if all(g % 256 == 0 for g in groups) else 128
    n_in = inner - 1 + len(near) + len(far)

    def body(where_ref, hidden_ref, *rest):
        blocks, rest = rest[: inner - 1], rest[inner - 1 :]
        near_refs, rest = rest[: len(near)], rest[len(near) :]
        far_refs, rest = rest[: len(far)], rest[len(far) :]
        outs = rest[:-3]
        x_all, w_all, sems = rest[-3:]
        me, dp = where_ref[0], where_ref[1]
        pairs = []
        for side, bit in enumerate((0, inner)):
            start = pl.multiple_of((me ^ bit) * rows_w, 128)
            pairs.append(
                (
                    hidden_ref.at[:, pl.ds(start, rows_w)],
                    x_all.at[pl.ds(0, tokens), pl.ds(side * rows_w, rows_w)],
                )
            )
        for k in range(1, inner):
            pairs.append((blocks[k - 1], x_all.at[pl.ds(k * tokens, tokens)]))
        to = 0
        for ref, (_, start, wide) in zip(near_refs, near):
            pairs.append((ref.at[:, pl.ds(start, wide)], w_all.at[pl.ds(0, rows_w), pl.ds(to, wide)]))
            to += wide
        for slot, o in enumerate(order):
            to = pl.multiple_of(rows_w + (dp ^ o) * share, 16)
            pairs.append((far_refs[slot // slots].at[slot % slots], w_all.at[pl.ds(to, share)]))
        run_copies([pltpu.make_async_copy(a, b, sems.at[i]) for i, (a, b) in enumerate(pairs)])

        base = 0
        for g, wide in enumerate(groups):

            @pl.loop(0, wide // step)
            def _(n, g=g, base=base):
                at = pl.multiple_of(n * step, 128)
                product = jnp.dot(
                    x_all[...], w_all[:, pl.ds(base + at, step)], preferred_element_type=F32
                )
                for k in range(inner):
                    outs[g * inner + k][:, pl.ds(at, step)] = product[k * tokens : (k + 1) * tokens]

            base += wide

    copies = 2 + (inner - 1) + len(near) + n_dp
    moved = inner * tokens * 2 * rows_w * 2 + 2 * rows_w * cols * 2 + inner * tokens * cols * 4
    out = pl.pallas_call(
        body,
        in_specs=[pl.BlockSpec(memory_space=pltpu.SMEM)]
        + [pl.BlockSpec(memory_space=pl.ANY)] * (1 + n_in),
        out_specs=[pl.BlockSpec(memory_space=pltpu.VMEM)] * (inner * len(groups)),
        out_shape=[jax.ShapeDtypeStruct((tokens, g), F32) for g in groups for _ in range(inner)],
        scratch_shapes=[
            pltpu.VMEM((inner * tokens, 2 * rows_w), BF16),
            pltpu.VMEM((2 * rows_w, cols), BF16),
            pltpu.SemaphoreType.DMA((copies,)),
        ],
        compiler_params=params(),
        cost_estimate=pl.CostEstimate(
            flops=2 * inner * tokens * 2 * rows_w * cols, bytes_accessed=moved, transcendentals=0
        ),
        name="multiply",
    )(where, hidden, *received, *[array for array, _, _ in near], *far)
    return [list(out[g * inner : (g + 1) * inner]) for g in range(len(groups))]


def attend(where, lengths, partials, d_attn, cache, c_order, group, g_order):
    tokens = d_attn.shape[0]
    n_blocks, block, head_dim = cache[0].shape
    slots = n_blocks // len(group)
    n_convs = lengths.shape[1]
    scale = head_dim ** (-0.5)
    to_log2 = scale * math.log2(math.e)
    n_heads = d_attn.shape[1] // head_dim
    pair = 2 if n_heads % 2 == 0 else 1
    lanes = pair * tokens
    n_cache = n_blocks * block
    n_group = n_blocks * tokens
    chunk = 512
    n_part = sum(len(terms) for terms in partials)

    def body(where_ref, len_ref, d_ref, *rest):
        cache_refs, rest = rest[:2], rest[2:]
        group_refs, rest = rest[: len(group)], rest[len(group) :]
        part_refs = list(rest[:n_part])
        keep_ref, give_ref, gk, gv, s_ref, p_ref, q_ref, ck_ref, cv_ref = rest[n_part:]
        me, dp = where_ref[0], where_ref[1]
        even = dp % 2 == 0

        @pl.when(even)
        def _():
            ck_ref[...] = cache_refs[0][...]
            cv_ref[...] = cache_refs[1][...]

        @pl.when(jnp.logical_not(even))
        def _():
            ck_ref[...] = cache_refs[1][...]
            cv_ref[...] = cache_refs[0][...]

        h = 0
        for terms in partials:
            refs, part_refs = part_refs[: len(terms)], part_refs[len(terms) :]
            for at in range(0, terms[0].shape[1], head_dim):
                q = refs[0][:, at : at + head_dim]
                for ref in refs[1:]:
                    q = q + ref[:, at : at + head_dim]
                q_ref[h, 0] = q.astype(BF16)
                q_ref[h, 1] = d_ref[:, h * head_dim : (h + 1) * head_dim]
                h += 1

        q_pos = me * tokens + lax.broadcasted_iota(jnp.int32, (1, lanes), 1) % tokens
        begin = jnp.zeros((1, lanes), jnp.int32)
        end = jnp.int32(0)
        for i in range(n_convs):
            end = end + len_ref[0, i]
            begin = jnp.where(end <= q_pos, end, begin)

        @pl.loop(0, n_heads // pair)
        def _(step):
            rows_q = jnp.concatenate([q_ref[step * pair + i, 0] for i in range(pair)], axis=0)
            rows_d = jnp.concatenate([q_ref[step * pair + i, 1] for i in range(pair)], axis=0)
            dims = (((1,), (1,)), ((), ()))
            top = jnp.full((1, lanes), -jnp.inf, F32)
            cache_spans = [
                (b, r, min(chunk, block)) for b in range(n_blocks) for r in range(0, block, min(chunk, block))
            ]
            for b, r, size in cache_spans:
                s = lax.dot_general(
                    ck_ref[b, r : r + size], rows_q, dims, preferred_element_type=F32
                )
                s_ref[pl.ds(b * block + r, size)] = s
                top = jnp.maximum(top, jnp.max(s, axis=0, keepdims=True))
            for b in range(n_blocks):
                s = lax.dot_general(group_refs[b // slots][b % slots, :, :head_dim], rows_q, dims, preferred_element_type=F32)
                pos = (me ^ g_order[b]) * tokens + lax.broadcasted_iota(jnp.int32, (tokens, lanes), 0)
                s = jnp.where((pos <= q_pos) & (pos >= begin), s, -jnp.inf)
                s_ref[pl.ds(n_cache + b * tokens, tokens)] = s
                top = jnp.maximum(top, jnp.max(s, axis=0, keepdims=True))
            total = jnp.zeros((1, lanes), F32)
            for r in range(0, n_cache + n_group, chunk):
                e = jnp.exp2((s_ref[pl.ds(r, chunk)] - top) * to_log2)
                s_ref[pl.ds(r, chunk)] = e
                total = total + jnp.sum(e, axis=0, keepdims=True)
            inv = 1.0 / total
            delta = jnp.zeros((1, lanes), F32)
            for b in range(n_blocks):
                p = s_ref[pl.ds(n_cache + b * tokens, tokens)] * inv
                dp_ = lax.dot_general(group_refs[b // slots][b % slots, :, head_dim:], rows_d, dims, preferred_element_type=F32)
                delta = delta + jnp.sum(p.astype(BF16).astype(F32) * dp_, axis=0, keepdims=True)
            for b, r, size in cache_spans:
                at = pl.ds(b * block + r, size)
                p = s_ref[at] * inv
                pb = p.astype(BF16)
                dp_ = lax.dot_general(
                    cv_ref[b, r : r + size], rows_d, dims, preferred_element_type=F32
                )
                s_ref[at] = p
                p_ref[at] = dp_
                delta = delta + jnp.sum(pb.astype(F32) * dp_, axis=0, keepdims=True)
                g = jnp.dot(pb, rows_d, preferred_element_type=F32)
                gv[at] = jnp.where(step == 0, 0.0, gv[at]) + g
            for b, r, size in cache_spans:
                at = pl.ds(b * block + r, size)
                ds = (s_ref[at] * (p_ref[at] - delta)).astype(BF16)
                g = jnp.dot(ds, rows_q, preferred_element_type=F32)
                gk[at] = jnp.where(step == 0, 0.0, gk[at]) + g

        @pl.when(even)
        def _():
            keep_ref[...] = gk[...] * scale
            give_ref[...] = gv[...]

        @pl.when(jnp.logical_not(even))
        def _():
            keep_ref[...] = gv[...]
            give_ref[...] = gk[...] * scale

    rows = n_heads * tokens
    flops = 2 * rows * head_dim * (5 * n_cache + 2 * n_group)
    return pl.pallas_call(
        body,
        in_specs=[pl.BlockSpec(memory_space=pltpu.SMEM)] * 2
        + [pl.BlockSpec(memory_space=pltpu.VMEM)] * (3 + len(group) + n_part),
        out_specs=[pl.BlockSpec(memory_space=pltpu.VMEM)] * 2,
        out_shape=[jax.ShapeDtypeStruct((n_cache, head_dim), F32)] * 2,
        scratch_shapes=[
            pltpu.VMEM((n_cache, head_dim), F32),
            pltpu.VMEM((n_cache, head_dim), F32),
            pltpu.VMEM((n_cache + n_group, lanes), F32),
            pltpu.VMEM((n_cache, lanes), F32),
            pltpu.VMEM((n_heads, 2, tokens, head_dim), BF16),
            pltpu.VMEM((n_blocks, block, head_dim), BF16),
            pltpu.VMEM((n_blocks, block, head_dim), BF16),
        ],
        compiler_params=params(),
        cost_estimate=pl.CostEstimate(
            flops=flops,
            bytes_accessed=12 * n_cache * head_dim,
            transcendentals=rows * (n_cache + n_group),
        ),
        name="attend",
    )(where, lengths, d_attn, *cache, *group, *[term for terms in partials for term in terms])


def make_on_device(n_dp, n_fsdp):
    inner = n_fsdp // 2

    def on_device(hidden, d_attn, w_query, w_key, w_value, cache_keys, cache_values, lengths):
        me = lax.axis_index("fsdp")
        dp = lax.axis_index("dp")
        where = jnp.stack([me, dp]).astype(jnp.int32)
        head_dim = w_key.shape[1]
        q_width = w_query.shape[1]
        even = dp % 2 == 0
        f_bits, d_bits = bits_down(n_fsdp), bits_down(n_dp)

        def from_owners(products):
            return [products[0]] + [swap(x, "fsdp", n_fsdp, k + 1) for k, x in enumerate(products[1:])]

        sent, part_kv, part_q = prepare(where, hidden, w_query, w_key, w_value, n_dp, n_fsdp)
        received = [swap(block, "fsdp", n_fsdp, k + 1) for k, block in enumerate(sent)]
        part_q = swap(part_q, "fsdp", n_fsdp, inner)
        part_kv = swap(part_kv, "fsdp", n_fsdp, inner)
        far_kv, order = double(part_kv[None], [0], "dp", n_dp, d_bits[0])
        middle = part_q.shape[0] // 2
        halves = [swap(part_q[:middle], "dp", n_dp, d_bits[0]), swap(part_q[middle:], "dp", n_dp, d_bits[0])]
        cache = jnp.where(even, cache_keys, cache_values)[None]
        tied = together(part_q, *halves, far_kv, cache, *received)
        part_q, halves, far_kv, cache, received = tied[0], tied[1:3], tied[3], tied[4], tied[5:]
        far_q = jnp.stack([part_q, jnp.concatenate(halves)])
        far_q, d_order = finish(far_q, order, "dp", n_dp, d_bits[1:])
        far_kv, _ = finish(far_kv, order, "dp", n_dp, d_bits[1:])
        near_kv = [(w_key, 0, head_dim), (w_value, 0, head_dim)]
        (out_kv,) = multiply(
            where, hidden, received, near_kv, far_kv, d_order, n_fsdp, (2 * head_dim,)
        )
        cache, f_order = double(cache, [0], "fsdp", n_fsdp, f_bits[0])
        far_q[1], cache, out_kv[0] = together(far_q[1], cache, out_kv[0])
        parts_kv = from_owners(out_kv)
        own = functools.reduce(lambda a, b: a + b, parts_kv).astype(BF16)
        group = [own] + [swap(own, "fsdp", n_fsdp, k) for k in range(1, inner)]
        (out_q,) = multiply(
            where, hidden, received, [(w_query, 0, q_width)], far_q, d_order, n_fsdp, (q_width,)
        )
        for bit in f_bits[1:]:
            cache, f_order = double(cache, f_order, "fsdp", n_fsdp, bit)
        tied = together(cache, *out_q, *group)
        cache, out_q, group = tied[0], tied[1 : 1 + inner], tied[1 + inner :]
        g_order = [o for o in f_order if o < inner]
        group = jnp.stack([group[o] for o in g_order])
        group, g_order = finish(group, g_order, "fsdp", n_fsdp, [inner])
        parts_q = from_owners(out_q)
        cache = (cache, swap(cache, "dp", n_dp, 1))

        keep, give = attend(where, lengths, [parts_q], d_attn, cache, f_order, group, g_order)

        half = keep + swap(give, "dp", n_dp, 1)
        size = half.shape[0] // n_fsdp
        mine = half[:size]
        for slot in range(1, n_fsdp):
            out = half[slot * size : (slot + 1) * size].astype(BF16)
            mine = mine + swap(out, "fsdp", n_fsdp, f_order[slot]).astype(F32)
        for bit in bits_down(n_dp)[:-2]:
            mine = mine + swap(mine, "dp", n_dp, bit)
        beside, other, across = (swap(mine, "dp", n_dp, bit) for bit in (2, 1, 3))
        mine = mine + beside
        other = other + across
        return jnp.where(even, mine, other), jnp.where(even, other, mine)

    return on_device


def solution(mesh):
    placed = (
        P(("dp", "fsdp"), None),
        P(("dp", "fsdp"), None),
        P("fsdp", None),
        P("fsdp", None),
        P("fsdp", None),
        P("fsdp", None),
        P("fsdp", None),
        P("dp", None),
    )
    return jax.shard_map(
        make_on_device(mesh.shape["dp"], mesh.shape["fsdp"]),
        mesh=mesh,
        in_specs=placed,
        out_specs=(P("fsdp", None), P("fsdp", None)),
        check_vma=False,
    )
```

```python
import functools
import math

import jax
import jax.numpy as jnp
from jax import lax
from jax.experimental import pallas as pl
from jax.experimental.pallas import tpu as pltpu
from jax.sharding import PartitionSpec as P

F32 = jnp.float32
BF16 = jnp.bfloat16
VMEM_LIMIT = 56 * 1024 * 1024


def swap(value, axis, size, bit):
    return lax.ppermute(value, axis, [(i, i ^ bit) for i in range(size)])


def bits_down(size):
    bits = []
    bit = size // 2
    while bit:
        bits.append(bit)
        bit //= 2
    return bits


def double(block, order, axis, size, bit):
    return jnp.concatenate([block, swap(block, axis, size, bit)]), order + [o ^ bit for o in order]


def finish(block, order, axis, size, bits):
    for bit in bits[:-1]:
        block, order = double(block, order, axis, size, bit)
    return [block, swap(block, axis, size, bits[-1])], order + [o ^ bits[-1] for o in order]


def together(*values):
    return lax.optimization_barrier(values)


def params():
    return pltpu.CompilerParams(vmem_limit_bytes=VMEM_LIMIT)


def run_copies(copies):
    for copy in copies:
        copy.start()
    for copy in copies:
        copy.wait()


def prepare(where, hidden, w_query, w_key, w_value, n_dp, n_fsdp):
    inner = n_fsdp // 2
    tokens = hidden.shape[0]
    rows_w, q_width = w_query.shape
    head_dim = w_key.shape[1]
    share = rows_w // n_dp

    def body(where_ref, hidden_ref, wq_ref, wk_ref, wv_ref, *rest):
        sent, part_kv, part_q, sems = rest[: inner - 1], rest[-3], rest[-2], rest[-1]
        me, dp = where_ref[0], where_ref[1]
        rows = pl.ds(pl.multiple_of(dp * share, 16), share)
        pairs = [
            (wk_ref.at[rows], part_kv.at[:, pl.ds(0, head_dim)]),
            (wv_ref.at[rows], part_kv.at[:, pl.ds(head_dim, head_dim)]),
            (wq_ref.at[rows], part_q),
        ]
        for k in range(1, inner):
            for side, bit in enumerate((0, inner)):
                start = pl.multiple_of((me ^ k ^ bit) * rows_w, 128)
                pairs.append(
                    (hidden_ref.at[:, pl.ds(start, rows_w)], sent[k - 1].at[:, pl.ds(side * rows_w, rows_w)])
                )
        run_copies([pltpu.make_async_copy(a, b, sems.at[i]) for i, (a, b) in enumerate(pairs)])

    moved = 2 * (tokens * 2 * rows_w * 2 * (inner - 1) + share * (q_width + 2 * head_dim) * 2)
    out = pl.pallas_call(
        body,
        in_specs=[pl.BlockSpec(memory_space=pltpu.SMEM)] + [pl.BlockSpec(memory_space=pl.ANY)] * 4,
        out_specs=[pl.BlockSpec(memory_space=pltpu.VMEM)] * (inner + 1),
        out_shape=[jax.ShapeDtypeStruct((tokens, 2 * rows_w), BF16)] * (inner - 1)
        + [
            jax.ShapeDtypeStruct((share, 2 * head_dim), BF16),
            jax.ShapeDtypeStruct((share, q_width), BF16),
        ],
        scratch_shapes=[pltpu.SemaphoreType.DMA((3 + 2 * (inner - 1),))],
        compiler_params=params(),
        cost_estimate=pl.CostEstimate(flops=0, bytes_accessed=moved, transcendentals=0),
        name="prepare",
    )(where, hidden, w_query, w_key, w_value)
    return out[: inner - 1], out[-2], out[-1]


def multiply(where, hidden, received, near, far, order, n_fsdp, groups):
    inner = n_fsdp // 2
    tokens = hidden.shape[0]
    slots, share, cols = far[0].shape
    n_dp = slots * len(far)
    rows_w = n_dp * share
    step = 256 if all(g % 256 == 0 for g in groups) else 128
    n_in = inner - 1 + len(near) + len(far)

    def body(where_ref, hidden_ref, *rest):
        blocks, rest = rest[: inner - 1], rest[inner - 1 :]
        near_refs, rest = rest[: len(near)], rest[len(near) :]
        far_refs, rest = rest[: len(far)], rest[len(far) :]
        outs = rest[:-3]
        x_all, w_all, sems = rest[-3:]
        me, dp = where_ref[0], where_ref[1]
        pairs = []
        for side, bit in enumerate((0, inner)):
            start = pl.multiple_of((me ^ bit) * rows_w, 128)
            pairs.append(
                (
                    hidden_ref.at[:, pl.ds(start, rows_w)],
                    x_all.at[pl.ds(0, tokens), pl.ds(side * rows_w, rows_w)],
                )
            )
        for k in range(1, inner):
            pairs.append((blocks[k - 1], x_all.at[pl.ds(k * tokens, tokens)]))
        to = 0
        for ref, (_, start, wide) in zip(near_refs, near):
            pairs.append((ref.at[:, pl.ds(start, wide)], w_all.at[pl.ds(0, rows_w), pl.ds(to, wide)]))
            to += wide
        for slot, o in enumerate(order):
            to = pl.multiple_of(rows_w + (dp ^ o) * share, 16)
            pairs.append((far_refs[slot // slots].at[slot % slots], w_all.at[pl.ds(to, share)]))
        run_copies([pltpu.make_async_copy(a, b, sems.at[i]) for i, (a, b) in enumerate(pairs)])

        base = 0
        for g, wide in enumerate(groups):

            @pl.loop(0, wide // step)
            def _(n, g=g, base=base):
                at = pl.multiple_of(n * step, 128)
                product = jnp.dot(
                    x_all[...], w_all[:, pl.ds(base + at, step)], preferred_element_type=F32
                )
                for k in range(inner):
                    outs[g * inner + k][:, pl.ds(at, step)] = product[k * tokens : (k + 1) * tokens]

            base += wide

    copies = 2 + (inner - 1) + len(near) + n_dp
    moved = inner * tokens * 2 * rows_w * 2 + 2 * rows_w * cols * 2 + inner * tokens * cols * 4
    out = pl.pallas_call(
        body,
        in_specs=[pl.BlockSpec(memory_space=pltpu.SMEM)]
        + [pl.BlockSpec(memory_space=pl.ANY)] * (1 + n_in),
        out_specs=[pl.BlockSpec(memory_space=pltpu.VMEM)] * (inner * len(groups)),
        out_shape=[jax.ShapeDtypeStruct((tokens, g), F32) for g in groups for _ in range(inner)],
        scratch_shapes=[
            pltpu.VMEM((inner * tokens, 2 * rows_w), BF16),
            pltpu.VMEM((2 * rows_w, cols), BF16),
            pltpu.SemaphoreType.DMA((copies,)),
        ],
        compiler_params=params(),
        cost_estimate=pl.CostEstimate(
            flops=2 * inner * tokens * 2 * rows_w * cols, bytes_accessed=moved, transcendentals=0
        ),
        name="multiply",
    )(where, hidden, *received, *[array for array, _, _ in near], *far)
    return [list(out[g * inner : (g + 1) * inner]) for g in range(len(groups))]


def attend(where, lengths, partials, d_attn, cache, c_order, group, g_order):
    tokens = d_attn.shape[0]
    n_blocks, block, head_dim = cache[0].shape
    slots = n_blocks // len(group)
    n_convs = lengths.shape[1]
    scale = head_dim ** (-0.5)
    to_log2 = scale * math.log2(math.e)
    n_heads = d_attn.shape[1] // head_dim
    pair = 2 if n_heads % 2 == 0 else 1
    lanes = pair * tokens
    n_cache = n_blocks * block
    n_group = n_blocks * tokens
    chunk = 512
    n_part = sum(len(terms) for terms in partials)

    def body(where_ref, len_ref, d_ref, *rest):
        cache_refs, rest = rest[:2], rest[2:]
        group_refs, rest = rest[: len(group)], rest[len(group) :]
        part_refs = list(rest[:n_part])
        keep_ref, give_ref, gk, gv, s_ref, p_ref, q_ref, ck_ref, cv_ref = rest[n_part:]
        me, dp = where_ref[0], where_ref[1]
        even = dp % 2 == 0

        @pl.when(even)
        def _():
            ck_ref[...] = cache_refs[0][...]
            cv_ref[...] = cache_refs[1][...]

        @pl.when(jnp.logical_not(even))
        def _():
            ck_ref[...] = cache_refs[1][...]
            cv_ref[...] = cache_refs[0][...]

        h = 0
        for terms in partials:
            refs, part_refs = part_refs[: len(terms)], part_refs[len(terms) :]
            for at in range(0, terms[0].shape[1], head_dim):
                q = refs[0][:, at : at + head_dim]
                for ref in refs[1:]:
                    q = q + ref[:, at : at + head_dim]
                q_ref[h, 0] = q.astype(BF16)
                q_ref[h, 1] = d_ref[:, h * head_dim : (h + 1) * head_dim]
                h += 1

        q_pos = me * tokens + lax.broadcasted_iota(jnp.int32, (1, lanes), 1) % tokens
        begin = jnp.zeros((1, lanes), jnp.int32)
        end = jnp.int32(0)
        for i in range(n_convs):
            end = end + len_ref[0, i]
            begin = jnp.where(end <= q_pos, end, begin)

        @pl.loop(0, n_heads // pair)
        def _(step):
            rows_q = jnp.concatenate([q_ref[step * pair + i, 0] for i in range(pair)], axis=0)
            rows_d = jnp.concatenate([q_ref[step * pair + i, 1] for i in range(pair)], axis=0)
            dims = (((1,), (1,)), ((), ()))
            top = jnp.full((1, lanes), -jnp.inf, F32)
            cache_spans = [
                (b, r, min(chunk, block)) for b in range(n_blocks) for r in range(0, block, min(chunk, block))
            ]
            for b, r, size in cache_spans:
                s = lax.dot_general(
                    ck_ref[b, r : r + size], rows_q, dims, preferred_element_type=F32
                )
                s_ref[pl.ds(b * block + r, size)] = s
                top = jnp.maximum(top, jnp.max(s, axis=0, keepdims=True))
            for b in range(n_blocks):
                s = lax.dot_general(group_refs[b // slots][b % slots, :, :head_dim], rows_q, dims, preferred_element_type=F32)
                pos = (me ^ g_order[b]) * tokens + lax.broadcasted_iota(jnp.int32, (tokens, lanes), 0)
                s = jnp.where((pos <= q_pos) & (pos >= begin), s, -jnp.inf)
                s_ref[pl.ds(n_cache + b * tokens, tokens)] = s
                top = jnp.maximum(top, jnp.max(s, axis=0, keepdims=True))
            total = jnp.zeros((1, lanes), F32)
            for r in range(0, n_cache + n_group, chunk):
                e = jnp.exp2((s_ref[pl.ds(r, chunk)] - top) * to_log2)
                s_ref[pl.ds(r, chunk)] = e
                total = total + jnp.sum(e, axis=0, keepdims=True)
            inv = 1.0 / total
            delta = jnp.zeros((1, lanes), F32)
            for b in range(n_blocks):
                p = s_ref[pl.ds(n_cache + b * tokens, tokens)] * inv
                dp_ = lax.dot_general(group_refs[b // slots][b % slots, :, head_dim:], rows_d, dims, preferred_element_type=F32)
                delta = delta + jnp.sum(p.astype(BF16).astype(F32) * dp_, axis=0, keepdims=True)
            for b, r, size in cache_spans:
                at = pl.ds(b * block + r, size)
                p = s_ref[at] * inv
                pb = p.astype(BF16)
                dp_ = lax.dot_general(
                    cv_ref[b, r : r + size], rows_d, dims, preferred_element_type=F32
                )
                s_ref[at] = p
                p_ref[at] = dp_
                delta = delta + jnp.sum(pb.astype(F32) * dp_, axis=0, keepdims=True)
                g = jnp.dot(pb, rows_d, preferred_element_type=F32)
                gv[at] = jnp.where(step == 0, 0.0, gv[at]) + g
            for b, r, size in cache_spans:
                at = pl.ds(b * block + r, size)
                ds = (s_ref[at] * (p_ref[at] - delta)).astype(BF16)
                g = jnp.dot(ds, rows_q, preferred_element_type=F32)
                gk[at] = jnp.where(step == 0, 0.0, gk[at]) + g

        @pl.when(even)
        def _():
            keep_ref[...] = gk[...] * scale
            give_ref[...] = gv[...]

        @pl.when(jnp.logical_not(even))
        def _():
            keep_ref[...] = gv[...]
            give_ref[...] = gk[...] * scale

    rows = n_heads * tokens
    flops = 2 * rows * head_dim * (5 * n_cache + 2 * n_group)
    return pl.pallas_call(
        body,
        in_specs=[pl.BlockSpec(memory_space=pltpu.SMEM)] * 2
        + [pl.BlockSpec(memory_space=pltpu.VMEM)] * (3 + len(group) + n_part),
        out_specs=[pl.BlockSpec(memory_space=pltpu.VMEM)] * 2,
        out_shape=[jax.ShapeDtypeStruct((n_cache, head_dim), F32)] * 2,
        scratch_shapes=[
            pltpu.VMEM((n_cache, head_dim), F32),
            pltpu.VMEM((n_cache, head_dim), F32),
            pltpu.VMEM((n_cache + n_group, lanes), F32),
            pltpu.VMEM((n_cache, lanes), F32),
            pltpu.VMEM((n_heads, 2, tokens, head_dim), BF16),
            pltpu.VMEM((n_blocks, block, head_dim), BF16),
            pltpu.VMEM((n_blocks, block, head_dim), BF16),
        ],
        compiler_params=params(),
        cost_estimate=pl.CostEstimate(
            flops=flops,
            bytes_accessed=12 * n_cache * head_dim,
            transcendentals=rows * (n_cache + n_group),
        ),
        name="attend",
    )(where, lengths, d_attn, *cache, *group, *[term for terms in partials for term in terms])


def make_on_device(n_dp, n_fsdp):
    inner = n_fsdp // 2

    def on_device(hidden, d_attn, w_query, w_key, w_value, cache_keys, cache_values, lengths):
        me = lax.axis_index("fsdp")
        dp = lax.axis_index("dp")
        where = jnp.stack([me, dp]).astype(jnp.int32)
        head_dim = w_key.shape[1]
        q_width = w_query.shape[1]
        even = dp % 2 == 0
        f_bits, d_bits = bits_down(n_fsdp), bits_down(n_dp)

        def from_owners(products):
            return [products[0]] + [swap(x, "fsdp", n_fsdp, k + 1) for k, x in enumerate(products[1:])]

        sent, part_kv, part_q = prepare(where, hidden, w_query, w_key, w_value, n_dp, n_fsdp)
        received = [swap(block, "fsdp", n_fsdp, k + 1) for k, block in enumerate(sent)]
        part_q = swap(part_q, "fsdp", n_fsdp, inner)
        part_kv = swap(part_kv, "fsdp", n_fsdp, inner)
        far_kv, order = double(part_kv[None], [0], "dp", n_dp, d_bits[0])
        cache = jnp.where(even, cache_keys, cache_values)[None]
        middle = part_q.shape[0] // 2
        halves = [swap(part_q[:middle], "dp", n_dp, d_bits[0]), swap(part_q[middle:], "dp", n_dp, d_bits[0])]
        far_kv, cache, halves[0], *received = together(far_kv, cache, halves[0], *received)
        far_kv, d_order = finish(far_kv, order, "dp", n_dp, d_bits[1:])
        near_kv = [(w_key, 0, head_dim), (w_value, 0, head_dim)]
        (out_kv,) = multiply(
            where, hidden, received, near_kv, far_kv, d_order, n_fsdp, (2 * head_dim,)
        )
        cache, f_order = double(cache, [0], "fsdp", n_fsdp, f_bits[0])
        part_q, cache, out_kv[0], *halves = together(part_q, cache, out_kv[0], *halves)
        far_q = jnp.stack([part_q, jnp.concatenate(halves)])
        far_q, _ = finish(far_q, order, "dp", n_dp, d_bits[1:])
        parts_kv = from_owners(out_kv)
        cache, f_order = double(cache, f_order, "fsdp", n_fsdp, f_bits[1])
        far_q[1], cache, *parts_kv = together(far_q[1], cache, *parts_kv)
        own = functools.reduce(lambda a, b: a + b, parts_kv).astype(BF16)
        group = [own] + [swap(own, "fsdp", n_fsdp, k) for k in range(1, inner)]
        (out_q,) = multiply(
            where, hidden, received, [(w_query, 0, q_width)], far_q, d_order, n_fsdp, (q_width,)
        )
        for bit in f_bits[2:]:
            cache, f_order = double(cache, f_order, "fsdp", n_fsdp, bit)
        tied = together(cache, *out_q, *group)
        cache, out_q, group = tied[0], tied[1 : 1 + inner], tied[1 + inner :]
        g_order = [o for o in f_order if o < inner]
        group = jnp.stack([group[o] for o in g_order])
        group, g_order = finish(group, g_order, "fsdp", n_fsdp, [inner])
        parts_q = from_owners(out_q)
        cache = (cache, swap(cache, "dp", n_dp, 1))

        keep, give = attend(where, lengths, [parts_q], d_attn, cache, f_order, group, g_order)

        half = keep + swap(give, "dp", n_dp, 1)
        size = half.shape[0] // n_fsdp
        mine = half[:size]
        for slot in range(1, n_fsdp):
            out = half[slot * size : (slot + 1) * size].astype(BF16)
            mine = mine + swap(out, "fsdp", n_fsdp, f_order[slot]).astype(F32)
        for bit in bits_down(n_dp)[:-2]:
            mine = mine + swap(mine, "dp", n_dp, bit)
        beside, other, across = (swap(mine, "dp", n_dp, bit) for bit in (2, 1, 3))
        mine = mine + beside
        other = other + across
        return jnp.where(even, mine, other), jnp.where(even, other, mine)

    return on_device


def solution(mesh):
    placed = (
        P(("dp", "fsdp"), None),
        P(("dp", "fsdp"), None),
        P("fsdp", None),
        P("fsdp", None),
        P("fsdp", None),
        P("fsdp", None),
        P("fsdp", None),
        P("dp", None),
    )
    return jax.shard_map(
        make_on_device(mesh.shape["dp"], mesh.shape["fsdp"]),
        mesh=mesh,
        in_specs=placed,
        out_specs=(P("fsdp", None), P("fsdp", None)),
        check_vma=False,
    )
```

```python
import functools
import math

import jax
import jax.numpy as jnp
from jax import lax
from jax.experimental import pallas as pl
from jax.experimental.pallas import tpu as pltpu
from jax.sharding import PartitionSpec as P

F32 = jnp.float32
BF16 = jnp.bfloat16
VMEM_LIMIT = 56 * 1024 * 1024


def swap(value, axis, size, bit):
    return lax.ppermute(value, axis, [(i, i ^ bit) for i in range(size)])


def bits_down(size):
    bits = []
    bit = size // 2
    while bit:
        bits.append(bit)
        bit //= 2
    return bits


def double(block, order, axis, size, bit):
    return jnp.concatenate([block, swap(block, axis, size, bit)]), order + [o ^ bit for o in order]


def finish(block, order, axis, size, bits):
    for bit in bits[:-1]:
        block, order = double(block, order, axis, size, bit)
    return [block, swap(block, axis, size, bits[-1])], order + [o ^ bits[-1] for o in order]


def together(*values):
    return lax.optimization_barrier(values)


def params():
    return pltpu.CompilerParams(vmem_limit_bytes=VMEM_LIMIT)


def run_copies(copies):
    for copy in copies:
        copy.start()
    for copy in copies:
        copy.wait()


def prepare(hidden, w_query, w_key, w_value, n_dp, n_fsdp):
    inner = n_fsdp // 2
    tokens = hidden.shape[0]
    rows_w, q_width = w_query.shape
    head_dim = w_key.shape[1]
    share = rows_w // n_dp
    cols = q_width // 2

    def body(hidden_ref, wq_ref, wk_ref, wv_ref, *rest):
        sent, part, sems = rest[: inner - 1], rest[-2], rest[-1]
        me, dp = lax.axis_index("fsdp"), lax.axis_index("dp")
        first = pl.multiple_of(dp * share, 16)
        rows = pl.ds(first, share)
        pairs = []
        for i in range(2):
            pairs.append((wq_ref.at[rows, pl.ds(i * cols, cols)], part.at[pl.ds(i * share, share)]))
            for j, ref in enumerate((wk_ref, wv_ref)):
                to = part.at[pl.ds(2 * share, share // 2), pl.ds((2 * i + j) * head_dim, head_dim)]
                pairs.append((ref.at[pl.ds(first + i * (share // 2), share // 2)], to))
        for k in range(1, inner):
            for side, bit in enumerate((0, inner)):
                start = pl.multiple_of((me ^ k ^ bit) * rows_w, 128)
                pairs.append(
                    (hidden_ref.at[:, pl.ds(start, rows_w)], sent[k - 1].at[:, pl.ds(side * rows_w, rows_w)])
                )
        run_copies([pltpu.make_async_copy(a, b, sems.at[i]) for i, (a, b) in enumerate(pairs)])

    moved = 2 * (tokens * 2 * rows_w * 2 * (inner - 1) + share * (q_width + 2 * head_dim) * 2)
    out = pl.pallas_call(
        body,
        in_specs=[pl.BlockSpec(memory_space=pl.ANY)] * 4,
        out_specs=[pl.BlockSpec(memory_space=pltpu.VMEM)] * inner,
        out_shape=[jax.ShapeDtypeStruct((tokens, 2 * rows_w), BF16)] * (inner - 1)
        + [jax.ShapeDtypeStruct((2 * share + share // 2, cols), BF16)],
        scratch_shapes=[pltpu.SemaphoreType.DMA((6 + 2 * (inner - 1),))],
        compiler_params=params(),
        cost_estimate=pl.CostEstimate(flops=0, bytes_accessed=moved, transcendentals=0),
        name="prepare",
    )(hidden, w_query, w_key, w_value)
    return out[:-1], out[-1]


def multiply(hidden, received, near, far, order, n_fsdp, groups):
    inner = n_fsdp // 2
    tokens = hidden.shape[0]
    cols = sum(wide for _, _, wide in near)
    slots, rows_far, cols_far = far[0].shape
    packed = cols_far // cols
    share = rows_far * packed
    n_dp = slots * len(far)
    rows_w = n_dp * share
    step = 256 if all(g % 256 == 0 for g in groups) else 128
    n_in = inner - 1 + len(near) + len(far)

    def body(hidden_ref, *rest):
        blocks, rest = rest[: inner - 1], rest[inner - 1 :]
        near_refs, rest = rest[: len(near)], rest[len(near) :]
        far_refs, rest = rest[: len(far)], rest[len(far) :]
        outs = rest[:-3]
        x_all, w_all, sems = rest[-3:]
        me, dp = lax.axis_index("fsdp"), lax.axis_index("dp")
        pairs = []
        for side, bit in enumerate((0, inner)):
            start = pl.multiple_of((me ^ bit) * rows_w, 128)
            pairs.append(
                (
                    hidden_ref.at[:, pl.ds(start, rows_w)],
                    x_all.at[pl.ds(0, tokens), pl.ds(side * rows_w, rows_w)],
                )
            )
        for k in range(1, inner):
            pairs.append((blocks[k - 1], x_all.at[pl.ds(k * tokens, tokens)]))
        to = 0
        for ref, (_, start, wide) in zip(near_refs, near):
            pairs.append((ref.at[:, pl.ds(start, wide)], w_all.at[pl.ds(0, rows_w), pl.ds(to, wide)]))
            to += wide
        for slot, o in enumerate(order):
            for i in range(packed):
                to = pl.multiple_of(rows_w + (dp ^ o) * share + i * rows_far, 16)
                block = far_refs[slot // slots].at[slot % slots]
                pairs.append((block.at[:, pl.ds(i * cols, cols)], w_all.at[pl.ds(to, rows_far)]))
        run_copies([pltpu.make_async_copy(a, b, sems.at[i]) for i, (a, b) in enumerate(pairs)])

        base = 0
        for g, wide in enumerate(groups):

            @pl.loop(0, wide // step)
            def _(n, g=g, base=base):
                at = pl.multiple_of(n * step, 128)
                product = jnp.dot(
                    x_all[...], w_all[:, pl.ds(base + at, step)], preferred_element_type=F32
                )
                for k in range(inner):
                    outs[g * inner + k][:, pl.ds(at, step)] = product[k * tokens : (k + 1) * tokens]

            base += wide

    copies = 2 + (inner - 1) + len(near) + n_dp * packed
    moved = inner * tokens * 2 * rows_w * 2 + 2 * rows_w * cols * 2 + inner * tokens * cols * 4
    out = pl.pallas_call(
        body,
        in_specs=[pl.BlockSpec(memory_space=pl.ANY)] * (1 + n_in),
        out_specs=[pl.BlockSpec(memory_space=pltpu.VMEM)] * (inner * len(groups)),
        out_shape=[jax.ShapeDtypeStruct((tokens, g), F32) for g in groups for _ in range(inner)],
        scratch_shapes=[
            pltpu.VMEM((inner * tokens, 2 * rows_w), BF16),
            pltpu.VMEM((2 * rows_w, cols), BF16),
            pltpu.SemaphoreType.DMA((copies,)),
        ],
        compiler_params=params(),
        cost_estimate=pl.CostEstimate(
            flops=2 * inner * tokens * 2 * rows_w * cols, bytes_accessed=moved, transcendentals=0
        ),
        name="multiply",
    )(hidden, *received, *[array for array, _, _ in near], *far)
    return [list(out[g * inner : (g + 1) * inner]) for g in range(len(groups))]


def attend(lengths, terms, d_attn, first_head, cache, group, g_order, sums):
    tokens = d_attn.shape[0]
    n_blocks, block, head_dim = cache[0].shape
    slots = n_blocks // len(group)
    n_convs = lengths.shape[1]
    scale = head_dim ** (-0.5)
    to_log2 = scale * math.log2(math.e)
    n_heads = terms[0].shape[1] // head_dim
    pair = 2 if n_heads % 2 == 0 else 1
    lanes = pair * tokens
    n_cache = n_blocks * block
    n_group = n_blocks * tokens
    chunk = 512
    n_part, n_sum = len(terms), len(sums)

    def body(len_ref, d_ref, *rest):
        cache_refs, rest = rest[:2], rest[2:]
        group_refs, rest = rest[: len(group)], rest[len(group) :]
        part_refs, rest = rest[:n_part], rest[n_part:]
        sum_refs, rest = rest[:n_sum], rest[n_sum:]
        keep_ref, give_ref, gk, gv, s_ref, p_ref, q_ref, ck_ref, cv_ref, sems = rest
        me, dp = lax.axis_index("fsdp"), lax.axis_index("dp")
        even = dp % 2 == 0

        @pl.when(even)
        def _():
            pltpu.make_async_copy(cache_refs[0], ck_ref, sems.at[0]).start()
            pltpu.make_async_copy(cache_refs[1], cv_ref, sems.at[1]).start()

        @pl.when(jnp.logical_not(even))
        def _():
            pltpu.make_async_copy(cache_refs[1], ck_ref, sems.at[0]).start()
            pltpu.make_async_copy(cache_refs[0], cv_ref, sems.at[1]).start()

        for h in range(n_heads):
            at = slice(h * head_dim, (h + 1) * head_dim)
            q = part_refs[0][:, at]
            for ref in part_refs[1:]:
                q = q + ref[:, at]
            q_ref[h, 0] = q.astype(BF16)
            at = (first_head + h) * head_dim
            q_ref[h, 1] = d_ref[:, at : at + head_dim]

        q_pos = me * tokens + lax.broadcasted_iota(jnp.int32, (1, lanes), 1) % tokens
        begin = jnp.zeros((1, lanes), jnp.int32)
        end = jnp.int32(0)
        for i in range(n_convs):
            end = end + len_ref[0, i]
            begin = jnp.where(end <= q_pos, end, begin)

        pltpu.make_async_copy(cache_refs[0], ck_ref, sems.at[0]).wait()
        pltpu.make_async_copy(cache_refs[1], cv_ref, sems.at[1]).wait()

        @pl.loop(0, n_heads // pair)
        def _(step):
            rows_q = jnp.concatenate([q_ref[step * pair + i, 0] for i in range(pair)], axis=0)
            rows_d = jnp.concatenate([q_ref[step * pair + i, 1] for i in range(pair)], axis=0)
            dims = (((1,), (1,)), ((), ()))
            top = jnp.full((1, lanes), -jnp.inf, F32)
            cache_spans = [
                (b, r, min(chunk, block)) for b in range(n_blocks) for r in range(0, block, min(chunk, block))
            ]
            for b, r, size in cache_spans:
                s = lax.dot_general(
                    ck_ref[b, r : r + size], rows_q, dims, preferred_element_type=F32
                )
                s_ref[pl.ds(b * block + r, size)] = s
                top = jnp.maximum(top, jnp.max(s, axis=0, keepdims=True))
            for b in range(n_blocks):
                s = lax.dot_general(group_refs[b // slots][b % slots, :, :head_dim], rows_q, dims, preferred_element_type=F32)
                pos = (me ^ g_order[b]) * tokens + lax.broadcasted_iota(jnp.int32, (tokens, lanes), 0)
                s = jnp.where((pos <= q_pos) & (pos >= begin), s, -jnp.inf)
                s_ref[pl.ds(n_cache + b * tokens, tokens)] = s
                top = jnp.maximum(top, jnp.max(s, axis=0, keepdims=True))
            total = jnp.zeros((1, lanes), F32)
            for r in range(0, n_cache + n_group, chunk):
                e = jnp.exp2((s_ref[pl.ds(r, chunk)] - top) * to_log2)
                s_ref[pl.ds(r, chunk)] = e
                total = total + jnp.sum(e, axis=0, keepdims=True)
            inv = 1.0 / total
            delta = jnp.zeros((1, lanes), F32)
            for b in range(n_blocks):
                p = s_ref[pl.ds(n_cache + b * tokens, tokens)] * inv
                dp_ = lax.dot_general(group_refs[b // slots][b % slots, :, head_dim:], rows_d, dims, preferred_element_type=F32)
                delta = delta + jnp.sum(p.astype(BF16).astype(F32) * dp_, axis=0, keepdims=True)
            for b, r, size in cache_spans:
                at = pl.ds(b * block + r, size)
                p = s_ref[at] * inv
                pb = p.astype(BF16)
                dp_ = lax.dot_general(
                    cv_ref[b, r : r + size], rows_d, dims, preferred_element_type=F32
                )
                s_ref[at] = p
                p_ref[at] = dp_
                delta = delta + jnp.sum(pb.astype(F32) * dp_, axis=0, keepdims=True)
                g = jnp.dot(pb, rows_d, preferred_element_type=F32)
                gv[at] = jnp.where(step == 0, 0.0, gv[at]) + g
            for b, r, size in cache_spans:
                at = pl.ds(b * block + r, size)
                ds = (s_ref[at] * (p_ref[at] - delta)).astype(BF16)
                g = jnp.dot(ds, rows_q, preferred_element_type=F32)
                gk[at] = jnp.where(step == 0, 0.0, gk[at]) + g

        keep_in, give_in = (sum_refs[0][...], sum_refs[1][...]) if n_sum else (0.0, 0.0)

        @pl.when(even)
        def _():
            keep_ref[...] = keep_in + gk[...] * scale
            give_ref[...] = give_in + gv[...]

        @pl.when(jnp.logical_not(even))
        def _():
            keep_ref[...] = keep_in + gv[...]
            give_ref[...] = give_in + gk[...] * scale

    rows = n_heads * tokens
    flops = 2 * rows * head_dim * (5 * n_cache + 2 * n_group)
    return pl.pallas_call(
        body,
        in_specs=[pl.BlockSpec(memory_space=pltpu.SMEM)]
        + [pl.BlockSpec(memory_space=pltpu.VMEM)]
        + [pl.BlockSpec(memory_space=pl.ANY)] * 2
        + [pl.BlockSpec(memory_space=pltpu.VMEM)] * (len(group) + n_part + n_sum),
        out_specs=[pl.BlockSpec(memory_space=pltpu.VMEM)] * 2,
        out_shape=[jax.ShapeDtypeStruct((n_cache, head_dim), F32)] * 2,
        scratch_shapes=[
            pltpu.VMEM((n_cache, head_dim), F32),
            pltpu.VMEM((n_cache, head_dim), F32),
            pltpu.VMEM((n_cache + n_group, lanes), F32),
            pltpu.VMEM((n_cache, lanes), F32),
            pltpu.VMEM((n_heads, 2, tokens, head_dim), BF16),
            pltpu.VMEM((n_blocks, block, head_dim), BF16),
            pltpu.VMEM((n_blocks, block, head_dim), BF16),
            pltpu.SemaphoreType.DMA((2,)),
        ],
        compiler_params=params(),
        cost_estimate=pl.CostEstimate(
            flops=flops,
            bytes_accessed=12 * n_cache * head_dim,
            transcendentals=rows * (n_cache + n_group),
        ),
        name="attend",
    )(lengths, d_attn, *cache, *group, *terms, *sums)


def make_on_device(n_dp, n_fsdp):
    inner = n_fsdp // 2

    def on_device(hidden, d_attn, w_query, w_key, w_value, cache_keys, cache_values, lengths):
        dp = lax.axis_index("dp")
        head_dim = w_key.shape[1]
        q_width = w_query.shape[1]
        even = dp % 2 == 0
        f_bits, d_bits = bits_down(n_fsdp), bits_down(n_dp)

        def from_owners(products):
            return [products[0]] + [swap(x, "fsdp", n_fsdp, k + 1) for k, x in enumerate(products[1:])]

        cuts = [(0, q_width // 2), (q_width // 2, q_width // 2)]
        cuts = [(0, q_width // 2), (q_width // 2, q_width // 2)]
        sent, part = prepare(hidden, w_query, w_key, w_value, n_dp, n_fsdp)
        received = [swap(block, "fsdp", n_fsdp, k + 1) for k, block in enumerate(sent)]
        part = swap(part, "fsdp", n_fsdp, inner)
        share = w_query.shape[0] // n_dp
        part_a, part_b, part_kv = part[:share], part[share : 2 * share], part[2 * share :]
        far_kv, order = double(part_kv[None], [0], "dp", n_dp, d_bits[0])
        far_a, _ = double(part_a[None], [0], "dp", n_dp, d_bits[0])
        cache = jnp.where(even, cache_keys, cache_values)[None]
        cache, f_order = double(cache, [0], "fsdp", n_fsdp, f_bits[0])
        far_kv, cache, far_a, *received = together(far_kv, cache, far_a, *received)
        far_b, _ = double(part_b[None], [0], "dp", n_dp, d_bits[0])
        far_kv, d_order = finish(far_kv, order, "dp", n_dp, d_bits[1:])
        far_a, _ = finish(far_a, order, "dp", n_dp, d_bits[1:])
        near_kv = [(w_key, 0, head_dim), (w_value, 0, head_dim)]
        (out_kv,) = multiply(
            hidden, received, near_kv, far_kv, d_order, n_fsdp, (2 * head_dim,)
        )
        cache, f_order = double(cache, f_order, "fsdp", n_fsdp, f_bits[1])
        far_a[1], far_b, cache, out_kv[0] = together(far_a[1], far_b, cache, out_kv[0])
        far_b, _ = finish(far_b, order, "dp", n_dp, d_bits[1:])
        for bit in f_bits[2:]:
            cache, f_order = double(cache, f_order, "fsdp", n_fsdp, bit)
        (out_a,) = multiply(
            hidden, received, [(w_query, *cuts[0])], far_a, d_order, n_fsdp, (cuts[0][1],)
        )
        parts_kv = from_owners(out_kv)
        far_b[1], cache, out_a[0], *parts_kv = together(far_b[1], cache, out_a[0], *parts_kv)
        own = functools.reduce(lambda a, b: a + b, parts_kv).astype(BF16)
        group = [own] + [swap(own, "fsdp", n_fsdp, k) for k in range(1, inner)]
        parts_a = from_owners(out_a)
        (out_b,) = multiply(
            hidden, received, [(w_query, *cuts[1])], far_b, d_order, n_fsdp, (cuts[1][1],)
        )
        tied = together(*out_b, *group, *parts_a)
        out_b, group, parts_a = tied[:inner], tied[inner : 2 * inner], tied[2 * inner :]
        g_order = [o for o in f_order if o < inner]
        group = jnp.stack([group[o] for o in g_order])
        group, g_order = finish(group, g_order, "fsdp", n_fsdp, [inner])
        parts_b = from_owners(out_b)
        cache = (cache, swap(cache, "dp", n_dp, 1))
        first = cuts[0][1] // head_dim
        sums = attend(lengths, parts_a, d_attn, 0, cache, group, g_order, ())
        keep, give = attend(lengths, parts_b, d_attn, first, cache, group, g_order, sums)

        half = keep + swap(give, "dp", n_dp, 1)
        size = half.shape[0] // n_fsdp
        mine = half[:size]
        for slot in range(1, n_fsdp):
            out = half[slot * size : (slot + 1) * size].astype(BF16)
            mine = mine + swap(out, "fsdp", n_fsdp, f_order[slot]).astype(F32)
        for bit in bits_down(n_dp)[:-2]:
            mine = mine + swap(mine, "dp", n_dp, bit)
        beside, other, across = (swap(mine, "dp", n_dp, bit) for bit in (2, 1, 3))
        mine = mine + beside
        other = other + across
        return jnp.where(even, mine, other), jnp.where(even, other, mine)

    return on_device


def solution(mesh):
    placed = (
        P(("dp", "fsdp"), None),
        P(("dp", "fsdp"), None),
        P("fsdp", None),
        P("fsdp", None),
        P("fsdp", None),
        P("fsdp", None),
        P("fsdp", None),
        P("dp", None),
    )
    return jax.shard_map(
        make_on_device(mesh.shape["dp"], mesh.shape["fsdp"]),
        mesh=mesh,
        in_specs=placed,
        out_specs=(P("fsdp", None), P("fsdp", None)),
        check_vma=False,
    )
```

```python
import functools
import math

import jax
import jax.numpy as jnp
from jax import lax
from jax.experimental import pallas as pl
from jax.experimental.pallas import tpu as pltpu
from jax.sharding import PartitionSpec as P

F32 = jnp.float32
BF16 = jnp.bfloat16
VMEM_LIMIT = 56 * 1024 * 1024


def swap(value, axis, size, bit):
    return lax.ppermute(value, axis, [(i, i ^ bit) for i in range(size)])


def bits_down(size):
    bits = []
    bit = size // 2
    while bit:
        bits.append(bit)
        bit //= 2
    return bits


def double(block, order, axis, size, bit):
    return jnp.concatenate([block, swap(block, axis, size, bit)]), order + [o ^ bit for o in order]


def finish(block, order, axis, size, bits):
    for bit in bits[:-1]:
        block, order = double(block, order, axis, size, bit)
    return [block, swap(block, axis, size, bits[-1])], order + [o ^ bits[-1] for o in order]


def together(*values):
    return lax.optimization_barrier(values)


def params():
    return pltpu.CompilerParams(vmem_limit_bytes=VMEM_LIMIT)


def run_copies(copies):
    for copy in copies:
        copy.start()
    for copy in copies:
        copy.wait()


def prepare(hidden, w_query, w_key, w_value, n_dp, n_fsdp):
    inner = n_fsdp // 2
    tokens = hidden.shape[0]
    rows_w, q_width = w_query.shape
    head_dim = w_key.shape[1]
    share = rows_w // n_dp
    cols = q_width // 2

    def body(hidden_ref, wq_ref, wk_ref, wv_ref, *rest):
        sent, part, sems = rest[: inner - 1], rest[-2], rest[-1]
        me, dp = lax.axis_index("fsdp"), lax.axis_index("dp")
        first = pl.multiple_of(dp * share, 16)
        rows = pl.ds(first, share)
        pairs = []
        for i in range(2):
            to = part.at[pl.ds(i * (share + share // 2), share)]
            pairs.append((wq_ref.at[rows, pl.ds(i * cols, cols)], to))
            for j, ref in enumerate((wk_ref, wv_ref)):
                to = part.at[pl.ds(share, share // 2), pl.ds((2 * i + j) * head_dim, head_dim)]
                pairs.append((ref.at[pl.ds(first + i * (share // 2), share // 2)], to))
        for k in range(1, inner):
            for side, bit in enumerate((0, inner)):
                start = pl.multiple_of((me ^ k ^ bit) * rows_w, 128)
                pairs.append(
                    (hidden_ref.at[:, pl.ds(start, rows_w)], sent[k - 1].at[:, pl.ds(side * rows_w, rows_w)])
                )
        run_copies([pltpu.make_async_copy(a, b, sems.at[i]) for i, (a, b) in enumerate(pairs)])

    moved = 2 * (tokens * 2 * rows_w * 2 * (inner - 1) + share * (q_width + 2 * head_dim) * 2)
    out = pl.pallas_call(
        body,
        in_specs=[pl.BlockSpec(memory_space=pl.ANY)] * 4,
        out_specs=[pl.BlockSpec(memory_space=pltpu.VMEM)] * inner,
        out_shape=[jax.ShapeDtypeStruct((tokens, 2 * rows_w), BF16)] * (inner - 1)
        + [jax.ShapeDtypeStruct((2 * share + share // 2, cols), BF16)],
        scratch_shapes=[pltpu.SemaphoreType.DMA((6 + 2 * (inner - 1),))],
        compiler_params=params(),
        cost_estimate=pl.CostEstimate(flops=0, bytes_accessed=moved, transcendentals=0),
        name="prepare",
    )(hidden, w_query, w_key, w_value)
    return out[:-1], out[-1]


def multiply(hidden, received, near, far, layout, order, n_fsdp, groups):
    inner = n_fsdp // 2
    tokens = hidden.shape[0]
    cols = sum(wide for _, _, wide in near)
    slots = far[0].shape[0]
    n_dp = slots * len(far)
    rows_w = near[0][0].shape[0]
    share = rows_w // n_dp
    step = 256 if all(g % 256 == 0 for g in groups) else 128
    n_in = inner - 1 + len(near) + len(far)

    def body(hidden_ref, *rest):
        blocks, rest = rest[: inner - 1], rest[inner - 1 :]
        near_refs, rest = rest[: len(near)], rest[len(near) :]
        far_refs, rest = rest[: len(far)], rest[len(far) :]
        outs = rest[:-3]
        x_all, w_all, sems = rest[-3:]
        me, dp = lax.axis_index("fsdp"), lax.axis_index("dp")
        pairs = []
        for side, bit in enumerate((0, inner)):
            start = pl.multiple_of((me ^ bit) * rows_w, 128)
            pairs.append(
                (
                    hidden_ref.at[:, pl.ds(start, rows_w)],
                    x_all.at[pl.ds(0, tokens), pl.ds(side * rows_w, rows_w)],
                )
            )
        for k in range(1, inner):
            pairs.append((blocks[k - 1], x_all.at[pl.ds(k * tokens, tokens)]))
        to = 0
        for ref, (_, start, wide) in zip(near_refs, near):
            pairs.append((ref.at[:, pl.ds(start, wide)], w_all.at[pl.ds(0, rows_w), pl.ds(to, wide)]))
            to += wide
        for slot, o in enumerate(order):
            block = far_refs[slot // slots].at[slot % slots]
            for row, col, rows, wide, to_row, to_col in layout:
                to = pl.multiple_of(rows_w + (dp ^ o) * share + to_row, 16)
                piece = block.at[pl.ds(row, rows), pl.ds(col, wide)]
                pairs.append((piece, w_all.at[pl.ds(to, rows), pl.ds(to_col, wide)]))
        run_copies([pltpu.make_async_copy(a, b, sems.at[i]) for i, (a, b) in enumerate(pairs)])

        base = 0
        for g, wide in enumerate(groups):

            @pl.loop(0, wide // step)
            def _(n, g=g, base=base):
                at = pl.multiple_of(n * step, 128)
                product = jnp.dot(
                    x_all[...], w_all[:, pl.ds(base + at, step)], preferred_element_type=F32
                )
                for k in range(inner):
                    outs[g * inner + k][:, pl.ds(at, step)] = product[k * tokens : (k + 1) * tokens]

            base += wide

    copies = 2 + (inner - 1) + len(near) + n_dp * len(layout)
    moved = inner * tokens * 2 * rows_w * 2 + 2 * rows_w * cols * 2 + inner * tokens * cols * 4
    out = pl.pallas_call(
        body,
        in_specs=[pl.BlockSpec(memory_space=pl.ANY)] * (1 + n_in),
        out_specs=[pl.BlockSpec(memory_space=pltpu.VMEM)] * (inner * len(groups)),
        out_shape=[jax.ShapeDtypeStruct((tokens, g), F32) for g in groups for _ in range(inner)],
        scratch_shapes=[
            pltpu.VMEM((inner * tokens, 2 * rows_w), BF16),
            pltpu.VMEM((2 * rows_w, cols), BF16),
            pltpu.SemaphoreType.DMA((copies,)),
        ],
        compiler_params=params(),
        cost_estimate=pl.CostEstimate(
            flops=2 * inner * tokens * 2 * rows_w * cols, bytes_accessed=moved, transcendentals=0
        ),
        name="multiply",
    )(hidden, *received, *[array for array, _, _ in near], *far)
    return [list(out[g * inner : (g + 1) * inner]) for g in range(len(groups))]


def attend(lengths, terms, d_attn, first_head, cache, group, g_order, sums):
    tokens = d_attn.shape[0]
    n_blocks, block, head_dim = cache[0].shape
    slots = n_blocks // len(group)
    n_convs = lengths.shape[1]
    scale = head_dim ** (-0.5)
    to_log2 = scale * math.log2(math.e)
    n_heads = terms[0].shape[1] // head_dim
    pair = 2 if n_heads % 2 == 0 else 1
    lanes = pair * tokens
    n_cache = n_blocks * block
    n_group = n_blocks * tokens
    chunk = 512
    n_part, n_sum = len(terms), len(sums)

    def body(len_ref, d_ref, *rest):
        cache_refs, rest = rest[:2], rest[2:]
        group_refs, rest = rest[: len(group)], rest[len(group) :]
        part_refs, rest = rest[:n_part], rest[n_part:]
        sum_refs, rest = rest[:n_sum], rest[n_sum:]
        keep_ref, give_ref, gk, gv, s_ref, p_ref, q_ref, ck_ref, cv_ref, sems = rest
        me, dp = lax.axis_index("fsdp"), lax.axis_index("dp")
        even = dp % 2 == 0

        @pl.when(even)
        def _():
            pltpu.make_async_copy(cache_refs[0], ck_ref, sems.at[0]).start()
            pltpu.make_async_copy(cache_refs[1], cv_ref, sems.at[1]).start()

        @pl.when(jnp.logical_not(even))
        def _():
            pltpu.make_async_copy(cache_refs[1], ck_ref, sems.at[0]).start()
            pltpu.make_async_copy(cache_refs[0], cv_ref, sems.at[1]).start()

        for h in range(n_heads):
            at = slice(h * head_dim, (h + 1) * head_dim)
            q = part_refs[0][:, at]
            for ref in part_refs[1:]:
                q = q + ref[:, at]
            q_ref[h, 0] = q.astype(BF16)
            at = (first_head + h) * head_dim
            q_ref[h, 1] = d_ref[:, at : at + head_dim]

        q_pos = me * tokens + lax.broadcasted_iota(jnp.int32, (1, lanes), 1) % tokens
        begin = jnp.zeros((1, lanes), jnp.int32)
        end = jnp.int32(0)
        for i in range(n_convs):
            end = end + len_ref[0, i]
            begin = jnp.where(end <= q_pos, end, begin)

        pltpu.make_async_copy(cache_refs[0], ck_ref, sems.at[0]).wait()
        pltpu.make_async_copy(cache_refs[1], cv_ref, sems.at[1]).wait()

        @pl.loop(0, n_heads // pair)
        def _(step):
            rows_q = jnp.concatenate([q_ref[step * pair + i, 0] for i in range(pair)], axis=0)
            rows_d = jnp.concatenate([q_ref[step * pair + i, 1] for i in range(pair)], axis=0)
            dims = (((1,), (1,)), ((), ()))
            top = jnp.full((1, lanes), -jnp.inf, F32)
            cache_spans = [
                (b, r, min(chunk, block)) for b in range(n_blocks) for r in range(0, block, min(chunk, block))
            ]
            for b, r, size in cache_spans:
                s = lax.dot_general(
                    ck_ref[b, r : r + size], rows_q, dims, preferred_element_type=F32
                )
                s_ref[pl.ds(b * block + r, size)] = s
                top = jnp.maximum(top, jnp.max(s, axis=0, keepdims=True))
            for b in range(n_blocks):
                s = lax.dot_general(group_refs[b // slots][b % slots, :, :head_dim], rows_q, dims, preferred_element_type=F32)
                pos = (me ^ g_order[b]) * tokens + lax.broadcasted_iota(jnp.int32, (tokens, lanes), 0)
                s = jnp.where((pos <= q_pos) & (pos >= begin), s, -jnp.inf)
                s_ref[pl.ds(n_cache + b * tokens, tokens)] = s
                top = jnp.maximum(top, jnp.max(s, axis=0, keepdims=True))
            total = jnp.zeros((1, lanes), F32)
            for r in range(0, n_cache + n_group, chunk):
                e = jnp.exp2((s_ref[pl.ds(r, chunk)] - top) * to_log2)
                s_ref[pl.ds(r, chunk)] = e
                total = total + jnp.sum(e, axis=0, keepdims=True)
            inv = 1.0 / total
            delta = jnp.zeros((1, lanes), F32)
            for b in range(n_blocks):
                p = s_ref[pl.ds(n_cache + b * tokens, tokens)] * inv
                dp_ = lax.dot_general(group_refs[b // slots][b % slots, :, head_dim:], rows_d, dims, preferred_element_type=F32)
                delta = delta + jnp.sum(p.astype(BF16).astype(F32) * dp_, axis=0, keepdims=True)
            for b, r, size in cache_spans:
                at = pl.ds(b * block + r, size)
                p = s_ref[at] * inv
                pb = p.astype(BF16)
                dp_ = lax.dot_general(
                    cv_ref[b, r : r + size], rows_d, dims, preferred_element_type=F32
                )
                s_ref[at] = p
                p_ref[at] = dp_
                delta = delta + jnp.sum(pb.astype(F32) * dp_, axis=0, keepdims=True)
                g = jnp.dot(pb, rows_d, preferred_element_type=F32)
                gv[at] = jnp.where(step == 0, 0.0, gv[at]) + g
            for b, r, size in cache_spans:
                at = pl.ds(b * block + r, size)
                ds = (s_ref[at] * (p_ref[at] - delta)).astype(BF16)
                g = jnp.dot(ds, rows_q, preferred_element_type=F32)
                gk[at] = jnp.where(step == 0, 0.0, gk[at]) + g

        keep_in, give_in = (sum_refs[0][...], sum_refs[1][...]) if n_sum else (0.0, 0.0)

        @pl.when(even)
        def _():
            keep_ref[...] = keep_in + gk[...] * scale
            give_ref[...] = give_in + gv[...]

        @pl.when(jnp.logical_not(even))
        def _():
            keep_ref[...] = keep_in + gv[...]
            give_ref[...] = give_in + gk[...] * scale

    rows = n_heads * tokens
    flops = 2 * rows * head_dim * (5 * n_cache + 2 * n_group)
    return pl.pallas_call(
        body,
        in_specs=[pl.BlockSpec(memory_space=pltpu.SMEM)]
        + [pl.BlockSpec(memory_space=pltpu.VMEM)]
        + [pl.BlockSpec(memory_space=pl.ANY)] * 2
        + [pl.BlockSpec(memory_space=pltpu.VMEM)] * (len(group) + n_part + n_sum),
        out_specs=[pl.BlockSpec(memory_space=pltpu.VMEM)] * 2,
        out_shape=[jax.ShapeDtypeStruct((n_cache, head_dim), F32)] * 2,
        scratch_shapes=[
            pltpu.VMEM((n_cache, head_dim), F32),
            pltpu.VMEM((n_cache, head_dim), F32),
            pltpu.VMEM((n_cache + n_group, lanes), F32),
            pltpu.VMEM((n_cache, lanes), F32),
            pltpu.VMEM((n_heads, 2, tokens, head_dim), BF16),
            pltpu.VMEM((n_blocks, block, head_dim), BF16),
            pltpu.VMEM((n_blocks, block, head_dim), BF16),
            pltpu.SemaphoreType.DMA((2,)),
        ],
        compiler_params=params(),
        cost_estimate=pl.CostEstimate(
            flops=flops,
            bytes_accessed=12 * n_cache * head_dim,
            transcendentals=rows * (n_cache + n_group),
        ),
        name="attend",
    )(lengths, d_attn, *cache, *group, *terms, *sums)


def make_on_device(n_dp, n_fsdp):
    inner = n_fsdp // 2

    def on_device(hidden, d_attn, w_query, w_key, w_value, cache_keys, cache_values, lengths):
        dp = lax.axis_index("dp")
        head_dim = w_key.shape[1]
        q_width = w_query.shape[1]
        even = dp % 2 == 0
        f_bits, d_bits = bits_down(n_fsdp), bits_down(n_dp)

        def from_owners(products):
            return [products[0]] + [swap(x, "fsdp", n_fsdp, k + 1) for k, x in enumerate(products[1:])]

        cuts = [(0, q_width // 2), (q_width // 2, q_width // 2)]
        cuts = [(0, q_width // 2), (q_width // 2, q_width // 2)]
        sent, part = prepare(hidden, w_query, w_key, w_value, n_dp, n_fsdp)
        received = [swap(block, "fsdp", n_fsdp, k + 1) for k, block in enumerate(sent)]
        part = swap(part, "fsdp", n_fsdp, inner)
        share = w_query.shape[0] // n_dp
        cut = share + share // 2
        part_a, part_b = part[:cut], part[cut:]
        far_a, order = double(part_a[None], [0], "dp", n_dp, d_bits[0])
        cache = jnp.where(even, cache_keys, cache_values)[None]
        cache, f_order = double(cache, [0], "fsdp", n_fsdp, f_bits[0])
        cache, far_a, *received = together(cache, far_a, *received)
        far_b, _ = double(part_b[None], [0], "dp", n_dp, d_bits[0])
        far_a, d_order = finish(far_a, order, "dp", n_dp, d_bits[1:])
        kv, (at_a, wide_a), (at_b, wide_b) = 2 * head_dim, *cuts
        near_a = [(w_key, 0, head_dim), (w_value, 0, head_dim), (w_query, at_a, wide_a)]
        layout_a = [(0, 0, share, wide_a, 0, kv)]
        layout_a += [(share, i * kv, share // 2, kv, i * (share // 2), 0) for i in range(2)]
        out_kv, out_a = multiply(
            hidden, received, near_a, far_a, layout_a, d_order, n_fsdp, (kv, wide_a)
        )
        cache, f_order = double(cache, f_order, "fsdp", n_fsdp, f_bits[1])
        far_b, cache, out_kv[0] = together(far_b, cache, out_kv[0])
        far_b, _ = finish(far_b, order, "dp", n_dp, d_bits[1:])
        for bit in f_bits[2:]:
            cache, f_order = double(cache, f_order, "fsdp", n_fsdp, bit)
        parts_kv = from_owners(out_kv)
        parts_a = from_owners(out_a)
        near_b, layout_b = [(w_query, at_b, wide_b)], [(0, 0, share, wide_b, 0, 0)]
        (out_b,) = multiply(
            hidden, received, near_b, far_b, layout_b, d_order, n_fsdp, (wide_b,)
        )
        out_b[0], cache, *parts_kv = together(out_b[0], cache, *parts_kv)
        own = functools.reduce(lambda a, b: a + b, parts_kv).astype(BF16)
        group = [own] + [swap(own, "fsdp", n_fsdp, k) for k in range(1, inner)]
        cache, *tied = together(cache, *out_b, *group, *parts_a)
        out_b, group, parts_a = tied[:inner], tied[inner : 2 * inner], tied[2 * inner :]
        g_order = [o for o in f_order if o < inner]
        group = jnp.stack([group[o] for o in g_order])
        group, g_order = finish(group, g_order, "fsdp", n_fsdp, [inner])
        parts_b = from_owners(out_b)
        cache = (cache, swap(cache, "dp", n_dp, 1))
        first = cuts[0][1] // head_dim
        sums = attend(lengths, parts_a, d_attn, 0, cache, group, g_order, ())
        keep, give = attend(lengths, parts_b, d_attn, first, cache, group, g_order, sums)

        half = keep + swap(give, "dp", n_dp, 1)
        size = half.shape[0] // n_fsdp
        mine = half[:size]
        for slot in range(1, n_fsdp):
            out = half[slot * size : (slot + 1) * size].astype(BF16)
            mine = mine + swap(out, "fsdp", n_fsdp, f_order[slot]).astype(F32)
        for bit in bits_down(n_dp)[:-2]:
            mine = mine + swap(mine, "dp", n_dp, bit)
        beside, other, across = (swap(mine, "dp", n_dp, bit) for bit in (2, 1, 3))
        mine = mine + beside
        other = other + across
        return jnp.where(even, mine, other), jnp.where(even, other, mine)

    return on_device


def solution(mesh):
    placed = (
        P(("dp", "fsdp"), None),
        P(("dp", "fsdp"), None),
        P("fsdp", None),
        P("fsdp", None),
        P("fsdp", None),
        P("fsdp", None),
        P("fsdp", None),
        P("dp", None),
    )
    return jax.shard_map(
        make_on_device(mesh.shape["dp"], mesh.shape["fsdp"]),
        mesh=mesh,
        in_specs=placed,
        out_specs=(P("fsdp", None), P("fsdp", None)),
        check_vma=False,
    )
```

```python
import functools
import math

import jax
import jax.numpy as jnp
from jax import lax
from jax.experimental import pallas as pl
from jax.experimental.pallas import tpu as pltpu
from jax.sharding import PartitionSpec as P

F32 = jnp.float32
BF16 = jnp.bfloat16
VMEM_LIMIT = 56 * 1024 * 1024


def swap(value, axis, size, bit):
    return lax.ppermute(value, axis, [(i, i ^ bit) for i in range(size)])


def bits_down(size):
    bits = []
    bit = size // 2
    while bit:
        bits.append(bit)
        bit //= 2
    return bits


def double(block, order, axis, size, bit):
    return jnp.concatenate([block, swap(block, axis, size, bit)]), order + [o ^ bit for o in order]


def finish(block, order, axis, size, bits):
    for bit in bits[:-1]:
        block, order = double(block, order, axis, size, bit)
    return [block, swap(block, axis, size, bits[-1])], order + [o ^ bits[-1] for o in order]


def together(*values):
    return lax.optimization_barrier(values)


def params():
    return pltpu.CompilerParams(vmem_limit_bytes=VMEM_LIMIT)


def run_copies(copies):
    for copy in copies:
        copy.start()
    for copy in copies:
        copy.wait()


def prepare(hidden, w_query, w_key, w_value, n_dp, n_fsdp):
    inner = n_fsdp // 2
    tokens = hidden.shape[0]
    rows_w, q_width = w_query.shape
    head_dim = w_key.shape[1]
    share = rows_w // n_dp
    cols = q_width // 2

    def body(hidden_ref, wq_ref, wk_ref, wv_ref, *rest):
        sent, part, sems = rest[: inner - 1], rest[-2], rest[-1]
        me, dp = lax.axis_index("fsdp"), lax.axis_index("dp")
        first = pl.multiple_of(dp * share, 16)
        rows = pl.ds(first, share)
        pairs = []
        for i in range(2):
            to = part.at[pl.ds(i * (share + share // 2), share)]
            pairs.append((wq_ref.at[rows, pl.ds(i * cols, cols)], to))
            for j, ref in enumerate((wk_ref, wv_ref)):
                to = part.at[pl.ds(share, share // 2), pl.ds((2 * i + j) * head_dim, head_dim)]
                pairs.append((ref.at[pl.ds(first + i * (share // 2), share // 2)], to))
        for k in range(1, inner):
            for side, bit in enumerate((0, inner)):
                start = pl.multiple_of((me ^ k ^ bit) * rows_w, 128)
                pairs.append(
                    (hidden_ref.at[:, pl.ds(start, rows_w)], sent[k - 1].at[:, pl.ds(side * rows_w, rows_w)])
                )
        run_copies([pltpu.make_async_copy(a, b, sems.at[i]) for i, (a, b) in enumerate(pairs)])

    moved = 2 * (tokens * 2 * rows_w * 2 * (inner - 1) + share * (q_width + 2 * head_dim) * 2)
    out = pl.pallas_call(
        body,
        in_specs=[pl.BlockSpec(memory_space=pl.ANY)] * 4,
        out_specs=[pl.BlockSpec(memory_space=pltpu.VMEM)] * inner,
        out_shape=[jax.ShapeDtypeStruct((tokens, 2 * rows_w), BF16)] * (inner - 1)
        + [jax.ShapeDtypeStruct((2 * share + share // 2, cols), BF16)],
        scratch_shapes=[pltpu.SemaphoreType.DMA((6 + 2 * (inner - 1),))],
        compiler_params=params(),
        cost_estimate=pl.CostEstimate(flops=0, bytes_accessed=moved, transcendentals=0),
        name="prepare",
    )(hidden, w_query, w_key, w_value)
    return out[:-1], out[-1]


def multiply(hidden, received, near, far, layout, order, n_fsdp, groups):
    inner = n_fsdp // 2
    tokens = hidden.shape[0]
    cols = sum(wide for _, _, wide in near)
    slots = far[0].shape[0]
    n_dp = slots * len(far)
    rows_w = near[0][0].shape[0]
    share = rows_w // n_dp
    step = 256 if all(g % 256 == 0 for g in groups) else 128
    n_in = inner - 1 + len(near) + len(far)

    def body(hidden_ref, *rest):
        blocks, rest = rest[: inner - 1], rest[inner - 1 :]
        near_refs, rest = rest[: len(near)], rest[len(near) :]
        far_refs, rest = rest[: len(far)], rest[len(far) :]
        outs = rest[:-3]
        x_all, w_all, sems = rest[-3:]
        me, dp = lax.axis_index("fsdp"), lax.axis_index("dp")
        pairs = []
        for side, bit in enumerate((0, inner)):
            start = pl.multiple_of((me ^ bit) * rows_w, 128)
            pairs.append(
                (
                    hidden_ref.at[:, pl.ds(start, rows_w)],
                    x_all.at[pl.ds(0, tokens), pl.ds(side * rows_w, rows_w)],
                )
            )
        for k in range(1, inner):
            pairs.append((blocks[k - 1], x_all.at[pl.ds(k * tokens, tokens)]))
        to = 0
        for ref, (_, start, wide) in zip(near_refs, near):
            pairs.append((ref.at[:, pl.ds(start, wide)], w_all.at[pl.ds(0, rows_w), pl.ds(to, wide)]))
            to += wide
        for slot, o in enumerate(order):
            block = far_refs[slot // slots].at[slot % slots]
            for row, col, rows, wide, to_row, to_col in layout:
                to = pl.multiple_of(rows_w + (dp ^ o) * share + to_row, 16)
                piece = block.at[pl.ds(row, rows), pl.ds(col, wide)]
                pairs.append((piece, w_all.at[pl.ds(to, rows), pl.ds(to_col, wide)]))
        run_copies([pltpu.make_async_copy(a, b, sems.at[i]) for i, (a, b) in enumerate(pairs)])

        base = 0
        for g, wide in enumerate(groups):

            @pl.loop(0, wide // step)
            def _(n, g=g, base=base):
                at = pl.multiple_of(n * step, 128)
                product = jnp.dot(
                    x_all[...], w_all[:, pl.ds(base + at, step)], preferred_element_type=F32
                )
                for k in range(inner):
                    outs[g * inner + k][:, pl.ds(at, step)] = product[k * tokens : (k + 1) * tokens]

            base += wide

    copies = 2 + (inner - 1) + len(near) + n_dp * len(layout)
    moved = inner * tokens * 2 * rows_w * 2 + 2 * rows_w * cols * 2 + inner * tokens * cols * 4
    out = pl.pallas_call(
        body,
        in_specs=[pl.BlockSpec(memory_space=pl.ANY)] * (1 + n_in),
        out_specs=[pl.BlockSpec(memory_space=pltpu.VMEM)] * (inner * len(groups)),
        out_shape=[jax.ShapeDtypeStruct((tokens, g), F32) for g in groups for _ in range(inner)],
        scratch_shapes=[
            pltpu.VMEM((inner * tokens, 2 * rows_w), BF16),
            pltpu.VMEM((2 * rows_w, cols), BF16),
            pltpu.SemaphoreType.DMA((copies,)),
        ],
        compiler_params=params(),
        cost_estimate=pl.CostEstimate(
            flops=2 * inner * tokens * 2 * rows_w * cols, bytes_accessed=moved, transcendentals=0
        ),
        name="multiply",
    )(hidden, *received, *[array for array, _, _ in near], *far)
    return [list(out[g * inner : (g + 1) * inner]) for g in range(len(groups))]


def attend(lengths, terms, d_attn, first_head, cache, group, g_order, sums):
    tokens = d_attn.shape[0]
    n_blocks, block, head_dim = cache[0].shape
    slots = n_blocks // len(group)
    n_convs = lengths.shape[1]
    scale = head_dim ** (-0.5)
    to_log2 = scale * math.log2(math.e)
    n_heads = terms[0].shape[1] // head_dim
    pair = 2 if n_heads % 2 == 0 else 1
    lanes = pair * tokens
    n_cache = n_blocks * block
    n_group = n_blocks * tokens
    chunk = 512
    n_part, n_sum = len(terms), len(sums)

    def body(len_ref, d_ref, *rest):
        cache_refs, rest = rest[:2], rest[2:]
        group_refs, rest = rest[: len(group)], rest[len(group) :]
        part_refs, rest = rest[:n_part], rest[n_part:]
        sum_refs, rest = rest[:n_sum], rest[n_sum:]
        keep_ref, give_ref, gk, gv, s_ref, p_ref, q_ref, ck_ref, cv_ref, sems = rest
        me, dp = lax.axis_index("fsdp"), lax.axis_index("dp")
        even = dp % 2 == 0

        @pl.when(even)
        def _():
            pltpu.make_async_copy(cache_refs[0], ck_ref, sems.at[0]).start()
            pltpu.make_async_copy(cache_refs[1], cv_ref, sems.at[1]).start()

        @pl.when(jnp.logical_not(even))
        def _():
            pltpu.make_async_copy(cache_refs[1], ck_ref, sems.at[0]).start()
            pltpu.make_async_copy(cache_refs[0], cv_ref, sems.at[1]).start()

        for h in range(n_heads):
            at = slice(h * head_dim, (h + 1) * head_dim)
            q = part_refs[0][:, at]
            for ref in part_refs[1:]:
                q = q + ref[:, at]
            q_ref[h, 0] = q.astype(BF16)
            at = (first_head + h) * head_dim
            q_ref[h, 1] = d_ref[:, at : at + head_dim]

        q_pos = me * tokens + lax.broadcasted_iota(jnp.int32, (1, lanes), 1) % tokens
        begin = jnp.zeros((1, lanes), jnp.int32)
        end = jnp.int32(0)
        for i in range(n_convs):
            end = end + len_ref[0, i]
            begin = jnp.where(end <= q_pos, end, begin)

        pltpu.make_async_copy(cache_refs[0], ck_ref, sems.at[0]).wait()
        pltpu.make_async_copy(cache_refs[1], cv_ref, sems.at[1]).wait()

        @pl.loop(0, n_heads // pair)
        def _(step):
            rows_q = jnp.concatenate([q_ref[step * pair + i, 0] for i in range(pair)], axis=0)
            rows_d = jnp.concatenate([q_ref[step * pair + i, 1] for i in range(pair)], axis=0)
            dims = (((1,), (1,)), ((), ()))
            top = jnp.full((1, lanes), -jnp.inf, F32)
            cache_spans = [
                (b, r, min(chunk, block)) for b in range(n_blocks) for r in range(0, block, min(chunk, block))
            ]
            for b, r, size in cache_spans:
                s = lax.dot_general(
                    ck_ref[b, r : r + size], rows_q, dims, preferred_element_type=F32
                )
                s_ref[pl.ds(b * block + r, size)] = s
                top = jnp.maximum(top, jnp.max(s, axis=0, keepdims=True))
            for b in range(n_blocks):
                s = lax.dot_general(group_refs[b // slots][b % slots, :, :head_dim], rows_q, dims, preferred_element_type=F32)
                pos = (me ^ g_order[b]) * tokens + lax.broadcasted_iota(jnp.int32, (tokens, lanes), 0)
                s = jnp.where((pos <= q_pos) & (pos >= begin), s, -jnp.inf)
                s_ref[pl.ds(n_cache + b * tokens, tokens)] = s
                top = jnp.maximum(top, jnp.max(s, axis=0, keepdims=True))
            total = jnp.zeros((1, lanes), F32)
            for r in range(0, n_cache + n_group, chunk):
                e = jnp.exp2((s_ref[pl.ds(r, chunk)] - top) * to_log2)
                s_ref[pl.ds(r, chunk)] = e
                total = total + jnp.sum(e, axis=0, keepdims=True)
            inv = 1.0 / total
            delta = jnp.zeros((1, lanes), F32)
            for b in range(n_blocks):
                p = s_ref[pl.ds(n_cache + b * tokens, tokens)] * inv
                dp_ = lax.dot_general(group_refs[b // slots][b % slots, :, head_dim:], rows_d, dims, preferred_element_type=F32)
                delta = delta + jnp.sum(p.astype(BF16).astype(F32) * dp_, axis=0, keepdims=True)
            for b, r, size in cache_spans:
                at = pl.ds(b * block + r, size)
                p = s_ref[at] * inv
                pb = p.astype(BF16)
                dp_ = lax.dot_general(
                    cv_ref[b, r : r + size], rows_d, dims, preferred_element_type=F32
                )
                s_ref[at] = p
                p_ref[at] = dp_
                delta = delta + jnp.sum(pb.astype(F32) * dp_, axis=0, keepdims=True)
                g = jnp.dot(pb, rows_d, preferred_element_type=F32)
                gv[at] = jnp.where(step == 0, 0.0, gv[at]) + g
            for b, r, size in cache_spans:
                at = pl.ds(b * block + r, size)
                ds = (s_ref[at] * (p_ref[at] - delta)).astype(BF16)
                g = jnp.dot(ds, rows_q, preferred_element_type=F32)
                gk[at] = jnp.where(step == 0, 0.0, gk[at]) + g

        keep_in, give_in = (sum_refs[0][...], sum_refs[1][...]) if n_sum else (0.0, 0.0)

        @pl.when(even)
        def _():
            keep_ref[...] = keep_in + gk[...] * scale
            give_ref[...] = give_in + gv[...]

        @pl.when(jnp.logical_not(even))
        def _():
            keep_ref[...] = keep_in + gv[...]
            give_ref[...] = give_in + gk[...] * scale

    rows = n_heads * tokens
    flops = 2 * rows * head_dim * (5 * n_cache + 2 * n_group)
    return pl.pallas_call(
        body,
        in_specs=[pl.BlockSpec(memory_space=pltpu.SMEM)]
        + [pl.BlockSpec(memory_space=pltpu.VMEM)]
        + [pl.BlockSpec(memory_space=pl.ANY)] * 2
        + [pl.BlockSpec(memory_space=pltpu.VMEM)] * (len(group) + n_part + n_sum),
        out_specs=[pl.BlockSpec(memory_space=pltpu.VMEM)] * 2,
        out_shape=[jax.ShapeDtypeStruct((n_cache, head_dim), F32)] * 2,
        scratch_shapes=[
            pltpu.VMEM((n_cache, head_dim), F32),
            pltpu.VMEM((n_cache, head_dim), F32),
            pltpu.VMEM((n_cache + n_group, lanes), F32),
            pltpu.VMEM((n_cache, lanes), F32),
            pltpu.VMEM((n_heads, 2, tokens, head_dim), BF16),
            pltpu.VMEM((n_blocks, block, head_dim), BF16),
            pltpu.VMEM((n_blocks, block, head_dim), BF16),
            pltpu.SemaphoreType.DMA((2,)),
        ],
        compiler_params=params(),
        cost_estimate=pl.CostEstimate(
            flops=flops,
            bytes_accessed=12 * n_cache * head_dim,
            transcendentals=rows * (n_cache + n_group),
        ),
        name="attend",
    )(lengths, d_attn, *cache, *group, *terms, *sums)


def make_on_device(n_dp, n_fsdp):
    inner = n_fsdp // 2

    def on_device(hidden, d_attn, w_query, w_key, w_value, cache_keys, cache_values, lengths):
        dp = lax.axis_index("dp")
        head_dim = w_key.shape[1]
        q_width = w_query.shape[1]
        even = dp % 2 == 0
        f_bits, d_bits = bits_down(n_fsdp), bits_down(n_dp)

        def from_owners(products):
            return [products[0]] + [swap(x, "fsdp", n_fsdp, k + 1) for k, x in enumerate(products[1:])]

        cuts = [(0, q_width // 2), (q_width // 2, q_width // 2)]
        cuts = [(0, q_width // 2), (q_width // 2, q_width // 2)]
        sent, part = prepare(hidden, w_query, w_key, w_value, n_dp, n_fsdp)
        received = [swap(block, "fsdp", n_fsdp, k + 1) for k, block in enumerate(sent)]
        part = swap(part, "fsdp", n_fsdp, inner)
        share = w_query.shape[0] // n_dp
        cut = share + share // 2
        part_a, part_b = part[:cut], part[cut:]
        far_a, order = double(part_a[None], [0], "dp", n_dp, d_bits[0])
        cache = jnp.where(even, cache_keys, cache_values)[None]
        cache, f_order = double(cache, [0], "fsdp", n_fsdp, f_bits[0])
        cache, far_a, *received = together(cache, far_a, *received)
        far_b, _ = double(part_b[None], [0], "dp", n_dp, d_bits[0])
        far_a, d_order = finish(far_a, order, "dp", n_dp, d_bits[1:])
        cache, f_order = double(cache, f_order, "fsdp", n_fsdp, f_bits[1])
        cache, far_a[1] = together(cache, far_a[1])
        kv, (at_a, wide_a), (at_b, wide_b) = 2 * head_dim, *cuts
        near_a = [(w_key, 0, head_dim), (w_value, 0, head_dim), (w_query, at_a, wide_a)]
        layout_a = [(0, 0, share, wide_a, 0, kv)]
        layout_a += [(share, i * kv, share // 2, kv, i * (share // 2), 0) for i in range(2)]
        out_kv, out_a = multiply(
            hidden, received, near_a, far_a, layout_a, d_order, n_fsdp, (kv, wide_a)
        )
        for bit in f_bits[2:]:
            cache, f_order = double(cache, f_order, "fsdp", n_fsdp, bit)
        far_b, cache, out_kv[0] = together(far_b, cache, out_kv[0])
        cache = [cache, swap(cache, "dp", n_dp, 1)]
        far_b, _ = finish(far_b, order, "dp", n_dp, d_bits[1:])
        parts_kv = from_owners(out_kv)
        parts_a = from_owners(out_a)
        near_b, layout_b = [(w_query, at_b, wide_b)], [(0, 0, share, wide_b, 0, 0)]
        (out_b,) = multiply(
            hidden, received, near_b, far_b, layout_b, d_order, n_fsdp, (wide_b,)
        )
        cache[1], out_b[0], *parts_kv = together(cache[1], out_b[0], *parts_kv)
        own = functools.reduce(lambda a, b: a + b, parts_kv).astype(BF16)
        group, _ = double(own[None], [0], "fsdp", n_fsdp, inner)
        group = [group] + [swap(group, "fsdp", n_fsdp, k) for k in range(1, inner)]
        tied = together(*out_b, *group, *parts_a)
        out_b, group, parts_a = tied[:inner], tied[inner : 2 * inner], tied[2 * inner :]
        g_order = [o for k in range(inner) for o in (k, k ^ inner)]
        parts_b = from_owners(out_b)
        first = cuts[0][1] // head_dim
        sums = attend(lengths, parts_a, d_attn, 0, cache, group, g_order, ())
        keep, give = attend(lengths, parts_b, d_attn, first, cache, group, g_order, sums)

        half = keep + swap(give, "dp", n_dp, 1)
        size = half.shape[0] // n_fsdp
        mine = half[:size]
        for slot in range(1, n_fsdp):
            out = half[slot * size : (slot + 1) * size].astype(BF16)
            mine = mine + swap(out, "fsdp", n_fsdp, f_order[slot]).astype(F32)
        for bit in bits_down(n_dp)[:-2]:
            mine = mine + swap(mine, "dp", n_dp, bit)
        beside, other, across = (swap(mine, "dp", n_dp, bit) for bit in (2, 1, 3))
        mine = mine + beside
        other = other + across
        return jnp.where(even, mine, other), jnp.where(even, other, mine)

    return on_device


def solution(mesh):
    placed = (
        P(("dp", "fsdp"), None),
        P(("dp", "fsdp"), None),
        P("fsdp", None),
        P("fsdp", None),
        P("fsdp", None),
        P("fsdp", None),
        P("fsdp", None),
        P("dp", None),
    )
    return jax.shard_map(
        make_on_device(mesh.shape["dp"], mesh.shape["fsdp"]),
        mesh=mesh,
        in_specs=placed,
        out_specs=(P("fsdp", None), P("fsdp", None)),
        check_vma=False,
    )
```

```python
import functools
import math

import jax
import jax.numpy as jnp
from jax import lax
from jax.experimental import pallas as pl
from jax.experimental.pallas import tpu as pltpu
from jax.sharding import PartitionSpec as P

F32 = jnp.float32
BF16 = jnp.bfloat16
VMEM_LIMIT = 56 * 1024 * 1024


def swap(value, axis, size, bit):
    return lax.ppermute(value, axis, [(i, i ^ bit) for i in range(size)])


def bits_down(size):
    bits = []
    bit = size // 2
    while bit:
        bits.append(bit)
        bit //= 2
    return bits


def double(block, order, axis, size, bit):
    return jnp.concatenate([block, swap(block, axis, size, bit)]), order + [o ^ bit for o in order]


def finish(block, order, axis, size, bits):
    for bit in bits[:-1]:
        block, order = double(block, order, axis, size, bit)
    return [block, swap(block, axis, size, bits[-1])], order + [o ^ bits[-1] for o in order]


def together(*values):
    return lax.optimization_barrier(values)


def params():
    return pltpu.CompilerParams(vmem_limit_bytes=VMEM_LIMIT)


def run_copies(copies):
    for copy in copies:
        copy.start()
    for copy in copies:
        copy.wait()


def prepare(hidden, w_query, w_key, w_value, n_dp, n_fsdp):
    inner = n_fsdp // 2
    tokens = hidden.shape[0]
    rows_w, q_width = w_query.shape
    head_dim = w_key.shape[1]
    share = rows_w // n_dp
    cols = q_width // 2

    def body(hidden_ref, wq_ref, wk_ref, wv_ref, *rest):
        sent, part, sems = rest[: inner - 1], rest[-2], rest[-1]
        me, dp = lax.axis_index("fsdp"), lax.axis_index("dp")
        first = pl.multiple_of(dp * share, 16)
        rows = pl.ds(first, share)
        pairs = []
        for i in range(2):
            to = part.at[pl.ds(i * (share + share // 2), share)]
            pairs.append((wq_ref.at[rows, pl.ds(i * cols, cols)], to))
            for j, ref in enumerate((wk_ref, wv_ref)):
                to = part.at[pl.ds(share, share // 2), pl.ds((2 * i + j) * head_dim, head_dim)]
                pairs.append((ref.at[pl.ds(first + i * (share // 2), share // 2)], to))
        for k in range(1, inner):
            for side, bit in enumerate((0, inner)):
                start = pl.multiple_of((me ^ k ^ bit) * rows_w, 128)
                pairs.append(
                    (hidden_ref.at[:, pl.ds(start, rows_w)], sent[k - 1].at[:, pl.ds(side * rows_w, rows_w)])
                )
        run_copies([pltpu.make_async_copy(a, b, sems.at[i]) for i, (a, b) in enumerate(pairs)])

    moved = 2 * (tokens * 2 * rows_w * 2 * (inner - 1) + share * (q_width + 2 * head_dim) * 2)
    out = pl.pallas_call(
        body,
        in_specs=[pl.BlockSpec(memory_space=pl.ANY)] * 4,
        out_specs=[pl.BlockSpec(memory_space=pltpu.VMEM)] * inner,
        out_shape=[jax.ShapeDtypeStruct((tokens, 2 * rows_w), BF16)] * (inner - 1)
        + [jax.ShapeDtypeStruct((2 * share + share // 2, cols), BF16)],
        scratch_shapes=[pltpu.SemaphoreType.DMA((6 + 2 * (inner - 1),))],
        compiler_params=params(),
        cost_estimate=pl.CostEstimate(flops=0, bytes_accessed=moved, transcendentals=0),
        name="prepare",
    )(hidden, w_query, w_key, w_value)
    return out[:-1], out[-1]


def multiply(hidden, received, near, far, layout, order, n_fsdp, groups):
    inner = n_fsdp // 2
    tokens = hidden.shape[0]
    cols = sum(wide for _, _, wide in near)
    slots = far[0].shape[0]
    n_dp = slots * len(far)
    rows_w = near[0][0].shape[0]
    share = rows_w // n_dp
    step = 256 if all(g % 256 == 0 for g in groups) else 128
    n_in = inner - 1 + len(near) + len(far)

    def body(hidden_ref, *rest):
        blocks, rest = rest[: inner - 1], rest[inner - 1 :]
        near_refs, rest = rest[: len(near)], rest[len(near) :]
        far_refs, rest = rest[: len(far)], rest[len(far) :]
        outs = rest[:-3]
        x_all, w_all, sems = rest[-3:]
        me, dp = lax.axis_index("fsdp"), lax.axis_index("dp")
        pairs = []
        for side, bit in enumerate((0, inner)):
            start = pl.multiple_of((me ^ bit) * rows_w, 128)
            pairs.append(
                (
                    hidden_ref.at[:, pl.ds(start, rows_w)],
                    x_all.at[pl.ds(0, tokens), pl.ds(side * rows_w, rows_w)],
                )
            )
        for k in range(1, inner):
            pairs.append((blocks[k - 1], x_all.at[pl.ds(k * tokens, tokens)]))
        to = 0
        for ref, (_, start, wide) in zip(near_refs, near):
            pairs.append((ref.at[:, pl.ds(start, wide)], w_all.at[pl.ds(0, rows_w), pl.ds(to, wide)]))
            to += wide
        for slot, o in enumerate(order):
            block = far_refs[slot // slots].at[slot % slots]
            for row, col, rows, wide, to_row, to_col in layout:
                to = pl.multiple_of(rows_w + (dp ^ o) * share + to_row, 16)
                piece = block.at[pl.ds(row, rows), pl.ds(col, wide)]
                pairs.append((piece, w_all.at[pl.ds(to, rows), pl.ds(to_col, wide)]))
        run_copies([pltpu.make_async_copy(a, b, sems.at[i]) for i, (a, b) in enumerate(pairs)])

        base = 0
        for g, wide in enumerate(groups):

            @pl.loop(0, wide // step)
            def _(n, g=g, base=base):
                at = pl.multiple_of(n * step, 128)
                product = jnp.dot(
                    x_all[...], w_all[:, pl.ds(base + at, step)], preferred_element_type=F32
                )
                for k in range(inner):
                    outs[g * inner + k][:, pl.ds(at, step)] = product[k * tokens : (k + 1) * tokens]

            base += wide

    copies = 2 + (inner - 1) + len(near) + n_dp * len(layout)
    moved = inner * tokens * 2 * rows_w * 2 + 2 * rows_w * cols * 2 + inner * tokens * cols * 4
    out = pl.pallas_call(
        body,
        in_specs=[pl.BlockSpec(memory_space=pl.ANY)] * (1 + n_in),
        out_specs=[pl.BlockSpec(memory_space=pltpu.VMEM)] * (inner * len(groups)),
        out_shape=[jax.ShapeDtypeStruct((tokens, g), F32) for g in groups for _ in range(inner)],
        scratch_shapes=[
            pltpu.VMEM((inner * tokens, 2 * rows_w), BF16),
            pltpu.VMEM((2 * rows_w, cols), BF16),
            pltpu.SemaphoreType.DMA((copies,)),
        ],
        compiler_params=params(),
        cost_estimate=pl.CostEstimate(
            flops=2 * inner * tokens * 2 * rows_w * cols, bytes_accessed=moved, transcendentals=0
        ),
        name="multiply",
    )(hidden, *received, *[array for array, _, _ in near], *far)
    return [list(out[g * inner : (g + 1) * inner]) for g in range(len(groups))]


def attend(lengths, terms, d_attn, first_head, cache, group, g_order, sums):
    tokens = d_attn.shape[0]
    n_blocks, block, head_dim = cache[0].shape
    slots = n_blocks // len(group)
    n_convs = lengths.shape[1]
    scale = head_dim ** (-0.5)
    to_log2 = scale * math.log2(math.e)
    n_heads = terms[0].shape[1] // head_dim
    pair = 2 if n_heads % 2 == 0 else 1
    lanes = pair * tokens
    n_cache = n_blocks * block
    n_group = n_blocks * tokens
    chunk = 512
    n_part, n_sum = len(terms), len(sums)

    def body(len_ref, d_ref, *rest):
        cache_refs, rest = rest[:2], rest[2:]
        group_refs, rest = rest[: len(group)], rest[len(group) :]
        part_refs, rest = rest[:n_part], rest[n_part:]
        sum_refs, rest = rest[:n_sum], rest[n_sum:]
        keep_ref, give_ref, gk, gv, s_ref, p_ref, q_ref, ck_ref, cv_ref, sems = rest
        me, dp = lax.axis_index("fsdp"), lax.axis_index("dp")
        even = dp % 2 == 0

        @pl.when(even)
        def _():
            pltpu.make_async_copy(cache_refs[0], ck_ref, sems.at[0]).start()
            pltpu.make_async_copy(cache_refs[1], cv_ref, sems.at[1]).start()

        @pl.when(jnp.logical_not(even))
        def _():
            pltpu.make_async_copy(cache_refs[1], ck_ref, sems.at[0]).start()
            pltpu.make_async_copy(cache_refs[0], cv_ref, sems.at[1]).start()

        for h in range(n_heads):
            at = slice(h * head_dim, (h + 1) * head_dim)
            q = part_refs[0][:, at]
            for ref in part_refs[1:]:
                q = q + ref[:, at]
            q_ref[h, 0] = q.astype(BF16)
            at = (first_head + h) * head_dim
            q_ref[h, 1] = d_ref[:, at : at + head_dim]

        q_pos = me * tokens + lax.broadcasted_iota(jnp.int32, (1, lanes), 1) % tokens
        begin = jnp.zeros((1, lanes), jnp.int32)
        end = jnp.int32(0)
        for i in range(n_convs):
            end = end + len_ref[0, i]
            begin = jnp.where(end <= q_pos, end, begin)

        pltpu.make_async_copy(cache_refs[0], ck_ref, sems.at[0]).wait()
        pltpu.make_async_copy(cache_refs[1], cv_ref, sems.at[1]).wait()

        @pl.loop(0, n_heads // pair)
        def _(step):
            rows_q = jnp.concatenate([q_ref[step * pair + i, 0] for i in range(pair)], axis=0)
            rows_d = jnp.concatenate([q_ref[step * pair + i, 1] for i in range(pair)], axis=0)
            dims = (((1,), (1,)), ((), ()))
            top = jnp.full((1, lanes), -jnp.inf, F32)
            cache_spans = [
                (b, r, min(chunk, block)) for b in range(n_blocks) for r in range(0, block, min(chunk, block))
            ]
            for b, r, size in cache_spans:
                s = lax.dot_general(
                    ck_ref[b, r : r + size], rows_q, dims, preferred_element_type=F32
                )
                s_ref[pl.ds(b * block + r, size)] = s
                top = jnp.maximum(top, jnp.max(s, axis=0, keepdims=True))
            for b in range(n_blocks):
                s = lax.dot_general(group_refs[b // slots][b % slots, :, :head_dim], rows_q, dims, preferred_element_type=F32)
                pos = (me ^ g_order[b]) * tokens + lax.broadcasted_iota(jnp.int32, (tokens, lanes), 0)
                s = jnp.where((pos <= q_pos) & (pos >= begin), s, -jnp.inf)
                s_ref[pl.ds(n_cache + b * tokens, tokens)] = s
                top = jnp.maximum(top, jnp.max(s, axis=0, keepdims=True))
            total = jnp.zeros((1, lanes), F32)
            for r in range(0, n_cache + n_group, chunk):
                e = jnp.exp2((s_ref[pl.ds(r, chunk)] - top) * to_log2)
                s_ref[pl.ds(r, chunk)] = e
                total = total + jnp.sum(e, axis=0, keepdims=True)
            inv = 1.0 / total
            delta = jnp.zeros((1, lanes), F32)
            for b in range(n_blocks):
                p = s_ref[pl.ds(n_cache + b * tokens, tokens)] * inv
                dp_ = lax.dot_general(group_refs[b // slots][b % slots, :, head_dim:], rows_d, dims, preferred_element_type=F32)
                delta = delta + jnp.sum(p.astype(BF16).astype(F32) * dp_, axis=0, keepdims=True)
            for b, r, size in cache_spans:
                at = pl.ds(b * block + r, size)
                p = s_ref[at] * inv
                pb = p.astype(BF16)
                dp_ = lax.dot_general(
                    cv_ref[b, r : r + size], rows_d, dims, preferred_element_type=F32
                )
                s_ref[at] = p
                p_ref[at] = dp_
                delta = delta + jnp.sum(pb.astype(F32) * dp_, axis=0, keepdims=True)
                g = jnp.dot(pb, rows_d, preferred_element_type=F32)
                gv[at] = jnp.where(step == 0, 0.0, gv[at]) + g
            for b, r, size in cache_spans:
                at = pl.ds(b * block + r, size)
                ds = (s_ref[at] * (p_ref[at] - delta)).astype(BF16)
                g = jnp.dot(ds, rows_q, preferred_element_type=F32)
                gk[at] = jnp.where(step == 0, 0.0, gk[at]) + g

        keep_in, give_in = (sum_refs[0][...], sum_refs[1][...]) if n_sum else (0.0, 0.0)

        @pl.when(even)
        def _():
            keep_ref[...] = keep_in + gk[...] * scale
            give_ref[...] = give_in + gv[...]

        @pl.when(jnp.logical_not(even))
        def _():
            keep_ref[...] = keep_in + gv[...]
            give_ref[...] = give_in + gk[...] * scale

    rows = n_heads * tokens
    flops = 2 * rows * head_dim * (5 * n_cache + 2 * n_group)
    return pl.pallas_call(
        body,
        in_specs=[pl.BlockSpec(memory_space=pltpu.SMEM)]
        + [pl.BlockSpec(memory_space=pltpu.VMEM)]
        + [pl.BlockSpec(memory_space=pl.ANY)] * 2
        + [pl.BlockSpec(memory_space=pltpu.VMEM)] * (len(group) + n_part + n_sum),
        out_specs=[pl.BlockSpec(memory_space=pltpu.VMEM)] * 2,
        out_shape=[jax.ShapeDtypeStruct((n_cache, head_dim), F32)] * 2,
        scratch_shapes=[
            pltpu.VMEM((n_cache, head_dim), F32),
            pltpu.VMEM((n_cache, head_dim), F32),
            pltpu.VMEM((n_cache + n_group, lanes), F32),
            pltpu.VMEM((n_cache, lanes), F32),
            pltpu.VMEM((n_heads, 2, tokens, head_dim), BF16),
            pltpu.VMEM((n_blocks, block, head_dim), BF16),
            pltpu.VMEM((n_blocks, block, head_dim), BF16),
            pltpu.SemaphoreType.DMA((2,)),
        ],
        compiler_params=params(),
        cost_estimate=pl.CostEstimate(
            flops=flops,
            bytes_accessed=12 * n_cache * head_dim,
            transcendentals=rows * (n_cache + n_group),
        ),
        name="attend",
    )(lengths, d_attn, *cache, *group, *terms, *sums)


def make_on_device(n_dp, n_fsdp):
    inner = n_fsdp // 2

    def on_device(hidden, d_attn, w_query, w_key, w_value, cache_keys, cache_values, lengths):
        dp = lax.axis_index("dp")
        head_dim = w_key.shape[1]
        q_width = w_query.shape[1]
        even = dp % 2 == 0
        f_bits, d_bits = bits_down(n_fsdp), bits_down(n_dp)

        def from_owners(products):
            return [products[0]] + [swap(x, "fsdp", n_fsdp, k + 1) for k, x in enumerate(products[1:])]

        cuts = [(0, q_width // 2), (q_width // 2, q_width // 2)]
        cuts = [(0, q_width // 2), (q_width // 2, q_width // 2)]
        sent, part = prepare(hidden, w_query, w_key, w_value, n_dp, n_fsdp)
        received = [swap(block, "fsdp", n_fsdp, k + 1) for k, block in enumerate(sent)]
        part = swap(part, "fsdp", n_fsdp, inner)
        share = w_query.shape[0] // n_dp
        cut = share + share // 2
        part_a, part_b = part[:cut], part[cut:]
        far_a, order = double(part_a[None], [0], "dp", n_dp, d_bits[0])
        cache = jnp.where(even, cache_keys, cache_values)[None]
        cache, f_order = double(cache, [0], "fsdp", n_fsdp, f_bits[0])
        cache, far_a, *received = together(cache, far_a, *received)
        far_b, _ = double(part_b[None], [0], "dp", n_dp, d_bits[0])
        far_a, d_order = finish(far_a, order, "dp", n_dp, d_bits[1:])
        cache, f_order = double(cache, f_order, "fsdp", n_fsdp, f_bits[1])
        cache, far_a[1] = together(cache, far_a[1])
        kv, (at_a, wide_a), (at_b, wide_b) = 2 * head_dim, *cuts
        near_a = [(w_key, 0, head_dim), (w_value, 0, head_dim), (w_query, at_a, wide_a)]
        layout_a = [(0, 0, share, wide_a, 0, kv)]
        layout_a += [(share, i * kv, share // 2, kv, i * (share // 2), 0) for i in range(2)]
        out_kv, out_a = multiply(
            hidden, received, near_a, far_a, layout_a, d_order, n_fsdp, (kv, wide_a)
        )
        for bit in f_bits[2:]:
            cache, f_order = double(cache, f_order, "fsdp", n_fsdp, bit)
        far_b, cache, out_kv[0] = together(far_b, cache, out_kv[0])
        far_b, _ = finish(far_b, order, "dp", n_dp, d_bits[1:])
        parts_kv = from_owners(out_kv)
        parts_a = from_owners(out_a)
        near_b, layout_b = [(w_query, at_b, wide_b)], [(0, 0, share, wide_b, 0, 0)]
        (out_b,) = multiply(
            hidden, received, near_b, far_b, layout_b, d_order, n_fsdp, (wide_b,)
        )
        out_b[0], parts_a[1], *parts_kv = together(out_b[0], parts_a[1], *parts_kv)
        own = functools.reduce(lambda a, b: a + b, parts_kv).astype(BF16)
        group, _ = double(own[None], [0], "fsdp", n_fsdp, inner)
        group, cache, *tied = together(group, cache, *out_b, *parts_a[2:])
        out_b, parts_a[2:] = tied[:inner], tied[inner:]
        group = [group] + [swap(group, "fsdp", n_fsdp, k) for k in range(1, inner)]
        g_order = [o for k in range(inner) for o in (k, k ^ inner)]
        cache = [cache, swap(cache, "dp", n_dp, 1)]
        parts_b = from_owners(out_b)
        first = cuts[0][1] // head_dim
        sums = attend(lengths, parts_a, d_attn, 0, cache, group, g_order, ())
        keep, give = attend(lengths, parts_b, d_attn, first, cache, group, g_order, sums)

        half = keep + swap(give, "dp", n_dp, 1)
        size = half.shape[0] // n_fsdp
        mine = half[:size]
        for slot in range(1, n_fsdp):
            out = half[slot * size : (slot + 1) * size].astype(BF16)
            mine = mine + swap(out, "fsdp", n_fsdp, f_order[slot]).astype(F32)
        for bit in d_bits[:-1]:
            mine = mine + swap(mine, "dp", n_dp, bit)
        other = swap(mine, "dp", n_dp, 1)
        return jnp.where(even, mine, other), jnp.where(even, other, mine)

    return on_device


def solution(mesh):
    placed = (
        P(("dp", "fsdp"), None),
        P(("dp", "fsdp"), None),
        P("fsdp", None),
        P("fsdp", None),
        P("fsdp", None),
        P("fsdp", None),
        P("fsdp", None),
        P("dp", None),
    )
    return jax.shard_map(
        make_on_device(mesh.shape["dp"], mesh.shape["fsdp"]),
        mesh=mesh,
        in_specs=placed,
        out_specs=(P("fsdp", None), P("fsdp", None)),
        check_vma=False,
    )
```

```python
import functools
import math

import jax
import jax.numpy as jnp
from jax import lax
from jax.experimental import pallas as pl
from jax.experimental.pallas import tpu as pltpu
from jax.sharding import PartitionSpec as P

F32 = jnp.float32
BF16 = jnp.bfloat16
VMEM_LIMIT = 56 * 1024 * 1024


def swap(value, axis, size, bit):
    return lax.ppermute(value, axis, [(i, i ^ bit) for i in range(size)])


def bits_down(size):
    bits = []
    bit = size // 2
    while bit:
        bits.append(bit)
        bit //= 2
    return bits


def double(block, order, axis, size, bit):
    return jnp.concatenate([block, swap(block, axis, size, bit)]), order + [o ^ bit for o in order]


def finish(block, order, axis, size, bits):
    for bit in bits[:-1]:
        block, order = double(block, order, axis, size, bit)
    return [block, swap(block, axis, size, bits[-1])], order + [o ^ bits[-1] for o in order]


def together(*values):
    return lax.optimization_barrier(values)


def params():
    return pltpu.CompilerParams(vmem_limit_bytes=VMEM_LIMIT)


def run_copies(copies):
    for copy in copies:
        copy.start()
    for copy in copies:
        copy.wait()


def prepare(hidden, w_query, w_key, w_value, n_dp, n_fsdp):
    inner = n_fsdp // 2
    tokens = hidden.shape[0]
    rows_w, q_width = w_query.shape
    head_dim = w_key.shape[1]
    share = rows_w // n_dp
    cols = q_width // 2

    def body(hidden_ref, wq_ref, wk_ref, wv_ref, *rest):
        sent, part, sems = rest[: inner - 1], rest[-2], rest[-1]
        me, dp = lax.axis_index("fsdp"), lax.axis_index("dp")
        first = pl.multiple_of(dp * share, 16)
        rows = pl.ds(first, share)
        pairs = []
        for i in range(2):
            to = part.at[pl.ds(i * (share + share // 2), share)]
            pairs.append((wq_ref.at[rows, pl.ds(i * cols, cols)], to))
            for j, ref in enumerate((wk_ref, wv_ref)):
                to = part.at[pl.ds(share, share // 2), pl.ds((2 * i + j) * head_dim, head_dim)]
                pairs.append((ref.at[pl.ds(first + i * (share // 2), share // 2)], to))
        for k in range(1, inner):
            for side, bit in enumerate((0, inner)):
                start = pl.multiple_of((me ^ k ^ bit) * rows_w, 128)
                pairs.append(
                    (hidden_ref.at[:, pl.ds(start, rows_w)], sent[k - 1].at[:, pl.ds(side * rows_w, rows_w)])
                )
        run_copies([pltpu.make_async_copy(a, b, sems.at[i]) for i, (a, b) in enumerate(pairs)])

    moved = 2 * (tokens * 2 * rows_w * 2 * (inner - 1) + share * (q_width + 2 * head_dim) * 2)
    out = pl.pallas_call(
        body,
        in_specs=[pl.BlockSpec(memory_space=pl.ANY)] * 4,
        out_specs=[pl.BlockSpec(memory_space=pltpu.VMEM)] * inner,
        out_shape=[jax.ShapeDtypeStruct((tokens, 2 * rows_w), BF16)] * (inner - 1)
        + [jax.ShapeDtypeStruct((2 * share + share // 2, cols), BF16)],
        scratch_shapes=[pltpu.SemaphoreType.DMA((6 + 2 * (inner - 1),))],
        compiler_params=params(),
        cost_estimate=pl.CostEstimate(flops=0, bytes_accessed=moved, transcendentals=0),
        name="prepare",
    )(hidden, w_query, w_key, w_value)
    return out[:-1], out[-1]


def multiply(hidden, received, near, far, layout, order, n_fsdp, groups):
    inner = n_fsdp // 2
    tokens = hidden.shape[0]
    cols = sum(wide for _, _, wide in near)
    slots = far[0].shape[0]
    n_dp = slots * len(far)
    rows_w = near[0][0].shape[0]
    share = rows_w // n_dp
    step = 256 if all(g % 256 == 0 for g in groups) else 128
    n_in = inner - 1 + len(near) + len(far)

    def body(hidden_ref, *rest):
        blocks, rest = rest[: inner - 1], rest[inner - 1 :]
        near_refs, rest = rest[: len(near)], rest[len(near) :]
        far_refs, rest = rest[: len(far)], rest[len(far) :]
        outs = rest[:-3]
        x_all, w_all, sems = rest[-3:]
        me, dp = lax.axis_index("fsdp"), lax.axis_index("dp")
        pairs = []
        for side, bit in enumerate((0, inner)):
            start = pl.multiple_of((me ^ bit) * rows_w, 128)
            pairs.append(
                (
                    hidden_ref.at[:, pl.ds(start, rows_w)],
                    x_all.at[pl.ds(0, tokens), pl.ds(side * rows_w, rows_w)],
                )
            )
        for k in range(1, inner):
            pairs.append((blocks[k - 1], x_all.at[pl.ds(k * tokens, tokens)]))
        to = 0
        for ref, (_, start, wide) in zip(near_refs, near):
            pairs.append((ref.at[:, pl.ds(start, wide)], w_all.at[pl.ds(0, rows_w), pl.ds(to, wide)]))
            to += wide
        for slot, o in enumerate(order):
            block = far_refs[slot // slots].at[slot % slots]
            for row, col, rows, wide, to_row, to_col in layout:
                to = pl.multiple_of(rows_w + (dp ^ o) * share + to_row, 16)
                piece = block.at[pl.ds(row, rows), pl.ds(col, wide)]
                pairs.append((piece, w_all.at[pl.ds(to, rows), pl.ds(to_col, wide)]))
        run_copies([pltpu.make_async_copy(a, b, sems.at[i]) for i, (a, b) in enumerate(pairs)])

        base = 0
        for g, wide in enumerate(groups):

            @pl.loop(0, wide // step)
            def _(n, g=g, base=base):
                at = pl.multiple_of(n * step, 128)
                product = jnp.dot(
                    x_all[...], w_all[:, pl.ds(base + at, step)], preferred_element_type=F32
                )
                for k in range(inner):
                    outs[g * inner + k][:, pl.ds(at, step)] = product[k * tokens : (k + 1) * tokens]

            base += wide

    copies = 2 + (inner - 1) + len(near) + n_dp * len(layout)
    moved = inner * tokens * 2 * rows_w * 2 + 2 * rows_w * cols * 2 + inner * tokens * cols * 4
    out = pl.pallas_call(
        body,
        in_specs=[pl.BlockSpec(memory_space=pl.ANY)] * (1 + n_in),
        out_specs=[pl.BlockSpec(memory_space=pltpu.VMEM)] * (inner * len(groups)),
        out_shape=[jax.ShapeDtypeStruct((tokens, g), F32) for g in groups for _ in range(inner)],
        scratch_shapes=[
            pltpu.VMEM((inner * tokens, 2 * rows_w), BF16),
            pltpu.VMEM((2 * rows_w, cols), BF16),
            pltpu.SemaphoreType.DMA((copies,)),
        ],
        compiler_params=params(),
        cost_estimate=pl.CostEstimate(
            flops=2 * inner * tokens * 2 * rows_w * cols, bytes_accessed=moved, transcendentals=0
        ),
        name="multiply",
    )(hidden, *received, *[array for array, _, _ in near], *far)
    return [list(out[g * inner : (g + 1) * inner]) for g in range(len(groups))]


def attend(lengths, terms, d_attn, first_head, cache, group, g_order, sums):
    tokens = d_attn.shape[0]
    n_blocks, block, head_dim = cache[0].shape
    n_convs = lengths.shape[1]
    scale = head_dim ** (-0.5)
    to_log2 = scale * math.log2(math.e)
    n_heads = terms[0].shape[1] // head_dim
    lanes = n_heads * tokens
    n_cache = n_blocks * block
    n_group = n_blocks * tokens
    slots = n_blocks // len(group)
    chunk = min(512, n_cache)
    n_part, n_sum = len(terms), len(sums)
    dims = (((1,), (1,)), ((), ()))
    spans = [(at, chunk) for at in range(0, n_cache, chunk)]
    spans += [(n_cache + i * slots * tokens, slots * tokens) for i in range(len(group))]
    n_first = n_cache // chunk

    def tiles(value):
        return value.reshape(value.shape[0] // 8, 8, lanes)

    def body(len_ref, d_ref, *rest):
        cache_refs, rest = rest[:2], rest[2:]
        group_refs, rest = rest[: len(group)], rest[len(group) :]
        part_refs, rest = rest[:n_part], rest[n_part:]
        sum_refs, rest = rest[:n_sum], rest[n_sum:]
        keep_ref, give_ref, out_ref, s_ref, p_ref, q_ref, dq_ref, ck_ref, cv_ref, sems = rest
        me, dp = lax.axis_index("fsdp"), lax.axis_index("dp")
        odd = dp % 2

        @pl.when(odd == 0)
        def _():
            pltpu.make_async_copy(cache_refs[0], ck_ref, sems.at[0]).start()
            pltpu.make_async_copy(cache_refs[1], cv_ref, sems.at[1]).start()

        @pl.when(odd == 1)
        def _():
            pltpu.make_async_copy(cache_refs[1], ck_ref, sems.at[0]).start()
            pltpu.make_async_copy(cache_refs[0], cv_ref, sems.at[1]).start()

        for h in range(n_heads):
            at = slice(h * head_dim, (h + 1) * head_dim)
            rows = pl.ds(h * tokens, tokens)
            q = part_refs[0][:, at]
            for ref in part_refs[1:]:
                q = q + ref[:, at]
            q_ref[rows] = q.astype(BF16)
            at = (first_head + h) * head_dim
            dq_ref[rows] = d_ref[:, at : at + head_dim]

        q_pos = me * tokens + lax.broadcasted_iota(jnp.int32, (1, lanes), 1) % tokens
        begin = jnp.zeros((1, lanes), jnp.int32)
        end = jnp.int32(0)
        for i in range(n_convs):
            end = end + len_ref[0, i]
            begin = jnp.where(end <= q_pos, end, begin)

        def group_rows(i, at):
            return group_refs[i][...].reshape(slots * tokens, 2 * head_dim)[:, at : at + head_dim]

        def cache_rows(ref, i):
            return ref[...].reshape(n_cache, head_dim)[i * chunk : (i + 1) * chunk]

        for i in range(len(group)):
            at, size = spans[n_first + i]
            s = lax.dot_general(group_rows(i, 0), q_ref[...], dims, preferred_element_type=F32)
            for j in range(slots):
                pos = (me ^ g_order[i * slots + j]) * tokens
                pos = pos + lax.broadcasted_iota(jnp.int32, (tokens, lanes), 0)
                allowed = (pos <= q_pos) & (pos >= begin)
                here = s[j * tokens : (j + 1) * tokens]
                s_ref[pl.ds(at + j * tokens, tokens)] = jnp.where(allowed, here, -jnp.inf)

        pltpu.make_async_copy(cache_refs[0], ck_ref, sems.at[0]).wait()
        pltpu.make_async_copy(cache_refs[1], cv_ref, sems.at[1]).wait()
        for i in range(n_first):
            at, size = spans[i]
            s_ref[pl.ds(at, size)] = lax.dot_general(
                cache_rows(ck_ref, i), q_ref[...], dims, preferred_element_type=F32
            )

        tops, totals = [], []
        for at, size in spans:
            top = jnp.max(tiles(s_ref[pl.ds(at, size)]), axis=0)
            top = jnp.maximum(top, -1e30)
            e = jnp.exp2((tiles(s_ref[pl.ds(at, size)]) - top) * to_log2)
            s_ref[pl.ds(at, size)] = e.reshape(size, lanes)
            tops.append(top)
            totals.append(jnp.sum(e, axis=0))
        top = functools.reduce(jnp.maximum, tops)
        top = jnp.max(top, axis=0, keepdims=True)
        factors = [jnp.exp2((own - top) * to_log2) for own in tops]
        total = functools.reduce(lambda a, b: a + b, [t * f for t, f in zip(totals, factors)])
        inv = 1.0 / jnp.sum(total, axis=0, keepdims=True)
        factors = [f * inv for f in factors]

        delta = jnp.zeros((8, lanes), F32)
        for i in range(len(group)):
            at, size = spans[n_first + i]
            d_prob = lax.dot_general(
                group_rows(i, head_dim), dq_ref[...], dims, preferred_element_type=F32
            )
            p = tiles(s_ref[pl.ds(at, size)]) * factors[n_first + i]
            delta = delta + jnp.sum(p.astype(BF16).astype(F32) * tiles(d_prob), axis=0)
        for i in range(n_first):
            at, size = spans[i]
            p_ref[pl.ds(at, size)] = lax.dot_general(
                cache_rows(cv_ref, i), dq_ref[...], dims, preferred_element_type=F32
            )
            p = (tiles(s_ref[pl.ds(at, size)]) * factors[i]).reshape(size, lanes).astype(BF16)
            delta = delta + jnp.sum(tiles(p.astype(F32)) * tiles(p_ref[pl.ds(at, size)]), axis=0)
            out_ref[1 - odd, pl.ds(at, size)] = jnp.dot(p, dq_ref[...], preferred_element_type=F32)
        delta = jnp.sum(delta, axis=0, keepdims=True)
        for i in range(n_first):
            at, size = spans[i]
            p = tiles(s_ref[pl.ds(at, size)]) * factors[i]
            ds = p * (tiles(p_ref[pl.ds(at, size)]) - delta)
            ds = ds.reshape(size, lanes).astype(BF16)
            g = jnp.dot(ds, q_ref[...], preferred_element_type=F32) * scale
            out_ref[odd, pl.ds(at, size)] = g

        for i, ref in enumerate((keep_ref, give_ref)):
            ref[...] = sum_refs[i][...] + out_ref[i] if n_sum else out_ref[i]

    flops = 2 * lanes * head_dim * (5 * n_cache + 2 * n_group)
    return pl.pallas_call(
        body,
        in_specs=[pl.BlockSpec(memory_space=pltpu.SMEM)]
        + [pl.BlockSpec(memory_space=pltpu.VMEM)]
        + [pl.BlockSpec(memory_space=pl.ANY)] * 2
        + [pl.BlockSpec(memory_space=pltpu.VMEM)] * (len(group) + n_part + n_sum),
        out_specs=[pl.BlockSpec(memory_space=pltpu.VMEM)] * 2,
        out_shape=[jax.ShapeDtypeStruct((n_cache, head_dim), F32)] * 2,
        scratch_shapes=[
            pltpu.VMEM((2, n_cache, head_dim), F32),
            pltpu.VMEM((n_cache + n_group, lanes), F32),
            pltpu.VMEM((n_cache, lanes), F32),
            pltpu.VMEM((lanes, head_dim), BF16),
            pltpu.VMEM((lanes, head_dim), BF16),
            pltpu.VMEM((n_blocks, block, head_dim), BF16),
            pltpu.VMEM((n_blocks, block, head_dim), BF16),
            pltpu.SemaphoreType.DMA((2,)),
        ],
        compiler_params=params(),
        cost_estimate=pl.CostEstimate(
            flops=flops,
            bytes_accessed=12 * n_cache * head_dim,
            transcendentals=lanes * (n_cache + n_group),
        ),
        name="attend",
    )(lengths, d_attn, *cache, *group, *terms, *sums)


def make_on_device(n_dp, n_fsdp):
    inner = n_fsdp // 2

    def on_device(hidden, d_attn, w_query, w_key, w_value, cache_keys, cache_values, lengths):
        dp = lax.axis_index("dp")
        head_dim = w_key.shape[1]
        q_width = w_query.shape[1]
        even = dp % 2 == 0
        f_bits, d_bits = bits_down(n_fsdp), bits_down(n_dp)

        def from_owners(products):
            return [products[0]] + [swap(x, "fsdp", n_fsdp, k + 1) for k, x in enumerate(products[1:])]

        cuts = [(0, q_width // 2), (q_width // 2, q_width // 2)]
        cuts = [(0, q_width // 2), (q_width // 2, q_width // 2)]
        sent, part = prepare(hidden, w_query, w_key, w_value, n_dp, n_fsdp)
        received = [swap(block, "fsdp", n_fsdp, k + 1) for k, block in enumerate(sent)]
        part = swap(part, "fsdp", n_fsdp, inner)
        share = w_query.shape[0] // n_dp
        cut = share + share // 2
        part_a, part_b = part[:cut], part[cut:]
        far_a, order = double(part_a[None], [0], "dp", n_dp, d_bits[0])
        cache = jnp.where(even, cache_keys, cache_values)[None]
        cache, f_order = double(cache, [0], "fsdp", n_fsdp, f_bits[0])
        cache, far_a, *received = together(cache, far_a, *received)
        far_b, _ = double(part_b[None], [0], "dp", n_dp, d_bits[0])
        far_a, d_order = finish(far_a, order, "dp", n_dp, d_bits[1:])
        cache, f_order = double(cache, f_order, "fsdp", n_fsdp, f_bits[1])
        cache, far_a[1] = together(cache, far_a[1])
        kv, (at_a, wide_a), (at_b, wide_b) = 2 * head_dim, *cuts
        near_a = [(w_key, 0, head_dim), (w_value, 0, head_dim), (w_query, at_a, wide_a)]
        layout_a = [(0, 0, share, wide_a, 0, kv)]
        layout_a += [(share, i * kv, share // 2, kv, i * (share // 2), 0) for i in range(2)]
        out_kv, out_a = multiply(
            hidden, received, near_a, far_a, layout_a, d_order, n_fsdp, (kv, wide_a)
        )
        for bit in f_bits[2:]:
            cache, f_order = double(cache, f_order, "fsdp", n_fsdp, bit)
        far_b, cache, out_kv[0] = together(far_b, cache, out_kv[0])
        far_b, _ = finish(far_b, order, "dp", n_dp, d_bits[1:])
        parts_kv = from_owners(out_kv)
        parts_a = from_owners(out_a)
        near_b, layout_b = [(w_query, at_b, wide_b)], [(0, 0, share, wide_b, 0, 0)]
        (out_b,) = multiply(
            hidden, received, near_b, far_b, layout_b, d_order, n_fsdp, (wide_b,)
        )
        out_b[0], parts_a[1], *parts_kv = together(out_b[0], parts_a[1], *parts_kv)
        own = functools.reduce(lambda a, b: a + b, parts_kv).astype(BF16)
        group, _ = double(own[None], [0], "fsdp", n_fsdp, inner)
        group, cache, *tied = together(group, cache, *out_b, *parts_a[2:])
        out_b, parts_a[2:] = tied[:inner], tied[inner:]
        group = [group] + [swap(group, "fsdp", n_fsdp, k) for k in range(1, inner)]
        g_order = [o for k in range(inner) for o in (k, k ^ inner)]
        cache = [cache, swap(cache, "dp", n_dp, 1)]
        parts_b = from_owners(out_b)
        first = cuts[0][1] // head_dim
        sums = attend(lengths, parts_a, d_attn, 0, cache, group, g_order, ())
        keep, give = attend(lengths, parts_b, d_attn, first, cache, group, g_order, sums)

        half = keep + swap(give, "dp", n_dp, 1)
        size = half.shape[0] // n_fsdp
        mine = half[:size]
        for slot in range(1, n_fsdp):
            out = half[slot * size : (slot + 1) * size].astype(BF16)
            mine = mine + swap(out, "fsdp", n_fsdp, f_order[slot]).astype(F32)
        for bit in d_bits[:-1]:
            mine = mine + swap(mine, "dp", n_dp, bit)
        other = swap(mine, "dp", n_dp, 1)
        return jnp.where(even, mine, other), jnp.where(even, other, mine)

    return on_device


def solution(mesh):
    placed = (
        P(("dp", "fsdp"), None),
        P(("dp", "fsdp"), None),
        P("fsdp", None),
        P("fsdp", None),
        P("fsdp", None),
        P("fsdp", None),
        P("fsdp", None),
        P("dp", None),
    )
    return jax.shard_map(
        make_on_device(mesh.shape["dp"], mesh.shape["fsdp"]),
        mesh=mesh,
        in_specs=placed,
        out_specs=(P("fsdp", None), P("fsdp", None)),
        check_vma=False,
    )
```

```python
import functools
import math

import jax
import jax.numpy as jnp
from jax import lax
from jax.experimental import pallas as pl
from jax.experimental.pallas import tpu as pltpu
from jax.sharding import PartitionSpec as P

F32 = jnp.float32
BF16 = jnp.bfloat16
VMEM_LIMIT = 56 * 1024 * 1024


def swap(value, axis, size, bit):
    return lax.ppermute(value, axis, [(i, i ^ bit) for i in range(size)])


def bits_down(size):
    bits = []
    bit = size // 2
    while bit:
        bits.append(bit)
        bit //= 2
    return bits


def double(block, order, axis, size, bit):
    return jnp.concatenate([block, swap(block, axis, size, bit)]), order + [o ^ bit for o in order]


def finish(block, order, axis, size, bits):
    for bit in bits[:-1]:
        block, order = double(block, order, axis, size, bit)
    return [block, swap(block, axis, size, bits[-1])], order + [o ^ bits[-1] for o in order]


def together(*values):
    return lax.optimization_barrier(values)


def params():
    return pltpu.CompilerParams(vmem_limit_bytes=VMEM_LIMIT)


def run_copies(copies):
    for copy in copies:
        copy.start()
    for copy in copies:
        copy.wait()


def prepare(hidden, w_query, w_key, w_value, n_dp, n_fsdp):
    inner = n_fsdp // 2
    tokens = hidden.shape[0]
    rows_w, q_width = w_query.shape
    head_dim = w_key.shape[1]
    share = rows_w // n_dp
    cols = q_width // 2

    def body(hidden_ref, wq_ref, wk_ref, wv_ref, *rest):
        sent, part, sems = rest[: inner - 1], rest[-2], rest[-1]
        me, dp = lax.axis_index("fsdp"), lax.axis_index("dp")
        first = pl.multiple_of(dp * share, 16)
        rows = pl.ds(first, share)
        pairs = []
        for i in range(2):
            to = part.at[pl.ds(i * (share + share // 2), share)]
            pairs.append((wq_ref.at[rows, pl.ds(i * cols, cols)], to))
            for j, ref in enumerate((wk_ref, wv_ref)):
                to = part.at[pl.ds(share, share // 2), pl.ds((2 * i + j) * head_dim, head_dim)]
                pairs.append((ref.at[pl.ds(first + i * (share // 2), share // 2)], to))
        for k in range(1, inner):
            for side, bit in enumerate((0, inner)):
                start = pl.multiple_of((me ^ k ^ bit) * rows_w, 128)
                pairs.append(
                    (hidden_ref.at[:, pl.ds(start, rows_w)], sent[k - 1].at[:, pl.ds(side * rows_w, rows_w)])
                )
        run_copies([pltpu.make_async_copy(a, b, sems.at[i]) for i, (a, b) in enumerate(pairs)])

    moved = 2 * (tokens * 2 * rows_w * 2 * (inner - 1) + share * (q_width + 2 * head_dim) * 2)
    out = pl.pallas_call(
        body,
        in_specs=[pl.BlockSpec(memory_space=pl.ANY)] * 4,
        out_specs=[pl.BlockSpec(memory_space=pltpu.VMEM)] * inner,
        out_shape=[jax.ShapeDtypeStruct((tokens, 2 * rows_w), BF16)] * (inner - 1)
        + [jax.ShapeDtypeStruct((2 * share + share // 2, cols), BF16)],
        scratch_shapes=[pltpu.SemaphoreType.DMA((6 + 2 * (inner - 1),))],
        compiler_params=params(),
        cost_estimate=pl.CostEstimate(flops=0, bytes_accessed=moved, transcendentals=0),
        name="prepare",
    )(hidden, w_query, w_key, w_value)
    return out[:-1], out[-1]


def multiply(hidden, received, near, far, layout, order, n_fsdp, groups):
    inner = n_fsdp // 2
    tokens = hidden.shape[0]
    cols = sum(wide for _, _, wide in near)
    slots = far[0].shape[0]
    n_dp = slots * len(far)
    rows_w = near[0][0].shape[0]
    share = rows_w // n_dp
    step = 256 if all(g % 256 == 0 for g in groups) else 128
    n_in = inner - 1 + len(near) + len(far)

    def body(hidden_ref, *rest):
        blocks, rest = rest[: inner - 1], rest[inner - 1 :]
        near_refs, rest = rest[: len(near)], rest[len(near) :]
        far_refs, rest = rest[: len(far)], rest[len(far) :]
        outs = rest[:-3]
        x_all, w_all, sems = rest[-3:]
        me, dp = lax.axis_index("fsdp"), lax.axis_index("dp")
        pairs = []
        for side, bit in enumerate((0, inner)):
            start = pl.multiple_of((me ^ bit) * rows_w, 128)
            pairs.append(
                (
                    hidden_ref.at[:, pl.ds(start, rows_w)],
                    x_all.at[pl.ds(0, tokens), pl.ds(side * rows_w, rows_w)],
                )
            )
        for k in range(1, inner):
            pairs.append((blocks[k - 1], x_all.at[pl.ds(k * tokens, tokens)]))
        to = 0
        for ref, (_, start, wide) in zip(near_refs, near):
            pairs.append((ref.at[:, pl.ds(start, wide)], w_all.at[pl.ds(0, rows_w), pl.ds(to, wide)]))
            to += wide
        for slot, o in enumerate(order):
            block = far_refs[slot // slots].at[slot % slots]
            for row, col, rows, wide, to_row, to_col in layout:
                to = pl.multiple_of(rows_w + (dp ^ o) * share + to_row, 16)
                piece = block.at[pl.ds(row, rows), pl.ds(col, wide)]
                pairs.append((piece, w_all.at[pl.ds(to, rows), pl.ds(to_col, wide)]))
        run_copies([pltpu.make_async_copy(a, b, sems.at[i]) for i, (a, b) in enumerate(pairs)])

        base = 0
        for g, wide in enumerate(groups):

            @pl.loop(0, wide // step)
            def _(n, g=g, base=base):
                at = pl.multiple_of(n * step, 128)
                product = jnp.dot(
                    x_all[...], w_all[:, pl.ds(base + at, step)], preferred_element_type=F32
                )
                for k in range(inner):
                    outs[g * inner + k][:, pl.ds(at, step)] = product[k * tokens : (k + 1) * tokens]

            base += wide

    copies = 2 + (inner - 1) + len(near) + n_dp * len(layout)
    moved = inner * tokens * 2 * rows_w * 2 + 2 * rows_w * cols * 2 + inner * tokens * cols * 4
    out = pl.pallas_call(
        body,
        in_specs=[pl.BlockSpec(memory_space=pl.ANY)] * (1 + n_in),
        out_specs=[pl.BlockSpec(memory_space=pltpu.VMEM)] * (inner * len(groups)),
        out_shape=[jax.ShapeDtypeStruct((tokens, g), F32) for g in groups for _ in range(inner)],
        scratch_shapes=[
            pltpu.VMEM((inner * tokens, 2 * rows_w), BF16),
            pltpu.VMEM((2 * rows_w, cols), BF16),
            pltpu.SemaphoreType.DMA((copies,)),
        ],
        compiler_params=params(),
        cost_estimate=pl.CostEstimate(
            flops=2 * inner * tokens * 2 * rows_w * cols, bytes_accessed=moved, transcendentals=0
        ),
        name="multiply",
    )(hidden, *received, *[array for array, _, _ in near], *far)
    return [list(out[g * inner : (g + 1) * inner]) for g in range(len(groups))]


def attend(lengths, terms, d_attn, first_head, cache, group, g_order, sums):
    tokens = d_attn.shape[0]
    n_blocks, block, head_dim = cache[0].shape
    n_convs = lengths.shape[1]
    scale = head_dim ** (-0.5)
    to_log2 = scale * math.log2(math.e)
    n_heads = terms[0].shape[1] // head_dim
    lanes = n_heads * tokens
    n_cache = n_blocks * block
    n_group = n_blocks * tokens
    slots = n_blocks // len(group)
    chunk = min(512, n_cache)
    n_part, n_sum = len(terms), len(sums)
    dims = (((1,), (1,)), ((), ()))
    spans = [(at, chunk) for at in range(0, n_cache, chunk)]
    spans += [(n_cache + i * slots * tokens, slots * tokens) for i in range(len(group))]
    n_first = n_cache // chunk

    def tiles(value):
        return value.reshape(value.shape[0] // 8, 8, lanes)

    def body(len_ref, d_ref, *rest):
        cache_refs, rest = rest[:2], rest[2:]
        group_refs, rest = rest[: len(group)], rest[len(group) :]
        part_refs, rest = rest[:n_part], rest[n_part:]
        sum_refs, rest = rest[:n_sum], rest[n_sum:]
        keep_ref, give_ref, out_ref, s_ref, p_ref, q_ref, dq_ref, ck_ref, cv_ref, sems = rest
        me, dp = lax.axis_index("fsdp"), lax.axis_index("dp")
        odd = dp % 2

        @pl.when(odd == 0)
        def _():
            pltpu.make_async_copy(cache_refs[0], ck_ref, sems.at[0]).start()
            pltpu.make_async_copy(cache_refs[1], cv_ref, sems.at[1]).start()

        @pl.when(odd == 1)
        def _():
            pltpu.make_async_copy(cache_refs[1], ck_ref, sems.at[0]).start()
            pltpu.make_async_copy(cache_refs[0], cv_ref, sems.at[1]).start()

        for h in range(n_heads):
            at = slice(h * head_dim, (h + 1) * head_dim)
            rows = pl.ds(h * tokens, tokens)
            q = part_refs[0][:, at]
            for ref in part_refs[1:]:
                q = q + ref[:, at]
            q_ref[rows] = q.astype(BF16)
            at = (first_head + h) * head_dim
            dq_ref[rows] = d_ref[:, at : at + head_dim]

        q_pos = me * tokens + lax.broadcasted_iota(jnp.int32, (1, lanes), 1) % tokens
        begin = jnp.zeros((1, lanes), jnp.int32)
        end = jnp.int32(0)
        for i in range(n_convs):
            end = end + len_ref[0, i]
            begin = jnp.where(end <= q_pos, end, begin)

        def group_rows(i, at):
            return group_refs[i][...].reshape(slots * tokens, 2 * head_dim)[:, at : at + head_dim]

        def cache_rows(ref, i):
            return ref[...].reshape(n_cache, head_dim)[i * chunk : (i + 1) * chunk]

        for i in range(len(group)):
            at, size = spans[n_first + i]
            s = lax.dot_general(group_rows(i, 0), q_ref[...], dims, preferred_element_type=F32)
            for j in range(slots):
                pos = (me ^ g_order[i * slots + j]) * tokens
                pos = pos + lax.broadcasted_iota(jnp.int32, (tokens, lanes), 0)
                allowed = (pos <= q_pos) & (pos >= begin)
                here = s[j * tokens : (j + 1) * tokens]
                s_ref[pl.ds(at + j * tokens, tokens)] = jnp.where(allowed, here, -jnp.inf)

        pltpu.make_async_copy(cache_refs[0], ck_ref, sems.at[0]).wait()
        pltpu.make_async_copy(cache_refs[1], cv_ref, sems.at[1]).wait()
        for i in range(n_first):
            at, size = spans[i]
            s_ref[pl.ds(at, size)] = lax.dot_general(
                cache_rows(ck_ref, i), q_ref[...], dims, preferred_element_type=F32
            )

        tops, totals = [], []
        for at, size in spans:
            top = jnp.max(tiles(s_ref[pl.ds(at, size)]), axis=0)
            top = jnp.maximum(top, -1e30)
            e = jnp.exp2((tiles(s_ref[pl.ds(at, size)]) - top) * to_log2)
            s_ref[pl.ds(at, size)] = e.reshape(size, lanes)
            tops.append(top)
            totals.append(jnp.sum(e, axis=0))
        top = functools.reduce(jnp.maximum, tops)
        top = jnp.max(top, axis=0, keepdims=True)
        factors = [jnp.exp2((own - top) * to_log2) for own in tops]
        total = functools.reduce(lambda a, b: a + b, [t * f for t, f in zip(totals, factors)])
        inv = 1.0 / jnp.sum(total, axis=0, keepdims=True)
        factors = [f * inv for f in factors]

        delta = jnp.zeros((8, lanes), F32)
        for i in range(len(group)):
            at, size = spans[n_first + i]
            d_prob = lax.dot_general(
                group_rows(i, head_dim), dq_ref[...], dims, preferred_element_type=F32
            )
            p = tiles(s_ref[pl.ds(at, size)]) * factors[n_first + i]
            delta = delta + jnp.sum(p.astype(BF16).astype(F32) * tiles(d_prob), axis=0)
        for i in range(n_first):
            at, size = spans[i]
            p_ref[pl.ds(at, size)] = lax.dot_general(
                cache_rows(cv_ref, i), dq_ref[...], dims, preferred_element_type=F32
            )
            p = (tiles(s_ref[pl.ds(at, size)]) * factors[i]).reshape(size, lanes).astype(BF16)
            delta = delta + jnp.sum(tiles(p.astype(F32)) * tiles(p_ref[pl.ds(at, size)]), axis=0)
            out_ref[1 - odd, pl.ds(at, size)] = jnp.dot(p, dq_ref[...], preferred_element_type=F32)
        delta = jnp.sum(delta, axis=0, keepdims=True)
        for i in range(n_first):
            at, size = spans[i]
            p = tiles(s_ref[pl.ds(at, size)]) * factors[i]
            ds = p * (tiles(p_ref[pl.ds(at, size)]) - delta)
            ds = ds.reshape(size, lanes).astype(BF16)
            g = jnp.dot(ds, q_ref[...], preferred_element_type=F32) * scale
            out_ref[odd, pl.ds(at, size)] = g

        for i, ref in enumerate((keep_ref, give_ref)):
            ref[...] = sum_refs[i][...] + out_ref[i] if n_sum else out_ref[i]

    flops = 2 * lanes * head_dim * (5 * n_cache + 2 * n_group)
    return pl.pallas_call(
        body,
        in_specs=[pl.BlockSpec(memory_space=pltpu.SMEM)]
        + [pl.BlockSpec(memory_space=pltpu.VMEM)]
        + [pl.BlockSpec(memory_space=pl.ANY)] * 2
        + [pl.BlockSpec(memory_space=pltpu.VMEM)] * (len(group) + n_part + n_sum),
        out_specs=[pl.BlockSpec(memory_space=pltpu.VMEM)] * 2,
        out_shape=[jax.ShapeDtypeStruct((n_cache, head_dim), F32)] * 2,
        scratch_shapes=[
            pltpu.VMEM((2, n_cache, head_dim), F32),
            pltpu.VMEM((n_cache + n_group, lanes), F32),
            pltpu.VMEM((n_cache, lanes), F32),
            pltpu.VMEM((lanes, head_dim), BF16),
            pltpu.VMEM((lanes, head_dim), BF16),
            pltpu.VMEM((n_blocks, block, head_dim), BF16),
            pltpu.VMEM((n_blocks, block, head_dim), BF16),
            pltpu.SemaphoreType.DMA((2,)),
        ],
        compiler_params=params(),
        cost_estimate=pl.CostEstimate(
            flops=flops,
            bytes_accessed=12 * n_cache * head_dim,
            transcendentals=lanes * (n_cache + n_group),
        ),
        name="attend",
    )(lengths, d_attn, *cache, *group, *terms, *sums)


def make_on_device(n_dp, n_fsdp):
    inner = n_fsdp // 2

    def on_device(hidden, d_attn, w_query, w_key, w_value, cache_keys, cache_values, lengths):
        dp = lax.axis_index("dp")
        head_dim = w_key.shape[1]
        q_width = w_query.shape[1]
        even = dp % 2 == 0
        f_bits, d_bits = bits_down(n_fsdp), bits_down(n_dp)

        def from_owners(products):
            return [products[0]] + [swap(x, "fsdp", n_fsdp, k + 1) for k, x in enumerate(products[1:])]

        cuts = [(0, q_width // 2), (q_width // 2, q_width // 2)]
        cuts = [(0, q_width // 2), (q_width // 2, q_width // 2)]
        sent, part = prepare(hidden, w_query, w_key, w_value, n_dp, n_fsdp)
        received = [swap(block, "fsdp", n_fsdp, k + 1) for k, block in enumerate(sent)]
        part = swap(part, "fsdp", n_fsdp, inner)
        share = w_query.shape[0] // n_dp
        cut = share + share // 2
        part_a, part_b = part[:cut], part[cut:]
        far_a, order = double(part_a[None], [0], "dp", n_dp, d_bits[0])
        cache = jnp.where(even, cache_keys, cache_values)[None]
        cache, f_order = double(cache, [0], "fsdp", n_fsdp, f_bits[0])
        cache, far_a, *received = together(cache, far_a, *received)
        far_b, _ = double(part_b[None], [0], "dp", n_dp, d_bits[0])
        far_a, d_order = finish(far_a, order, "dp", n_dp, d_bits[1:])
        cache, f_order = double(cache, f_order, "fsdp", n_fsdp, f_bits[1])
        cache, far_a[1] = together(cache, far_a[1])
        kv, (at_a, wide_a), (at_b, wide_b) = 2 * head_dim, *cuts
        near_a = [(w_key, 0, head_dim), (w_value, 0, head_dim), (w_query, at_a, wide_a)]
        layout_a = [(0, 0, share, wide_a, 0, kv)]
        layout_a += [(share, i * kv, share // 2, kv, i * (share // 2), 0) for i in range(2)]
        out_kv, out_a = multiply(
            hidden, received, near_a, far_a, layout_a, d_order, n_fsdp, (kv, wide_a)
        )
        for bit in f_bits[2:]:
            cache, f_order = double(cache, f_order, "fsdp", n_fsdp, bit)
        far_b, cache, out_kv[0] = together(far_b, cache, out_kv[0])
        far_b, _ = finish(far_b, order, "dp", n_dp, d_bits[1:])
        parts_kv = from_owners(out_kv)
        parts_a = from_owners(out_a)
        own = functools.reduce(lambda a, b: a + b, parts_kv).astype(BF16)
        far_b[1], own = together(far_b[1], own)
        group, _ = double(own[None], [0], "fsdp", n_fsdp, inner)
        near_b, layout_b = [(w_query, at_b, wide_b)], [(0, 0, share, wide_b, 0, 0)]
        (out_b,) = multiply(
            hidden, received, near_b, far_b, layout_b, d_order, n_fsdp, (wide_b,)
        )
        group, cache, *tied = together(group, cache, *out_b, *parts_a[1:])
        out_b, parts_a[1:] = tied[:inner], tied[inner:]
        group = [group] + [swap(group, "fsdp", n_fsdp, k) for k in range(1, inner)]
        g_order = [o for k in range(inner) for o in (k, k ^ inner)]
        cache = [cache, swap(cache, "dp", n_dp, 1)]
        parts_b = from_owners(out_b)
        first = cuts[0][1] // head_dim
        sums = attend(lengths, parts_a, d_attn, 0, cache, group, g_order, ())
        keep, give = attend(lengths, parts_b, d_attn, first, cache, group, g_order, sums)

        half = keep + swap(give, "dp", n_dp, 1)
        size = half.shape[0] // n_fsdp
        mine = half[:size]
        for slot in range(1, n_fsdp):
            out = half[slot * size : (slot + 1) * size].astype(BF16)
            mine = mine + swap(out, "fsdp", n_fsdp, f_order[slot]).astype(F32)
        for bit in d_bits[:-1]:
            mine = mine + swap(mine, "dp", n_dp, bit)
        other = swap(mine, "dp", n_dp, 1)
        return jnp.where(even, mine, other), jnp.where(even, other, mine)

    return on_device


def solution(mesh):
    placed = (
        P(("dp", "fsdp"), None),
        P(("dp", "fsdp"), None),
        P("fsdp", None),
        P("fsdp", None),
        P("fsdp", None),
        P("fsdp", None),
        P("fsdp", None),
        P("dp", None),
    )
    return jax.shard_map(
        make_on_device(mesh.shape["dp"], mesh.shape["fsdp"]),
        mesh=mesh,
        in_specs=placed,
        out_specs=(P("fsdp", None), P("fsdp", None)),
        check_vma=False,
    )
```

```python
import functools
import math

import jax
import jax.numpy as jnp
from jax import lax
from jax.experimental import pallas as pl
from jax.experimental.pallas import tpu as pltpu
from jax.sharding import PartitionSpec as P

F32 = jnp.float32
BF16 = jnp.bfloat16
VMEM_LIMIT = 56 * 1024 * 1024


def swap(value, axis, size, bit):
    return lax.ppermute(value, axis, [(i, i ^ bit) for i in range(size)])


def bits_down(size):
    bits = []
    bit = size // 2
    while bit:
        bits.append(bit)
        bit //= 2
    return bits


def double(block, order, axis, size, bit):
    return jnp.concatenate([block, swap(block, axis, size, bit)]), order + [o ^ bit for o in order]


def finish(block, order, axis, size, bits):
    for bit in bits[:-1]:
        block, order = double(block, order, axis, size, bit)
    return [block, swap(block, axis, size, bits[-1])], order + [o ^ bits[-1] for o in order]


def together(*values):
    return lax.optimization_barrier(values)


def params():
    return pltpu.CompilerParams(vmem_limit_bytes=VMEM_LIMIT)


def run_copies(copies):
    for copy in copies:
        copy.start()
    for copy in copies:
        copy.wait()


def prepare(hidden, w_query, w_key, w_value, n_dp, n_fsdp):
    inner = n_fsdp // 2
    tokens = hidden.shape[0]
    rows_w, q_width = w_query.shape
    head_dim = w_key.shape[1]
    share = rows_w // n_dp
    cols = q_width // 2

    def body(hidden_ref, wq_ref, wk_ref, wv_ref, *rest):
        sent, part, sems = rest[: inner - 1], rest[-2], rest[-1]
        me, dp = lax.axis_index("fsdp"), lax.axis_index("dp")
        first = pl.multiple_of(dp * share, 16)
        rows = pl.ds(first, share)
        pairs = []
        for i in range(2):
            to = part.at[pl.ds(i * (share + share // 2), share)]
            pairs.append((wq_ref.at[rows, pl.ds(i * cols, cols)], to))
            for j, ref in enumerate((wk_ref, wv_ref)):
                to = part.at[pl.ds(share, share // 2), pl.ds((2 * i + j) * head_dim, head_dim)]
                pairs.append((ref.at[pl.ds(first + i * (share // 2), share // 2)], to))
        for k in range(1, inner):
            for side, bit in enumerate((0, inner)):
                start = pl.multiple_of((me ^ k ^ bit) * rows_w, 128)
                pairs.append(
                    (hidden_ref.at[:, pl.ds(start, rows_w)], sent[k - 1].at[:, pl.ds(side * rows_w, rows_w)])
                )
        run_copies([pltpu.make_async_copy(a, b, sems.at[i]) for i, (a, b) in enumerate(pairs)])

    moved = 2 * (tokens * 2 * rows_w * 2 * (inner - 1) + share * (q_width + 2 * head_dim) * 2)
    out = pl.pallas_call(
        body,
        in_specs=[pl.BlockSpec(memory_space=pl.ANY)] * 4,
        out_specs=[pl.BlockSpec(memory_space=pltpu.VMEM)] * inner,
        out_shape=[jax.ShapeDtypeStruct((tokens, 2 * rows_w), BF16)] * (inner - 1)
        + [jax.ShapeDtypeStruct((2 * share + share // 2, cols), BF16)],
        scratch_shapes=[pltpu.SemaphoreType.DMA((6 + 2 * (inner - 1),))],
        compiler_params=params(),
        cost_estimate=pl.CostEstimate(flops=0, bytes_accessed=moved, transcendentals=0),
        name="prepare",
    )(hidden, w_query, w_key, w_value)
    return out[:-1], out[-1]


def multiply(hidden, received, near, far, layout, order, n_fsdp, groups):
    inner = n_fsdp // 2
    tokens = hidden.shape[0]
    cols = sum(wide for _, _, wide in near)
    slots = far[0].shape[0]
    n_dp = slots * len(far)
    rows_w = near[0][0].shape[0]
    share = rows_w // n_dp
    step = 256 if all(g % 256 == 0 for g in groups) else 128
    n_in = inner - 1 + len(near) + len(far)

    def body(hidden_ref, *rest):
        blocks, rest = rest[: inner - 1], rest[inner - 1 :]
        near_refs, rest = rest[: len(near)], rest[len(near) :]
        far_refs, rest = rest[: len(far)], rest[len(far) :]
        outs = rest[:-3]
        x_all, w_all, sems = rest[-3:]
        me, dp = lax.axis_index("fsdp"), lax.axis_index("dp")
        pairs = []
        for side, bit in enumerate((0, inner)):
            start = pl.multiple_of((me ^ bit) * rows_w, 128)
            pairs.append(
                (
                    hidden_ref.at[:, pl.ds(start, rows_w)],
                    x_all.at[pl.ds(0, tokens), pl.ds(side * rows_w, rows_w)],
                )
            )
        for k in range(1, inner):
            pairs.append((blocks[k - 1], x_all.at[pl.ds(k * tokens, tokens)]))
        to = 0
        for ref, (_, start, wide) in zip(near_refs, near):
            pairs.append((ref.at[:, pl.ds(start, wide)], w_all.at[pl.ds(0, rows_w), pl.ds(to, wide)]))
            to += wide
        for slot, o in enumerate(order):
            block = far_refs[slot // slots].at[slot % slots]
            for row, col, rows, wide, to_row, to_col in layout:
                to = pl.multiple_of(rows_w + (dp ^ o) * share + to_row, 16)
                piece = block.at[pl.ds(row, rows), pl.ds(col, wide)]
                pairs.append((piece, w_all.at[pl.ds(to, rows), pl.ds(to_col, wide)]))
        run_copies([pltpu.make_async_copy(a, b, sems.at[i]) for i, (a, b) in enumerate(pairs)])

        base = 0
        for g, wide in enumerate(groups):

            @pl.loop(0, wide // step)
            def _(n, g=g, base=base):
                at = pl.multiple_of(n * step, 128)
                product = jnp.dot(
                    x_all[...], w_all[:, pl.ds(base + at, step)], preferred_element_type=F32
                )
                for k in range(inner):
                    outs[g * inner + k][:, pl.ds(at, step)] = product[k * tokens : (k + 1) * tokens]

            base += wide

    copies = 2 + (inner - 1) + len(near) + n_dp * len(layout)
    moved = inner * tokens * 2 * rows_w * 2 + 2 * rows_w * cols * 2 + inner * tokens * cols * 4
    out = pl.pallas_call(
        body,
        in_specs=[pl.BlockSpec(memory_space=pl.ANY)] * (1 + n_in),
        out_specs=[pl.BlockSpec(memory_space=pltpu.VMEM)] * (inner * len(groups)),
        out_shape=[jax.ShapeDtypeStruct((tokens, g), F32) for g in groups for _ in range(inner)],
        scratch_shapes=[
            pltpu.VMEM((inner * tokens, 2 * rows_w), BF16),
            pltpu.VMEM((2 * rows_w, cols), BF16),
            pltpu.SemaphoreType.DMA((copies,)),
        ],
        compiler_params=params(),
        cost_estimate=pl.CostEstimate(
            flops=2 * inner * tokens * 2 * rows_w * cols, bytes_accessed=moved, transcendentals=0
        ),
        name="multiply",
    )(hidden, *received, *[array for array, _, _ in near], *far)
    return [list(out[g * inner : (g + 1) * inner]) for g in range(len(groups))]


def attend(lengths, terms, d_attn, first_head, cache, c_order, group, g_order, sums):
    tokens = d_attn.shape[0]
    n_blocks, block, head_dim = cache[0].shape
    n_convs = lengths.shape[1]
    scale = head_dim ** (-0.5)
    to_log2 = scale * math.log2(math.e)
    n_heads = terms[0].shape[1] // head_dim
    lanes = n_heads * tokens
    n_cache = n_blocks * block
    n_group = n_blocks * tokens
    slots = n_blocks // len(group)
    chunk = min(512, n_cache)
    n_part, n_sum = len(terms), len(sums)
    dims = (((1,), (1,)), ((), ()))
    spans = [(at, chunk) for at in range(0, n_cache, chunk)]
    spans += [(n_cache + i * slots * tokens, slots * tokens) for i in range(len(group))]
    n_first = n_cache // chunk

    def tiles(value):
        return value.reshape(value.shape[0] // 8, 8, lanes)

    def body(len_ref, d_ref, *rest):
        cache_refs, rest = rest[:2], rest[2:]
        group_refs, rest = rest[: len(group)], rest[len(group) :]
        part_refs, rest = rest[:n_part], rest[n_part:]
        sum_refs, rest = rest[:n_sum], rest[n_sum:]
        keep_ref, give_ref, out_ref, s_ref, p_ref, q_ref, dq_ref, ck_ref, cv_ref, sems = rest
        me, dp = lax.axis_index("fsdp"), lax.axis_index("dp")
        odd = dp % 2

        @pl.when(odd == 0)
        def _():
            pltpu.make_async_copy(cache_refs[0], ck_ref, sems.at[0]).start()
            pltpu.make_async_copy(cache_refs[1], cv_ref, sems.at[1]).start()

        @pl.when(odd == 1)
        def _():
            pltpu.make_async_copy(cache_refs[1], ck_ref, sems.at[0]).start()
            pltpu.make_async_copy(cache_refs[0], cv_ref, sems.at[1]).start()

        for h in range(n_heads):
            at = slice(h * head_dim, (h + 1) * head_dim)
            rows = pl.ds(h * tokens, tokens)
            q = part_refs[0][:, at]
            for ref in part_refs[1:]:
                q = q + ref[:, at]
            q_ref[rows] = q.astype(BF16)
            at = (first_head + h) * head_dim
            dq_ref[rows] = d_ref[:, at : at + head_dim]

        q_pos = me * tokens + lax.broadcasted_iota(jnp.int32, (1, lanes), 1) % tokens
        begin = jnp.zeros((1, lanes), jnp.int32)
        end = jnp.int32(0)
        for i in range(n_convs):
            end = end + len_ref[0, i]
            begin = jnp.where(end <= q_pos, end, begin)

        def group_rows(i, at):
            return group_refs[i][...].reshape(slots * tokens, 2 * head_dim)[:, at : at + head_dim]

        def cache_rows(ref, i):
            return ref[...].reshape(n_cache, head_dim)[i * chunk : (i + 1) * chunk]

        for i in range(len(group)):
            at, size = spans[n_first + i]
            s = lax.dot_general(group_rows(i, 0), q_ref[...], dims, preferred_element_type=F32)
            for j in range(slots):
                pos = (me ^ g_order[i * slots + j]) * tokens
                pos = pos + lax.broadcasted_iota(jnp.int32, (tokens, lanes), 0)
                allowed = (pos <= q_pos) & (pos >= begin)
                here = s[j * tokens : (j + 1) * tokens]
                s_ref[pl.ds(at + j * tokens, tokens)] = jnp.where(allowed, here, -jnp.inf)

        pltpu.make_async_copy(cache_refs[0], ck_ref, sems.at[0]).wait()
        pltpu.make_async_copy(cache_refs[1], cv_ref, sems.at[1]).wait()
        for i in range(n_first):
            at, size = spans[i]
            s_ref[pl.ds(at, size)] = lax.dot_general(
                cache_rows(ck_ref, i), q_ref[...], dims, preferred_element_type=F32
            )

        tops, totals = [], []
        for at, size in spans:
            top = jnp.max(tiles(s_ref[pl.ds(at, size)]), axis=0)
            top = jnp.maximum(top, -1e30)
            e = jnp.exp2((tiles(s_ref[pl.ds(at, size)]) - top) * to_log2)
            s_ref[pl.ds(at, size)] = e.reshape(size, lanes)
            tops.append(top)
            totals.append(jnp.sum(e, axis=0))
        top = functools.reduce(jnp.maximum, tops)
        top = jnp.max(top, axis=0, keepdims=True)
        factors = [jnp.exp2((own - top) * to_log2) for own in tops]
        total = functools.reduce(lambda a, b: a + b, [t * f for t, f in zip(totals, factors)])
        inv = 1.0 / jnp.sum(total, axis=0, keepdims=True)
        factors = [f * inv for f in factors]

        delta = jnp.zeros((8, lanes), F32)
        for i in range(len(group)):
            at, size = spans[n_first + i]
            d_prob = lax.dot_general(
                group_rows(i, head_dim), dq_ref[...], dims, preferred_element_type=F32
            )
            p = tiles(s_ref[pl.ds(at, size)]) * factors[n_first + i]
            delta = delta + jnp.sum(p.astype(BF16).astype(F32) * tiles(d_prob), axis=0)
        for i in range(n_first):
            at, size = spans[i]
            p_ref[pl.ds(at, size)] = lax.dot_general(
                cache_rows(cv_ref, i), dq_ref[...], dims, preferred_element_type=F32
            )
            p = (tiles(s_ref[pl.ds(at, size)]) * factors[i]).reshape(size, lanes).astype(BF16)
            delta = delta + jnp.sum(tiles(p.astype(F32)) * tiles(p_ref[pl.ds(at, size)]), axis=0)
            out_ref[1 - odd, pl.ds(at, size)] = jnp.dot(p, dq_ref[...], preferred_element_type=F32)
        delta = jnp.sum(delta, axis=0, keepdims=True)
        for i in range(n_first):
            at, size = spans[i]
            p = tiles(s_ref[pl.ds(at, size)]) * factors[i]
            ds = p * (tiles(p_ref[pl.ds(at, size)]) - delta)
            ds = ds.reshape(size, lanes).astype(BF16)
            g = jnp.dot(ds, q_ref[...], preferred_element_type=F32) * scale
            out_ref[odd, pl.ds(at, size)] = g

        for i, ref in enumerate((keep_ref, give_ref)):
            if n_sum:
                for b, o in enumerate(c_order):
                    at = pl.ds(b * block, block)
                    to = pl.multiple_of((me ^ o) * block, block)
                    ref[pl.ds(to, block)] = sum_refs[i][at] + out_ref[i, at]
            else:
                ref[...] = out_ref[i]

    flops = 2 * lanes * head_dim * (5 * n_cache + 2 * n_group)
    return pl.pallas_call(
        body,
        in_specs=[pl.BlockSpec(memory_space=pltpu.SMEM)]
        + [pl.BlockSpec(memory_space=pltpu.VMEM)]
        + [pl.BlockSpec(memory_space=pl.ANY)] * 2
        + [pl.BlockSpec(memory_space=pltpu.VMEM)] * (len(group) + n_part + n_sum),
        out_specs=[pl.BlockSpec(memory_space=pltpu.VMEM)] * 2,
        out_shape=[jax.ShapeDtypeStruct((n_cache, head_dim), F32)] * 2,
        scratch_shapes=[
            pltpu.VMEM((2, n_cache, head_dim), F32),
            pltpu.VMEM((n_cache + n_group, lanes), F32),
            pltpu.VMEM((n_cache, lanes), F32),
            pltpu.VMEM((lanes, head_dim), BF16),
            pltpu.VMEM((lanes, head_dim), BF16),
            pltpu.VMEM((n_blocks, block, head_dim), BF16),
            pltpu.VMEM((n_blocks, block, head_dim), BF16),
            pltpu.SemaphoreType.DMA((2,)),
        ],
        compiler_params=params(),
        cost_estimate=pl.CostEstimate(
            flops=flops,
            bytes_accessed=12 * n_cache * head_dim,
            transcendentals=lanes * (n_cache + n_group),
        ),
        name="attend",
    )(lengths, d_attn, *cache, *group, *terms, *sums)


def make_on_device(n_dp, n_fsdp):
    inner = n_fsdp // 2

    def on_device(hidden, d_attn, w_query, w_key, w_value, cache_keys, cache_values, lengths):
        dp = lax.axis_index("dp")
        head_dim = w_key.shape[1]
        q_width = w_query.shape[1]
        even = dp % 2 == 0
        f_bits, d_bits = bits_down(n_fsdp), bits_down(n_dp)

        def from_owners(products):
            return [products[0]] + [swap(x, "fsdp", n_fsdp, k + 1) for k, x in enumerate(products[1:])]

        cuts = [(0, q_width // 2), (q_width // 2, q_width // 2)]
        cuts = [(0, q_width // 2), (q_width // 2, q_width // 2)]
        sent, part = prepare(hidden, w_query, w_key, w_value, n_dp, n_fsdp)
        received = [swap(block, "fsdp", n_fsdp, k + 1) for k, block in enumerate(sent)]
        part = swap(part, "fsdp", n_fsdp, inner)
        share = w_query.shape[0] // n_dp
        cut = share + share // 2
        part_a, part_b = part[:cut], part[cut:]
        far_a, order = double(part_a[None], [0], "dp", n_dp, d_bits[0])
        cache = jnp.where(even, cache_keys, cache_values)[None]
        cache, f_order = double(cache, [0], "fsdp", n_fsdp, f_bits[0])
        cache, far_a, *received = together(cache, far_a, *received)
        far_b, _ = double(part_b[None], [0], "dp", n_dp, d_bits[0])
        far_a, d_order = finish(far_a, order, "dp", n_dp, d_bits[1:])
        cache, f_order = double(cache, f_order, "fsdp", n_fsdp, f_bits[1])
        cache, far_a[1] = together(cache, far_a[1])
        kv, (at_a, wide_a), (at_b, wide_b) = 2 * head_dim, *cuts
        near_a = [(w_key, 0, head_dim), (w_value, 0, head_dim), (w_query, at_a, wide_a)]
        layout_a = [(0, 0, share, wide_a, 0, kv)]
        layout_a += [(share, i * kv, share // 2, kv, i * (share // 2), 0) for i in range(2)]
        out_kv, out_a = multiply(
            hidden, received, near_a, far_a, layout_a, d_order, n_fsdp, (kv, wide_a)
        )
        for bit in f_bits[2:]:
            cache, f_order = double(cache, f_order, "fsdp", n_fsdp, bit)
        far_b, cache, out_kv[0] = together(far_b, cache, out_kv[0])
        far_b, _ = finish(far_b, order, "dp", n_dp, d_bits[1:])
        parts_kv = from_owners(out_kv)
        parts_a = from_owners(out_a)
        own = functools.reduce(lambda a, b: a + b, parts_kv).astype(BF16)
        far_b[1], own = together(far_b[1], own)
        group, _ = double(own[None], [0], "fsdp", n_fsdp, inner)
        near_b, layout_b = [(w_query, at_b, wide_b)], [(0, 0, share, wide_b, 0, 0)]
        (out_b,) = multiply(
            hidden, received, near_b, far_b, layout_b, d_order, n_fsdp, (wide_b,)
        )
        group, cache, *tied = together(group, cache, *out_b, *parts_a[1:])
        out_b, parts_a[1:] = tied[:inner], tied[inner:]
        group = [group] + [swap(group, "fsdp", n_fsdp, k) for k in range(1, inner)]
        g_order = [o for k in range(inner) for o in (k, k ^ inner)]
        cache = [cache, swap(cache, "dp", n_dp, 1)]
        parts_b = from_owners(out_b)
        first = cuts[0][1] // head_dim
        sums = attend(lengths, parts_a, d_attn, 0, cache, f_order, group, g_order, ())
        keep, give = attend(lengths, parts_b, d_attn, first, cache, f_order, group, g_order, sums)

        half = keep + swap(give, "dp", n_dp, 1)
        blocks = half.astype(BF16).reshape(n_fsdp, half.shape[0] // n_fsdp, head_dim)
        blocks = lax.all_to_all(blocks, "fsdp", 0, 0)
        mine = jnp.sum(blocks.astype(F32), axis=0)
        for bit in d_bits[:-1]:
            mine = mine + swap(mine, "dp", n_dp, bit)
        other = swap(mine, "dp", n_dp, 1)
        return jnp.where(even, mine, other), jnp.where(even, other, mine)

    return on_device


def solution(mesh):
    placed = (
        P(("dp", "fsdp"), None),
        P(("dp", "fsdp"), None),
        P("fsdp", None),
        P("fsdp", None),
        P("fsdp", None),
        P("fsdp", None),
        P("fsdp", None),
        P("dp", None),
    )
    return jax.shard_map(
        make_on_device(mesh.shape["dp"], mesh.shape["fsdp"]),
        mesh=mesh,
        in_specs=placed,
        out_specs=(P("fsdp", None), P("fsdp", None)),
        check_vma=False,
    )
```

```python
import functools
import math

import jax
import jax.numpy as jnp
from jax import lax
from jax.experimental import pallas as pl
from jax.experimental.pallas import tpu as pltpu
from jax.sharding import PartitionSpec as P

F32 = jnp.float32
BF16 = jnp.bfloat16
VMEM_LIMIT = 56 * 1024 * 1024


def swap(value, axis, size, bit):
    return lax.ppermute(value, axis, [(i, i ^ bit) for i in range(size)])


def bits_down(size):
    bits = []
    bit = size // 2
    while bit:
        bits.append(bit)
        bit //= 2
    return bits


def double(block, order, axis, size, bit):
    return jnp.concatenate([block, swap(block, axis, size, bit)]), order + [o ^ bit for o in order]


def finish(block, order, axis, size, bits):
    for bit in bits[:-1]:
        block, order = double(block, order, axis, size, bit)
    return [block, swap(block, axis, size, bits[-1])], order + [o ^ bits[-1] for o in order]


def together(*values):
    return lax.optimization_barrier(values)


def params():
    return pltpu.CompilerParams(vmem_limit_bytes=VMEM_LIMIT)


def run_copies(copies):
    for copy in copies:
        copy.start()
    for copy in copies:
        copy.wait()


def prepare(hidden, w_query, w_key, w_value, n_dp, n_fsdp):
    inner = n_fsdp // 2
    tokens = hidden.shape[0]
    rows_w, q_width = w_query.shape
    head_dim = w_key.shape[1]
    share = rows_w // n_dp
    cols = q_width // 2

    def body(hidden_ref, wq_ref, wk_ref, wv_ref, *rest):
        sent, part, sems = rest[: inner - 1], rest[-2], rest[-1]
        me, dp = lax.axis_index("fsdp"), lax.axis_index("dp")
        first = pl.multiple_of(dp * share, 16)
        rows = pl.ds(first, share)
        pairs = []
        for i in range(2):
            to = part.at[pl.ds(i * (share + share // 2), share)]
            pairs.append((wq_ref.at[rows, pl.ds(i * cols, cols)], to))
            for j, ref in enumerate((wk_ref, wv_ref)):
                to = part.at[pl.ds(share, share // 2), pl.ds((2 * i + j) * head_dim, head_dim)]
                pairs.append((ref.at[pl.ds(first + i * (share // 2), share // 2)], to))
        for k in range(1, inner):
            for side, bit in enumerate((0, inner)):
                start = pl.multiple_of((me ^ k ^ bit) * rows_w, 128)
                pairs.append(
                    (hidden_ref.at[:, pl.ds(start, rows_w)], sent[k - 1].at[:, pl.ds(side * rows_w, rows_w)])
                )
        run_copies([pltpu.make_async_copy(a, b, sems.at[i]) for i, (a, b) in enumerate(pairs)])

    moved = 2 * (tokens * 2 * rows_w * 2 * (inner - 1) + share * (q_width + 2 * head_dim) * 2)
    out = pl.pallas_call(
        body,
        in_specs=[pl.BlockSpec(memory_space=pl.ANY)] * 4,
        out_specs=[pl.BlockSpec(memory_space=pltpu.VMEM)] * inner,
        out_shape=[jax.ShapeDtypeStruct((tokens, 2 * rows_w), BF16)] * (inner - 1)
        + [jax.ShapeDtypeStruct((2 * share + share // 2, cols), BF16)],
        scratch_shapes=[pltpu.SemaphoreType.DMA((6 + 2 * (inner - 1),))],
        compiler_params=params(),
        cost_estimate=pl.CostEstimate(flops=0, bytes_accessed=moved, transcendentals=0),
        name="prepare",
    )(hidden, w_query, w_key, w_value)
    return out[:-1], out[-1]


def multiply(hidden, received, near, far, layout, order, n_fsdp, groups):
    inner = n_fsdp // 2
    tokens = hidden.shape[0]
    cols = sum(wide for _, _, wide in near)
    slots = far[0].shape[0]
    n_dp = slots * len(far)
    rows_w = near[0][0].shape[0]
    share = rows_w // n_dp
    step = 256 if all(g % 256 == 0 for g in groups) else 128
    n_in = inner - 1 + len(near) + len(far)

    def body(hidden_ref, *rest):
        blocks, rest = rest[: inner - 1], rest[inner - 1 :]
        near_refs, rest = rest[: len(near)], rest[len(near) :]
        far_refs, rest = rest[: len(far)], rest[len(far) :]
        outs = rest[:-3]
        x_all, w_all, sems = rest[-3:]
        me, dp = lax.axis_index("fsdp"), lax.axis_index("dp")
        pairs = []
        for side, bit in enumerate((0, inner)):
            start = pl.multiple_of((me ^ bit) * rows_w, 128)
            pairs.append(
                (
                    hidden_ref.at[:, pl.ds(start, rows_w)],
                    x_all.at[pl.ds(0, tokens), pl.ds(side * rows_w, rows_w)],
                )
            )
        for k in range(1, inner):
            pairs.append((blocks[k - 1], x_all.at[pl.ds(k * tokens, tokens)]))
        to = 0
        for ref, (_, start, wide) in zip(near_refs, near):
            pairs.append((ref.at[:, pl.ds(start, wide)], w_all.at[pl.ds(0, rows_w), pl.ds(to, wide)]))
            to += wide
        for slot, o in enumerate(order):
            block = far_refs[slot // slots].at[slot % slots]
            for row, col, rows, wide, to_row, to_col in layout:
                to = pl.multiple_of(rows_w + (dp ^ o) * share + to_row, 16)
                piece = block.at[pl.ds(row, rows), pl.ds(col, wide)]
                pairs.append((piece, w_all.at[pl.ds(to, rows), pl.ds(to_col, wide)]))
        run_copies([pltpu.make_async_copy(a, b, sems.at[i]) for i, (a, b) in enumerate(pairs)])

        base = 0
        for g, wide in enumerate(groups):

            @pl.loop(0, wide // step)
            def _(n, g=g, base=base):
                at = pl.multiple_of(n * step, 128)
                product = jnp.dot(
                    x_all[...], w_all[:, pl.ds(base + at, step)], preferred_element_type=F32
                )
                for k in range(inner):
                    outs[g * inner + k][:, pl.ds(at, step)] = product[k * tokens : (k + 1) * tokens]

            base += wide

    copies = 2 + (inner - 1) + len(near) + n_dp * len(layout)
    moved = inner * tokens * 2 * rows_w * 2 + 2 * rows_w * cols * 2 + inner * tokens * cols * 4
    out = pl.pallas_call(
        body,
        in_specs=[pl.BlockSpec(memory_space=pl.ANY)] * (1 + n_in),
        out_specs=[pl.BlockSpec(memory_space=pltpu.VMEM)] * (inner * len(groups)),
        out_shape=[jax.ShapeDtypeStruct((tokens, g), F32) for g in groups for _ in range(inner)],
        scratch_shapes=[
            pltpu.VMEM((inner * tokens, 2 * rows_w), BF16),
            pltpu.VMEM((2 * rows_w, cols), BF16),
            pltpu.SemaphoreType.DMA((copies,)),
        ],
        compiler_params=params(),
        cost_estimate=pl.CostEstimate(
            flops=2 * inner * tokens * 2 * rows_w * cols, bytes_accessed=moved, transcendentals=0
        ),
        name="multiply",
    )(hidden, *received, *[array for array, _, _ in near], *far)
    return [list(out[g * inner : (g + 1) * inner]) for g in range(len(groups))]


def attend(lengths, partials, d_attn, cache, group, g_order):
    tokens = d_attn.shape[0]
    n_blocks, block, head_dim = cache[0].shape
    n_convs = lengths.shape[1]
    scale = head_dim ** (-0.5)
    to_log2 = scale * math.log2(math.e)
    n_heads = d_attn.shape[1] // head_dim
    lanes = n_heads * tokens
    n_cache = n_blocks * block
    n_group = n_blocks * tokens
    slots = n_blocks // len(group)
    chunk = min(512, n_cache)
    n_part = sum(len(terms) for terms in partials)
    dims = (((1,), (1,)), ((), ()))
    spans = [(at, chunk) for at in range(0, n_cache, chunk)]
    spans += [(n_cache + i * slots * tokens, slots * tokens) for i in range(len(group))]
    n_first = n_cache // chunk

    def tiles(value):
        return value.reshape(value.shape[0] // 8, 8, lanes)

    def body(len_ref, d_ref, *rest):
        cache_refs, rest = rest[:2], rest[2:]
        group_refs, rest = rest[: len(group)], rest[len(group) :]
        part_refs, rest = list(rest[:n_part]), rest[n_part:]
        keep_ref, give_ref, out_ref, s_ref, p_ref, q_ref, dq_ref, ck_ref, cv_ref, sems = rest
        me, dp = lax.axis_index("fsdp"), lax.axis_index("dp")
        odd = dp % 2

        @pl.when(odd == 0)
        def _():
            pltpu.make_async_copy(cache_refs[0], ck_ref, sems.at[0]).start()
            pltpu.make_async_copy(cache_refs[1], cv_ref, sems.at[1]).start()

        @pl.when(odd == 1)
        def _():
            pltpu.make_async_copy(cache_refs[1], ck_ref, sems.at[0]).start()
            pltpu.make_async_copy(cache_refs[0], cv_ref, sems.at[1]).start()

        h = 0
        for terms in partials:
            refs, part_refs = part_refs[: len(terms)], part_refs[len(terms) :]
            for at in range(0, terms[0].shape[1], head_dim):
                rows = pl.ds(h * tokens, tokens)
                q = refs[0][:, at : at + head_dim]
                for ref in refs[1:]:
                    q = q + ref[:, at : at + head_dim]
                q_ref[rows] = q.astype(BF16)
                dq_ref[rows] = d_ref[:, h * head_dim : (h + 1) * head_dim]
                h += 1

        q_pos = me * tokens + lax.broadcasted_iota(jnp.int32, (1, lanes), 1) % tokens
        begin = jnp.zeros((1, lanes), jnp.int32)
        end = jnp.int32(0)
        for i in range(n_convs):
            end = end + len_ref[0, i]
            begin = jnp.where(end <= q_pos, end, begin)

        def group_rows(i, at):
            return group_refs[i][...].reshape(slots * tokens, 2 * head_dim)[:, at : at + head_dim]

        def cache_rows(ref, i):
            return ref[...].reshape(n_cache, head_dim)[i * chunk : (i + 1) * chunk]

        for i in range(len(group)):
            at, size = spans[n_first + i]
            s = lax.dot_general(group_rows(i, 0), q_ref[...], dims, preferred_element_type=F32)
            for j in range(slots):
                pos = (me ^ g_order[i * slots + j]) * tokens
                pos = pos + lax.broadcasted_iota(jnp.int32, (tokens, lanes), 0)
                allowed = (pos <= q_pos) & (pos >= begin)
                here = s[j * tokens : (j + 1) * tokens]
                s_ref[pl.ds(at + j * tokens, tokens)] = jnp.where(allowed, here, -jnp.inf)

        pltpu.make_async_copy(cache_refs[0], ck_ref, sems.at[0]).wait()
        pltpu.make_async_copy(cache_refs[1], cv_ref, sems.at[1]).wait()
        for i in range(n_first):
            at, size = spans[i]
            s_ref[pl.ds(at, size)] = lax.dot_general(
                cache_rows(ck_ref, i), q_ref[...], dims, preferred_element_type=F32
            )

        tops, totals = [], []
        for at, size in spans:
            top = jnp.max(tiles(s_ref[pl.ds(at, size)]), axis=0)
            top = jnp.maximum(top, -1e30)
            e = jnp.exp2((tiles(s_ref[pl.ds(at, size)]) - top) * to_log2)
            s_ref[pl.ds(at, size)] = e.reshape(size, lanes)
            tops.append(top)
            totals.append(jnp.sum(e, axis=0))
        top = functools.reduce(jnp.maximum, tops)
        top = jnp.max(top, axis=0, keepdims=True)
        factors = [jnp.exp2((own - top) * to_log2) for own in tops]
        total = functools.reduce(lambda a, b: a + b, [t * f for t, f in zip(totals, factors)])
        inv = 1.0 / jnp.sum(total, axis=0, keepdims=True)
        factors = [f * inv for f in factors]

        delta = jnp.zeros((8, lanes), F32)
        for i in range(len(group)):
            at, size = spans[n_first + i]
            d_prob = lax.dot_general(
                group_rows(i, head_dim), dq_ref[...], dims, preferred_element_type=F32
            )
            p = tiles(s_ref[pl.ds(at, size)]) * factors[n_first + i]
            delta = delta + jnp.sum(p.astype(BF16).astype(F32) * tiles(d_prob), axis=0)
        for i in range(n_first):
            at, size = spans[i]
            p_ref[pl.ds(at, size)] = lax.dot_general(
                cache_rows(cv_ref, i), dq_ref[...], dims, preferred_element_type=F32
            )
            p = (tiles(s_ref[pl.ds(at, size)]) * factors[i]).reshape(size, lanes).astype(BF16)
            delta = delta + jnp.sum(tiles(p.astype(F32)) * tiles(p_ref[pl.ds(at, size)]), axis=0)
            out_ref[1 - odd, pl.ds(at, size)] = jnp.dot(p, dq_ref[...], preferred_element_type=F32)
        delta = jnp.sum(delta, axis=0, keepdims=True)
        for i in range(n_first):
            at, size = spans[i]
            p = tiles(s_ref[pl.ds(at, size)]) * factors[i]
            ds = p * (tiles(p_ref[pl.ds(at, size)]) - delta)
            ds = ds.reshape(size, lanes).astype(BF16)
            g = jnp.dot(ds, q_ref[...], preferred_element_type=F32) * scale
            out_ref[odd, pl.ds(at, size)] = g

        for i, ref in enumerate((keep_ref, give_ref)):
            ref[...] = out_ref[i]

    flops = 2 * lanes * head_dim * (5 * n_cache + 2 * n_group)
    return pl.pallas_call(
        body,
        in_specs=[pl.BlockSpec(memory_space=pltpu.SMEM)]
        + [pl.BlockSpec(memory_space=pltpu.VMEM)]
        + [pl.BlockSpec(memory_space=pl.ANY)] * 2
        + [pl.BlockSpec(memory_space=pltpu.VMEM)] * (len(group) + n_part),
        out_specs=[pl.BlockSpec(memory_space=pltpu.VMEM)] * 2,
        out_shape=[jax.ShapeDtypeStruct((n_cache, head_dim), F32)] * 2,
        scratch_shapes=[
            pltpu.VMEM((2, n_cache, head_dim), F32),
            pltpu.VMEM((n_cache + n_group, lanes), F32),
            pltpu.VMEM((n_cache, lanes), F32),
            pltpu.VMEM((lanes, head_dim), BF16),
            pltpu.VMEM((lanes, head_dim), BF16),
            pltpu.VMEM((n_blocks, block, head_dim), BF16),
            pltpu.VMEM((n_blocks, block, head_dim), BF16),
            pltpu.SemaphoreType.DMA((2,)),
        ],
        compiler_params=params(),
        cost_estimate=pl.CostEstimate(
            flops=flops,
            bytes_accessed=12 * n_cache * head_dim,
            transcendentals=lanes * (n_cache + n_group),
        ),
        name="attend",
    )(lengths, d_attn, *cache, *group, *[term for terms in partials for term in terms])


def make_on_device(n_dp, n_fsdp):
    inner = n_fsdp // 2

    def on_device(hidden, d_attn, w_query, w_key, w_value, cache_keys, cache_values, lengths):
        dp = lax.axis_index("dp")
        head_dim = w_key.shape[1]
        q_width = w_query.shape[1]
        even = dp % 2 == 0
        f_bits, d_bits = bits_down(n_fsdp), bits_down(n_dp)

        def from_owners(products):
            return [products[0]] + [swap(x, "fsdp", n_fsdp, k + 1) for k, x in enumerate(products[1:])]

        cuts = [(0, q_width // 2), (q_width // 2, q_width // 2)]
        cuts = [(0, q_width // 2), (q_width // 2, q_width // 2)]
        sent, part = prepare(hidden, w_query, w_key, w_value, n_dp, n_fsdp)
        received = [swap(block, "fsdp", n_fsdp, k + 1) for k, block in enumerate(sent)]
        part = swap(part, "fsdp", n_fsdp, inner)
        share = w_query.shape[0] // n_dp
        cut = share + share // 2
        part_a, part_b = part[:cut], part[cut:]
        far_a, order = double(part_a[None], [0], "dp", n_dp, d_bits[0])
        cache = jnp.where(even, cache_keys, cache_values)[None]
        cache, f_order = double(cache, [0], "fsdp", n_fsdp, f_bits[0])
        cache, far_a, *received = together(cache, far_a, *received)
        far_b, _ = double(part_b[None], [0], "dp", n_dp, d_bits[0])
        far_a, d_order = finish(far_a, order, "dp", n_dp, d_bits[1:])
        cache, f_order = double(cache, f_order, "fsdp", n_fsdp, f_bits[1])
        cache, far_a[1] = together(cache, far_a[1])
        kv, (at_a, wide_a), (at_b, wide_b) = 2 * head_dim, *cuts
        near_a = [(w_key, 0, head_dim), (w_value, 0, head_dim), (w_query, at_a, wide_a)]
        layout_a = [(0, 0, share, wide_a, 0, kv)]
        layout_a += [(share, i * kv, share // 2, kv, i * (share // 2), 0) for i in range(2)]
        out_kv, out_a = multiply(
            hidden, received, near_a, far_a, layout_a, d_order, n_fsdp, (kv, wide_a)
        )
        for bit in f_bits[2:]:
            cache, f_order = double(cache, f_order, "fsdp", n_fsdp, bit)
        far_b, cache, out_kv[0] = together(far_b, cache, out_kv[0])
        far_b, _ = finish(far_b, order, "dp", n_dp, d_bits[1:])
        parts_kv = from_owners(out_kv)
        parts_a = from_owners(out_a)
        own = functools.reduce(lambda a, b: a + b, parts_kv).astype(BF16)
        far_b[1], own, cache = together(far_b[1], own, cache)
        cache = [cache, swap(cache, "dp", n_dp, 1)]
        group, _ = double(own[None], [0], "fsdp", n_fsdp, inner)
        near_b, layout_b = [(w_query, at_b, wide_b)], [(0, 0, share, wide_b, 0, 0)]
        (out_b,) = multiply(
            hidden, received, near_b, far_b, layout_b, d_order, n_fsdp, (wide_b,)
        )
        group, cache[1], *tied = together(group, cache[1], *out_b, *parts_a[1:])
        out_b, parts_a[1:] = tied[:inner], tied[inner:]
        parts_b = from_owners(out_b)
        group, parts_b[1] = together(group, parts_b[1])
        group = [group] + [swap(group, "fsdp", n_fsdp, k) for k in range(1, inner)]
        g_order = [o for k in range(inner) for o in (k, k ^ inner)]
        keep, give = attend(lengths, [parts_a, parts_b], d_attn, cache, group, g_order)

        half = keep + swap(give, "dp", n_dp, 1)
        size = half.shape[0] // n_fsdp
        mine = half[:size]
        for slot in range(1, n_fsdp):
            out = half[slot * size : (slot + 1) * size].astype(BF16)
            mine = mine + swap(out, "fsdp", n_fsdp, f_order[slot]).astype(F32)
        for bit in d_bits[:-1]:
            mine = mine + swap(mine, "dp", n_dp, bit)
        other = swap(mine, "dp", n_dp, 1)
        return jnp.where(even, mine, other), jnp.where(even, other, mine)

    return on_device


def solution(mesh):
    placed = (
        P(("dp", "fsdp"), None),
        P(("dp", "fsdp"), None),
        P("fsdp", None),
        P("fsdp", None),
        P("fsdp", None),
        P("fsdp", None),
        P("fsdp", None),
        P("dp", None),
    )
    return jax.shard_map(
        make_on_device(mesh.shape["dp"], mesh.shape["fsdp"]),
        mesh=mesh,
        in_specs=placed,
        out_specs=(P("fsdp", None), P("fsdp", None)),
        check_vma=False,
    )
```

```python
import functools
import math

import jax
import jax.numpy as jnp
from jax import lax
from jax.experimental import pallas as pl
from jax.experimental.pallas import tpu as pltpu
from jax.sharding import PartitionSpec as P

F32 = jnp.float32
BF16 = jnp.bfloat16
VMEM_LIMIT = 56 * 1024 * 1024


def swap(value, axis, size, bit):
    return lax.ppermute(value, axis, [(i, i ^ bit) for i in range(size)])


def bits_down(size):
    bits = []
    bit = size // 2
    while bit:
        bits.append(bit)
        bit //= 2
    return bits


def double(block, order, axis, size, bit):
    return jnp.concatenate([block, swap(block, axis, size, bit)]), order + [o ^ bit for o in order]


def finish(block, order, axis, size, bits):
    for bit in bits[:-1]:
        block, order = double(block, order, axis, size, bit)
    return [block, swap(block, axis, size, bits[-1])], order + [o ^ bits[-1] for o in order]


def together(*values):
    return lax.optimization_barrier(values)


def params():
    return pltpu.CompilerParams(vmem_limit_bytes=VMEM_LIMIT)


def run_copies(copies):
    for copy in copies:
        copy.start()
    for copy in copies:
        copy.wait()


def prepare(hidden, w_query, w_key, w_value, n_dp, n_fsdp):
    inner = n_fsdp // 2
    tokens = hidden.shape[0]
    rows_w, q_width = w_query.shape
    head_dim = w_key.shape[1]
    share = rows_w // n_dp
    cols = q_width // 2

    def body(hidden_ref, wq_ref, wk_ref, wv_ref, *rest):
        sent, part, sems = rest[: inner - 1], rest[-2], rest[-1]
        me, dp = lax.axis_index("fsdp"), lax.axis_index("dp")
        first = pl.multiple_of(dp * share, 16)
        rows = pl.ds(first, share)
        pairs = []
        for i in range(2):
            to = part.at[pl.ds(i * (share + share // 2), share)]
            pairs.append((wq_ref.at[rows, pl.ds(i * cols, cols)], to))
            for j, ref in enumerate((wk_ref, wv_ref)):
                to = part.at[pl.ds(share, share // 2), pl.ds((2 * i + j) * head_dim, head_dim)]
                pairs.append((ref.at[pl.ds(first + i * (share // 2), share // 2)], to))
        for k in range(1, inner):
            for side, bit in enumerate((0, inner)):
                start = pl.multiple_of((me ^ k ^ bit) * rows_w, 128)
                pairs.append(
                    (hidden_ref.at[:, pl.ds(start, rows_w)], sent[k - 1].at[:, pl.ds(side * rows_w, rows_w)])
                )
        run_copies([pltpu.make_async_copy(a, b, sems.at[i]) for i, (a, b) in enumerate(pairs)])

    moved = 2 * (tokens * 2 * rows_w * 2 * (inner - 1) + share * (q_width + 2 * head_dim) * 2)
    out = pl.pallas_call(
        body,
        in_specs=[pl.BlockSpec(memory_space=pl.ANY)] * 4,
        out_specs=[pl.BlockSpec(memory_space=pltpu.VMEM)] * inner,
        out_shape=[jax.ShapeDtypeStruct((tokens, 2 * rows_w), BF16)] * (inner - 1)
        + [jax.ShapeDtypeStruct((2 * share + share // 2, cols), BF16)],
        scratch_shapes=[pltpu.SemaphoreType.DMA((6 + 2 * (inner - 1),))],
        compiler_params=params(),
        cost_estimate=pl.CostEstimate(flops=0, bytes_accessed=moved, transcendentals=0),
        name="prepare",
    )(hidden, w_query, w_key, w_value)
    return out[:-1], out[-1]


def multiply(hidden, received, near, far, layout, order, n_fsdp, groups):
    inner = n_fsdp // 2
    tokens = hidden.shape[0]
    cols = sum(wide for _, _, wide in near)
    slots = far[0].shape[0]
    n_dp = slots * len(far)
    rows_w = near[0][0].shape[0]
    share = rows_w // n_dp
    step = 256 if all(g % 256 == 0 for g in groups) else 128
    n_in = inner - 1 + len(near) + len(far)

    def body(hidden_ref, *rest):
        blocks, rest = rest[: inner - 1], rest[inner - 1 :]
        near_refs, rest = rest[: len(near)], rest[len(near) :]
        far_refs, rest = rest[: len(far)], rest[len(far) :]
        outs = rest[:-3]
        x_all, w_all, sems = rest[-3:]
        me, dp = lax.axis_index("fsdp"), lax.axis_index("dp")
        pairs = []
        for side, bit in enumerate((0, inner)):
            start = pl.multiple_of((me ^ bit) * rows_w, 128)
            pairs.append(
                (
                    hidden_ref.at[:, pl.ds(start, rows_w)],
                    x_all.at[pl.ds(0, tokens), pl.ds(side * rows_w, rows_w)],
                )
            )
        for k in range(1, inner):
            pairs.append((blocks[k - 1], x_all.at[pl.ds(k * tokens, tokens)]))
        to = 0
        for ref, (_, start, wide) in zip(near_refs, near):
            pairs.append((ref.at[:, pl.ds(start, wide)], w_all.at[pl.ds(0, rows_w), pl.ds(to, wide)]))
            to += wide
        for slot, o in enumerate(order):
            block = far_refs[slot // slots].at[slot % slots]
            for row, col, rows, wide, to_row, to_col in layout:
                to = pl.multiple_of(rows_w + (dp ^ o) * share + to_row, 16)
                piece = block.at[pl.ds(row, rows), pl.ds(col, wide)]
                pairs.append((piece, w_all.at[pl.ds(to, rows), pl.ds(to_col, wide)]))
        run_copies([pltpu.make_async_copy(a, b, sems.at[i]) for i, (a, b) in enumerate(pairs)])

        base = 0
        for g, wide in enumerate(groups):

            @pl.loop(0, wide // step)
            def _(n, g=g, base=base):
                at = pl.multiple_of(n * step, 128)
                product = jnp.dot(
                    x_all[...], w_all[:, pl.ds(base + at, step)], preferred_element_type=F32
                )
                for k in range(inner):
                    outs[g * inner + k][:, pl.ds(at, step)] = product[k * tokens : (k + 1) * tokens]

            base += wide

    copies = 2 + (inner - 1) + len(near) + n_dp * len(layout)
    moved = inner * tokens * 2 * rows_w * 2 + 2 * rows_w * cols * 2 + inner * tokens * cols * 4
    out = pl.pallas_call(
        body,
        in_specs=[pl.BlockSpec(memory_space=pl.ANY)] * (1 + n_in),
        out_specs=[pl.BlockSpec(memory_space=pltpu.VMEM)] * (inner * len(groups)),
        out_shape=[jax.ShapeDtypeStruct((tokens, g), F32) for g in groups for _ in range(inner)],
        scratch_shapes=[
            pltpu.VMEM((inner * tokens, 2 * rows_w), BF16),
            pltpu.VMEM((2 * rows_w, cols), BF16),
            pltpu.SemaphoreType.DMA((copies,)),
        ],
        compiler_params=params(),
        cost_estimate=pl.CostEstimate(
            flops=2 * inner * tokens * 2 * rows_w * cols, bytes_accessed=moved, transcendentals=0
        ),
        name="multiply",
    )(hidden, *received, *[array for array, _, _ in near], *far)
    return [list(out[g * inner : (g + 1) * inner]) for g in range(len(groups))]


def attend(lengths, partials, d_attn, cache, group, g_order):
    tokens = d_attn.shape[0]
    n_blocks, block, head_dim = cache[0].shape
    n_convs = lengths.shape[1]
    scale = head_dim ** (-0.5)
    to_log2 = scale * math.log2(math.e)
    n_heads = d_attn.shape[1] // head_dim
    lanes = n_heads * tokens
    n_cache = n_blocks * block
    n_group = n_blocks * tokens
    slots = n_blocks // len(group)
    chunk = min(512, n_cache)
    n_part = sum(len(terms) for terms in partials)
    dims = (((1,), (1,)), ((), ()))
    spans = [(at, chunk) for at in range(0, n_cache, chunk)]
    spans += [(n_cache + i * slots * tokens, slots * tokens) for i in range(len(group))]
    n_first = n_cache // chunk

    def tiles(value):
        return value.reshape(value.shape[0] // 8, 8, lanes)

    def body(len_ref, d_ref, *rest):
        cache_refs, rest = rest[:2], rest[2:]
        group_refs, rest = rest[: len(group)], rest[len(group) :]
        part_refs, rest = list(rest[:n_part]), rest[n_part:]
        keep_ref, give_ref, out_ref, s_ref, p_ref, q_ref, dq_ref, ck_ref, cv_ref, sems = rest
        me, dp = lax.axis_index("fsdp"), lax.axis_index("dp")
        odd = dp % 2

        @pl.when(odd == 0)
        def _():
            pltpu.make_async_copy(cache_refs[0], ck_ref, sems.at[0]).start()
            pltpu.make_async_copy(cache_refs[1], cv_ref, sems.at[1]).start()

        @pl.when(odd == 1)
        def _():
            pltpu.make_async_copy(cache_refs[1], ck_ref, sems.at[0]).start()
            pltpu.make_async_copy(cache_refs[0], cv_ref, sems.at[1]).start()

        h = 0
        for terms in partials:
            refs, part_refs = part_refs[: len(terms)], part_refs[len(terms) :]
            for at in range(0, terms[0].shape[1], head_dim):
                rows = pl.ds(h * tokens, tokens)
                q = refs[0][:, at : at + head_dim]
                for ref in refs[1:]:
                    q = q + ref[:, at : at + head_dim]
                q_ref[rows] = q.astype(BF16)
                dq_ref[rows] = d_ref[:, h * head_dim : (h + 1) * head_dim]
                h += 1

        q_pos = me * tokens + lax.broadcasted_iota(jnp.int32, (1, lanes), 1) % tokens
        begin = jnp.zeros((1, lanes), jnp.int32)
        end = jnp.int32(0)
        for i in range(n_convs):
            end = end + len_ref[0, i]
            begin = jnp.where(end <= q_pos, end, begin)

        def group_rows(i, at):
            return group_refs[i][...].reshape(slots * tokens, 2 * head_dim)[:, at : at + head_dim]

        def cache_rows(ref, i):
            return ref[...].reshape(n_cache, head_dim)[i * chunk : (i + 1) * chunk]

        for i in range(len(group)):
            at, size = spans[n_first + i]
            s = lax.dot_general(group_rows(i, 0), q_ref[...], dims, preferred_element_type=F32)
            for j in range(slots):
                pos = (me ^ g_order[i * slots + j]) * tokens
                pos = pos + lax.broadcasted_iota(jnp.int32, (tokens, lanes), 0)
                allowed = (pos <= q_pos) & (pos >= begin)
                here = s[j * tokens : (j + 1) * tokens]
                s_ref[pl.ds(at + j * tokens, tokens)] = jnp.where(allowed, here, -jnp.inf)

        pltpu.make_async_copy(cache_refs[0], ck_ref, sems.at[0]).wait()
        pltpu.make_async_copy(cache_refs[1], cv_ref, sems.at[1]).wait()
        for i in range(n_first):
            at, size = spans[i]
            s_ref[pl.ds(at, size)] = lax.dot_general(
                cache_rows(ck_ref, i), q_ref[...], dims, preferred_element_type=F32
            )

        tops, totals = [], []
        for at, size in spans:
            top = jnp.max(tiles(s_ref[pl.ds(at, size)]), axis=0)
            top = jnp.maximum(top, -1e30)
            e = jnp.exp2((tiles(s_ref[pl.ds(at, size)]) - top) * to_log2)
            s_ref[pl.ds(at, size)] = e.reshape(size, lanes)
            tops.append(top)
            totals.append(jnp.sum(e, axis=0))
        top = functools.reduce(jnp.maximum, tops)
        top = jnp.max(top, axis=0, keepdims=True)
        factors = [jnp.exp2((own - top) * to_log2) for own in tops]
        total = functools.reduce(lambda a, b: a + b, [t * f for t, f in zip(totals, factors)])
        inv = 1.0 / jnp.sum(total, axis=0, keepdims=True)
        factors = [f * inv for f in factors]

        delta = jnp.zeros((8, lanes), F32)
        for i in range(len(group)):
            at, size = spans[n_first + i]
            d_prob = lax.dot_general(
                group_rows(i, head_dim), dq_ref[...], dims, preferred_element_type=F32
            )
            p = tiles(s_ref[pl.ds(at, size)]) * factors[n_first + i]
            delta = delta + jnp.sum(p.astype(BF16).astype(F32) * tiles(d_prob), axis=0)
        for i in range(n_first):
            at, size = spans[i]
            p_ref[pl.ds(at, size)] = lax.dot_general(
                cache_rows(cv_ref, i), dq_ref[...], dims, preferred_element_type=F32
            )
            p = (tiles(s_ref[pl.ds(at, size)]) * factors[i]).reshape(size, lanes).astype(BF16)
            delta = delta + jnp.sum(tiles(p.astype(F32)) * tiles(p_ref[pl.ds(at, size)]), axis=0)
            out_ref[1 - odd, pl.ds(at, size)] = jnp.dot(p, dq_ref[...], preferred_element_type=F32)
        delta = jnp.sum(delta, axis=0, keepdims=True)
        for i in range(n_first):
            at, size = spans[i]
            p = tiles(s_ref[pl.ds(at, size)]) * factors[i]
            ds = p * (tiles(p_ref[pl.ds(at, size)]) - delta)
            ds = ds.reshape(size, lanes).astype(BF16)
            g = jnp.dot(ds, q_ref[...], preferred_element_type=F32) * scale
            out_ref[odd, pl.ds(at, size)] = g

        for i, ref in enumerate((keep_ref, give_ref)):
            ref[...] = out_ref[i]

    flops = 2 * lanes * head_dim * (5 * n_cache + 2 * n_group)
    return pl.pallas_call(
        body,
        in_specs=[pl.BlockSpec(memory_space=pltpu.SMEM)]
        + [pl.BlockSpec(memory_space=pltpu.VMEM)]
        + [pl.BlockSpec(memory_space=pl.ANY)] * 2
        + [pl.BlockSpec(memory_space=pltpu.VMEM)] * (len(group) + n_part),
        out_specs=[pl.BlockSpec(memory_space=pltpu.VMEM)] * 2,
        out_shape=[jax.ShapeDtypeStruct((n_cache, head_dim), F32)] * 2,
        scratch_shapes=[
            pltpu.VMEM((2, n_cache, head_dim), F32),
            pltpu.VMEM((n_cache + n_group, lanes), F32),
            pltpu.VMEM((n_cache, lanes), F32),
            pltpu.VMEM((lanes, head_dim), BF16),
            pltpu.VMEM((lanes, head_dim), BF16),
            pltpu.VMEM((n_blocks, block, head_dim), BF16),
            pltpu.VMEM((n_blocks, block, head_dim), BF16),
            pltpu.SemaphoreType.DMA((2,)),
        ],
        compiler_params=params(),
        cost_estimate=pl.CostEstimate(
            flops=flops,
            bytes_accessed=12 * n_cache * head_dim,
            transcendentals=lanes * (n_cache + n_group),
        ),
        name="attend",
    )(lengths, d_attn, *cache, *group, *[term for terms in partials for term in terms])


def make_on_device(n_dp, n_fsdp):
    inner = n_fsdp // 2

    def on_device(hidden, d_attn, w_query, w_key, w_value, cache_keys, cache_values, lengths):
        dp = lax.axis_index("dp")
        head_dim = w_key.shape[1]
        q_width = w_query.shape[1]
        even = dp % 2 == 0
        f_bits, d_bits = bits_down(n_fsdp), bits_down(n_dp)

        def from_owners(products):
            return [products[0]] + [swap(x, "fsdp", n_fsdp, k + 1) for k, x in enumerate(products[1:])]

        cuts = [(0, q_width // 2), (q_width // 2, q_width // 2)]
        cuts = [(0, q_width // 2), (q_width // 2, q_width // 2)]
        sent, part = prepare(hidden, w_query, w_key, w_value, n_dp, n_fsdp)
        received = [swap(block, "fsdp", n_fsdp, k + 1) for k, block in enumerate(sent)]
        part = swap(part, "fsdp", n_fsdp, inner)
        share = w_query.shape[0] // n_dp
        cut = share + share // 2
        part_a, part_b = part[:cut], part[cut:]
        far_a, order = double(part_a[None], [0], "dp", n_dp, d_bits[0])
        cache = jnp.where(even, cache_keys, cache_values)[None]
        cache, f_order = double(cache, [0], "fsdp", n_fsdp, f_bits[0])
        cache, far_a, *received = together(cache, far_a, *received)
        far_b, _ = double(part_b[None], [0], "dp", n_dp, d_bits[0])
        far_a, d_order = finish(far_a, order, "dp", n_dp, d_bits[1:])
        cache, f_order = double(cache, f_order, "fsdp", n_fsdp, f_bits[1])
        cache, far_a[1] = together(cache, far_a[1])
        kv, (at_a, wide_a), (at_b, wide_b) = 2 * head_dim, *cuts
        near_a = [(w_key, 0, head_dim), (w_value, 0, head_dim), (w_query, at_a, wide_a)]
        layout_a = [(0, 0, share, wide_a, 0, kv)]
        layout_a += [(share, i * kv, share // 2, kv, i * (share // 2), 0) for i in range(2)]
        out_kv, out_a = multiply(
            hidden, received, near_a, far_a, layout_a, d_order, n_fsdp, (kv, wide_a)
        )
        for bit in f_bits[2:]:
            cache, f_order = double(cache, f_order, "fsdp", n_fsdp, bit)
        far_b, cache, out_kv[0] = together(far_b, cache, out_kv[0])
        far_b, _ = finish(far_b, order, "dp", n_dp, d_bits[1:])
        parts_kv = from_owners(out_kv)
        parts_a = from_owners(out_a)
        own = functools.reduce(lambda a, b: a + b, parts_kv).astype(BF16)
        far_b[1], own = together(far_b[1], own)
        group, _ = double(own[None], [0], "fsdp", n_fsdp, inner)
        near_b, layout_b = [(w_query, at_b, wide_b)], [(0, 0, share, wide_b, 0, 0)]
        (out_b,) = multiply(
            hidden, received, near_b, far_b, layout_b, d_order, n_fsdp, (wide_b,)
        )
        group, cache, *tied = together(group, cache, *out_b, *parts_a[1:])
        out_b, parts_a[1:] = tied[:inner], tied[inner:]
        parts_b = from_owners(out_b)
        cache = [cache, swap(cache, "dp", n_dp, 1)]
        group, parts_b[1], cache[1] = together(group, parts_b[1], cache[1])
        group = [group] + [swap(group, "fsdp", n_fsdp, k) for k in range(1, inner)]
        g_order = [o for k in range(inner) for o in (k, k ^ inner)]
        keep, give = attend(lengths, [parts_a, parts_b], d_attn, cache, group, g_order)

        half = keep + swap(give, "dp", n_dp, 1)
        size = half.shape[0] // n_fsdp
        mine = half[:size]
        for slot in range(1, n_fsdp):
            out = half[slot * size : (slot + 1) * size].astype(BF16)
            mine = mine + swap(out, "fsdp", n_fsdp, f_order[slot]).astype(F32)
        for bit in d_bits[:-1]:
            mine = mine + swap(mine, "dp", n_dp, bit)
        other = swap(mine, "dp", n_dp, 1)
        return jnp.where(even, mine, other), jnp.where(even, other, mine)

    return on_device


def solution(mesh):
    placed = (
        P(("dp", "fsdp"), None),
        P(("dp", "fsdp"), None),
        P("fsdp", None),
        P("fsdp", None),
        P("fsdp", None),
        P("fsdp", None),
        P("fsdp", None),
        P("dp", None),
    )
    return jax.shard_map(
        make_on_device(mesh.shape["dp"], mesh.shape["fsdp"]),
        mesh=mesh,
        in_specs=placed,
        out_specs=(P("fsdp", None), P("fsdp", None)),
        check_vma=False,
    )
```

```python
import functools
import math

import jax
import jax.numpy as jnp
from jax import lax
from jax.experimental import pallas as pl
from jax.experimental.pallas import tpu as pltpu
from jax.sharding import PartitionSpec as P

F32 = jnp.float32
BF16 = jnp.bfloat16
VMEM_LIMIT = 56 * 1024 * 1024


def swap(value, axis, size, bit):
    return lax.ppermute(value, axis, [(i, i ^ bit) for i in range(size)])


def bits_down(size):
    bits = []
    bit = size // 2
    while bit:
        bits.append(bit)
        bit //= 2
    return bits


def double(block, order, axis, size, bit):
    return jnp.concatenate([block, swap(block, axis, size, bit)]), order + [o ^ bit for o in order]


def finish(block, order, axis, size, bits):
    for bit in bits[:-1]:
        block, order = double(block, order, axis, size, bit)
    return [block, swap(block, axis, size, bits[-1])], order + [o ^ bits[-1] for o in order]


def together(*values):
    return lax.optimization_barrier(values)


def params():
    return pltpu.CompilerParams(vmem_limit_bytes=VMEM_LIMIT)


def run_copies(copies):
    for copy in copies:
        copy.start()
    for copy in copies:
        copy.wait()


def prepare(hidden, w_query, w_key, w_value, n_dp, n_fsdp):
    inner = n_fsdp // 2
    tokens = hidden.shape[0]
    rows_w, q_width = w_query.shape
    head_dim = w_key.shape[1]
    share = rows_w // n_dp
    cols = q_width // 2

    def body(hidden_ref, wq_ref, wk_ref, wv_ref, *rest):
        sent, part, sems = rest[: inner - 1], rest[-2], rest[-1]
        me, dp = lax.axis_index("fsdp"), lax.axis_index("dp")
        first = pl.multiple_of(dp * share, 16)
        rows = pl.ds(first, share)
        pairs = []
        for i in range(2):
            to = part.at[pl.ds(i * (share + share // 2), share)]
            pairs.append((wq_ref.at[rows, pl.ds(i * cols, cols)], to))
            for j, ref in enumerate((wk_ref, wv_ref)):
                to = part.at[pl.ds(share, share // 2), pl.ds((2 * i + j) * head_dim, head_dim)]
                pairs.append((ref.at[pl.ds(first + i * (share // 2), share // 2)], to))
        for k in range(1, inner):
            for side, bit in enumerate((0, inner)):
                start = pl.multiple_of((me ^ k ^ bit) * rows_w, 128)
                pairs.append(
                    (hidden_ref.at[:, pl.ds(start, rows_w)], sent[k - 1].at[:, pl.ds(side * rows_w, rows_w)])
                )
        run_copies([pltpu.make_async_copy(a, b, sems.at[i]) for i, (a, b) in enumerate(pairs)])

    moved = 2 * (tokens * 2 * rows_w * 2 * (inner - 1) + share * (q_width + 2 * head_dim) * 2)
    out = pl.pallas_call(
        body,
        in_specs=[pl.BlockSpec(memory_space=pl.ANY)] * 4,
        out_specs=[pl.BlockSpec(memory_space=pltpu.VMEM)] * inner,
        out_shape=[jax.ShapeDtypeStruct((tokens, 2 * rows_w), BF16)] * (inner - 1)
        + [jax.ShapeDtypeStruct((2 * share + share // 2, cols), BF16)],
        scratch_shapes=[pltpu.SemaphoreType.DMA((6 + 2 * (inner - 1),))],
        compiler_params=params(),
        cost_estimate=pl.CostEstimate(flops=0, bytes_accessed=moved, transcendentals=0),
        name="prepare",
    )(hidden, w_query, w_key, w_value)
    return out[:-1], out[-1]


def multiply(hidden, received, near, far, layout, order, n_fsdp, groups):
    inner = n_fsdp // 2
    tokens = hidden.shape[0]
    cols = sum(wide for _, _, wide in near)
    slots = far[0].shape[0]
    n_dp = slots * len(far)
    rows_w = near[0][0].shape[0]
    share = rows_w // n_dp
    step = 256 if all(g % 256 == 0 for g in groups) else 128
    n_in = inner - 1 + len(near) + len(far)

    def body(hidden_ref, *rest):
        blocks, rest = rest[: inner - 1], rest[inner - 1 :]
        near_refs, rest = rest[: len(near)], rest[len(near) :]
        far_refs, rest = rest[: len(far)], rest[len(far) :]
        outs = rest[:-3]
        x_all, w_all, sems = rest[-3:]
        me, dp = lax.axis_index("fsdp"), lax.axis_index("dp")
        pairs = []
        for side, bit in enumerate((0, inner)):
            start = pl.multiple_of((me ^ bit) * rows_w, 128)
            pairs.append(
                (
                    hidden_ref.at[:, pl.ds(start, rows_w)],
                    x_all.at[pl.ds(0, tokens), pl.ds(side * rows_w, rows_w)],
                )
            )
        for k in range(1, inner):
            pairs.append((blocks[k - 1], x_all.at[pl.ds(k * tokens, tokens)]))
        to = 0
        for ref, (_, start, wide) in zip(near_refs, near):
            pairs.append((ref.at[:, pl.ds(start, wide)], w_all.at[pl.ds(0, rows_w), pl.ds(to, wide)]))
            to += wide
        for slot, o in enumerate(order):
            block = far_refs[slot // slots].at[slot % slots]
            for row, col, rows, wide, to_row, to_col in layout:
                to = pl.multiple_of(rows_w + (dp ^ o) * share + to_row, 16)
                piece = block.at[pl.ds(row, rows), pl.ds(col, wide)]
                pairs.append((piece, w_all.at[pl.ds(to, rows), pl.ds(to_col, wide)]))
        run_copies([pltpu.make_async_copy(a, b, sems.at[i]) for i, (a, b) in enumerate(pairs)])

        base = 0
        for g, wide in enumerate(groups):

            @pl.loop(0, wide // step)
            def _(n, g=g, base=base):
                at = pl.multiple_of(n * step, 128)
                product = jnp.dot(
                    x_all[...], w_all[:, pl.ds(base + at, step)], preferred_element_type=F32
                )
                for k in range(inner):
                    outs[g * inner + k][:, pl.ds(at, step)] = product[k * tokens : (k + 1) * tokens]

            base += wide

    copies = 2 + (inner - 1) + len(near) + n_dp * len(layout)
    moved = inner * tokens * 2 * rows_w * 2 + 2 * rows_w * cols * 2 + inner * tokens * cols * 4
    out = pl.pallas_call(
        body,
        in_specs=[pl.BlockSpec(memory_space=pl.ANY)] * (1 + n_in),
        out_specs=[pl.BlockSpec(memory_space=pltpu.VMEM)] * (inner * len(groups)),
        out_shape=[jax.ShapeDtypeStruct((tokens, g), F32) for g in groups for _ in range(inner)],
        scratch_shapes=[
            pltpu.VMEM((inner * tokens, 2 * rows_w), BF16),
            pltpu.VMEM((2 * rows_w, cols), BF16),
            pltpu.SemaphoreType.DMA((copies,)),
        ],
        compiler_params=params(),
        cost_estimate=pl.CostEstimate(
            flops=2 * inner * tokens * 2 * rows_w * cols, bytes_accessed=moved, transcendentals=0
        ),
        name="multiply",
    )(hidden, *received, *[array for array, _, _ in near], *far)
    return [list(out[g * inner : (g + 1) * inner]) for g in range(len(groups))]


def attend(lengths, terms, d_attn, first_head, cache, group, g_order, sums):
    tokens = d_attn.shape[0]
    n_blocks, block, head_dim = cache[0].shape
    n_convs = lengths.shape[1]
    scale = head_dim ** (-0.5)
    to_log2 = scale * math.log2(math.e)
    n_heads = terms[0].shape[1] // head_dim
    lanes = n_heads * tokens
    n_cache = n_blocks * block
    n_group = n_blocks * tokens
    slots = n_blocks // len(group)
    chunk = min(512, n_cache)
    n_part, n_sum = len(terms), len(sums)
    dims = (((1,), (1,)), ((), ()))
    spans = [(at, chunk) for at in range(0, n_cache, chunk)]
    spans += [(n_cache + i * slots * tokens, slots * tokens) for i in range(len(group))]
    n_first = n_cache // chunk

    def tiles(value):
        return value.reshape(value.shape[0] // 8, 8, lanes)

    def body(len_ref, d_ref, *rest):
        cache_refs, rest = rest[:2], rest[2:]
        group_refs, rest = rest[: len(group)], rest[len(group) :]
        part_refs, rest = rest[:n_part], rest[n_part:]
        sum_refs, rest = rest[:n_sum], rest[n_sum:]
        keep_ref, give_ref, out_ref, s_ref, p_ref, q_ref, dq_ref, ck_ref, cv_ref, sems = rest
        me, dp = lax.axis_index("fsdp"), lax.axis_index("dp")
        odd = dp % 2

        @pl.when(odd == 0)
        def _():
            pltpu.make_async_copy(cache_refs[0], ck_ref, sems.at[0]).start()
            pltpu.make_async_copy(cache_refs[1], cv_ref, sems.at[1]).start()

        @pl.when(odd == 1)
        def _():
            pltpu.make_async_copy(cache_refs[1], ck_ref, sems.at[0]).start()
            pltpu.make_async_copy(cache_refs[0], cv_ref, sems.at[1]).start()

        for h in range(n_heads):
            at = slice(h * head_dim, (h + 1) * head_dim)
            rows = pl.ds(h * tokens, tokens)
            q = part_refs[0][:, at]
            for ref in part_refs[1:]:
                q = q + ref[:, at]
            q_ref[rows] = q.astype(BF16)
            at = (first_head + h) * head_dim
            dq_ref[rows] = d_ref[:, at : at + head_dim]

        q_pos = me * tokens + lax.broadcasted_iota(jnp.int32, (1, lanes), 1) % tokens
        begin = jnp.zeros((1, lanes), jnp.int32)
        end = jnp.int32(0)
        for i in range(n_convs):
            end = end + len_ref[0, i]
            begin = jnp.where(end <= q_pos, end, begin)

        def group_rows(i, at):
            return group_refs[i][...].reshape(slots * tokens, 2 * head_dim)[:, at : at + head_dim]

        def cache_rows(ref, i):
            return ref[...].reshape(n_cache, head_dim)[i * chunk : (i + 1) * chunk]

        for i in range(len(group)):
            at, size = spans[n_first + i]
            s = lax.dot_general(group_rows(i, 0), q_ref[...], dims, preferred_element_type=F32)
            for j in range(slots):
                pos = (me ^ g_order[i * slots + j]) * tokens
                pos = pos + lax.broadcasted_iota(jnp.int32, (tokens, lanes), 0)
                allowed = (pos <= q_pos) & (pos >= begin)
                here = s[j * tokens : (j + 1) * tokens]
                s_ref[pl.ds(at + j * tokens, tokens)] = jnp.where(allowed, here, -jnp.inf)

        pltpu.make_async_copy(cache_refs[0], ck_ref, sems.at[0]).wait()
        pltpu.make_async_copy(cache_refs[1], cv_ref, sems.at[1]).wait()
        for i in range(n_first):
            at, size = spans[i]
            s_ref[pl.ds(at, size)] = lax.dot_general(
                cache_rows(ck_ref, i), q_ref[...], dims, preferred_element_type=F32
            )

        tops, totals = [], []
        for at, size in spans:
            top = jnp.max(tiles(s_ref[pl.ds(at, size)]), axis=0)
            top = jnp.maximum(top, -1e30)
            e = jnp.exp2((tiles(s_ref[pl.ds(at, size)]) - top) * to_log2)
            s_ref[pl.ds(at, size)] = e.reshape(size, lanes)
            tops.append(top)
            totals.append(jnp.sum(e, axis=0))
        top = functools.reduce(jnp.maximum, tops)
        top = jnp.max(top, axis=0, keepdims=True)
        factors = [jnp.exp2((own - top) * to_log2) for own in tops]
        total = functools.reduce(lambda a, b: a + b, [t * f for t, f in zip(totals, factors)])
        inv = 1.0 / jnp.sum(total, axis=0, keepdims=True)
        factors = [f * inv for f in factors]

        delta = jnp.zeros((8, lanes), F32)
        for i in range(len(group)):
            at, size = spans[n_first + i]
            d_prob = lax.dot_general(
                group_rows(i, head_dim), dq_ref[...], dims, preferred_element_type=F32
            )
            p = tiles(s_ref[pl.ds(at, size)]) * factors[n_first + i]
            delta = delta + jnp.sum(p.astype(BF16).astype(F32) * tiles(d_prob), axis=0)
        for i in range(n_first):
            at, size = spans[i]
            p_ref[pl.ds(at, size)] = lax.dot_general(
                cache_rows(cv_ref, i), dq_ref[...], dims, preferred_element_type=F32
            )
            p = (tiles(s_ref[pl.ds(at, size)]) * factors[i]).reshape(size, lanes).astype(BF16)
            delta = delta + jnp.sum(tiles(p.astype(F32)) * tiles(p_ref[pl.ds(at, size)]), axis=0)
            out_ref[1 - odd, pl.ds(at, size)] = jnp.dot(p, dq_ref[...], preferred_element_type=F32)
        delta = jnp.sum(delta, axis=0, keepdims=True)
        for i in range(n_first):
            at, size = spans[i]
            p = tiles(s_ref[pl.ds(at, size)]) * factors[i]
            ds = p * (tiles(p_ref[pl.ds(at, size)]) - delta)
            ds = ds.reshape(size, lanes).astype(BF16)
            g = jnp.dot(ds, q_ref[...], preferred_element_type=F32) * scale
            out_ref[odd, pl.ds(at, size)] = g

        for i, ref in enumerate((keep_ref, give_ref)):
            ref[...] = sum_refs[i][...] + out_ref[i] if n_sum else out_ref[i]

    flops = 2 * lanes * head_dim * (5 * n_cache + 2 * n_group)
    return pl.pallas_call(
        body,
        in_specs=[pl.BlockSpec(memory_space=pltpu.SMEM)]
        + [pl.BlockSpec(memory_space=pltpu.VMEM)]
        + [pl.BlockSpec(memory_space=pl.ANY)] * 2
        + [pl.BlockSpec(memory_space=pltpu.VMEM)] * (len(group) + n_part + n_sum),
        out_specs=[pl.BlockSpec(memory_space=pltpu.VMEM)] * 2,
        out_shape=[jax.ShapeDtypeStruct((n_cache, head_dim), F32)] * 2,
        scratch_shapes=[
            pltpu.VMEM((2, n_cache, head_dim), F32),
            pltpu.VMEM((n_cache + n_group, lanes), F32),
            pltpu.VMEM((n_cache, lanes), F32),
            pltpu.VMEM((lanes, head_dim), BF16),
            pltpu.VMEM((lanes, head_dim), BF16),
            pltpu.VMEM((n_blocks, block, head_dim), BF16),
            pltpu.VMEM((n_blocks, block, head_dim), BF16),
            pltpu.SemaphoreType.DMA((2,)),
        ],
        compiler_params=params(),
        cost_estimate=pl.CostEstimate(
            flops=flops,
            bytes_accessed=12 * n_cache * head_dim,
            transcendentals=lanes * (n_cache + n_group),
        ),
        name="attend",
    )(lengths, d_attn, *cache, *group, *terms, *sums)


def make_on_device(n_dp, n_fsdp):
    inner = n_fsdp // 2

    def on_device(hidden, d_attn, w_query, w_key, w_value, cache_keys, cache_values, lengths):
        dp = lax.axis_index("dp")
        head_dim = w_key.shape[1]
        q_width = w_query.shape[1]
        even = dp % 2 == 0
        d_bits = bits_down(n_dp)

        def from_owners(products):
            return [products[0]] + [swap(x, "fsdp", n_fsdp, k + 1) for k, x in enumerate(products[1:])]

        cuts = [(0, q_width // 2), (q_width // 2, q_width // 2)]
        sent, part = prepare(hidden, w_query, w_key, w_value, n_dp, n_fsdp)
        received = [swap(block, "fsdp", n_fsdp, k + 1) for k, block in enumerate(sent)]
        part = swap(part, "fsdp", n_fsdp, inner)
        share = w_query.shape[0] // n_dp
        cut = share + share // 2
        part_a, part_b = part[:cut], part[cut:]
        far_a, order = double(part_a[None], [0], "dp", n_dp, d_bits[0])
        cache = jnp.where(even, cache_keys, cache_values)[None]
        cache, _ = double(cache, [0], "fsdp", n_fsdp, inner)
        cache, far_a, *received = together(cache, far_a, *received)
        far_b, _ = double(part_b[None], [0], "dp", n_dp, d_bits[0])
        far_a, d_order = finish(far_a, order, "dp", n_dp, d_bits[1:])
        cache = [cache] + [swap(cache, "fsdp", n_fsdp, k) for k in range(1, inner)]
        far_a[1], far_b, *cache = together(far_a[1], far_b, *cache)
        cache = jnp.concatenate(cache)
        f_order = [o for k in range(inner) for o in (k, k ^ inner)]
        cache = [cache, swap(cache, "dp", n_dp, 1)]
        kv, (at_a, wide_a), (at_b, wide_b) = 2 * head_dim, *cuts
        near_a = [(w_key, 0, head_dim), (w_value, 0, head_dim), (w_query, at_a, wide_a)]
        layout_a = [(0, 0, share, wide_a, 0, kv)]
        layout_a += [(share, i * kv, share // 2, kv, i * (share // 2), 0) for i in range(2)]
        out_kv, out_a = multiply(
            hidden, received, near_a, far_a, layout_a, d_order, n_fsdp, (kv, wide_a)
        )
        far_b, cache[1], out_kv[0] = together(far_b, cache[1], out_kv[0])
        far_b, _ = finish(far_b, order, "dp", n_dp, d_bits[1:])
        parts_kv = from_owners(out_kv)
        parts_a = from_owners(out_a)
        own = functools.reduce(lambda a, b: a + b, parts_kv).astype(BF16)
        far_b[1], own = together(far_b[1], own)
        group, _ = double(own[None], [0], "fsdp", n_fsdp, inner)
        near_b, layout_b = [(w_query, at_b, wide_b)], [(0, 0, share, wide_b, 0, 0)]
        (out_b,) = multiply(
            hidden, received, near_b, far_b, layout_b, d_order, n_fsdp, (wide_b,)
        )
        group, *tied = together(group, *out_b, *parts_a[1:])
        out_b, parts_a[1:] = tied[:inner], tied[inner:]
        group = [group] + [swap(group, "fsdp", n_fsdp, k) for k in range(1, inner)]
        parts_b = from_owners(out_b)
        first = cuts[0][1] // head_dim
        sums = attend(lengths, parts_a, d_attn, 0, cache, group, f_order, ())
        keep, give = attend(lengths, parts_b, d_attn, first, cache, group, f_order, sums)

        half = keep + swap(give, "dp", n_dp, 1)
        size = half.shape[0] // n_fsdp
        mine = half[:size]
        for slot in range(1, n_fsdp):
            out = half[slot * size : (slot + 1) * size].astype(BF16)
            mine = mine + swap(out, "fsdp", n_fsdp, f_order[slot]).astype(F32)
        for bit in d_bits[:-1]:
            mine = mine + swap(mine, "dp", n_dp, bit)
        other = swap(mine, "dp", n_dp, 1)
        return jnp.where(even, mine, other), jnp.where(even, other, mine)

    return on_device


def solution(mesh):
    placed = (
        P(("dp", "fsdp"), None),
        P(("dp", "fsdp"), None),
        P("fsdp", None),
        P("fsdp", None),
        P("fsdp", None),
        P("fsdp", None),
        P("fsdp", None),
        P("dp", None),
    )
    return jax.shard_map(
        make_on_device(mesh.shape["dp"], mesh.shape["fsdp"]),
        mesh=mesh,
        in_specs=placed,
        out_specs=(P("fsdp", None), P("fsdp", None)),
        check_vma=False,
    )
```

```python
import functools
import math

import jax
import jax.numpy as jnp
from jax import lax
from jax.experimental import pallas as pl
from jax.experimental.pallas import tpu as pltpu
from jax.sharding import PartitionSpec as P

F32 = jnp.float32
BF16 = jnp.bfloat16
VMEM_LIMIT = 56 * 1024 * 1024


def swap(value, axis, size, bit):
    return lax.ppermute(value, axis, [(i, i ^ bit) for i in range(size)])


def bits_down(size):
    bits = []
    bit = size // 2
    while bit:
        bits.append(bit)
        bit //= 2
    return bits


def double(block, order, axis, size, bit):
    return jnp.concatenate([block, swap(block, axis, size, bit)]), order + [o ^ bit for o in order]


def finish(block, order, axis, size, bits):
    for bit in bits[:-1]:
        block, order = double(block, order, axis, size, bit)
    return [block, swap(block, axis, size, bits[-1])], order + [o ^ bits[-1] for o in order]


def together(*values):
    return lax.optimization_barrier(values)


def params():
    return pltpu.CompilerParams(vmem_limit_bytes=VMEM_LIMIT)


def run_copies(copies):
    for copy in copies:
        copy.start()
    for copy in copies:
        copy.wait()


def prepare(hidden, w_query, w_key, w_value, n_dp, n_fsdp):
    inner = n_fsdp // 2
    tokens = hidden.shape[0]
    rows_w, q_width = w_query.shape
    head_dim = w_key.shape[1]
    share = rows_w // n_dp
    cols = q_width // 2

    def body(hidden_ref, wq_ref, wk_ref, wv_ref, *rest):
        sent, part, sems = rest[: inner - 1], rest[-2], rest[-1]
        me, dp = lax.axis_index("fsdp"), lax.axis_index("dp")
        first = pl.multiple_of(dp * share, 16)
        rows = pl.ds(first, share)
        pairs = []
        for i in range(2):
            to = part.at[pl.ds(i * (share + share // 2), share)]
            pairs.append((wq_ref.at[rows, pl.ds(i * cols, cols)], to))
            for j, ref in enumerate((wk_ref, wv_ref)):
                to = part.at[pl.ds(share, share // 2), pl.ds((2 * i + j) * head_dim, head_dim)]
                pairs.append((ref.at[pl.ds(first + i * (share // 2), share // 2)], to))
        for k in range(1, inner):
            for side, bit in enumerate((0, inner)):
                start = pl.multiple_of((me ^ k ^ bit) * rows_w, 128)
                pairs.append(
                    (hidden_ref.at[:, pl.ds(start, rows_w)], sent[k - 1].at[:, pl.ds(side * rows_w, rows_w)])
                )
        run_copies([pltpu.make_async_copy(a, b, sems.at[i]) for i, (a, b) in enumerate(pairs)])

    moved = 2 * (tokens * 2 * rows_w * 2 * (inner - 1) + share * (q_width + 2 * head_dim) * 2)
    out = pl.pallas_call(
        body,
        in_specs=[pl.BlockSpec(memory_space=pl.ANY)] * 4,
        out_specs=[pl.BlockSpec(memory_space=pltpu.VMEM)] * inner,
        out_shape=[jax.ShapeDtypeStruct((tokens, 2 * rows_w), BF16)] * (inner - 1)
        + [jax.ShapeDtypeStruct((2 * share + share // 2, cols), BF16)],
        scratch_shapes=[pltpu.SemaphoreType.DMA((6 + 2 * (inner - 1),))],
        compiler_params=params(),
        cost_estimate=pl.CostEstimate(flops=0, bytes_accessed=moved, transcendentals=0),
        name="prepare",
    )(hidden, w_query, w_key, w_value)
    return out[:-1], out[-1]


def multiply(hidden, received, near, far, layout, order, n_fsdp, groups):
    inner = n_fsdp // 2
    tokens = hidden.shape[0]
    cols = sum(wide for _, _, wide in near)
    slots = far[0].shape[0]
    n_dp = slots * len(far)
    rows_w = near[0][0].shape[0]
    share = rows_w // n_dp
    step = 256 if all(g % 256 == 0 for g in groups) else 128
    n_in = inner - 1 + len(near) + len(far)

    def body(hidden_ref, *rest):
        blocks, rest = rest[: inner - 1], rest[inner - 1 :]
        near_refs, rest = rest[: len(near)], rest[len(near) :]
        far_refs, rest = rest[: len(far)], rest[len(far) :]
        outs = rest[:-3]
        x_all, w_all, sems = rest[-3:]
        me, dp = lax.axis_index("fsdp"), lax.axis_index("dp")
        pairs = []
        for side, bit in enumerate((0, inner)):
            start = pl.multiple_of((me ^ bit) * rows_w, 128)
            pairs.append(
                (
                    hidden_ref.at[:, pl.ds(start, rows_w)],
                    x_all.at[pl.ds(0, tokens), pl.ds(side * rows_w, rows_w)],
                )
            )
        for k in range(1, inner):
            pairs.append((blocks[k - 1], x_all.at[pl.ds(k * tokens, tokens)]))
        to = 0
        for ref, (_, start, wide) in zip(near_refs, near):
            pairs.append((ref.at[:, pl.ds(start, wide)], w_all.at[pl.ds(0, rows_w), pl.ds(to, wide)]))
            to += wide
        for slot, o in enumerate(order):
            block = far_refs[slot // slots].at[slot % slots]
            for row, col, rows, wide, to_row, to_col in layout:
                to = pl.multiple_of(rows_w + (dp ^ o) * share + to_row, 16)
                piece = block.at[pl.ds(row, rows), pl.ds(col, wide)]
                pairs.append((piece, w_all.at[pl.ds(to, rows), pl.ds(to_col, wide)]))
        run_copies([pltpu.make_async_copy(a, b, sems.at[i]) for i, (a, b) in enumerate(pairs)])

        base = 0
        for g, wide in enumerate(groups):

            @pl.loop(0, wide // step)
            def _(n, g=g, base=base):
                at = pl.multiple_of(n * step, 128)
                product = jnp.dot(
                    x_all[...], w_all[:, pl.ds(base + at, step)], preferred_element_type=F32
                )
                for k in range(inner):
                    outs[g * inner + k][:, pl.ds(at, step)] = product[k * tokens : (k + 1) * tokens]

            base += wide

    copies = 2 + (inner - 1) + len(near) + n_dp * len(layout)
    moved = inner * tokens * 2 * rows_w * 2 + 2 * rows_w * cols * 2 + inner * tokens * cols * 4
    out = pl.pallas_call(
        body,
        in_specs=[pl.BlockSpec(memory_space=pl.ANY)] * (1 + n_in),
        out_specs=[pl.BlockSpec(memory_space=pltpu.VMEM)] * (inner * len(groups)),
        out_shape=[jax.ShapeDtypeStruct((tokens, g), F32) for g in groups for _ in range(inner)],
        scratch_shapes=[
            pltpu.VMEM((inner * tokens, 2 * rows_w), BF16),
            pltpu.VMEM((2 * rows_w, cols), BF16),
            pltpu.SemaphoreType.DMA((copies,)),
        ],
        compiler_params=params(),
        cost_estimate=pl.CostEstimate(
            flops=2 * inner * tokens * 2 * rows_w * cols, bytes_accessed=moved, transcendentals=0
        ),
        name="multiply",
    )(hidden, *received, *[array for array, _, _ in near], *far)
    return [list(out[g * inner : (g + 1) * inner]) for g in range(len(groups))]


def attend(lengths, terms, d_attn, first_head, cache, group, g_order, sums):
    tokens = d_attn.shape[0]
    n_blocks, block, head_dim = cache[0].shape
    n_convs = lengths.shape[1]
    scale = head_dim ** (-0.5)
    to_log2 = scale * math.log2(math.e)
    n_heads = terms[0].shape[1] // head_dim
    lanes = n_heads * tokens
    n_cache = n_blocks * block
    n_group = n_blocks * tokens
    slots = n_blocks // len(group)
    chunk = min(512, n_cache)
    n_part, n_sum = len(terms), len(sums)
    dims = (((1,), (1,)), ((), ()))
    spans = [(at, chunk) for at in range(0, n_cache, chunk)]
    spans += [(n_cache + i * slots * tokens, slots * tokens) for i in range(len(group))]
    n_first = n_cache // chunk

    def tiles(value):
        return value.reshape(value.shape[0] // 8, 8, lanes)

    def body(len_ref, d_ref, *rest):
        cache_refs, rest = rest[:2], rest[2:]
        group_refs, rest = rest[: len(group)], rest[len(group) :]
        part_refs, rest = rest[:n_part], rest[n_part:]
        sum_refs, rest = rest[:n_sum], rest[n_sum:]
        keep_ref, give_ref, out_ref, s_ref, p_ref, q_ref, dq_ref, ck_ref, cv_ref, sems = rest
        me, dp = lax.axis_index("fsdp"), lax.axis_index("dp")
        odd = dp % 2

        @pl.when(odd == 0)
        def _():
            pltpu.make_async_copy(cache_refs[0], ck_ref, sems.at[0]).start()
            pltpu.make_async_copy(cache_refs[1], cv_ref, sems.at[1]).start()

        @pl.when(odd == 1)
        def _():
            pltpu.make_async_copy(cache_refs[1], ck_ref, sems.at[0]).start()
            pltpu.make_async_copy(cache_refs[0], cv_ref, sems.at[1]).start()

        for h in range(n_heads):
            at = slice(h * head_dim, (h + 1) * head_dim)
            rows = pl.ds(h * tokens, tokens)
            q = part_refs[0][:, at]
            for ref in part_refs[1:]:
                q = q + ref[:, at]
            q_ref[rows] = q.astype(BF16)
            at = (first_head + h) * head_dim
            dq_ref[rows] = d_ref[:, at : at + head_dim]

        q_pos = me * tokens + lax.broadcasted_iota(jnp.int32, (1, lanes), 1) % tokens
        begin = jnp.zeros((1, lanes), jnp.int32)
        end = jnp.int32(0)
        for i in range(n_convs):
            end = end + len_ref[0, i]
            begin = jnp.where(end <= q_pos, end, begin)

        def group_rows(i, at):
            return group_refs[i][...].reshape(slots * tokens, 2 * head_dim)[:, at : at + head_dim]

        def cache_rows(ref, i):
            return ref[...].reshape(n_cache, head_dim)[i * chunk : (i + 1) * chunk]

        for i in range(len(group)):
            at, size = spans[n_first + i]
            s = lax.dot_general(group_rows(i, 0), q_ref[...], dims, preferred_element_type=F32)
            for j in range(slots):
                pos = (me ^ g_order[i * slots + j]) * tokens
                pos = pos + lax.broadcasted_iota(jnp.int32, (tokens, lanes), 0)
                allowed = (pos <= q_pos) & (pos >= begin)
                here = s[j * tokens : (j + 1) * tokens]
                s_ref[pl.ds(at + j * tokens, tokens)] = jnp.where(allowed, here, -jnp.inf)

        pltpu.make_async_copy(cache_refs[0], ck_ref, sems.at[0]).wait()
        pltpu.make_async_copy(cache_refs[1], cv_ref, sems.at[1]).wait()
        for i in range(n_first):
            at, size = spans[i]
            s_ref[pl.ds(at, size)] = lax.dot_general(
                cache_rows(ck_ref, i), q_ref[...], dims, preferred_element_type=F32
            )

        tops, totals = [], []
        for at, size in spans:
            top = jnp.max(tiles(s_ref[pl.ds(at, size)]), axis=0)
            top = jnp.maximum(top, -1e30)
            e = jnp.exp2((tiles(s_ref[pl.ds(at, size)]) - top) * to_log2)
            s_ref[pl.ds(at, size)] = e.reshape(size, lanes)
            tops.append(top)
            totals.append(jnp.sum(e, axis=0))
        top = functools.reduce(jnp.maximum, tops)
        top = jnp.max(top, axis=0, keepdims=True)
        factors = [jnp.exp2((own - top) * to_log2) for own in tops]
        total = functools.reduce(lambda a, b: a + b, [t * f for t, f in zip(totals, factors)])
        inv = 1.0 / jnp.sum(total, axis=0, keepdims=True)
        factors = [f * inv for f in factors]

        delta = jnp.zeros((8, lanes), F32)
        for i in range(len(group)):
            at, size = spans[n_first + i]
            d_prob = lax.dot_general(
                group_rows(i, head_dim), dq_ref[...], dims, preferred_element_type=F32
            )
            p = tiles(s_ref[pl.ds(at, size)]) * factors[n_first + i]
            delta = delta + jnp.sum(p.astype(BF16).astype(F32) * tiles(d_prob), axis=0)
        for i in range(n_first):
            at, size = spans[i]
            p_ref[pl.ds(at, size)] = lax.dot_general(
                cache_rows(cv_ref, i), dq_ref[...], dims, preferred_element_type=F32
            )
            p = (tiles(s_ref[pl.ds(at, size)]) * factors[i]).reshape(size, lanes).astype(BF16)
            delta = delta + jnp.sum(tiles(p.astype(F32)) * tiles(p_ref[pl.ds(at, size)]), axis=0)
            out_ref[1 - odd, pl.ds(at, size)] = jnp.dot(p, dq_ref[...], preferred_element_type=F32)
        delta = jnp.sum(delta, axis=0, keepdims=True)
        for i in range(n_first):
            at, size = spans[i]
            p = tiles(s_ref[pl.ds(at, size)]) * factors[i]
            ds = p * (tiles(p_ref[pl.ds(at, size)]) - delta)
            ds = ds.reshape(size, lanes).astype(BF16)
            g = jnp.dot(ds, q_ref[...], preferred_element_type=F32) * scale
            out_ref[odd, pl.ds(at, size)] = g

        for i, ref in enumerate((keep_ref, give_ref)):
            value = sum_refs[i][...] + out_ref[i] if n_sum else out_ref[i]
            ref[...] = value.astype(ref.dtype)

    flops = 2 * lanes * head_dim * (5 * n_cache + 2 * n_group)
    return pl.pallas_call(
        body,
        in_specs=[pl.BlockSpec(memory_space=pltpu.SMEM)]
        + [pl.BlockSpec(memory_space=pltpu.VMEM)]
        + [pl.BlockSpec(memory_space=pl.ANY)] * 2
        + [pl.BlockSpec(memory_space=pltpu.VMEM)] * (len(group) + n_part + n_sum),
        out_specs=[pl.BlockSpec(memory_space=pltpu.VMEM)] * 2,
        out_shape=[
            jax.ShapeDtypeStruct((n_cache, head_dim), F32),
            jax.ShapeDtypeStruct((n_cache, head_dim), BF16 if n_sum else F32),
        ],
        scratch_shapes=[
            pltpu.VMEM((2, n_cache, head_dim), F32),
            pltpu.VMEM((n_cache + n_group, lanes), F32),
            pltpu.VMEM((n_cache, lanes), F32),
            pltpu.VMEM((lanes, head_dim), BF16),
            pltpu.VMEM((lanes, head_dim), BF16),
            pltpu.VMEM((n_blocks, block, head_dim), BF16),
            pltpu.VMEM((n_blocks, block, head_dim), BF16),
            pltpu.SemaphoreType.DMA((2,)),
        ],
        compiler_params=params(),
        cost_estimate=pl.CostEstimate(
            flops=flops,
            bytes_accessed=12 * n_cache * head_dim,
            transcendentals=lanes * (n_cache + n_group),
        ),
        name="attend",
    )(lengths, d_attn, *cache, *group, *terms, *sums)


def make_on_device(n_dp, n_fsdp):
    inner = n_fsdp // 2

    def on_device(hidden, d_attn, w_query, w_key, w_value, cache_keys, cache_values, lengths):
        dp = lax.axis_index("dp")
        head_dim = w_key.shape[1]
        q_width = w_query.shape[1]
        even = dp % 2 == 0
        d_bits = bits_down(n_dp)

        def from_owners(products):
            return [products[0]] + [swap(x, "fsdp", n_fsdp, k + 1) for k, x in enumerate(products[1:])]

        cuts = [(0, q_width // 2), (q_width // 2, q_width // 2)]
        sent, part = prepare(hidden, w_query, w_key, w_value, n_dp, n_fsdp)
        received = [swap(block, "fsdp", n_fsdp, k + 1) for k, block in enumerate(sent)]
        part = swap(part, "fsdp", n_fsdp, inner)
        share = w_query.shape[0] // n_dp
        cut = share + share // 2
        part_a, part_b = part[:cut], part[cut:]
        far_a, order = double(part_a[None], [0], "dp", n_dp, d_bits[0])
        cache = jnp.where(even, cache_keys, cache_values)[None]
        cache, _ = double(cache, [0], "fsdp", n_fsdp, inner)
        cache, far_a, *received = together(cache, far_a, *received)
        far_b, _ = double(part_b[None], [0], "dp", n_dp, d_bits[0])
        far_a, d_order = finish(far_a, order, "dp", n_dp, d_bits[1:])
        cache = [cache] + [swap(cache, "fsdp", n_fsdp, k) for k in range(1, inner)]
        far_a[1], far_b, *cache = together(far_a[1], far_b, *cache)
        cache = jnp.concatenate(cache)
        f_order = [o for k in range(inner) for o in (k, k ^ inner)]
        cache = [cache, swap(cache, "dp", n_dp, 1)]
        kv, (at_a, wide_a), (at_b, wide_b) = 2 * head_dim, *cuts
        near_a = [(w_key, 0, head_dim), (w_value, 0, head_dim), (w_query, at_a, wide_a)]
        layout_a = [(0, 0, share, wide_a, 0, kv)]
        layout_a += [(share, i * kv, share // 2, kv, i * (share // 2), 0) for i in range(2)]
        out_kv, out_a = multiply(
            hidden, received, near_a, far_a, layout_a, d_order, n_fsdp, (kv, wide_a)
        )
        far_b, cache[1], out_kv[0] = together(far_b, cache[1], out_kv[0])
        far_b, _ = finish(far_b, order, "dp", n_dp, d_bits[1:])
        parts_kv = from_owners(out_kv)
        parts_a = from_owners(out_a)
        own = functools.reduce(lambda a, b: a + b, parts_kv).astype(BF16)
        far_b[1], own = together(far_b[1], own)
        group, _ = double(own[None], [0], "fsdp", n_fsdp, inner)
        near_b, layout_b = [(w_query, at_b, wide_b)], [(0, 0, share, wide_b, 0, 0)]
        (out_b,) = multiply(
            hidden, received, near_b, far_b, layout_b, d_order, n_fsdp, (wide_b,)
        )
        group, *tied = together(group, *out_b, *parts_a[1:])
        out_b, parts_a[1:] = tied[:inner], tied[inner:]
        group = [group] + [swap(group, "fsdp", n_fsdp, k) for k in range(1, inner)]
        parts_b = from_owners(out_b)
        first = cuts[0][1] // head_dim
        sums = attend(lengths, parts_a, d_attn, 0, cache, group, f_order, ())
        keep, give = attend(lengths, parts_b, d_attn, first, cache, group, f_order, sums)

        half = keep + swap(give, "dp", n_dp, 1).astype(F32)
        size = half.shape[0] // n_fsdp
        mine = half[:size]
        far = [slot for slot in range(n_fsdp) if f_order[slot] >= inner]
        near = [slot for slot in range(1, n_fsdp) if f_order[slot] < inner]
        for slot in far[:1] + near + far[:0:-1]:
            out = half[slot * size : (slot + 1) * size].astype(BF16)
            mine = mine + swap(out, "fsdp", n_fsdp, f_order[slot]).astype(F32)
        for bit in d_bits[:-1]:
            mine = mine.astype(BF16)
            mine = mine.astype(F32) + swap(mine, "dp", n_dp, bit).astype(F32)
        other = swap(mine, "dp", n_dp, 1)
        return jnp.where(even, mine, other), jnp.where(even, other, mine)

    return on_device


def solution(mesh):
    placed = (
        P(("dp", "fsdp"), None),
        P(("dp", "fsdp"), None),
        P("fsdp", None),
        P("fsdp", None),
        P("fsdp", None),
        P("fsdp", None),
        P("fsdp", None),
        P("dp", None),
    )
    return jax.shard_map(
        make_on_device(mesh.shape["dp"], mesh.shape["fsdp"]),
        mesh=mesh,
        in_specs=placed,
        out_specs=(P("fsdp", None), P("fsdp", None)),
        check_vma=False,
    )
```

```python
import functools
import math

import jax
import jax.numpy as jnp
from jax import lax
from jax.experimental import pallas as pl
from jax.experimental.pallas import tpu as pltpu
from jax.sharding import PartitionSpec as P

F32 = jnp.float32
BF16 = jnp.bfloat16
VMEM_LIMIT = 56 * 1024 * 1024


def swap(value, axis, size, bit):
    return lax.ppermute(value, axis, [(i, i ^ bit) for i in range(size)])


def bits_down(size):
    bits = []
    bit = size // 2
    while bit:
        bits.append(bit)
        bit //= 2
    return bits


def double(block, order, axis, size, bit):
    return jnp.concatenate([block, swap(block, axis, size, bit)]), order + [o ^ bit for o in order]


def finish(block, order, axis, size, bits):
    for bit in bits[:-1]:
        block, order = double(block, order, axis, size, bit)
    return [block, swap(block, axis, size, bits[-1])], order + [o ^ bits[-1] for o in order]


def together(*values):
    return lax.optimization_barrier(values)


def params():
    return pltpu.CompilerParams(vmem_limit_bytes=VMEM_LIMIT)


def run_copies(copies):
    for copy in copies:
        copy.start()
    for copy in copies:
        copy.wait()


def prepare(hidden, w_query, w_key, w_value, n_dp, n_fsdp):
    inner = n_fsdp // 2
    tokens = hidden.shape[0]
    rows_w, q_width = w_query.shape
    head_dim = w_key.shape[1]
    share = rows_w // n_dp
    cols = q_width // 2

    def body(hidden_ref, wq_ref, wk_ref, wv_ref, *rest):
        sent, part, sems = rest[: inner - 1], rest[-2], rest[-1]
        me, dp = lax.axis_index("fsdp"), lax.axis_index("dp")
        first = pl.multiple_of(dp * share, 16)
        rows = pl.ds(first, share)
        pairs = []
        for i in range(2):
            to = part.at[pl.ds(i * (share + share // 2), share)]
            pairs.append((wq_ref.at[rows, pl.ds(i * cols, cols)], to))
            for j, ref in enumerate((wk_ref, wv_ref)):
                to = part.at[pl.ds(share, share // 2), pl.ds((2 * i + j) * head_dim, head_dim)]
                pairs.append((ref.at[pl.ds(first + i * (share // 2), share // 2)], to))
        for k in range(1, inner):
            for side, bit in enumerate((0, inner)):
                start = pl.multiple_of((me ^ k ^ bit) * rows_w, 128)
                pairs.append(
                    (hidden_ref.at[:, pl.ds(start, rows_w)], sent[k - 1].at[:, pl.ds(side * rows_w, rows_w)])
                )
        run_copies([pltpu.make_async_copy(a, b, sems.at[i]) for i, (a, b) in enumerate(pairs)])

    moved = 2 * (tokens * 2 * rows_w * 2 * (inner - 1) + share * (q_width + 2 * head_dim) * 2)
    out = pl.pallas_call(
        body,
        in_specs=[pl.BlockSpec(memory_space=pl.ANY)] * 4,
        out_specs=[pl.BlockSpec(memory_space=pltpu.VMEM)] * inner,
        out_shape=[jax.ShapeDtypeStruct((tokens, 2 * rows_w), BF16)] * (inner - 1)
        + [jax.ShapeDtypeStruct((2 * share + share // 2, cols), BF16)],
        scratch_shapes=[pltpu.SemaphoreType.DMA((6 + 2 * (inner - 1),))],
        compiler_params=params(),
        cost_estimate=pl.CostEstimate(flops=0, bytes_accessed=moved, transcendentals=0),
        name="prepare",
    )(hidden, w_query, w_key, w_value)
    return out[:-1], out[-1]


def multiply(hidden, received, near, far, layout, order, n_fsdp, groups):
    inner = n_fsdp // 2
    tokens = hidden.shape[0]
    cols = sum(wide for _, _, wide in near)
    slots = far[0].shape[0]
    n_dp = slots * len(far)
    rows_w = near[0][0].shape[0]
    share = rows_w // n_dp
    step = 256 if all(g % 256 == 0 for g in groups) else 128
    n_in = inner - 1 + len(near) + len(far)

    def body(hidden_ref, *rest):
        blocks, rest = rest[: inner - 1], rest[inner - 1 :]
        near_refs, rest = rest[: len(near)], rest[len(near) :]
        far_refs, rest = rest[: len(far)], rest[len(far) :]
        outs = rest[:-3]
        x_all, w_all, sems = rest[-3:]
        me, dp = lax.axis_index("fsdp"), lax.axis_index("dp")
        pairs = []
        for side, bit in enumerate((0, inner)):
            start = pl.multiple_of((me ^ bit) * rows_w, 128)
            pairs.append(
                (
                    hidden_ref.at[:, pl.ds(start, rows_w)],
                    x_all.at[pl.ds(0, tokens), pl.ds(side * rows_w, rows_w)],
                )
            )
        for k in range(1, inner):
            pairs.append((blocks[k - 1], x_all.at[pl.ds(k * tokens, tokens)]))
        to = 0
        for ref, (_, start, wide) in zip(near_refs, near):
            pairs.append((ref.at[:, pl.ds(start, wide)], w_all.at[pl.ds(0, rows_w), pl.ds(to, wide)]))
            to += wide
        for slot, o in enumerate(order):
            block = far_refs[slot // slots].at[slot % slots]
            for row, col, rows, wide, to_row, to_col in layout:
                to = pl.multiple_of(rows_w + (dp ^ o) * share + to_row, 16)
                piece = block.at[pl.ds(row, rows), pl.ds(col, wide)]
                pairs.append((piece, w_all.at[pl.ds(to, rows), pl.ds(to_col, wide)]))
        run_copies([pltpu.make_async_copy(a, b, sems.at[i]) for i, (a, b) in enumerate(pairs)])

        base = 0
        for g, wide in enumerate(groups):

            @pl.loop(0, wide // step)
            def _(n, g=g, base=base):
                at = pl.multiple_of(n * step, 128)
                product = jnp.dot(
                    x_all[...], w_all[:, pl.ds(base + at, step)], preferred_element_type=F32
                )
                for k in range(inner):
                    outs[g * inner + k][:, pl.ds(at, step)] = product[k * tokens : (k + 1) * tokens]

            base += wide

    copies = 2 + (inner - 1) + len(near) + n_dp * len(layout)
    moved = inner * tokens * 2 * rows_w * 2 + 2 * rows_w * cols * 2 + inner * tokens * cols * 4
    out = pl.pallas_call(
        body,
        in_specs=[pl.BlockSpec(memory_space=pl.ANY)] * (1 + n_in),
        out_specs=[pl.BlockSpec(memory_space=pltpu.VMEM)] * (inner * len(groups)),
        out_shape=[jax.ShapeDtypeStruct((tokens, g), F32) for g in groups for _ in range(inner)],
        scratch_shapes=[
            pltpu.VMEM((inner * tokens, 2 * rows_w), BF16),
            pltpu.VMEM((2 * rows_w, cols), BF16),
            pltpu.SemaphoreType.DMA((copies,)),
        ],
        compiler_params=params(),
        cost_estimate=pl.CostEstimate(
            flops=2 * inner * tokens * 2 * rows_w * cols, bytes_accessed=moved, transcendentals=0
        ),
        name="multiply",
    )(hidden, *received, *[array for array, _, _ in near], *far)
    return [list(out[g * inner : (g + 1) * inner]) for g in range(len(groups))]


def attend(lengths, partials, d_attn, cache, group, g_order):
    tokens = d_attn.shape[0]
    n_blocks, block, head_dim = cache[0].shape
    n_convs = lengths.shape[1]
    scale = head_dim ** (-0.5)
    to_log2 = scale * math.log2(math.e)
    n_heads = d_attn.shape[1] // head_dim
    lanes = n_heads * tokens
    n_cache = n_blocks * block
    n_group = n_blocks * tokens
    slots = n_blocks // len(group)
    chunk = min(512, n_cache)
    n_part = sum(len(terms) for terms, _ in partials)
    dims = (((1,), (1,)), ((), ()))
    spans = [(at, chunk) for at in range(0, n_cache, chunk)]
    spans += [(n_cache + i * slots * tokens, slots * tokens) for i in range(len(group))]
    n_first = n_cache // chunk

    def tiles(value):
        return value.reshape(value.shape[0] // 8, 8, lanes)

    def body(len_ref, d_ref, *rest):
        cache_refs, rest = rest[:2], rest[2:]
        group_refs, rest = rest[: len(group)], rest[len(group) :]
        part_refs, rest = list(rest[:n_part]), rest[n_part:]
        keep_ref, give_ref, out_ref, s_ref, p_ref, q_ref, dq_ref, ck_ref, cv_ref, sems = rest
        me, dp = lax.axis_index("fsdp"), lax.axis_index("dp")
        odd = dp % 2

        @pl.when(odd == 0)
        def _():
            pltpu.make_async_copy(cache_refs[0], ck_ref, sems.at[0]).start()
            pltpu.make_async_copy(cache_refs[1], cv_ref, sems.at[1]).start()

        @pl.when(odd == 1)
        def _():
            pltpu.make_async_copy(cache_refs[1], ck_ref, sems.at[0]).start()
            pltpu.make_async_copy(cache_refs[0], cv_ref, sems.at[1]).start()

        h = 0
        for terms, start in partials:
            refs, part_refs = part_refs[: len(terms)], part_refs[len(terms) :]
            for at in range(start, terms[0].shape[1], head_dim):
                rows = pl.ds(h * tokens, tokens)
                q = refs[0][:, at : at + head_dim]
                for ref in refs[1:]:
                    q = q + ref[:, at : at + head_dim]
                q_ref[rows] = q.astype(BF16)
                dq_ref[rows] = d_ref[:, h * head_dim : (h + 1) * head_dim]
                h += 1

        q_pos = me * tokens + lax.broadcasted_iota(jnp.int32, (1, lanes), 1) % tokens
        begin = jnp.zeros((1, lanes), jnp.int32)
        end = jnp.int32(0)
        for i in range(n_convs):
            end = end + len_ref[0, i]
            begin = jnp.where(end <= q_pos, end, begin)

        def group_rows(i, at):
            return group_refs[i][...].reshape(slots * tokens, 2 * head_dim)[:, at : at + head_dim]

        def cache_rows(ref, i):
            return ref[...].reshape(n_cache, head_dim)[i * chunk : (i + 1) * chunk]

        for i in range(len(group)):
            at, size = spans[n_first + i]
            s = lax.dot_general(group_rows(i, 0), q_ref[...], dims, preferred_element_type=F32)
            for j in range(slots):
                pos = (me ^ g_order[i * slots + j]) * tokens
                pos = pos + lax.broadcasted_iota(jnp.int32, (tokens, lanes), 0)
                allowed = (pos <= q_pos) & (pos >= begin)
                here = s[j * tokens : (j + 1) * tokens]
                s_ref[pl.ds(at + j * tokens, tokens)] = jnp.where(allowed, here, -jnp.inf)

        pltpu.make_async_copy(cache_refs[0], ck_ref, sems.at[0]).wait()
        pltpu.make_async_copy(cache_refs[1], cv_ref, sems.at[1]).wait()
        for i in range(n_first):
            at, size = spans[i]
            s_ref[pl.ds(at, size)] = lax.dot_general(
                cache_rows(ck_ref, i), q_ref[...], dims, preferred_element_type=F32
            )

        tops, totals = [], []
        for at, size in spans:
            top = jnp.max(tiles(s_ref[pl.ds(at, size)]), axis=0)
            top = jnp.maximum(top, -1e30)
            e = jnp.exp2((tiles(s_ref[pl.ds(at, size)]) - top) * to_log2)
            s_ref[pl.ds(at, size)] = e.reshape(size, lanes)
            tops.append(top)
            totals.append(jnp.sum(e, axis=0))
        top = functools.reduce(jnp.maximum, tops)
        top = jnp.max(top, axis=0, keepdims=True)
        factors = [jnp.exp2((own - top) * to_log2) for own in tops]
        total = functools.reduce(lambda a, b: a + b, [t * f for t, f in zip(totals, factors)])
        inv = 1.0 / jnp.sum(total, axis=0, keepdims=True)
        factors = [f * inv for f in factors]

        delta = jnp.zeros((8, lanes), F32)
        for i in range(len(group)):
            at, size = spans[n_first + i]
            d_prob = lax.dot_general(
                group_rows(i, head_dim), dq_ref[...], dims, preferred_element_type=F32
            )
            p = tiles(s_ref[pl.ds(at, size)]) * factors[n_first + i]
            delta = delta + jnp.sum(p.astype(BF16).astype(F32) * tiles(d_prob), axis=0)
        for i in range(n_first):
            at, size = spans[i]
            p_ref[pl.ds(at, size)] = lax.dot_general(
                cache_rows(cv_ref, i), dq_ref[...], dims, preferred_element_type=F32
            )
            p = (tiles(s_ref[pl.ds(at, size)]) * factors[i]).reshape(size, lanes).astype(BF16)
            delta = delta + jnp.sum(tiles(p.astype(F32)) * tiles(p_ref[pl.ds(at, size)]), axis=0)
            out_ref[1 - odd, pl.ds(at, size)] = jnp.dot(p, dq_ref[...], preferred_element_type=F32)
        delta = jnp.sum(delta, axis=0, keepdims=True)
        for i in range(n_first):
            at, size = spans[i]
            p = tiles(s_ref[pl.ds(at, size)]) * factors[i]
            ds = p * (tiles(p_ref[pl.ds(at, size)]) - delta)
            ds = ds.reshape(size, lanes).astype(BF16)
            g = jnp.dot(ds, q_ref[...], preferred_element_type=F32) * scale
            out_ref[odd, pl.ds(at, size)] = g

        for i, ref in enumerate((keep_ref, give_ref)):
            ref[...] = out_ref[i].astype(ref.dtype)

    flops = 2 * lanes * head_dim * (5 * n_cache + 2 * n_group)
    return pl.pallas_call(
        body,
        in_specs=[pl.BlockSpec(memory_space=pltpu.SMEM)]
        + [pl.BlockSpec(memory_space=pltpu.VMEM)]
        + [pl.BlockSpec(memory_space=pl.ANY)] * 2
        + [pl.BlockSpec(memory_space=pltpu.VMEM)] * (len(group) + n_part),
        out_specs=[pl.BlockSpec(memory_space=pltpu.VMEM)] * 2,
        out_shape=[jax.ShapeDtypeStruct((n_cache, head_dim), kind) for kind in (F32, BF16)],
        scratch_shapes=[
            pltpu.VMEM((2, n_cache, head_dim), F32),
            pltpu.VMEM((n_cache + n_group, lanes), F32),
            pltpu.VMEM((n_cache, lanes), F32),
            pltpu.VMEM((lanes, head_dim), BF16),
            pltpu.VMEM((lanes, head_dim), BF16),
            pltpu.VMEM((n_blocks, block, head_dim), BF16),
            pltpu.VMEM((n_blocks, block, head_dim), BF16),
            pltpu.SemaphoreType.DMA((2,)),
        ],
        compiler_params=params(),
        cost_estimate=pl.CostEstimate(
            flops=flops,
            bytes_accessed=12 * n_cache * head_dim,
            transcendentals=lanes * (n_cache + n_group),
        ),
        name="attend",
    )(lengths, d_attn, *cache, *group, *[term for terms, _ in partials for term in terms])


def make_on_device(n_dp, n_fsdp):
    inner = n_fsdp // 2

    def on_device(hidden, d_attn, w_query, w_key, w_value, cache_keys, cache_values, lengths):
        dp = lax.axis_index("dp")
        head_dim = w_key.shape[1]
        q_width = w_query.shape[1]
        even = dp % 2 == 0
        d_bits = bits_down(n_dp)

        def from_owners(products):
            return [products[0]] + [swap(x, "fsdp", n_fsdp, k + 1) for k, x in enumerate(products[1:])]

        cuts = [(0, q_width // 2), (q_width // 2, q_width // 2)]
        sent, part = prepare(hidden, w_query, w_key, w_value, n_dp, n_fsdp)
        received = [swap(block, "fsdp", n_fsdp, k + 1) for k, block in enumerate(sent)]
        part = swap(part, "fsdp", n_fsdp, inner)
        share = w_query.shape[0] // n_dp
        cut = share + share // 2
        part_a, part_b = part[:cut], part[cut:]
        far_a, order = double(part_a[None], [0], "dp", n_dp, d_bits[0])
        cache = jnp.where(even, cache_keys, cache_values)[None]
        cache, _ = double(cache, [0], "fsdp", n_fsdp, inner)
        cache, far_a, *received = together(cache, far_a, *received)
        far_b, _ = double(part_b[None], [0], "dp", n_dp, d_bits[0])
        far_a, d_order = finish(far_a, order, "dp", n_dp, d_bits[1:])
        cache = [cache] + [swap(cache, "fsdp", n_fsdp, k) for k in range(1, inner)]
        far_a[1], far_b, *cache = together(far_a[1], far_b, *cache)
        cache = jnp.concatenate(cache)
        f_order = [o for k in range(inner) for o in (k, k ^ inner)]
        cache = [cache, swap(cache, "dp", n_dp, 1)]
        kv, (at_a, wide_a), (at_b, wide_b) = 2 * head_dim, *cuts
        near_a = [(w_key, 0, head_dim), (w_value, 0, head_dim), (w_query, at_a, wide_a)]
        layout_a = [(0, 0, share, wide_a, 0, kv)]
        layout_a += [(share, i * kv, share // 2, kv, i * (share // 2), 0) for i in range(2)]
        (out_a,) = multiply(
            hidden, received, near_a, far_a, layout_a, d_order, n_fsdp, (kv + wide_a,)
        )
        far_b, cache[1], out_a[0] = together(far_b, cache[1], out_a[0])
        far_b, _ = finish(far_b, order, "dp", n_dp, d_bits[1:])
        parts_a = from_owners(out_a)
        near_b, layout_b = [(w_query, at_b, wide_b)], [(0, 0, share, wide_b, 0, 0)]
        (out_b,) = multiply(
            hidden, received, near_b, far_b, layout_b, d_order, n_fsdp, (wide_b,)
        )
        parts_b = from_owners(out_b)
        parts_b[0], parts_b[1], *parts_a = together(*parts_b[:2], *parts_a)
        own = functools.reduce(lambda a, b: a + b, [x[:, :kv] for x in parts_a]).astype(BF16)
        group, _ = double(own[None], [0], "fsdp", n_fsdp, inner)
        group, *parts_b[2:] = together(group, *parts_b[2:])
        group = [group] + [swap(group, "fsdp", n_fsdp, k) for k in range(1, inner)]
        partials = [(parts_a, kv), (parts_b, 0)]
        keep, give = attend(lengths, partials, d_attn, cache, group, f_order)

        half = keep + swap(give, "dp", n_dp, 1).astype(F32)
        size = half.shape[0] // n_fsdp
        mine = half[:size]
        far = [slot for slot in range(n_fsdp) if f_order[slot] >= inner]
        near = [slot for slot in range(1, n_fsdp) if f_order[slot] < inner]
        for slot in far[:1] + near + far[:0:-1]:
            out = half[slot * size : (slot + 1) * size].astype(BF16)
            mine = mine + swap(out, "fsdp", n_fsdp, f_order[slot]).astype(F32)
        for bit in d_bits[:-1]:
            mine = mine.astype(BF16)
            mine = mine.astype(F32) + swap(mine, "dp", n_dp, bit).astype(F32)
        other = swap(mine, "dp", n_dp, 1)
        return jnp.where(even, mine, other), jnp.where(even, other, mine)

    return on_device


def solution(mesh):
    placed = (
        P(("dp", "fsdp"), None),
        P(("dp", "fsdp"), None),
        P("fsdp", None),
        P("fsdp", None),
        P("fsdp", None),
        P("fsdp", None),
        P("fsdp", None),
        P("dp", None),
    )
    return jax.shard_map(
        make_on_device(mesh.shape["dp"], mesh.shape["fsdp"]),
        mesh=mesh,
        in_specs=placed,
        out_specs=(P("fsdp", None), P("fsdp", None)),
        check_vma=False,
    )
```

```python
import functools
import math

import jax
import jax.numpy as jnp
from jax import lax
from jax.experimental import pallas as pl
from jax.experimental.pallas import tpu as pltpu
from jax.sharding import PartitionSpec as P

F32 = jnp.float32
BF16 = jnp.bfloat16
VMEM_LIMIT = 56 * 1024 * 1024


def swap(value, axis, size, bit):
    return lax.ppermute(value, axis, [(i, i ^ bit) for i in range(size)])


def bits_down(size):
    bits = []
    bit = size // 2
    while bit:
        bits.append(bit)
        bit //= 2
    return bits


def double(block, order, axis, size, bit):
    return jnp.concatenate([block, swap(block, axis, size, bit)]), order + [o ^ bit for o in order]


def finish(block, order, axis, size, bits):
    for bit in bits[:-1]:
        block, order = double(block, order, axis, size, bit)
    return [block, swap(block, axis, size, bits[-1])], order + [o ^ bits[-1] for o in order]


def together(*values):
    return lax.optimization_barrier(values)


def params():
    return pltpu.CompilerParams(vmem_limit_bytes=VMEM_LIMIT)


def run_copies(copies):
    for copy in copies:
        copy.start()
    for copy in copies:
        copy.wait()


def prepare(hidden, w_query, w_key, w_value, n_dp, n_fsdp):
    inner = n_fsdp // 2
    tokens = hidden.shape[0]
    rows_w, q_width = w_query.shape
    head_dim = w_key.shape[1]
    share = rows_w // n_dp
    cols = q_width // 2

    def body(hidden_ref, wq_ref, wk_ref, wv_ref, *rest):
        sent, part, sems = rest[: inner - 1], rest[-2], rest[-1]
        me, dp = lax.axis_index("fsdp"), lax.axis_index("dp")
        first = pl.multiple_of(dp * share, 16)
        rows = pl.ds(first, share)
        pairs = []
        for i in range(2):
            to = part.at[pl.ds(i * (share + share // 2), share)]
            pairs.append((wq_ref.at[rows, pl.ds(i * cols, cols)], to))
            for j, ref in enumerate((wk_ref, wv_ref)):
                to = part.at[pl.ds(share, share // 2), pl.ds((2 * i + j) * head_dim, head_dim)]
                pairs.append((ref.at[pl.ds(first + i * (share // 2), share // 2)], to))
        for k in range(1, inner):
            for side, bit in enumerate((0, inner)):
                start = pl.multiple_of((me ^ k ^ bit) * rows_w, 128)
                pairs.append(
                    (hidden_ref.at[:, pl.ds(start, rows_w)], sent[k - 1].at[:, pl.ds(side * rows_w, rows_w)])
                )
        run_copies([pltpu.make_async_copy(a, b, sems.at[i]) for i, (a, b) in enumerate(pairs)])

    moved = 2 * (tokens * 2 * rows_w * 2 * (inner - 1) + share * (q_width + 2 * head_dim) * 2)
    out = pl.pallas_call(
        body,
        in_specs=[pl.BlockSpec(memory_space=pl.ANY)] * 4,
        out_specs=[pl.BlockSpec(memory_space=pltpu.VMEM)] * inner,
        out_shape=[jax.ShapeDtypeStruct((tokens, 2 * rows_w), BF16)] * (inner - 1)
        + [jax.ShapeDtypeStruct((2 * share + share // 2, cols), BF16)],
        scratch_shapes=[pltpu.SemaphoreType.DMA((6 + 2 * (inner - 1),))],
        compiler_params=params(),
        cost_estimate=pl.CostEstimate(flops=0, bytes_accessed=moved, transcendentals=0),
        name="prepare",
    )(hidden, w_query, w_key, w_value)
    return out[:-1], out[-1]


def multiply(hidden, received, near, far, layout, order, n_fsdp, groups):
    inner = n_fsdp // 2
    tokens = hidden.shape[0]
    cols = sum(wide for _, _, wide in near)
    slots = far[0].shape[0]
    n_dp = slots * len(far)
    rows_w = near[0][0].shape[0]
    share = rows_w // n_dp
    step = 256 if all(g % 256 == 0 for g in groups) else 128
    n_in = inner - 1 + len(near) + len(far)

    def body(hidden_ref, *rest):
        blocks, rest = rest[: inner - 1], rest[inner - 1 :]
        near_refs, rest = rest[: len(near)], rest[len(near) :]
        far_refs, rest = rest[: len(far)], rest[len(far) :]
        outs = rest[:-3]
        x_all, w_all, sems = rest[-3:]
        me, dp = lax.axis_index("fsdp"), lax.axis_index("dp")
        pairs = []
        for side, bit in enumerate((0, inner)):
            start = pl.multiple_of((me ^ bit) * rows_w, 128)
            pairs.append(
                (
                    hidden_ref.at[:, pl.ds(start, rows_w)],
                    x_all.at[pl.ds(0, tokens), pl.ds(side * rows_w, rows_w)],
                )
            )
        for k in range(1, inner):
            pairs.append((blocks[k - 1], x_all.at[pl.ds(k * tokens, tokens)]))
        to = 0
        for ref, (_, start, wide) in zip(near_refs, near):
            pairs.append((ref.at[:, pl.ds(start, wide)], w_all.at[pl.ds(0, rows_w), pl.ds(to, wide)]))
            to += wide
        for slot, o in enumerate(order):
            block = far_refs[slot // slots].at[slot % slots]
            for row, col, rows, wide, to_row, to_col in layout:
                to = pl.multiple_of(rows_w + (dp ^ o) * share + to_row, 16)
                piece = block.at[pl.ds(row, rows), pl.ds(col, wide)]
                pairs.append((piece, w_all.at[pl.ds(to, rows), pl.ds(to_col, wide)]))
        run_copies([pltpu.make_async_copy(a, b, sems.at[i]) for i, (a, b) in enumerate(pairs)])

        base = 0
        for g, wide in enumerate(groups):

            @pl.loop(0, wide // step)
            def _(n, g=g, base=base):
                at = pl.multiple_of(n * step, 128)
                product = jnp.dot(
                    x_all[...], w_all[:, pl.ds(base + at, step)], preferred_element_type=F32
                )
                for k in range(inner):
                    outs[g * inner + k][:, pl.ds(at, step)] = product[k * tokens : (k + 1) * tokens]

            base += wide

    copies = 2 + (inner - 1) + len(near) + n_dp * len(layout)
    moved = inner * tokens * 2 * rows_w * 2 + 2 * rows_w * cols * 2 + inner * tokens * cols * 4
    out = pl.pallas_call(
        body,
        in_specs=[pl.BlockSpec(memory_space=pl.ANY)] * (1 + n_in),
        out_specs=[pl.BlockSpec(memory_space=pltpu.VMEM)] * (inner * len(groups)),
        out_shape=[jax.ShapeDtypeStruct((tokens, g), F32) for g in groups for _ in range(inner)],
        scratch_shapes=[
            pltpu.VMEM((inner * tokens, 2 * rows_w), BF16),
            pltpu.VMEM((2 * rows_w, cols), BF16),
            pltpu.SemaphoreType.DMA((copies,)),
        ],
        compiler_params=params(),
        cost_estimate=pl.CostEstimate(
            flops=2 * inner * tokens * 2 * rows_w * cols, bytes_accessed=moved, transcendentals=0
        ),
        name="multiply",
    )(hidden, *received, *[array for array, _, _ in near], *far)
    return [list(out[g * inner : (g + 1) * inner]) for g in range(len(groups))]


def attend(lengths, terms, d_attn, first_head, cache, group, g_order, sums):
    tokens = d_attn.shape[0]
    n_blocks, block, head_dim = cache[0].shape
    n_convs = lengths.shape[1]
    scale = head_dim ** (-0.5)
    to_log2 = scale * math.log2(math.e)
    n_heads = terms[0].shape[1] // head_dim
    lanes = n_heads * tokens
    n_cache = n_blocks * block
    n_group = n_blocks * tokens
    slots = n_blocks // len(group)
    chunk = min(512, n_cache)
    n_part, n_sum = len(terms), len(sums)
    dims = (((1,), (1,)), ((), ()))
    spans = [(at, chunk) for at in range(0, n_cache, chunk)]
    spans += [(n_cache + i * slots * tokens, slots * tokens) for i in range(len(group))]
    n_first = n_cache // chunk

    def tiles(value):
        return value.reshape(value.shape[0] // 8, 8, lanes)

    def body(len_ref, d_ref, *rest):
        cache_refs, rest = rest[:2], rest[2:]
        group_refs, rest = rest[: len(group)], rest[len(group) :]
        part_refs, rest = rest[:n_part], rest[n_part:]
        sum_refs, rest = rest[:n_sum], rest[n_sum:]
        keep_ref, give_ref, out_ref, s_ref, p_ref, q_ref, dq_ref, ck_ref, cv_ref, sems = rest
        me, dp = lax.axis_index("fsdp"), lax.axis_index("dp")
        odd = dp % 2

        @pl.when(odd == 0)
        def _():
            pltpu.make_async_copy(cache_refs[0], ck_ref, sems.at[0]).start()
            pltpu.make_async_copy(cache_refs[1], cv_ref, sems.at[1]).start()

        @pl.when(odd == 1)
        def _():
            pltpu.make_async_copy(cache_refs[1], ck_ref, sems.at[0]).start()
            pltpu.make_async_copy(cache_refs[0], cv_ref, sems.at[1]).start()

        for h in range(n_heads):
            at = slice(h * head_dim, (h + 1) * head_dim)
            rows = pl.ds(h * tokens, tokens)
            q = part_refs[0][:, at]
            for ref in part_refs[1:]:
                q = q + ref[:, at]
            q_ref[rows] = q.astype(BF16)
            at = (first_head + h) * head_dim
            dq_ref[rows] = d_ref[:, at : at + head_dim]

        q_pos = me * tokens + lax.broadcasted_iota(jnp.int32, (1, lanes), 1) % tokens
        begin = jnp.zeros((1, lanes), jnp.int32)
        end = jnp.int32(0)
        for i in range(n_convs):
            end = end + len_ref[0, i]
            begin = jnp.where(end <= q_pos, end, begin)

        def group_rows(i, at):
            return group_refs[i][...].reshape(slots * tokens, 2 * head_dim)[:, at : at + head_dim]

        def cache_rows(ref, i):
            return ref[...].reshape(n_cache, head_dim)[i * chunk : (i + 1) * chunk]

        for i in range(len(group)):
            at, size = spans[n_first + i]
            s = lax.dot_general(group_rows(i, 0), q_ref[...], dims, preferred_element_type=F32)
            for j in range(slots):
                pos = (me ^ g_order[i * slots + j]) * tokens
                pos = pos + lax.broadcasted_iota(jnp.int32, (tokens, lanes), 0)
                allowed = (pos <= q_pos) & (pos >= begin)
                here = s[j * tokens : (j + 1) * tokens]
                s_ref[pl.ds(at + j * tokens, tokens)] = jnp.where(allowed, here, -jnp.inf)

        pltpu.make_async_copy(cache_refs[0], ck_ref, sems.at[0]).wait()
        pltpu.make_async_copy(cache_refs[1], cv_ref, sems.at[1]).wait()
        for i in range(n_first):
            at, size = spans[i]
            s_ref[pl.ds(at, size)] = lax.dot_general(
                cache_rows(ck_ref, i), q_ref[...], dims, preferred_element_type=F32
            )

        tops, totals = [], []
        for at, size in spans:
            top = jnp.max(tiles(s_ref[pl.ds(at, size)]), axis=0)
            top = jnp.maximum(top, -1e30)
            e = jnp.exp2((tiles(s_ref[pl.ds(at, size)]) - top) * to_log2)
            s_ref[pl.ds(at, size)] = e.reshape(size, lanes)
            tops.append(top)
            totals.append(jnp.sum(e, axis=0))
        top = functools.reduce(jnp.maximum, tops)
        top = jnp.max(top, axis=0, keepdims=True)
        factors = [jnp.exp2((own - top) * to_log2) for own in tops]
        total = functools.reduce(lambda a, b: a + b, [t * f for t, f in zip(totals, factors)])
        inv = 1.0 / jnp.sum(total, axis=0, keepdims=True)
        factors = [f * inv for f in factors]

        delta = jnp.zeros((8, lanes), F32)
        for i in range(len(group)):
            at, size = spans[n_first + i]
            d_prob = lax.dot_general(
                group_rows(i, head_dim), dq_ref[...], dims, preferred_element_type=F32
            )
            p = tiles(s_ref[pl.ds(at, size)]) * factors[n_first + i]
            delta = delta + jnp.sum(p.astype(BF16).astype(F32) * tiles(d_prob), axis=0)
        for i in range(n_first):
            at, size = spans[i]
            p_ref[pl.ds(at, size)] = lax.dot_general(
                cache_rows(cv_ref, i), dq_ref[...], dims, preferred_element_type=F32
            )
            p = (tiles(s_ref[pl.ds(at, size)]) * factors[i]).reshape(size, lanes).astype(BF16)
            delta = delta + jnp.sum(tiles(p.astype(F32)) * tiles(p_ref[pl.ds(at, size)]), axis=0)
            out_ref[1 - odd, pl.ds(at, size)] = jnp.dot(p, dq_ref[...], preferred_element_type=F32)
        delta = jnp.sum(delta, axis=0, keepdims=True)
        for i in range(n_first):
            at, size = spans[i]
            p = tiles(s_ref[pl.ds(at, size)]) * factors[i]
            ds = p * (tiles(p_ref[pl.ds(at, size)]) - delta)
            ds = ds.reshape(size, lanes).astype(BF16)
            g = jnp.dot(ds, q_ref[...], preferred_element_type=F32) * scale
            out_ref[odd, pl.ds(at, size)] = g

        for i, ref in enumerate((keep_ref, give_ref)):
            value = sum_refs[i][...] + out_ref[i] if n_sum else out_ref[i]
            ref[...] = value.astype(ref.dtype)

    flops = 2 * lanes * head_dim * (5 * n_cache + 2 * n_group)
    return pl.pallas_call(
        body,
        in_specs=[pl.BlockSpec(memory_space=pltpu.SMEM)]
        + [pl.BlockSpec(memory_space=pltpu.VMEM)]
        + [pl.BlockSpec(memory_space=pl.ANY)] * 2
        + [pl.BlockSpec(memory_space=pltpu.VMEM)] * (len(group) + n_part + n_sum),
        out_specs=[pl.BlockSpec(memory_space=pltpu.VMEM)] * 2,
        out_shape=[
            jax.ShapeDtypeStruct((n_cache, head_dim), F32),
            jax.ShapeDtypeStruct((n_cache, head_dim), BF16 if n_sum else F32),
        ],
        scratch_shapes=[
            pltpu.VMEM((2, n_cache, head_dim), F32),
            pltpu.VMEM((n_cache + n_group, lanes), F32),
            pltpu.VMEM((n_cache, lanes), F32),
            pltpu.VMEM((lanes, head_dim), BF16),
            pltpu.VMEM((lanes, head_dim), BF16),
            pltpu.VMEM((n_blocks, block, head_dim), BF16),
            pltpu.VMEM((n_blocks, block, head_dim), BF16),
            pltpu.SemaphoreType.DMA((2,)),
        ],
        compiler_params=params(),
        cost_estimate=pl.CostEstimate(
            flops=flops,
            bytes_accessed=12 * n_cache * head_dim,
            transcendentals=lanes * (n_cache + n_group),
        ),
        name="attend",
    )(lengths, d_attn, *cache, *group, *terms, *sums)


def make_on_device(n_dp, n_fsdp):
    inner = n_fsdp // 2

    def on_device(hidden, d_attn, w_query, w_key, w_value, cache_keys, cache_values, lengths):
        dp = lax.axis_index("dp")
        head_dim = w_key.shape[1]
        q_width = w_query.shape[1]
        even = dp % 2 == 0
        f_bits, d_bits = bits_down(n_fsdp), bits_down(n_dp)

        def from_owners(products):
            return [products[0]] + [swap(x, "fsdp", n_fsdp, k + 1) for k, x in enumerate(products[1:])]

        cuts = [(0, q_width // 2), (q_width // 2, q_width // 2)]
        sent, part = prepare(hidden, w_query, w_key, w_value, n_dp, n_fsdp)
        received = [swap(block, "fsdp", n_fsdp, k + 1) for k, block in enumerate(sent)]
        part = swap(part, "fsdp", n_fsdp, inner)
        share = w_query.shape[0] // n_dp
        cut = share + share // 2
        part_a, part_b = part[:cut], part[cut:]
        far_a, order = double(part_a[None], [0], "dp", n_dp, d_bits[0])
        cache = jnp.where(even, cache_keys, cache_values)[None]
        cache, f_order = double(cache, [0], "fsdp", n_fsdp, f_bits[0])
        cache, far_a, *received = together(cache, far_a, *received)
        far_b, _ = double(part_b[None], [0], "dp", n_dp, d_bits[0])
        far_a, d_order = finish(far_a, order, "dp", n_dp, d_bits[1:])
        cache, f_order = double(cache, f_order, "fsdp", n_fsdp, f_bits[1])
        cache, far_a[1] = together(cache, far_a[1])
        kv, (at_a, wide_a), (at_b, wide_b) = 2 * head_dim, *cuts
        near_a = [(w_key, 0, head_dim), (w_value, 0, head_dim), (w_query, at_a, wide_a)]
        layout_a = [(0, 0, share, wide_a, 0, kv)]
        layout_a += [(share, i * kv, share // 2, kv, i * (share // 2), 0) for i in range(2)]
        out_kv, out_a = multiply(
            hidden, received, near_a, far_a, layout_a, d_order, n_fsdp, (kv, wide_a)
        )
        for bit in f_bits[2:]:
            cache, f_order = double(cache, f_order, "fsdp", n_fsdp, bit)
        far_b, cache, out_kv[0] = together(far_b, cache, out_kv[0])
        far_b, _ = finish(far_b, order, "dp", n_dp, d_bits[1:])
        parts_kv = from_owners(out_kv)
        parts_a = from_owners(out_a)
        own = functools.reduce(lambda a, b: a + b, parts_kv).astype(BF16)
        far_b[1], own = together(far_b[1], own)
        group, _ = double(own[None], [0], "fsdp", n_fsdp, inner)
        near_b, layout_b = [(w_query, at_b, wide_b)], [(0, 0, share, wide_b, 0, 0)]
        (out_b,) = multiply(
            hidden, received, near_b, far_b, layout_b, d_order, n_fsdp, (wide_b,)
        )
        group, cache, *tied = together(group, cache, *out_b, *parts_a[1:])
        out_b, parts_a[1:] = tied[:inner], tied[inner:]
        group = [group] + [swap(group, "fsdp", n_fsdp, k) for k in range(1, inner)]
        g_order = [o for k in range(inner) for o in (k, k ^ inner)]
        cache = [cache, swap(cache, "dp", n_dp, 1)]
        parts_b = from_owners(out_b)
        first = cuts[0][1] // head_dim
        sums = attend(lengths, parts_a, d_attn, 0, cache, group, g_order, ())
        keep, give = attend(lengths, parts_b, d_attn, first, cache, group, g_order, sums)

        half = keep + swap(give, "dp", n_dp, 1).astype(F32)
        size = half.shape[0] // n_fsdp
        mine = half[:size]
        far = [slot for slot in range(n_fsdp) if f_order[slot] >= inner]
        near = [slot for slot in range(1, n_fsdp) if f_order[slot] < inner]
        for slot in far[:1] + near + far[:0:-1]:
            out = half[slot * size : (slot + 1) * size].astype(BF16)
            mine = mine + swap(out, "fsdp", n_fsdp, f_order[slot]).astype(F32)
        for bit in d_bits[:-1]:
            mine = mine.astype(BF16)
            mine = mine.astype(F32) + swap(mine, "dp", n_dp, bit).astype(F32)
        other = swap(mine, "dp", n_dp, 1)
        return jnp.where(even, mine, other), jnp.where(even, other, mine)

    return on_device


def solution(mesh):
    placed = (
        P(("dp", "fsdp"), None),
        P(("dp", "fsdp"), None),
        P("fsdp", None),
        P("fsdp", None),
        P("fsdp", None),
        P("fsdp", None),
        P("fsdp", None),
        P("dp", None),
    )
    return jax.shard_map(
        make_on_device(mesh.shape["dp"], mesh.shape["fsdp"]),
        mesh=mesh,
        in_specs=placed,
        out_specs=(P("fsdp", None), P("fsdp", None)),
        check_vma=False,
    )
```

```python
import functools
import math

import jax
import jax.numpy as jnp
from jax import lax
from jax.experimental import pallas as pl
from jax.experimental.pallas import tpu as pltpu
from jax.sharding import PartitionSpec as P

F32 = jnp.float32
BF16 = jnp.bfloat16
VMEM_LIMIT = 56 * 1024 * 1024


def swap(value, axis, size, bit):
    return lax.ppermute(value, axis, [(i, i ^ bit) for i in range(size)])


def bits_down(size):
    bits = []
    bit = size // 2
    while bit:
        bits.append(bit)
        bit //= 2
    return bits


def double(block, order, axis, size, bit):
    return jnp.concatenate([block, swap(block, axis, size, bit)]), order + [o ^ bit for o in order]


def finish(block, order, axis, size, bits):
    for bit in bits[:-1]:
        block, order = double(block, order, axis, size, bit)
    return [block, swap(block, axis, size, bits[-1])], order + [o ^ bits[-1] for o in order]


def together(*values):
    return lax.optimization_barrier(values)


def params():
    return pltpu.CompilerParams(vmem_limit_bytes=VMEM_LIMIT)


def run_copies(copies):
    for copy in copies:
        copy.start()
    for copy in copies:
        copy.wait()


def prepare(hidden, w_query, w_key, w_value, n_dp, n_fsdp):
    inner = n_fsdp // 2
    tokens = hidden.shape[0]
    rows_w, q_width = w_query.shape
    head_dim = w_key.shape[1]
    share = rows_w // n_dp
    cols = q_width // 2

    def body(hidden_ref, wq_ref, wk_ref, wv_ref, *rest):
        sent, part, sems = rest[: inner - 1], rest[-2], rest[-1]
        me, dp = lax.axis_index("fsdp"), lax.axis_index("dp")
        first = pl.multiple_of(dp * share, 16)
        rows = pl.ds(first, share)
        pairs = []
        for i in range(2):
            to = part.at[pl.ds(i * (share + share // 2), share)]
            pairs.append((wq_ref.at[rows, pl.ds(i * cols, cols)], to))
            for j, ref in enumerate((wk_ref, wv_ref)):
                to = part.at[pl.ds(share, share // 2), pl.ds((2 * i + j) * head_dim, head_dim)]
                pairs.append((ref.at[pl.ds(first + i * (share // 2), share // 2)], to))
        for k in range(1, inner):
            for side, bit in enumerate((0, inner)):
                start = pl.multiple_of((me ^ k ^ bit) * rows_w, 128)
                pairs.append(
                    (hidden_ref.at[:, pl.ds(start, rows_w)], sent[k - 1].at[:, pl.ds(side * rows_w, rows_w)])
                )
        run_copies([pltpu.make_async_copy(a, b, sems.at[i]) for i, (a, b) in enumerate(pairs)])

    moved = 2 * (tokens * 2 * rows_w * 2 * (inner - 1) + share * (q_width + 2 * head_dim) * 2)
    out = pl.pallas_call(
        body,
        in_specs=[pl.BlockSpec(memory_space=pl.ANY)] * 4,
        out_specs=[pl.BlockSpec(memory_space=pltpu.VMEM)] * inner,
        out_shape=[jax.ShapeDtypeStruct((tokens, 2 * rows_w), BF16)] * (inner - 1)
        + [jax.ShapeDtypeStruct((2 * share + share // 2, cols), BF16)],
        scratch_shapes=[pltpu.SemaphoreType.DMA((6 + 2 * (inner - 1),))],
        compiler_params=params(),
        cost_estimate=pl.CostEstimate(flops=0, bytes_accessed=moved, transcendentals=0),
        name="prepare",
    )(hidden, w_query, w_key, w_value)
    return out[:-1], out[-1]


def multiply(hidden, received, near, far, layout, order, n_fsdp, groups):
    inner = n_fsdp // 2
    tokens = hidden.shape[0]
    cols = sum(wide for _, _, wide in near)
    slots = far[0].shape[0]
    n_dp = slots * len(far)
    rows_w = near[0][0].shape[0]
    share = rows_w // n_dp
    step = 256 if all(g % 256 == 0 for g in groups) else 128
    n_in = inner - 1 + len(near) + len(far)

    def body(hidden_ref, *rest):
        blocks, rest = rest[: inner - 1], rest[inner - 1 :]
        near_refs, rest = rest[: len(near)], rest[len(near) :]
        far_refs, rest = rest[: len(far)], rest[len(far) :]
        outs = rest[:-3]
        x_all, w_all, sems = rest[-3:]
        me, dp = lax.axis_index("fsdp"), lax.axis_index("dp")
        pairs = []
        for side, bit in enumerate((0, inner)):
            start = pl.multiple_of((me ^ bit) * rows_w, 128)
            pairs.append(
                (
                    hidden_ref.at[:, pl.ds(start, rows_w)],
                    x_all.at[pl.ds(0, tokens), pl.ds(side * rows_w, rows_w)],
                )
            )
        for k in range(1, inner):
            pairs.append((blocks[k - 1], x_all.at[pl.ds(k * tokens, tokens)]))
        to = 0
        for ref, (_, start, wide) in zip(near_refs, near):
            pairs.append((ref.at[:, pl.ds(start, wide)], w_all.at[pl.ds(0, rows_w), pl.ds(to, wide)]))
            to += wide
        for slot, o in enumerate(order):
            block = far_refs[slot // slots].at[slot % slots]
            for row, col, rows, wide, to_row, to_col in layout:
                to = pl.multiple_of(rows_w + (dp ^ o) * share + to_row, 16)
                piece = block.at[pl.ds(row, rows), pl.ds(col, wide)]
                pairs.append((piece, w_all.at[pl.ds(to, rows), pl.ds(to_col, wide)]))
        run_copies([pltpu.make_async_copy(a, b, sems.at[i]) for i, (a, b) in enumerate(pairs)])

        base = 0
        for g, wide in enumerate(groups):

            @pl.loop(0, wide // step)
            def _(n, g=g, base=base):
                at = pl.multiple_of(n * step, 128)
                product = jnp.dot(
                    x_all[...], w_all[:, pl.ds(base + at, step)], preferred_element_type=F32
                )
                for k in range(inner):
                    outs[g * inner + k][:, pl.ds(at, step)] = product[k * tokens : (k + 1) * tokens]

            base += wide

    copies = 2 + (inner - 1) + len(near) + n_dp * len(layout)
    moved = inner * tokens * 2 * rows_w * 2 + 2 * rows_w * cols * 2 + inner * tokens * cols * 4
    out = pl.pallas_call(
        body,
        in_specs=[pl.BlockSpec(memory_space=pl.ANY)] * (1 + n_in),
        out_specs=[pl.BlockSpec(memory_space=pltpu.VMEM)] * (inner * len(groups)),
        out_shape=[jax.ShapeDtypeStruct((tokens, g), F32) for g in groups for _ in range(inner)],
        scratch_shapes=[
            pltpu.VMEM((inner * tokens, 2 * rows_w), BF16),
            pltpu.VMEM((2 * rows_w, cols), BF16),
            pltpu.SemaphoreType.DMA((copies,)),
        ],
        compiler_params=params(),
        cost_estimate=pl.CostEstimate(
            flops=2 * inner * tokens * 2 * rows_w * cols, bytes_accessed=moved, transcendentals=0
        ),
        name="multiply",
    )(hidden, *received, *[array for array, _, _ in near], *far)
    return [list(out[g * inner : (g + 1) * inner]) for g in range(len(groups))]


def attend(lengths, terms, d_attn, first_head, cache, group, g_order, sums):
    tokens = d_attn.shape[0]
    n_blocks, block, head_dim = cache[0].shape
    n_convs = lengths.shape[1]
    scale = head_dim ** (-0.5)
    to_log2 = scale * math.log2(math.e)
    n_heads = terms[0].shape[1] // head_dim
    lanes = n_heads * tokens
    n_cache = n_blocks * block
    n_group = n_blocks * tokens
    slots = n_blocks // len(group)
    chunk = min(512, n_cache)
    n_part, n_sum = len(terms), len(sums)
    dims = (((1,), (1,)), ((), ()))
    spans = [(at, chunk) for at in range(0, n_cache, chunk)]
    spans += [(n_cache + i * slots * tokens, slots * tokens) for i in range(len(group))]
    n_first = n_cache // chunk

    def tiles(value):
        return value.reshape(value.shape[0] // 8, 8, lanes)

    def body(len_ref, d_ref, *rest):
        cache_refs, rest = rest[:2], rest[2:]
        group_refs, rest = rest[: len(group)], rest[len(group) :]
        part_refs, rest = rest[:n_part], rest[n_part:]
        sum_refs, rest = rest[:n_sum], rest[n_sum:]
        keep_ref, give_ref, out_ref, s_ref, p_ref, q_ref, dq_ref, ck_ref, cv_ref, sems = rest
        me, dp = lax.axis_index("fsdp"), lax.axis_index("dp")
        odd = dp % 2

        @pl.when(odd == 0)
        def _():
            pltpu.make_async_copy(cache_refs[0], ck_ref, sems.at[0]).start()
            pltpu.make_async_copy(cache_refs[1], cv_ref, sems.at[1]).start()

        @pl.when(odd == 1)
        def _():
            pltpu.make_async_copy(cache_refs[1], ck_ref, sems.at[0]).start()
            pltpu.make_async_copy(cache_refs[0], cv_ref, sems.at[1]).start()

        for h in range(n_heads):
            at = slice(h * head_dim, (h + 1) * head_dim)
            rows = pl.ds(h * tokens, tokens)
            q = part_refs[0][:, at]
            for ref in part_refs[1:]:
                q = q + ref[:, at]
            q_ref[rows] = q.astype(BF16)
            at = (first_head + h) * head_dim
            dq_ref[rows] = d_ref[:, at : at + head_dim]

        q_pos = me * tokens + lax.broadcasted_iota(jnp.int32, (1, lanes), 1) % tokens
        begin = jnp.zeros((1, lanes), jnp.int32)
        end = jnp.int32(0)
        for i in range(n_convs):
            end = end + len_ref[0, i]
            begin = jnp.where(end <= q_pos, end, begin)

        def group_rows(i, at):
            return group_refs[i][...].reshape(slots * tokens, 2 * head_dim)[:, at : at + head_dim]

        def cache_rows(ref, i):
            return ref[...].reshape(n_cache, head_dim)[i * chunk : (i + 1) * chunk]

        for i in range(len(group)):
            at, size = spans[n_first + i]
            s = lax.dot_general(group_rows(i, 0), q_ref[...], dims, preferred_element_type=F32)
            for j in range(slots):
                pos = (me ^ g_order[i * slots + j]) * tokens
                pos = pos + lax.broadcasted_iota(jnp.int32, (tokens, lanes), 0)
                allowed = (pos <= q_pos) & (pos >= begin)
                here = s[j * tokens : (j + 1) * tokens]
                s_ref[pl.ds(at + j * tokens, tokens)] = jnp.where(allowed, here, -jnp.inf)

        pltpu.make_async_copy(cache_refs[0], ck_ref, sems.at[0]).wait()
        pltpu.make_async_copy(cache_refs[1], cv_ref, sems.at[1]).wait()
        for i in range(n_first):
            at, size = spans[i]
            s_ref[pl.ds(at, size)] = lax.dot_general(
                cache_rows(ck_ref, i), q_ref[...], dims, preferred_element_type=F32
            )

        tops, totals = [], []
        for at, size in spans:
            top = jnp.max(tiles(s_ref[pl.ds(at, size)]), axis=0)
            top = jnp.maximum(top, -1e30)
            e = jnp.exp2((tiles(s_ref[pl.ds(at, size)]) - top) * to_log2)
            s_ref[pl.ds(at, size)] = e.reshape(size, lanes)
            tops.append(top)
            totals.append(jnp.sum(e, axis=0))
        top = functools.reduce(jnp.maximum, tops)
        top = jnp.max(top, axis=0, keepdims=True)
        factors = [jnp.exp2((own - top) * to_log2) for own in tops]
        total = functools.reduce(lambda a, b: a + b, [t * f for t, f in zip(totals, factors)])
        inv = 1.0 / jnp.sum(total, axis=0, keepdims=True)
        factors = [f * inv for f in factors]

        delta = jnp.zeros((8, lanes), F32)
        for i in range(len(group)):
            at, size = spans[n_first + i]
            d_prob = lax.dot_general(
                group_rows(i, head_dim), dq_ref[...], dims, preferred_element_type=F32
            )
            p = tiles(s_ref[pl.ds(at, size)]) * factors[n_first + i]
            delta = delta + jnp.sum(p.astype(BF16).astype(F32) * tiles(d_prob), axis=0)
        for i in range(n_first):
            at, size = spans[i]
            p_ref[pl.ds(at, size)] = lax.dot_general(
                cache_rows(cv_ref, i), dq_ref[...], dims, preferred_element_type=F32
            )
            p = (tiles(s_ref[pl.ds(at, size)]) * factors[i]).reshape(size, lanes).astype(BF16)
            delta = delta + jnp.sum(tiles(p.astype(F32)) * tiles(p_ref[pl.ds(at, size)]), axis=0)
            out_ref[1 - odd, pl.ds(at, size)] = jnp.dot(p, dq_ref[...], preferred_element_type=F32)
        delta = jnp.sum(delta, axis=0, keepdims=True)
        for i in range(n_first):
            at, size = spans[i]
            p = tiles(s_ref[pl.ds(at, size)]) * factors[i]
            ds = p * (tiles(p_ref[pl.ds(at, size)]) - delta)
            ds = ds.reshape(size, lanes).astype(BF16)
            g = jnp.dot(ds, q_ref[...], preferred_element_type=F32) * scale
            out_ref[odd, pl.ds(at, size)] = g

        for i, ref in enumerate((keep_ref, give_ref)):
            value = sum_refs[i][...] + out_ref[i] if n_sum else out_ref[i]
            ref[...] = value.astype(ref.dtype)

    flops = 2 * lanes * head_dim * (5 * n_cache + 2 * n_group)
    return pl.pallas_call(
        body,
        in_specs=[pl.BlockSpec(memory_space=pltpu.SMEM)]
        + [pl.BlockSpec(memory_space=pltpu.VMEM)]
        + [pl.BlockSpec(memory_space=pl.ANY)] * 2
        + [pl.BlockSpec(memory_space=pltpu.VMEM)] * (len(group) + n_part + n_sum),
        out_specs=[pl.BlockSpec(memory_space=pltpu.VMEM)] * 2,
        out_shape=[
            jax.ShapeDtypeStruct((n_cache, head_dim), F32),
            jax.ShapeDtypeStruct((n_cache, head_dim), BF16 if n_sum else F32),
        ],
        scratch_shapes=[
            pltpu.VMEM((2, n_cache, head_dim), F32),
            pltpu.VMEM((n_cache + n_group, lanes), F32),
            pltpu.VMEM((n_cache, lanes), F32),
            pltpu.VMEM((lanes, head_dim), BF16),
            pltpu.VMEM((lanes, head_dim), BF16),
            pltpu.VMEM((n_blocks, block, head_dim), BF16),
            pltpu.VMEM((n_blocks, block, head_dim), BF16),
            pltpu.SemaphoreType.DMA((2,)),
        ],
        compiler_params=params(),
        cost_estimate=pl.CostEstimate(
            flops=flops,
            bytes_accessed=12 * n_cache * head_dim,
            transcendentals=lanes * (n_cache + n_group),
        ),
        name="attend",
    )(lengths, d_attn, *cache, *group, *terms, *sums)


def make_on_device(n_dp, n_fsdp):
    inner = n_fsdp // 2

    def on_device(hidden, d_attn, w_query, w_key, w_value, cache_keys, cache_values, lengths):
        dp = lax.axis_index("dp")
        head_dim = w_key.shape[1]
        q_width = w_query.shape[1]
        even = dp % 2 == 0
        f_bits, d_bits = bits_down(n_fsdp), bits_down(n_dp)

        def from_owners(products):
            return [products[0]] + [swap(x, "fsdp", n_fsdp, k + 1) for k, x in enumerate(products[1:])]

        cuts = [(0, q_width // 2), (q_width // 2, q_width // 2)]
        sent, part = prepare(hidden, w_query, w_key, w_value, n_dp, n_fsdp)
        received = [swap(block, "fsdp", n_fsdp, k + 1) for k, block in enumerate(sent)]
        part = swap(part, "fsdp", n_fsdp, inner)
        share = w_query.shape[0] // n_dp
        cut = share + share // 2
        part_a, part_b = part[:cut], part[cut:]
        far_a, order = double(part_a[None], [0], "dp", n_dp, d_bits[0])
        cache = jnp.where(even, cache_keys, cache_values)[None]
        cache, f_order = double(cache, [0], "fsdp", n_fsdp, f_bits[0])
        cache, far_a, *received = together(cache, far_a, *received)
        far_b, _ = double(part_b[None], [0], "dp", n_dp, d_bits[0])
        far_a, d_order = finish(far_a, order, "dp", n_dp, d_bits[1:])
        cache, f_order = double(cache, f_order, "fsdp", n_fsdp, f_bits[1])
        cache, far_a[1] = together(cache, far_a[1])
        kv, (at_a, wide_a), (at_b, wide_b) = 2 * head_dim, *cuts
        near_a = [(w_key, 0, head_dim), (w_value, 0, head_dim), (w_query, at_a, wide_a)]
        layout_a = [(0, 0, share, wide_a, 0, kv)]
        layout_a += [(share, i * kv, share // 2, kv, i * (share // 2), 0) for i in range(2)]
        out_kv, out_a = multiply(
            hidden, received, near_a, far_a, layout_a, d_order, n_fsdp, (kv, wide_a)
        )
        for bit in f_bits[2:]:
            cache, f_order = double(cache, f_order, "fsdp", n_fsdp, bit)
        far_b, cache, out_kv[0] = together(far_b, cache, out_kv[0])
        far_b, _ = finish(far_b, order, "dp", n_dp, d_bits[1:])
        parts_kv = from_owners(out_kv)
        parts_a = from_owners(out_a)
        own = functools.reduce(lambda a, b: a + b, parts_kv).astype(BF16)
        far_b[1], own = together(far_b[1], own)
        group, _ = double(own[None], [0], "fsdp", n_fsdp, inner)
        near_b, layout_b = [(w_query, at_b, wide_b)], [(0, 0, share, wide_b, 0, 0)]
        (out_b,) = multiply(
            hidden, received, near_b, far_b, layout_b, d_order, n_fsdp, (wide_b,)
        )
        group, cache, *tied = together(group, cache, *out_b, *parts_a[1:])
        out_b, parts_a[1:] = tied[:inner], tied[inner:]
        group = [group] + [swap(group, "fsdp", n_fsdp, k) for k in range(1, inner)]
        g_order = [o for k in range(inner) for o in (k, k ^ inner)]
        cache = [cache, swap(cache, "dp", n_dp, 1)]
        parts_b = from_owners(out_b)
        first = cuts[0][1] // head_dim
        sums = attend(lengths, parts_a, d_attn, 0, cache, group, g_order, ())
        keep, give = attend(lengths, parts_b, d_attn, first, cache, group, g_order, sums)

        given = swap(give, "dp", n_dp, 1)
        size = keep.shape[0] // n_fsdp
        mine = keep[:size] + given[:size].astype(F32)
        far = [slot for slot in range(n_fsdp) if f_order[slot] >= inner]
        near = [slot for slot in range(1, n_fsdp) if f_order[slot] < inner]
        for slot in far[:1] + near + far[:0:-1]:
            rows = slice(slot * size, (slot + 1) * size)
            out = (keep[rows] + given[rows].astype(F32)).astype(BF16)
            mine = mine + swap(out, "fsdp", n_fsdp, f_order[slot]).astype(F32)
        for bit in d_bits[:-1]:
            mine = mine.astype(BF16)
            mine = mine.astype(F32) + swap(mine, "dp", n_dp, bit).astype(F32)
        other = swap(mine, "dp", n_dp, 1)
        return jnp.where(even, mine, other), jnp.where(even, other, mine)

    return on_device


def solution(mesh):
    placed = (
        P(("dp", "fsdp"), None),
        P(("dp", "fsdp"), None),
        P("fsdp", None),
        P("fsdp", None),
        P("fsdp", None),
        P("fsdp", None),
        P("fsdp", None),
        P("dp", None),
    )
    return jax.shard_map(
        make_on_device(mesh.shape["dp"], mesh.shape["fsdp"]),
        mesh=mesh,
        in_specs=placed,
        out_specs=(P("fsdp", None), P("fsdp", None)),
        check_vma=False,
    )
```
